32 devices in a mesh: lon: 8 (over y, x, core), lat: 4 (over z).
Axes of the slice: x: 2, y: 2, z: 4, core: 2. Of those that a mesh axis runs over, the one named last changes fastest.
Arguments:
- temp: float32 [6, 1536, 2048], P(None, 'lat', 'lon'), may hold values from -6 to 6
- salt: float32 [6, 1536, 2048], P(None, 'lat', 'lon'), may hold values from 32 to 36
- east_vel: float32 [6, 1536, 2048], P(None, 'lat', 'lon'), may hold values from -0.2 to 0.2
- north_vel: float32 [6, 1536, 2048], P(None, 'lat', 'lon'), may hold values from -0.2 to 0.2
- land_mask: int32 [1536, 2048], P('lat', 'lon'), may hold values 0 or 1
- ice_mask: int32 [1536, 2048], P('lat', 'lon'), may hold values 0 or 1
- ice_u: float32 [1536, 2048], P('lat', 'lon'), may hold values from -3 to 3
- ice_v: float32 [1536, 2048], P('lat', 'lon'), may hold values from -3 to 3
- ice_pressure_field: float32 [1536, 2048], P('lat', 'lon'), may hold values from 1 to 3
- wind_x: float32 [1536, 2048], P('lat', 'lon'), may hold values from -3 to 3
- wind_y: float32 [1536, 2048], P('lat', 'lon'), may hold values from -3 to 3
Outputs:
- temp_out: float32 [6, 1536, 2048], P(None, 'lat', 'lon')
- salt_out: float32 [6, 1536, 2048], P(None, 'lat', 'lon')
- ice_u_out: float32 [1536, 2048], P('lat', 'lon')
- ice_v_out: float32 [1536, 2048], P('lat', 'lon')
The draws below stay inside these ranges and needn't reach their ends.
All inputs are finite; a program needn't handle non-finite values. No bound on the sum of `land_mask` or of `ice_mask` on one device may be relied on, other than what follows from the above.
Results may differ from the reference program's by a relative error of at most 0.0003.
Values sent between devices are 32-bit elements; how exact they have to be, the bound alone decides.
No kernel may reach another device: no remote copies, remote signals or barrier semaphores. Data moves between devices by JAX's collectives and lax.ppermute only.
A program may use at most 192 MiB of HBM per device.

```python
import math
import jax
import jax.numpy as jnp

LEVELS = 6
SUBCYCLES = 4
GRID_X = 2048
GRID_Y = 1536


def place_ends(drawn, key, least, high):
    spot = [jax.random.randint(jax.random.fold_in(key, axis), (), 0, length) for axis, length in enumerate(drawn.shape)]
    longest = drawn.shape.index(max(drawn.shape))
    neighbour = spot[:longest] + [(spot[longest] + 1) % drawn.shape[longest]] + spot[longest + 1:]
    return drawn.at[tuple(spot)].set(least).at[tuple(neighbour)].set(high)


def levels(rng, shape, shards, smallest, largest):
    gain = 1.0
    for dim, shards_of in shards:
        heights = jax.random.uniform(jax.random.fold_in(jax.random.fold_in(rng, 6), dim), (shards_of,), jnp.float32, smallest / len(shards), largest / len(shards))
        gain = gain * jnp.repeat(jnp.exp(heights), shape[dim] // shards_of).reshape((-1,) + (1,) * (len(shape) - 1 - dim))
    return gain


def normal_values(rng, shape, spread, bound, shards=(), kind=jnp.bfloat16):
    level = levels(rng, shape, shards, -0.22, 0.18) if shards else 1.0
    drawn = jax.random.normal(rng, shape, jnp.float32) * spread * level
    return jnp.minimum(jnp.maximum(drawn, -bound), bound).astype(kind)


def setup_inputs(seed: int = 0) -> dict:
    splits = jax.random.split(jax.random.key(seed), 12)
    temp = normal_values(splits[0], (LEVELS, GRID_Y, GRID_X), 1.0, 6.0, ((1, 4), (2, 8)), jnp.float32)
    salt = jnp.clip(32.0 + 4.0 * jax.random.uniform(splits[1], (LEVELS, GRID_Y, GRID_X), jnp.float32) ** levels(splits[1], (LEVELS, GRID_Y, GRID_X), ((1, 4), (2, 8)), -0.2, 0.2), 32.0, 36.0)
    east_vel = jnp.clip(jax.random.uniform(splits[2], (LEVELS, GRID_Y, GRID_X), jnp.float32, -0.2, 0.2) * levels(splits[2], (LEVELS, GRID_Y, GRID_X), ((1, 4), (2, 8)), -0.4, 0.0), -0.2, 0.2)
    north_vel = jnp.clip(jax.random.uniform(splits[3], (LEVELS, GRID_Y, GRID_X), jnp.float32, -0.2, 0.2) * levels(splits[3], (LEVELS, GRID_Y, GRID_X), ((1, 4), (2, 8)), -0.4, 0.0), -0.2, 0.2)
    land_mask = place_ends((jax.random.randint(splits[4], (GRID_Y, GRID_X), 0, 16) < 15).astype(jnp.int32), jax.random.fold_in(splits[4], 1), 0, 1)
    ice_mask = place_ends((jax.random.randint(splits[5], (GRID_Y, GRID_X), 0, 16) < 15).astype(jnp.int32), jax.random.fold_in(splits[5], 1), 0, 1)
    ice_u = normal_values(splits[6], (GRID_Y, GRID_X), 0.5, 3.0, ((0, 4), (1, 8)), jnp.float32)
    ice_v = normal_values(splits[7], (GRID_Y, GRID_X), 0.5, 3.0, ((0, 4), (1, 8)), jnp.float32)
    ice_pressure_field = jnp.clip(jnp.exp(math.log(3.0) - 1.0986123 * jax.random.uniform(splits[8], (GRID_Y, GRID_X), jnp.float32) ** levels(splits[8], (GRID_Y, GRID_X), ((0, 4), (1, 8)), -0.2, 0.2)), 1.0, 3.0)
    wind_x = normal_values(splits[9], (GRID_Y, GRID_X), 0.5, 3.0, ((0, 4), (1, 8)), jnp.float32)
    wind_y = normal_values(splits[10], (GRID_Y, GRID_X), 0.5, 3.0, ((0, 4), (1, 8)), jnp.float32)
    return {"temp": temp, "salt": salt, "east_vel": east_vel, "north_vel": north_vel, "land_mask": land_mask, "ice_mask": ice_mask, "ice_u": ice_u, "ice_v": ice_v, "ice_pressure_field": ice_pressure_field, "wind_x": wind_x, "wind_y": wind_y}


TIME_STEP = 1.0
RELAX_RATE = 2.0
ELLIPSE_SQ = 4.0
DELTA_FLOOR = 0.25
MOMENTUM_STEP = 0.5
WATER_DRAG = 1.0
CORIOLIS_SCALE = 0.5
HEAT_RATE = 0.1
SALT_RATE = 0.5
FREEZE_SLOPE = 0.054

def advect(tracers, east_face, north_face, ocean_pad):
    face_x = ocean_pad[1:-1, :-1] * ocean_pad[1:-1, 1:]
    face_y = ocean_pad[:-1, 1:-1] * ocean_pad[1:, 1:-1]
    east_part = east_face[..., 1:-1, :-1]
    north_part = north_face[..., :-1, 1:-1]
    flux_x = east_part * jnp.where(east_part > 0, tracers[..., 1:-1, :-1], tracers[..., 1:-1, 1:]) * face_x
    flux_y = north_part * jnp.where(north_part > 0, tracers[..., :-1, 1:-1], tracers[..., 1:, 1:-1]) * face_y
    return tracers[..., 1:-1, 1:-1] - TIME_STEP * (flux_x[..., 1:] - flux_x[..., :-1] + (flux_y[..., 1:, :] - flux_y[..., :-1, :]))

def strain_rates(padded_eastward_velocity, padded_northward_velocity):
    dudx = (padded_eastward_velocity[1:-1, 2:] - padded_eastward_velocity[1:-1, :-2]) * 0.5
    dudy = (padded_eastward_velocity[2:, 1:-1] - padded_eastward_velocity[:-2, 1:-1]) * 0.5
    northward_velocity_xgrad = (padded_northward_velocity[1:-1, 2:] - padded_northward_velocity[1:-1, :-2]) * 0.5
    northward_velocity_ygrad = (padded_northward_velocity[2:, 1:-1] - padded_northward_velocity[:-2, 1:-1]) * 0.5
    return (dudx + northward_velocity_ygrad, dudx - northward_velocity_ygrad, dudy + northward_velocity_xgrad)

def stress_tensor(stress_old, strain, strength, covered_region):
    diverge, tension, shearing = strain
    delta = jnp.sqrt(diverge * diverge + (tension * tension + shearing * shearing) / ELLIPSE_SQ + DELTA_FLOOR)
    zeta = strength / (2.0 * delta)
    first = (stress_old[0] + RELAX_RATE * (2.0 * zeta * diverge - strength)) / (1.0 + RELAX_RATE) * covered_region
    second = (stress_old[1] + RELAX_RATE * (2.0 * zeta * tension / ELLIPSE_SQ)) / (1.0 + RELAX_RATE) * covered_region
    third = (stress_old[2] + RELAX_RATE * (zeta * shearing / ELLIPSE_SQ)) / (1.0 + RELAX_RATE) * covered_region
    return (first, second, third)

def momentum(ice_east, northward_ice_velocity, stress_pad, forcing, coriolis, covered_region):
    sxx = 0.5 * (stress_pad[0] + stress_pad[1])
    syy = 0.5 * (stress_pad[0] - stress_pad[1])
    sxy = stress_pad[2]
    force_x = (sxx[1:-1, 2:] - sxx[1:-1, :-2]) * 0.5 + (sxy[2:, 1:-1] - sxy[:-2, 1:-1]) * 0.5
    force_y = (sxy[1:-1, 2:] - sxy[1:-1, :-2]) * 0.5 + (syy[2:, 1:-1] - syy[:-2, 1:-1]) * 0.5
    wind_east, wind_north, ocean_u, ocean_v = forcing
    right_u = ice_east + MOMENTUM_STEP * (force_x + wind_east + WATER_DRAG * ocean_u)
    right_v = northward_ice_velocity + MOMENTUM_STEP * (force_y + wind_north + WATER_DRAG * ocean_v)
    diagonal = 1.0 + MOMENTUM_STEP * WATER_DRAG
    turning = MOMENTUM_STEP * coriolis
    determ = diagonal * diagonal + turning * turning
    new_east = (diagonal * right_u + turning * right_v) / determ * covered_region
    new_north = (diagonal * right_v - turning * right_u) / determ * covered_region
    return (new_east, new_north)

def wall_pad(values):
    padded = jnp.pad(values, [(0, 0)] * (values.ndim - 2) + [(1, 1), (0, 0)])
    return jnp.concatenate([padded[..., -1:], padded, padded[..., :1]], axis=-1)

def tripole_seam_padding(values, fold_sign, rim_depth):
    top_rows = fold_sign * values[GRID_Y - rim_depth:, :][::-1, ::-1]
    bottom = jnp.zeros((rim_depth, values.shape[1]), values.dtype)
    stacked = jnp.concatenate([bottom, values, top_rows], axis=0)
    return jnp.concatenate([stacked[:, -rim_depth:], stacked, stacked[:, :rim_depth]], axis=1)

def reference(temp, salt, east_vel, north_vel, land_mask, ice_mask, ice_u, ice_v, ice_pressure_field, wind_x, wind_y):
    ocean_cells = land_mask.astype(jnp.float32)
    covered_region = ocean_cells * ice_mask.astype(jnp.float32)
    ocean_pad = wall_pad(ocean_cells)
    moved_temp = []
    moved_salt = []
    for layer_index in range(LEVELS):
        tracers = wall_pad(jnp.stack([temp[layer_index], salt[layer_index]]))
        result = advect(tracers, wall_pad(east_vel[layer_index]), wall_pad(north_vel[layer_index]), ocean_pad)
        moved_temp.append(result[0])
        moved_salt.append(result[1])
    moved_temp = jnp.stack(moved_temp)
    moved_salt = jnp.stack(moved_salt)
    surface_t = moved_temp[0]
    surface_s = moved_salt[0]
    ocean_u = east_vel[0]
    ocean_v = north_vel[0]
    global_rows = jnp.arange(GRID_Y, dtype=jnp.int32)
    coriolis = CORIOLIS_SCALE * (2 * global_rows + 1 - GRID_Y).astype(jnp.float32)[:, None] / GRID_Y
    forcing = (wind_x, wind_y, ocean_u, ocean_v)
    ice_east = ice_u * covered_region
    northward_ice_velocity = ice_v * covered_region
    zero_field = jnp.zeros_like(ice_east)
    current_stress = (zero_field, zero_field, zero_field)
    for subcycle in range(SUBCYCLES):
        padded_eastward_velocity = tripole_seam_padding(ice_east, -1.0, 1)
        padded_northward_velocity = tripole_seam_padding(northward_ice_velocity, -1.0, 1)
        current_stress = stress_tensor(current_stress, strain_rates(padded_eastward_velocity, padded_northward_velocity), ice_pressure_field, covered_region)
        stress_pad = jnp.stack([tripole_seam_padding(member, 1.0, 1) for member in current_stress])
        ice_east, northward_ice_velocity = momentum(ice_east, northward_ice_velocity, stress_pad, forcing, coriolis, covered_region)
    slip_u = ice_east - ocean_u
    slip_v = northward_ice_velocity - ocean_v
    heat = HEAT_RATE * covered_region * (1.0 + WATER_DRAG * (slip_u * slip_u + slip_v * slip_v)) * (surface_t + FREEZE_SLOPE * surface_s)
    temp_out = moved_temp.at[0].set(surface_t - heat)
    salt_out = moved_salt.at[0].set(surface_s - SALT_RATE * heat)
    return (temp_out, salt_out, ice_east, northward_ice_velocity)
```

```python
import jax
import jax.numpy as jnp
from jax import lax
from jax.experimental import pallas as pl
from jax.experimental.pallas import tpu as pltpu
from jax.sharding import PartitionSpec as P

SUBCYCLES = 4
HEAT_RATE = 0.1
SALT_RATE = 0.5
FREEZE_SLOPE = 0.054
DIAGONAL = 1.5
HALO = 2 * SUBCYCLES
LANES = 128
SUBLANES = 8
ICE = 6
FOLD_SIGN = (-1.0, -1.0, 1.0, 1.0, -1.0, -1.0)
TRACER_LANE = 64
MIB = 1 << 20
F32 = jnp.float32


def lane_ids():
    return lax.broadcasted_iota(jnp.int32, (SUBLANES, LANES), 1)


def sublane_ids():
    return lax.broadcasted_iota(jnp.int32, (SUBLANES, LANES), 0)


def turn(x, shift, axis=1):
    shift = shift % x.shape[axis]
    return pltpu.roll(x, shift, axis) if shift else x


def ice_fields(land, ice, u, v, pressure, wind_x, wind_y, ocean_u, ocean_v):
    covered = land.astype(F32) * ice.astype(F32)
    return (u * covered, v * covered, pressure, covered, wind_x + ocean_u, wind_y + ocean_v)


def east_columns(fields, lane):
    packed = jnp.zeros((SUBLANES, LANES), F32)
    for f, tile in enumerate(fields):
        start = HALO * f + 2 * HALO
        moved = turn(tile, start - (LANES - HALO))
        packed = jnp.where((lane >= start) & (lane < start + HALO), moved, packed)
    return packed


def west_columns(fields, lane):
    packed = jnp.zeros((SUBLANES, LANES), F32)
    for f, tile in enumerate(fields):
        start = HALO * f
        packed = jnp.where((lane >= start) & (lane < start + HALO), turn(tile, start), packed)
    return packed


def rows_kernel(levels, *refs):
    tops, bottoms = refs[0:12], refs[12:24]
    first_ref, second_ref = refs[24:26]
    even = lax.rem(lax.axis_index("lat"), 2) == 0

    def message(group, row, northward):
        land, ice, u, v, pressure, wind_x, wind_y, east, north, temp, salt = (
            r for r in group[:11]
        )
        fields = ice_fields(
            land[...], ice[...], u[...], v[...], pressure[...], wind_x[...], wind_y[...],
            east[0], north[0],
        )
        sea = land[row : row + 1, :].astype(F32)
        parts = list(fields) + [temp[:, row, :], salt[:, row, :]]
        if northward:
            parts.append(north[:, row, :] * sea)
        else:
            parts.append(jnp.broadcast_to(sea, (levels, sea.shape[1])))
        return parts

    top = message(tops, SUBLANES - 1, True)
    bottom = message(bottoms, 0, False)
    at = 0
    for t, b in zip(top, bottom):
        size = t.shape[0]
        first_ref[at : at + size, :] = jnp.where(even, t, b)
        second_ref[at : at + size, :] = jnp.where(even, b, t)
        at += size
    pad = first_ref.shape[0] - at
    if pad:
        first_ref[at:, :] = jnp.zeros((pad, first_ref.shape[1]), F32)
        second_ref[at:, :] = jnp.zeros((pad, second_ref.shape[1]), F32)


def pack_rows(arrays, levels, rows, cols, height):
    temp, salt, east, north, land, ice, u, v, pressure, wind_x, wind_y = arrays
    operands = [land, ice, u, v, pressure, wind_x, wind_y, east, north, temp, salt, land]
    last = rows // SUBLANES - 1

    def spec(array, block, count):
        if array.ndim == 2:
            return pl.BlockSpec((SUBLANES, cols), lambda _: (block, 0))
        return pl.BlockSpec((count, SUBLANES, cols), lambda _: (0, block, 0))

    counts = [1] * 7 + [1, levels, levels, levels, 1]
    specs = [spec(a, last, c) for a, c in zip(operands, counts)]
    specs += [spec(a, 0, c) for a, c in zip(operands, counts)]
    out = jax.ShapeDtypeStruct((height, cols), F32)
    return pl.pallas_call(
        lambda *refs: rows_kernel(levels, *refs),
        grid=(1,),
        in_specs=specs,
        out_specs=[pl.BlockSpec((height, cols), lambda _: (0, 0))] * 2,
        out_shape=[out, out],
        name="edge_rows",
        cost_estimate=pl.CostEstimate(flops=100000, bytes_accessed=1 << 20, transcendentals=0),
    )(*operands, *operands)


def columns_kernel(levels, land, ice, u, v, pressure, wind_x, wind_y, east, north, temp, salt,
                   east_out, west_out):
    lane = lane_ids()
    tracers = 2 * levels
    last = land.shape[1] - LANES
    first_lane = TRACER_LANE
    mask_lane = TRACER_LANE + tracers

    def step(k, carry):
        rows = pl.ds(pl.multiple_of(k * SUBLANES, SUBLANES), SUBLANES)
        for side, out in ((last, east_out), (0, west_out)):
            cols = slice(side, side + LANES)
            fields = ice_fields(
                land[rows, cols], ice[rows, cols], u[rows, cols], v[rows, cols],
                pressure[rows, cols], wind_x[rows, cols], wind_y[rows, cols],
                east[0, rows, cols], north[0, rows, cols],
            )
            eastward = out is east_out
            source = LANES - 1 if eastward else 0
            packed = (east_columns if eastward else west_columns)(fields, lane)
            for f in range(tracers):
                tile = temp[f, rows, cols] if f < levels else salt[f - levels, rows, cols]
                packed = jnp.where(lane == first_lane + f, turn(tile, first_lane + f - source), packed)
            sea = jnp.broadcast_to(
                land[rows, side + source : side + source + 1].astype(F32), (SUBLANES, LANES)
            )
            if eastward:
                speeds = jnp.zeros((SUBLANES, LANES), F32)
                for f in range(levels):
                    moved = turn(east[f, rows, cols], mask_lane + f - source)
                    speeds = jnp.where(lane == mask_lane + f, moved, speeds)
                speeds = speeds + turn(speeds, levels)
                packed = jnp.where(
                    (lane >= mask_lane) & (lane < mask_lane + tracers), speeds * sea, packed
                )
            else:
                packed = jnp.where((lane >= mask_lane) & (lane < mask_lane + tracers), sea, packed)
            out[rows, :] = packed
        return carry

    lax.fori_loop(0, land.shape[0] // SUBLANES, step, 0, unroll=2)


def pack_columns(arrays, levels, rows, cols):
    temp, salt, east, north, land, ice, u, v, pressure, wind_x, wind_y = arrays
    height = next(h for h in (64, 32, 16) if rows % h == 0)
    flat = pl.BlockSpec((height, cols), lambda k: (k, 0))
    deep = pl.BlockSpec((levels, height, cols), lambda k: (0, k, 0))
    surface = pl.BlockSpec((1, height, cols), lambda k: (0, k, 0))
    out = jax.ShapeDtypeStruct((rows + 2 * HALO, LANES), F32)
    return pl.pallas_call(
        lambda *refs: columns_kernel(levels, *refs),
        grid=(rows // height,),
        in_specs=[flat] * 7 + [deep, surface, deep, deep],
        out_specs=[pl.BlockSpec((height, LANES), lambda k: (k, 0))] * 2,
        out_shape=[out, out],
        name="edge_columns",
        compiler_params=pltpu.CompilerParams(vmem_limit_bytes=32 * MIB),
        cost_estimate=pl.CostEstimate(flops=5000000, bytes_accessed=10 << 20, transcendentals=0),
    )(land, ice, u, v, pressure, wind_x, wind_y, east, north, temp, salt)


def halo_kernel(levels, first, second, east_in, west_in, halo_ref, east_out, west_out):
    lat = lax.axis_index("lat")
    even = lax.rem(lat, 2) == 0
    top = lat == lax.axis_size("lat") - 1
    lane, sublane = lane_ids(), sublane_ids()
    tiles = halo_ref.shape[2] // LANES
    south_fields, north_fields = [], []
    for f in range(ICE):
        rows = slice(HALO * f, HALO * (f + 1))
        north_row, south_row = [], []
        for t in range(tiles):
            cols = slice(LANES * t, LANES * (t + 1))
            mirror = slice(LANES * (tiles - 1 - t), LANES * (tiles - t))
            south = jnp.where(even, second[rows, cols], first[rows, cols])
            plain = jnp.where(even, first[rows, cols], second[rows, cols])
            turned = jnp.take_along_axis(second[rows, mirror], LANES - 1 - lane, axis=1)
            turned = jnp.take_along_axis(turned, SUBLANES - 1 - sublane, axis=0)
            north = jnp.where(top, turned * FOLD_SIGN[f], plain)
            halo_ref[0, rows, cols] = south
            halo_ref[1, rows, cols] = north
            south_row.append(south)
            north_row.append(north)
        south_fields.append(south_row)
        north_fields.append(north_row)
    rest = slice(HALO * ICE, halo_ref.shape[1])
    halo_ref[0, rest, :] = jnp.where(even, second[rest, :], first[rest, :])
    halo_ref[1, rest, :] = jnp.where(top, 0.0, jnp.where(even, first[rest, :], second[rest, :]))
    for at, fields in ((0, south_fields), (HALO, north_fields)):
        east_out[at : at + HALO, :] = east_columns([f[-1] for f in fields], lane)
        west_out[at : at + HALO, :] = west_columns([f[0] for f in fields], lane)


def merge_halo(first, second, east_msg, west_msg, levels):
    height, cols = first.shape
    rows = east_msg.shape[0] - 2 * HALO
    tail = pl.BlockSpec((2 * HALO, LANES), lambda _: (rows // (2 * HALO), 0))
    whole = pl.BlockSpec((height, cols), lambda _: (0, 0))
    return pl.pallas_call(
        lambda *refs: halo_kernel(levels, *refs),
        grid=(1,),
        in_specs=[whole, whole] + [pl.BlockSpec(memory_space=pl.ANY)] * 2,
        out_specs=[pl.BlockSpec((2, height, cols), lambda _: (0, 0, 0)), tail, tail],
        out_shape=[
            jax.ShapeDtypeStruct((2, height, cols), F32),
            jax.ShapeDtypeStruct(east_msg.shape, F32),
            jax.ShapeDtypeStruct(west_msg.shape, F32),
        ],
        input_output_aliases={2: 1, 3: 2},
        name="halo_rows",
        cost_estimate=pl.CostEstimate(flops=100000, bytes_accessed=1 << 19, transcendentals=0),
    )(first, second, east_msg, west_msg)


def advect_kernel(levels, tiles, *refs):
    temp, salt, east, north = (refs[tiles * n : tiles * (n + 1)] for n in range(4))
    land = refs[4 * tiles : 5 * tiles]
    halo, temp_out, salt_out, mask_e, mask_n = refs[5 * tiles :]
    level = pl.program_id(0)
    count = temp[0].shape[1] // SUBLANES
    lane, sublane = lane_ids(), sublane_ids()
    tracer_row = HALO * ICE
    extra_row = tracer_row + 2 * levels

    def spread(ref, i, *lead):
        return ref[(*lead, pl.ds(i, SUBLANES, stride=count), slice(None))]

    def row(side, index, t):
        cols = slice(LANES * t, LANES * (t + 1))
        return jnp.broadcast_to(halo[side, index : index + 1, cols], (SUBLANES, LANES))

    def level_row(side, index, t):
        picked = row(side, index, t)
        for l in range(1, levels):
            picked = jnp.where(level == l, row(side, index + l, t), picked)
        return picked

    def from_next(values, keep):
        turned = [turn(v, -1) for v in values]
        return [
            jnp.where(lane == LANES - 1, turned[t + 1], turned[t]) if t + 1 < tiles else turned[t]
            for t in range(tiles)
        ]

    def from_last(values):
        turned = [turn(v, 1) for v in values]
        return [jnp.where(lane == 0, turned[t - 1], turned[t]) for t in range(tiles)]

    @pl.when(level == 0)
    def _():
        def sea_at(i):
            return [spread(r, i).astype(F32) for r in land]

        def put(i, here, above):
            beside = from_next(here, None)
            for t in range(tiles):
                face = here[t] * beside[t]
                if t == tiles - 1:
                    face = jnp.where(lane == LANES - 1, 0.0, face)
                mask_e[t, i] = face
                mask_n[t, i] = here[t] * above[t]

        def body(i, carry):
            put(i, sea_at(i), sea_at(i + 1))
            return carry

        lax.fori_loop(0, count - 1, body, 0)
        wrapped = [
            jnp.where(sublane == SUBLANES - 1, row(1, extra_row, t), turn(v, -1, 0))
            for t, v in enumerate(sea_at(0))
        ]
        put(count - 1, sea_at(count - 1), wrapped)

    def north_flux(speed, here, above):
        return [
            speed[t] * jnp.where(speed[t] > 0, here[t], above[t]) for t in range(tiles)
        ]

    sources = ((temp, temp_out, 0), (salt, salt_out, levels))

    def tracer_at(source, i):
        return [spread(r, i, 0) for r in source]

    def speeds(i):
        return (
            [spread(east[t], i, 0) * mask_e[t, i] for t in range(tiles)],
            [spread(north[t], i, 0) * mask_n[t, i] for t in range(tiles)],
        )

    def advance(i, here, above, flux_below, fast_e, flux_n, out):
        beside = from_next(here, None)
        flux_e = [fast_e[t] * jnp.where(fast_e[t] > 0, here[t], beside[t]) for t in range(tiles)]
        before = from_last(flux_e)
        for t in range(tiles):
            value = here[t] - ((flux_e[t] - before[t]) + (flux_n[t] - flux_below[t]))
            out[0, t, pl.ds(i, SUBLANES, stride=count), :] = value

    last = count - 1
    last_e, last_n = speeds(last)
    starts, ends = [], []
    for source, out, at in sources:
        low, high = tracer_at(source, 0), tracer_at(source, last)
        above = [
            jnp.where(sublane == SUBLANES - 1, level_row(1, tracer_row + at, t), turn(low[t], -1, 0))
            for t in range(tiles)
        ]
        flux_top = north_flux(last_n, high, above)
        below = []
        for t in range(tiles):
            speed = level_row(0, extra_row, t) * spread(land[t], 0).astype(F32)
            south = level_row(0, tracer_row + at, t)
            entering = speed * jnp.where(speed > 0, south, low[t])
            below.append(jnp.where(sublane == 0, entering, turn(flux_top[t], 1, 0)))
        starts.append((low, below))
        ends.append((above, flux_top))

    def body(i, carry):
        fast_e, fast_n = speeds(i)
        result = []
        for (here, below), (source, out, _) in zip(carry, sources):
            above = tracer_at(source, i + 1)
            flux_n = north_flux(fast_n, here, above)
            advance(i, here, above, below, fast_e, flux_n, out)
            result.append((above, flux_n))
        return tuple(result)

    carry = lax.fori_loop(0, last, body, tuple(starts))
    for (here, below), (above, flux_top), (_, out, _) in zip(carry, ends, sources):
        advance(last, here, above, below, last_e, flux_top, out)


def advect(arrays, halo, levels, rows, cols):
    temp, salt, east, north, land = arrays[:5]
    tiles = cols // LANES

    def deep(t):
        return pl.BlockSpec((1, rows, LANES), lambda l: (l, 0, t))

    def flat(t):
        return pl.BlockSpec((rows, LANES), lambda l: (0, t))

    specs = [deep(t) for _ in range(4) for t in range(tiles)] + [flat(t) for t in range(tiles)]
    operands = [a for a in (temp, salt, east, north, land) for _ in range(tiles)]
    out = jax.ShapeDtypeStruct((levels, tiles, rows, LANES), F32)
    return pl.pallas_call(
        lambda *refs: advect_kernel(levels, tiles, *refs),
        grid=(levels,),
        in_specs=specs + [pl.BlockSpec(halo.shape, lambda l: (0, 0, 0))],
        out_specs=[pl.BlockSpec((1, tiles, rows, LANES), lambda l: (l, 0, 0, 0))] * 2,
        out_shape=[out, out],
        scratch_shapes=[pltpu.VMEM((tiles, rows // SUBLANES, SUBLANES, LANES), F32)] * 2,
        name="advect",
        compiler_params=pltpu.CompilerParams(vmem_limit_bytes=32 * MIB),
        cost_estimate=pl.CostEstimate(flops=30000000, bytes_accessed=16 << 20, transcendentals=0),
    )(*operands, halo)


def ice_kernel(levels, rows, cols, row_total, *refs):
    (land, ice, u_in, v_in, pressure, wind_x, wind_y, east, north, halo, east_own, west_own,
     from_west, from_east, temp_raw, salt_raw, temp_out, salt_out, u_out, v_out,
     ints, floats, messages, raw, done, vel_u, vel_v, str_a, str_b, str_c,
     third, force, push_x, push_y, turn_a, turn_b, edge_w, edge_e,
     in_sem, msg_sem, raw_sem, out_sem, vel_sem) = refs
    tiles = cols // LANES
    extended = rows + 2 * HALO
    count = extended // SUBLANES
    tracers = 2 * levels
    lane = lane_ids()
    own = pl.ds(HALO, rows)
    wide = tiles + 1

    copies = []
    for n, ref in enumerate((land, ice)):
        for t in range(tiles):
            cut = pl.ds(LANES * t, LANES)
            copies.append((ref.at[:, cut], ints.at[n, t, own, :]))
    for n, ref in enumerate((u_in, v_in, pressure, wind_x, wind_y, east, north)):
        for t in range(tiles):
            cut = pl.ds(LANES * t, LANES)
            source = ref.at[0, :, cut] if ref is east or ref is north else ref.at[:, cut]
            copies.append((source, floats.at[n, t, own, :]))
    loads = [pltpu.make_async_copy(a, b, in_sem.at[k]) for k, (a, b) in enumerate(copies)]
    copies = []
    for n, ref in enumerate((from_west, from_east, east_own, west_own)):
        copies.append((ref.at[pl.ds(0, rows), :], messages.at[n, own, :]))
        if n < 2:
            copies.append((ref.at[pl.ds(rows, HALO), :], messages.at[n, pl.ds(0, HALO), :]))
            copies.append(
                (ref.at[pl.ds(rows + HALO, HALO), :], messages.at[n, pl.ds(rows + HALO, HALO), :])
            )
    loads += [pltpu.make_async_copy(a, b, msg_sem.at[k]) for k, (a, b) in enumerate(copies)]
    for copy in loads:
        copy.start()
    raw_loads = []
    for f in range(tracers):
        source = temp_raw.at[f] if f < levels else salt_raw.at[f - levels]
        raw_loads.append(pltpu.make_async_copy(source, raw.at[f], raw_sem.at[f]))
        raw_loads[-1].start()

    for side, at in ((0, 0), (1, rows + HALO)):
        put = slice(at, at + HALO)
        for t in range(tiles):
            cut = slice(LANES * t, LANES * (t + 1))

            def field(f):
                return halo[side, HALO * f : HALO * (f + 1), cut]

            ints[0, t, put, :] = field(3).astype(jnp.int32)
            ints[1, t, put, :] = jnp.ones((HALO, LANES), jnp.int32)
            for n, f in ((0, 0), (1, 1), (2, 2), (3, 4), (4, 5)):
                floats[n, t, put, :] = field(f)
            for n in (5, 6):
                floats[n, t, put, :] = jnp.zeros((HALO, LANES), F32)
    for copy in loads:
        copy.wait()

    def spread(ref, i, *lead):
        return ref[(*lead, pl.ds(i, SUBLANES, stride=count), slice(None))]

    lat = lax.axis_index("lat")
    sublane = sublane_ids()

    def prepare(i, carry):
        per_tile = [
            ice_fields(
                spread(ints, i, 0, t), spread(ints, i, 1, t),
                *[spread(floats, i, n, t) for n in range(7)],
            )
            for t in range(tiles)
        ]
        west, east_side = spread(messages, i, 0), spread(messages, i, 1)
        extra = []
        for f in range(ICE):
            low, high = per_tile[0][f], per_tile[-1][f]
            middle = turn(jnp.where(lane < LANES // 2, high, low), 48)
            border = turn(high, -24)
            start = HALO * f + 2 * HALO
            beyond = jnp.where((lane >= start) & (lane < start + HALO), west, east_side)
            beyond = turn(beyond, 104 - HALO * f)
            x = jnp.where(lane < 32, low, middle)
            x = jnp.where(lane >= 64, border, x)
            extra.append(jnp.where(lane >= 104, beyond, x))
        for t, fields in enumerate(per_tile + [extra]):
            u0, v0, strength, covered, drive_x, drive_y = fields
            cut = slice(LANES * t, LANES * (t + 1))
            vel_u[i + 1, :, cut] = u0
            vel_v[i + 1, :, cut] = v0
            third[i, :, cut] = covered * (1.0 / 3.0)
            force[i, :, cut] = strength * covered * (1.0 / 12.0)
            push_x[i, :, cut] = 0.5 * drive_x
            push_y[i, :, cut] = 0.5 * drive_y
        y = lat * rows - HALO + sublane * count + i
        y = jnp.where(y >= row_total, 2 * row_total - 1 - y, y)
        coriolis = 0.5 * (2 * y + 1 - row_total).astype(F32) / row_total
        turning = 0.5 * coriolis
        scale = 3.0 / (DIAGONAL * DIAGONAL + turning * turning)
        turn_a[i] = DIAGONAL * scale
        turn_b[i] = turning * scale
        return carry

    lax.fori_loop(0, count, prepare, 0)

    def wrap(*fields):
        for ref in fields:
            ref[0] = turn(ref[count], 1, 0)
            ref[count + 1] = turn(ref[1], -1, 0)

    def strain_stress(first):
        def body(i, carry):
            for t in range(wide):
                cut = slice(LANES * t, LANES * (t + 1))
                u, v = vel_u[i + 1, :, cut], vel_v[i + 1, :, cut]
                dudx, dvdx = turn(u, -1) - turn(u, 1), turn(v, -1) - turn(v, 1)
                dudy = vel_u[i + 2, :, cut] - vel_u[i, :, cut]
                dvdy = vel_v[i + 2, :, cut] - vel_v[i, :, cut]
                div, ten, shr = dudx + dvdy, dudx - dvdy, dudy + dvdx
                square = div * div + 0.25 * (ten * ten + shr * shr) + 1.0
                base = force[i, :, cut]
                zeta = base * lax.rsqrt(square)
                quarter = 0.25 * zeta
                even = zeta * div - base
                odd = quarter * ten
                a, b, c = even + odd, even - odd, quarter * shr
                if not first:
                    keep = third[i, :, cut]
                    a = a + keep * str_a[i + 1, :, cut]
                    b = b + keep * str_b[i + 1, :, cut]
                    c = c + keep * str_c[i + 1, :, cut]
                str_a[i + 1, :, cut] = a
                str_b[i + 1, :, cut] = b
                str_c[i + 1, :, cut] = c
            return carry

        lax.fori_loop(0, count, body, 0, unroll=2)
        wrap(str_a, str_b, str_c)

    def momentum():
        def body(i, carry):
            ar, br = turn_a[i], turn_b[i]
            for t in range(wide):
                cut = slice(LANES * t, LANES * (t + 1))
                a, c = str_a[i + 1, :, cut], str_c[i + 1, :, cut]
                fx = (turn(a, -1) - turn(a, 1)) + (str_c[i + 2, :, cut] - str_c[i, :, cut])
                fy = (turn(c, -1) - turn(c, 1)) + (str_b[i + 2, :, cut] - str_b[i, :, cut])
                ru = (vel_u[i + 1, :, cut] + push_x[i, :, cut]) + fx
                rv = (vel_v[i + 1, :, cut] + push_y[i, :, cut]) + fy
                keep = third[i, :, cut]
                vel_u[i + 1, :, cut] = (ar * ru + br * rv) * keep
                vel_v[i + 1, :, cut] = (ar * rv - br * ru) * keep
            return carry

        lax.fori_loop(0, count, body, 0, unroll=2)
        wrap(vel_u, vel_v)

    def edge_fluxes(k, carry):
        at = pl.ds(pl.multiple_of(k * SUBLANES + HALO, SUBLANES), SUBLANES)
        put = pl.ds(pl.multiple_of(k * SUBLANES, SUBLANES), SUBLANES)
        west, east_side = messages[0, at, :], messages[1, at, :]
        mine_e, mine_w = messages[2, at, :], messages[3, at, :]
        speed = turn(west, -tracers)
        edge_w[put, :] = speed * jnp.where(speed > 0, west, mine_w) * turn(mine_w, -tracers)
        speed = turn(mine_e, -tracers)
        edge_e[put, :] = speed * jnp.where(speed > 0, mine_e, east_side) * turn(east_side, -tracers)
        return carry

    lax.fori_loop(0, rows // SUBLANES, edge_fluxes, 0)

    def fixed(f, put):
        low, high = raw[f, 0, put, :], raw[f, tiles - 1, put, :]
        inflow = jnp.where(lane == 0, turn(edge_w[put, :], -(TRACER_LANE + f)), 0.0)
        outflow = jnp.where(
            lane == LANES - 1, turn(edge_e[put, :], LANES - 1 - TRACER_LANE - f), 0.0
        )
        return low + inflow, high - outflow

    def stores(f):
        out = temp_out.at[f] if f < levels else salt_out.at[f - levels]
        return [
            pltpu.make_async_copy(
                raw.at[f, t], out.at[:, pl.ds(LANES * t, LANES)], out_sem.at[f, t]
            )
            for t in range(tiles)
        ]

    wrap(vel_u, vel_v)
    pending = []
    for subcycle in range(SUBCYCLES):
        strain_stress(subcycle == 0)
        momentum()
        if subcycle == 1:
            deep = [f for f in range(tracers) if f % levels]
            for f in deep:
                raw_loads[f].wait()

            def fix(k, carry):
                put = pl.ds(pl.multiple_of(k * SUBLANES, SUBLANES), SUBLANES)
                for f in deep:
                    low, high = fixed(f, put)
                    raw[f, 0, put, :] = low
                    raw[f, tiles - 1, put, :] = high
                return carry

            lax.fori_loop(0, rows // SUBLANES, fix, 0)
            for f in deep:
                pending += stores(f)
            for copy in pending:
                copy.start()

    def gather(i, carry):
        for n, ref in enumerate((vel_u, vel_v)):
            borders = ref[i + 1, :, LANES * tiles :]
            middle, outer = turn(borders, -48), turn(borders, 24)
            low = ref[i + 1, :, 0:LANES]
            high = ref[i + 1, :, LANES * (tiles - 1) : LANES * tiles]
            low = jnp.where(lane < HALO, borders, jnp.where(lane >= LANES - HALO, middle, low))
            high = jnp.where(lane < HALO, middle, jnp.where(lane >= LANES - HALO, outer, high))
            done[n, 0, pl.ds(i, SUBLANES, stride=count), :] = low
            done[n, tiles - 1, pl.ds(i, SUBLANES, stride=count), :] = high
        return carry

    lax.fori_loop(0, count, gather, 0, unroll=2)
    finals = []
    for n, out in enumerate((u_out, v_out)):
        for t in range(tiles):
            finals.append(
                pltpu.make_async_copy(
                    done.at[n, t, own, :], out.at[:, pl.ds(LANES * t, LANES)], vel_sem.at[n, t]
                )
            )
            finals[-1].start()
    raw_loads[0].wait()
    raw_loads[levels].wait()

    def warm(k, carry):
        put = pl.ds(pl.multiple_of(k * SUBLANES, SUBLANES), SUBLANES)
        at = pl.ds(pl.multiple_of(k * SUBLANES + HALO, SUBLANES), SUBLANES)
        sst, sss = fixed(0, put), fixed(levels, put)
        for t in range(tiles):
            slip_u = done[0, t, at, :] - floats[5, t, at, :]
            slip_v = done[1, t, at, :] - floats[6, t, at, :]
            covered = ints[0, t, at, :].astype(F32) * ints[1, t, at, :].astype(F32)
            heat = HEAT_RATE * covered * (1.0 + (slip_u * slip_u + slip_v * slip_v))
            heat = heat * (sst[t] + FREEZE_SLOPE * sss[t])
            raw[0, t, put, :] = sst[t] - heat
            raw[levels, t, put, :] = sss[t] - SALT_RATE * heat
        return carry

    lax.fori_loop(0, rows // SUBLANES, warm, 0, unroll=2)
    for f in (0, levels):
        copies = stores(f)
        for copy in copies:
            copy.start()
        finals += copies
    for copy in pending + finals:
        copy.wait()


def ice_and_edges(arrays, halo, east_own, west_own, from_west, from_east, temp_raw, salt_raw,
                  levels, rows, cols, row_total):
    temp, salt, east, north, land, ice, u, v, pressure, wind_x, wind_y = arrays
    tiles = cols // LANES
    extended = rows + 2 * HALO
    count = extended // SUBLANES
    anywhere = pl.BlockSpec(memory_space=pl.ANY)
    deep = jax.ShapeDtypeStruct((levels, rows, cols), F32)
    flat = jax.ShapeDtypeStruct((rows, cols), F32)
    wide = LANES * (tiles + 1)
    looped = pltpu.VMEM((count + 2, SUBLANES, wide), F32)
    plain = pltpu.VMEM((count, SUBLANES, wide), F32)
    narrow = pltpu.VMEM((count, SUBLANES, LANES), F32)
    edge = pltpu.VMEM((rows, LANES), F32)
    return pl.pallas_call(
        lambda *refs: ice_kernel(levels, rows, cols, row_total, *refs),
        in_specs=[anywhere] * 9 + [pl.BlockSpec(memory_space=pltpu.VMEM)] + [anywhere] * 6,
        out_specs=[anywhere] * 4,
        out_shape=[deep, deep, flat, flat],
        scratch_shapes=[
            pltpu.VMEM((2, tiles, extended, LANES), jnp.int32),
            pltpu.VMEM((7, tiles, extended, LANES), F32),
            pltpu.VMEM((4, extended, LANES), F32),
            pltpu.VMEM((2 * levels, tiles, rows, LANES), F32),
            pltpu.VMEM((2, tiles, extended, LANES), F32),
            looped, looped, looped, looped, looped,
            plain, plain, plain, plain, narrow, narrow, edge, edge,
            pltpu.SemaphoreType.DMA((9 * tiles,)),
            pltpu.SemaphoreType.DMA((8,)),
            pltpu.SemaphoreType.DMA((2 * levels,)),
            pltpu.SemaphoreType.DMA((2 * levels, tiles)),
            pltpu.SemaphoreType.DMA((2, tiles)),
        ],
        name="ice",
        compiler_params=pltpu.CompilerParams(vmem_limit_bytes=48 * MIB),
        cost_estimate=pl.CostEstimate(flops=60000000, bytes_accessed=16 << 20, transcendentals=0),
    )(land, ice, u, v, pressure, wind_x, wind_y, east, north, halo, east_own, west_own,
      from_west, from_east, temp_raw, salt_raw)


def per_device(*arrays):
    levels, rows, cols = arrays[0].shape
    lon_count, lat_count = lax.axis_size("lon"), lax.axis_size("lat")
    assert cols == 2 * LANES and rows % (2 * HALO) == 0 and lat_count % 2 == 0
    height = -(-(HALO * ICE + 3 * levels) // SUBLANES) * SUBLANES

    def place(lat, lon):
        return lon * lat_count + lat

    first_pairs, second_pairs = [], []
    for lon in range(lon_count):
        for lat in range(lat_count):
            first_pairs.append((place(lat, lon), place(lat ^ 1, lon)))
            if lat == lat_count - 1:
                second_pairs.append((place(lat, lon), place(lat, lon_count - 1 - lon)))
            elif lat:
                second_pairs.append((place(lat, lon), place(((lat + 1) ^ 1) - 1, lon)))
    first, second = pack_rows(arrays, levels, rows, cols, height)
    first = lax.ppermute(first, ("lon", "lat"), first_pairs)
    second = lax.ppermute(second, ("lon", "lat"), second_pairs)
    east_msg, west_msg = pack_columns(arrays, levels, rows, cols)
    halo, east_msg, west_msg = merge_halo(first, second, east_msg, west_msg, levels)
    eastward = [(i, (i + 1) % lon_count) for i in range(lon_count)]
    from_west = lax.ppermute(east_msg, "lon", eastward)
    from_east = lax.ppermute(west_msg, "lon", [(b, a) for a, b in eastward])
    temp_raw, salt_raw = advect(arrays, halo, levels, rows, cols)
    return ice_and_edges(arrays, halo, east_msg, west_msg, from_west, from_east, temp_raw, salt_raw,
                         levels, rows, cols, rows * lat_count)


def solution(mesh):
    deep, flat = P(None, "lat", "lon"), P("lat", "lon")
    return jax.shard_map(
        per_device,
        mesh=mesh,
        in_specs=(deep,) * 4 + (flat,) * 7,
        out_specs=(deep, deep, flat, flat),
        check_vma=False,
    )
```

```python
import jax
import jax.numpy as jnp
from jax import lax
from jax.experimental import pallas as pl
from jax.experimental.pallas import tpu as pltpu
from jax.sharding import PartitionSpec as P

SUBCYCLES = 4
HEAT_RATE = 0.1
SALT_RATE = 0.5
FREEZE_SLOPE = 0.054
DIAGONAL = 1.5
HALO = 2 * SUBCYCLES
LANES = 128
SUBLANES = 8
ICE = 6
FOLD_SIGN = (-1.0, -1.0, 1.0, 1.0, -1.0, -1.0)
TRACER_LANE = 64
VMEM_LIMIT = 60 << 20
F32 = jnp.float32


def lane_ids():
    return lax.broadcasted_iota(jnp.int32, (SUBLANES, LANES), 1)


def sublane_ids():
    return lax.broadcasted_iota(jnp.int32, (SUBLANES, LANES), 0)


def turn(x, shift, axis=1):
    shift = shift % x.shape[axis]
    return pltpu.roll(x, shift, axis) if shift else x


def ice_fields(land, ice, u, v, pressure, wind_x, wind_y, ocean_u, ocean_v):
    covered = land.astype(F32) * ice.astype(F32)
    return (u * covered, v * covered, pressure, covered, wind_x + ocean_u, wind_y + ocean_v)


def east_columns(fields, lane):
    packed = jnp.zeros((SUBLANES, LANES), F32)
    for f, tile in enumerate(fields):
        start = HALO * f + 2 * HALO
        moved = turn(tile, start - (LANES - HALO))
        packed = jnp.where((lane >= start) & (lane < start + HALO), moved, packed)
    return packed


def west_columns(fields, lane):
    packed = jnp.zeros((SUBLANES, LANES), F32)
    for f, tile in enumerate(fields):
        start = HALO * f
        packed = jnp.where((lane >= start) & (lane < start + HALO), turn(tile, start), packed)
    return packed


def rows_kernel(levels, *refs):
    tops, bottoms = refs[0:12], refs[12:24]
    first_ref, second_ref = refs[24:26]
    even = lax.rem(lax.axis_index("lat"), 2) == 0

    def message(group, row, northward):
        land, ice, u, v, pressure, wind_x, wind_y, east, north, temp, salt = (
            r for r in group[:11]
        )
        fields = ice_fields(
            land[...], ice[...], u[...], v[...], pressure[...], wind_x[...], wind_y[...],
            east[0], north[0],
        )
        sea = land[row : row + 1, :].astype(F32)
        parts = list(fields) + [temp[:, row, :], salt[:, row, :]]
        if northward:
            parts.append(north[:, row, :] * sea)
        else:
            parts.append(jnp.broadcast_to(sea, (levels, sea.shape[1])))
        return parts

    top = message(tops, SUBLANES - 1, True)
    bottom = message(bottoms, 0, False)
    at = 0
    for t, b in zip(top, bottom):
        size = t.shape[0]
        first_ref[at : at + size, :] = jnp.where(even, t, b)
        second_ref[at : at + size, :] = jnp.where(even, b, t)
        at += size
    pad = first_ref.shape[0] - at
    if pad:
        first_ref[at:, :] = jnp.zeros((pad, first_ref.shape[1]), F32)
        second_ref[at:, :] = jnp.zeros((pad, second_ref.shape[1]), F32)


def pack_rows(arrays, levels, rows, cols, height):
    temp, salt, east, north, land, ice, u, v, pressure, wind_x, wind_y = arrays
    operands = [land, ice, u, v, pressure, wind_x, wind_y, east, north, temp, salt, land]
    last = rows // SUBLANES - 1

    def spec(array, block, count):
        if array.ndim == 2:
            return pl.BlockSpec((SUBLANES, cols), lambda _: (block, 0))
        return pl.BlockSpec((count, SUBLANES, cols), lambda _: (0, block, 0))

    counts = [1] * 7 + [1, levels, levels, levels, 1]
    specs = [spec(a, last, c) for a, c in zip(operands, counts)]
    specs += [spec(a, 0, c) for a, c in zip(operands, counts)]
    out = jax.ShapeDtypeStruct((height, cols), F32)
    return pl.pallas_call(
        lambda *refs: rows_kernel(levels, *refs),
        grid=(1,),
        in_specs=specs,
        out_specs=[pl.BlockSpec((height, cols), lambda _: (0, 0))] * 2,
        out_shape=[out, out],
        name="edge_rows",
        compiler_params=pltpu.CompilerParams(vmem_limit_bytes=VMEM_LIMIT),
        cost_estimate=pl.CostEstimate(flops=100000, bytes_accessed=1 << 20, transcendentals=0),
    )(*operands, *operands)


def columns_kernel(levels, land, ice, u, v, pressure, wind_x, wind_y, east, north, temp, salt,
                   east_out, west_out):
    lane = lane_ids()
    tracers = 2 * levels
    last = land.shape[1] - LANES
    first_lane = TRACER_LANE
    mask_lane = TRACER_LANE + tracers

    def step(k, carry):
        rows = pl.ds(pl.multiple_of(k * SUBLANES, SUBLANES), SUBLANES)
        for side, out in ((last, east_out), (0, west_out)):
            cols = slice(side, side + LANES)
            fields = ice_fields(
                land[rows, cols], ice[rows, cols], u[rows, cols], v[rows, cols],
                pressure[rows, cols], wind_x[rows, cols], wind_y[rows, cols],
                east[0, rows, cols], north[0, rows, cols],
            )
            eastward = out is east_out
            source = LANES - 1 if eastward else 0
            packed = (east_columns if eastward else west_columns)(fields, lane)
            for f in range(tracers):
                tile = temp[f, rows, cols] if f < levels else salt[f - levels, rows, cols]
                packed = jnp.where(lane == first_lane + f, turn(tile, first_lane + f - source), packed)
            sea = jnp.broadcast_to(
                land[rows, side + source : side + source + 1].astype(F32), (SUBLANES, LANES)
            )
            if eastward:
                speeds = jnp.zeros((SUBLANES, LANES), F32)
                for f in range(levels):
                    moved = turn(east[f, rows, cols], mask_lane + f - source)
                    speeds = jnp.where(lane == mask_lane + f, moved, speeds)
                speeds = speeds + turn(speeds, levels)
                packed = jnp.where(
                    (lane >= mask_lane) & (lane < mask_lane + tracers), speeds * sea, packed
                )
            else:
                packed = jnp.where((lane >= mask_lane) & (lane < mask_lane + tracers), sea, packed)
            out[rows, :] = packed
        return carry

    lax.fori_loop(0, land.shape[0] // SUBLANES, step, 0, unroll=True)


def pack_columns(arrays, levels, rows, cols):
    temp, salt, east, north, land, ice, u, v, pressure, wind_x, wind_y = arrays
    height = next(h for h in (64, 32, 16) if rows % h == 0)
    flat = pl.BlockSpec((height, cols), lambda k: (k, 0))
    deep = pl.BlockSpec((levels, height, cols), lambda k: (0, k, 0))
    surface = pl.BlockSpec((1, height, cols), lambda k: (0, k, 0))
    out = jax.ShapeDtypeStruct((rows + 2 * HALO, LANES), F32)
    return pl.pallas_call(
        lambda *refs: columns_kernel(levels, *refs),
        grid=(rows // height,),
        in_specs=[flat] * 7 + [deep, surface, deep, deep],
        out_specs=[pl.BlockSpec((height, LANES), lambda k: (k, 0))] * 2,
        out_shape=[out, out],
        name="edge_columns",
        compiler_params=pltpu.CompilerParams(vmem_limit_bytes=VMEM_LIMIT),
        cost_estimate=pl.CostEstimate(flops=5000000, bytes_accessed=10 << 20, transcendentals=0),
    )(land, ice, u, v, pressure, wind_x, wind_y, east, north, temp, salt)


def halo_kernel(levels, first, second, east_in, west_in, halo_ref, east_out, west_out):
    lat = lax.axis_index("lat")
    even = lax.rem(lat, 2) == 0
    top = lat == lax.axis_size("lat") - 1
    lane, sublane = lane_ids(), sublane_ids()
    tiles = halo_ref.shape[2] // LANES
    south_fields, north_fields = [], []
    for f in range(ICE):
        rows = slice(HALO * f, HALO * (f + 1))
        north_row, south_row = [], []
        for t in range(tiles):
            cols = slice(LANES * t, LANES * (t + 1))
            mirror = slice(LANES * (tiles - 1 - t), LANES * (tiles - t))
            south = jnp.where(even, second[rows, cols], first[rows, cols])
            plain = jnp.where(even, first[rows, cols], second[rows, cols])
            turned = jnp.take_along_axis(second[rows, mirror], LANES - 1 - lane, axis=1)
            turned = jnp.take_along_axis(turned, SUBLANES - 1 - sublane, axis=0)
            north = jnp.where(top, turned * FOLD_SIGN[f], plain)
            halo_ref[0, rows, cols] = south
            halo_ref[1, rows, cols] = north
            south_row.append(south)
            north_row.append(north)
        south_fields.append(south_row)
        north_fields.append(north_row)
    rest = slice(HALO * ICE, halo_ref.shape[1])
    halo_ref[0, rest, :] = jnp.where(even, second[rest, :], first[rest, :])
    halo_ref[1, rest, :] = jnp.where(top, 0.0, jnp.where(even, first[rest, :], second[rest, :]))
    for at, fields in ((0, south_fields), (HALO, north_fields)):
        east_out[at : at + HALO, :] = east_columns([f[-1] for f in fields], lane)
        west_out[at : at + HALO, :] = west_columns([f[0] for f in fields], lane)


def merge_halo(first, second, east_msg, west_msg, levels):
    height, cols = first.shape
    rows = east_msg.shape[0] - 2 * HALO
    tail = pl.BlockSpec((2 * HALO, LANES), lambda _: (rows // (2 * HALO), 0))
    whole = pl.BlockSpec((height, cols), lambda _: (0, 0))
    return pl.pallas_call(
        lambda *refs: halo_kernel(levels, *refs),
        grid=(1,),
        in_specs=[whole, whole] + [pl.BlockSpec(memory_space=pl.ANY)] * 2,
        out_specs=[pl.BlockSpec((2, height, cols), lambda _: (0, 0, 0)), tail, tail],
        out_shape=[
            jax.ShapeDtypeStruct((2, height, cols), F32),
            jax.ShapeDtypeStruct(east_msg.shape, F32),
            jax.ShapeDtypeStruct(west_msg.shape, F32),
        ],
        input_output_aliases={2: 1, 3: 2},
        name="halo_rows",
        compiler_params=pltpu.CompilerParams(vmem_limit_bytes=VMEM_LIMIT),
        cost_estimate=pl.CostEstimate(flops=100000, bytes_accessed=1 << 19, transcendentals=0),
    )(first, second, east_msg, west_msg)


def advect_kernel(levels, tiles, *refs):
    temp, salt, east, north = (refs[tiles * n : tiles * (n + 1)] for n in range(4))
    land = refs[4 * tiles : 5 * tiles]
    halo, temp_out, salt_out, mask_e, mask_n = refs[5 * tiles :]
    level = pl.program_id(0)
    count = temp[0].shape[1] // SUBLANES
    chunk = next(c for c in (6, 4, 2) if count % c == 0)
    lane, sublane = lane_ids(), sublane_ids()
    tracer_row = HALO * ICE
    extra_row = tracer_row + 2 * levels

    def rows_at(k, offset=0):
        start = pl.multiple_of(k * SUBLANES, SUBLANES)
        return pl.ds(start + offset if offset else start, SUBLANES)

    def row(side, index, t):
        cols = slice(LANES * t, LANES * (t + 1))
        return jnp.broadcast_to(halo[side, index : index + 1, cols], (SUBLANES, LANES))

    def level_row(side, index, t):
        picked = row(side, index, t)
        for l in range(1, levels):
            picked = jnp.where(level == l, row(side, index + l, t), picked)
        return picked

    def with_last(values, last, past):
        if not last:
            return values
        return jnp.where(sublane == SUBLANES - 1, past, turn(values, -1, 0))

    def from_next(values):
        turned = [turn(v, -1) for v in values]
        return [
            jnp.where(lane == LANES - 1, turned[t + 1], turned[t]) if t + 1 < tiles else turned[t]
            for t in range(tiles)
        ]

    def from_last(values):
        turned = [turn(v, 1) for v in values]
        return [jnp.where(lane == 0, turned[t - 1], turned[t]) for t in range(tiles)]

    def in_chunks(body, carry):
        def step(n, carry):
            for j in range(chunk):
                carry = body(n * chunk + j, False, carry)
            return carry

        chunks = count // chunk
        carry = lax.fori_loop(0, chunks - 1, step, carry)
        for k in range((chunks - 1) * chunk, count):
            carry = body(k, k == count - 1, carry)

    @pl.when(level == 0)
    def _():
        past = [row(1, extra_row, t) for t in range(tiles)]

        def body(k, last, carry):
            here = [land[t][rows_at(k), :].astype(F32) for t in range(tiles)]
            beside = from_next(here)
            for t in range(tiles):
                if last:
                    above = with_last(here[t], last, past[t])
                else:
                    above = land[t][rows_at(k, 1), :].astype(F32)
                face = here[t] * beside[t]
                if t == tiles - 1:
                    face = jnp.where(lane == LANES - 1, 0.0, face)
                mask_e[t, rows_at(k), :] = face
                mask_n[t, rows_at(k), :] = here[t] * above
            return carry

        in_chunks(body, 0)

    sources = ((temp, temp_out, 0), (salt, salt_out, levels))
    entering = []
    for source, _, at in sources:
        for t in range(tiles):
            speed = level_row(0, extra_row, t) * land[t][0:SUBLANES, :].astype(F32)
            south = level_row(0, tracer_row + at, t)
            flux = speed * jnp.where(speed > 0, south, source[t][0, 0:SUBLANES, :])
            entering.append(flux)
    past = [[level_row(1, tracer_row + at, t) for t in range(tiles)] for _, _, at in sources]

    def body(k, last, carry):
        at = rows_at(k)
        fast_e = [east[t][0, at, :] * mask_e[t, at, :] for t in range(tiles)]
        fast_n = [north[t][0, at, :] * mask_n[t, at, :] for t in range(tiles)]
        result = []
        for n, (source, out, _) in enumerate(sources):
            here = [source[t][0, at, :] for t in range(tiles)]
            beside = from_next(here)
            flux_e = [
                fast_e[t] * jnp.where(fast_e[t] > 0, here[t], beside[t]) for t in range(tiles)
            ]
            before = from_last(flux_e)
            for t in range(tiles):
                if last:
                    above = with_last(here[t], last, past[n][t])
                else:
                    above = source[t][0, rows_at(k, 1), :]
                flux_n = fast_n[t] * jnp.where(fast_n[t] > 0, here[t], above)
                turned = turn(flux_n, 1, 0)
                below = jnp.where(sublane == 0, carry[n * tiles + t], turned)
                out[0, t, at, :] = here[t] - ((flux_e[t] - before[t]) + (flux_n - below))
                result.append(turned)
        return tuple(result)

    in_chunks(body, tuple(entering))


def advect(arrays, halo, levels, rows, cols):
    temp, salt, east, north, land = arrays[:5]
    tiles = cols // LANES

    def deep(t):
        return pl.BlockSpec((1, rows, LANES), lambda l: (l, 0, t))

    def flat(t):
        return pl.BlockSpec((rows, LANES), lambda l: (0, t))

    specs = [deep(t) for _ in range(4) for t in range(tiles)] + [flat(t) for t in range(tiles)]
    operands = [a for a in (temp, salt, east, north, land) for _ in range(tiles)]
    out = jax.ShapeDtypeStruct((levels, tiles, rows, LANES), F32)
    return pl.pallas_call(
        lambda *refs: advect_kernel(levels, tiles, *refs),
        grid=(levels,),
        in_specs=specs + [pl.BlockSpec(halo.shape, lambda l: (0, 0, 0))],
        out_specs=[pl.BlockSpec((1, tiles, rows, LANES), lambda l: (l, 0, 0, 0))] * 2,
        out_shape=[out, out],
        scratch_shapes=[pltpu.VMEM((tiles, rows, LANES), F32)] * 2,
        name="advect",
        compiler_params=pltpu.CompilerParams(vmem_limit_bytes=VMEM_LIMIT),
        cost_estimate=pl.CostEstimate(flops=30000000, bytes_accessed=16 << 20, transcendentals=0),
    )(*operands, halo)


def sublane_rows(rows):
    return (rows + 2 * HALO) // SUBLANES | 1


def in_chunks_of(count, body):
    size = max(c for c in range(1, 21) if count % c == 0)

    def step(n, carry):
        for j in range(size):
            body(n * size + j)
        return carry

    lax.fori_loop(0, count // size, step, 0)


def ice_kernel(levels, rows, cols, row_total, *refs):
    (land, ice, u_in, v_in, pressure, wind_x, wind_y, east, north, halo, east_own, west_own,
     from_west, from_east, temp_raw, salt_raw, temp_out, salt_out, u_out, v_out,
     ints, floats, messages, raw, done, vel_u, vel_v, str_a, str_b, str_c,
     third, force, push_x, push_y, turn_a, turn_b, edge_w, edge_e,
     in_sem, msg_sem, raw_sem, out_sem, vel_sem) = refs
    tiles = cols // LANES
    count = sublane_rows(rows)
    tracers = 2 * levels
    lane = lane_ids()
    own = pl.ds(HALO, rows)
    wide = tiles + 1

    copies = []
    for n, ref in enumerate((land, ice)):
        for t in range(tiles):
            cut = pl.ds(LANES * t, LANES)
            copies.append((ref.at[:, cut], ints.at[n, t, own, :]))
    for n, ref in enumerate((u_in, v_in, pressure, wind_x, wind_y, east, north)):
        for t in range(tiles):
            cut = pl.ds(LANES * t, LANES)
            source = ref.at[0, :, cut] if ref is east or ref is north else ref.at[:, cut]
            copies.append((source, floats.at[n, t, own, :]))
    loads = [pltpu.make_async_copy(a, b, in_sem.at[k]) for k, (a, b) in enumerate(copies)]
    copies = []
    for n, ref in enumerate((from_west, from_east, east_own, west_own)):
        copies.append((ref.at[pl.ds(0, rows), :], messages.at[n, own, :]))
        if n < 2:
            copies.append((ref.at[pl.ds(rows, HALO), :], messages.at[n, pl.ds(0, HALO), :]))
            copies.append(
                (ref.at[pl.ds(rows + HALO, HALO), :], messages.at[n, pl.ds(rows + HALO, HALO), :])
            )
    loads += [pltpu.make_async_copy(a, b, msg_sem.at[k]) for k, (a, b) in enumerate(copies)]
    for copy in loads:
        copy.start()
    raw_loads = []
    for f in range(tracers):
        source = temp_raw.at[f] if f < levels else salt_raw.at[f - levels]
        raw_loads.append(pltpu.make_async_copy(source, raw.at[f], raw_sem.at[f]))
        raw_loads[-1].start()

    for side, at in ((0, 0), (1, rows + HALO)):
        put = slice(at, at + HALO)
        for t in range(tiles):
            cut = slice(LANES * t, LANES * (t + 1))

            def field(f):
                return halo[side, HALO * f : HALO * (f + 1), cut]

            ints[0, t, put, :] = field(3).astype(jnp.int32)
            ints[1, t, put, :] = jnp.ones((HALO, LANES), jnp.int32)
            for n, f in ((0, 0), (1, 1), (2, 2), (3, 4), (4, 5)):
                floats[n, t, put, :] = field(f)
            for n in (5, 6):
                floats[n, t, put, :] = jnp.zeros((HALO, LANES), F32)
    past = (rows + 2 * HALO, count * SUBLANES)
    if past[0] < past[1]:
        blank = (past[1] - past[0], LANES)
        for t in range(tiles):
            for n in range(2):
                ints[n, t, past[0] : past[1], :] = jnp.zeros(blank, jnp.int32)
            for n in range(7):
                floats[n, t, past[0] : past[1], :] = jnp.zeros(blank, F32)
        for n in range(2):
            messages[n, past[0] : past[1], :] = jnp.zeros(blank, F32)
    for copy in loads:
        copy.wait()

    def spread(ref, i, *lead):
        return ref[(*lead, pl.ds(i, SUBLANES, stride=count), slice(None))]

    lat = lax.axis_index("lat")
    sublane = sublane_ids()

    def prepare(i):
        per_tile = [
            ice_fields(
                spread(ints, i, 0, t), spread(ints, i, 1, t),
                *[spread(floats, i, n, t) for n in range(7)],
            )
            for t in range(tiles)
        ]
        west, east_side = spread(messages, i, 0), spread(messages, i, 1)
        extra = []
        for f in range(ICE):
            low, high = per_tile[0][f], per_tile[-1][f]
            middle = turn(jnp.where(lane < LANES // 2, high, low), 48)
            border = turn(high, -24)
            start = HALO * f + 2 * HALO
            beyond = jnp.where((lane >= start) & (lane < start + HALO), west, east_side)
            beyond = turn(beyond, 104 - HALO * f)
            x = jnp.where(lane < 32, low, middle)
            x = jnp.where(lane >= 64, border, x)
            extra.append(jnp.where(lane >= 104, beyond, x))
        for t, fields in enumerate(per_tile + [extra]):
            u0, v0, strength, covered, drive_x, drive_y = fields
            cut = slice(LANES * t, LANES * (t + 1))
            vel_u[i + 1, :, cut] = u0
            vel_v[i + 1, :, cut] = v0
            third[i, :, cut] = covered * (1.0 / 3.0)
            force[i, :, cut] = strength * covered * (1.0 / 12.0)
            push_x[i, :, cut] = 0.5 * drive_x
            push_y[i, :, cut] = 0.5 * drive_y
        y = lat * rows - HALO + sublane * count + i
        y = jnp.where(y >= row_total, 2 * row_total - 1 - y, y)
        coriolis = 0.5 * (2 * y + 1 - row_total).astype(F32) / row_total
        turning = 0.5 * coriolis
        scale = 3.0 / (DIAGONAL * DIAGONAL + turning * turning)
        turn_a[i] = DIAGONAL * scale
        turn_b[i] = turning * scale

    in_chunks_of(count, prepare)

    def wrap(*fields):
        for ref in fields:
            ref[0] = turn(ref[count], 1, 0)
            ref[count + 1] = turn(ref[1], -1, 0)

    def strain_stress(first):
        def body(i):
            for t in range(wide):
                cut = slice(LANES * t, LANES * (t + 1))
                u, v = vel_u[i + 1, :, cut], vel_v[i + 1, :, cut]
                dudx, dvdx = turn(u, -1) - turn(u, 1), turn(v, -1) - turn(v, 1)
                dudy = vel_u[i + 2, :, cut] - vel_u[i, :, cut]
                dvdy = vel_v[i + 2, :, cut] - vel_v[i, :, cut]
                div, ten, shr = dudx + dvdy, dudx - dvdy, dudy + dvdx
                square = div * div + 0.25 * (ten * ten + shr * shr) + 1.0
                base = force[i, :, cut]
                zeta = base * lax.rsqrt(square)
                quarter = 0.25 * zeta
                even = zeta * div - base
                odd = quarter * ten
                a, b, c = even + odd, even - odd, quarter * shr
                if not first:
                    keep = third[i, :, cut]
                    a = a + keep * str_a[i + 1, :, cut]
                    b = b + keep * str_b[i + 1, :, cut]
                    c = c + keep * str_c[i + 1, :, cut]
                str_a[i + 1, :, cut] = a
                str_b[i + 1, :, cut] = b
                str_c[i + 1, :, cut] = c

        in_chunks_of(count, body)
        wrap(str_a, str_b, str_c)

    def momentum():
        def body(i):
            ar, br = turn_a[i], turn_b[i]
            for t in range(wide):
                cut = slice(LANES * t, LANES * (t + 1))
                a, c = str_a[i + 1, :, cut], str_c[i + 1, :, cut]
                fx = (turn(a, -1) - turn(a, 1)) + (str_c[i + 2, :, cut] - str_c[i, :, cut])
                fy = (turn(c, -1) - turn(c, 1)) + (str_b[i + 2, :, cut] - str_b[i, :, cut])
                ru = (vel_u[i + 1, :, cut] + push_x[i, :, cut]) + fx
                rv = (vel_v[i + 1, :, cut] + push_y[i, :, cut]) + fy
                keep = third[i, :, cut]
                vel_u[i + 1, :, cut] = (ar * ru + br * rv) * keep
                vel_v[i + 1, :, cut] = (ar * rv - br * ru) * keep

        in_chunks_of(count, body)
        wrap(vel_u, vel_v)

    def edge_fluxes(k, carry):
        at = pl.ds(pl.multiple_of(k * SUBLANES + HALO, SUBLANES), SUBLANES)
        put = pl.ds(pl.multiple_of(k * SUBLANES, SUBLANES), SUBLANES)
        west, east_side = messages[0, at, :], messages[1, at, :]
        mine_e, mine_w = messages[2, at, :], messages[3, at, :]
        speed = turn(west, -tracers)
        edge_w[put, :] = speed * jnp.where(speed > 0, west, mine_w) * turn(mine_w, -tracers)
        speed = turn(mine_e, -tracers)
        edge_e[put, :] = speed * jnp.where(speed > 0, mine_e, east_side) * turn(east_side, -tracers)
        return carry

    lax.fori_loop(0, rows // SUBLANES, edge_fluxes, 0, unroll=8)

    def fixed(f, put):
        low, high = raw[f, 0, put, :], raw[f, tiles - 1, put, :]
        inflow = jnp.where(lane == 0, turn(edge_w[put, :], -(TRACER_LANE + f)), 0.0)
        outflow = jnp.where(
            lane == LANES - 1, turn(edge_e[put, :], LANES - 1 - TRACER_LANE - f), 0.0
        )
        return low + inflow, high - outflow

    def stores(f):
        out = temp_out.at[f] if f < levels else salt_out.at[f - levels]
        return [
            pltpu.make_async_copy(
                raw.at[f, t], out.at[:, pl.ds(LANES * t, LANES)], out_sem.at[f, t]
            )
            for t in range(tiles)
        ]

    wrap(vel_u, vel_v)
    pending = []
    for subcycle in range(SUBCYCLES):
        strain_stress(subcycle == 0)
        momentum()
        if subcycle == 1:
            deep = [f for f in range(tracers) if f % levels]
            for f in deep:
                raw_loads[f].wait()

            def fix(k, carry):
                put = pl.ds(pl.multiple_of(k * SUBLANES, SUBLANES), SUBLANES)
                for f in deep:
                    low, high = fixed(f, put)
                    raw[f, 0, put, :] = low
                    raw[f, tiles - 1, put, :] = high
                return carry

            lax.fori_loop(0, rows // SUBLANES, fix, 0, unroll=4)
            for f in deep:
                pending += stores(f)
            for copy in pending:
                copy.start()

    def gather(i):
        for n, ref in enumerate((vel_u, vel_v)):
            borders = ref[i + 1, :, LANES * tiles :]
            middle, outer = turn(borders, -48), turn(borders, 24)
            low = ref[i + 1, :, 0:LANES]
            high = ref[i + 1, :, LANES * (tiles - 1) : LANES * tiles]
            low = jnp.where(lane < HALO, borders, jnp.where(lane >= LANES - HALO, middle, low))
            high = jnp.where(lane < HALO, middle, jnp.where(lane >= LANES - HALO, outer, high))
            done[n, 0, pl.ds(i, SUBLANES, stride=count), :] = low
            done[n, tiles - 1, pl.ds(i, SUBLANES, stride=count), :] = high

    in_chunks_of(count, gather)
    finals = []
    for n, out in enumerate((u_out, v_out)):
        for t in range(tiles):
            finals.append(
                pltpu.make_async_copy(
                    done.at[n, t, own, :], out.at[:, pl.ds(LANES * t, LANES)], vel_sem.at[n, t]
                )
            )
            finals[-1].start()
    raw_loads[0].wait()
    raw_loads[levels].wait()

    def warm(k, carry):
        put = pl.ds(pl.multiple_of(k * SUBLANES, SUBLANES), SUBLANES)
        at = pl.ds(pl.multiple_of(k * SUBLANES + HALO, SUBLANES), SUBLANES)
        sst, sss = fixed(0, put), fixed(levels, put)
        for t in range(tiles):
            slip_u = done[0, t, at, :] - floats[5, t, at, :]
            slip_v = done[1, t, at, :] - floats[6, t, at, :]
            covered = ints[0, t, at, :].astype(F32) * ints[1, t, at, :].astype(F32)
            heat = HEAT_RATE * covered * (1.0 + (slip_u * slip_u + slip_v * slip_v))
            heat = heat * (sst[t] + FREEZE_SLOPE * sss[t])
            raw[0, t, put, :] = sst[t] - heat
            raw[levels, t, put, :] = sss[t] - SALT_RATE * heat
        return carry

    lax.fori_loop(0, rows // SUBLANES, warm, 0, unroll=8)
    for f in (0, levels):
        copies = stores(f)
        for copy in copies:
            copy.start()
        finals += copies
    for copy in pending + finals:
        copy.wait()


def ice_and_edges(arrays, halo, east_own, west_own, from_west, from_east, temp_raw, salt_raw,
                  levels, rows, cols, row_total):
    temp, salt, east, north, land, ice, u, v, pressure, wind_x, wind_y = arrays
    tiles = cols // LANES
    count = sublane_rows(rows)
    extended = count * SUBLANES
    anywhere = pl.BlockSpec(memory_space=pl.ANY)
    deep = jax.ShapeDtypeStruct((levels, rows, cols), F32)
    flat = jax.ShapeDtypeStruct((rows, cols), F32)
    wide = LANES * (tiles + 1)
    looped = pltpu.VMEM((count + 2, SUBLANES, wide), F32)
    plain = pltpu.VMEM((count, SUBLANES, wide), F32)
    narrow = pltpu.VMEM((count, SUBLANES, LANES), F32)
    edge = pltpu.VMEM((rows, LANES), F32)
    return pl.pallas_call(
        lambda *refs: ice_kernel(levels, rows, cols, row_total, *refs),
        in_specs=[anywhere] * 9 + [pl.BlockSpec(memory_space=pltpu.VMEM)] + [anywhere] * 6,
        out_specs=[anywhere] * 4,
        out_shape=[deep, deep, flat, flat],
        scratch_shapes=[
            pltpu.VMEM((2, tiles, extended, LANES), jnp.int32),
            pltpu.VMEM((7, tiles, extended, LANES), F32),
            pltpu.VMEM((4, extended, LANES), F32),
            pltpu.VMEM((2 * levels, tiles, rows, LANES), F32),
            pltpu.VMEM((2, tiles, extended, LANES), F32),
            looped, looped, looped, looped, looped,
            plain, plain, plain, plain, narrow, narrow, edge, edge,
            pltpu.SemaphoreType.DMA((9 * tiles,)),
            pltpu.SemaphoreType.DMA((8,)),
            pltpu.SemaphoreType.DMA((2 * levels,)),
            pltpu.SemaphoreType.DMA((2 * levels, tiles)),
            pltpu.SemaphoreType.DMA((2, tiles)),
        ],
        name="ice",
        compiler_params=pltpu.CompilerParams(vmem_limit_bytes=VMEM_LIMIT),
        cost_estimate=pl.CostEstimate(flops=60000000, bytes_accessed=16 << 20, transcendentals=0),
    )(land, ice, u, v, pressure, wind_x, wind_y, east, north, halo, east_own, west_own,
      from_west, from_east, temp_raw, salt_raw)


def per_device(*arrays):
    levels, rows, cols = arrays[0].shape
    lon_count, lat_count = lax.axis_size("lon"), lax.axis_size("lat")
    assert cols == 2 * LANES and rows % (2 * HALO) == 0 and lat_count % 2 == 0
    height = -(-(HALO * ICE + 3 * levels) // SUBLANES) * SUBLANES

    def place(lat, lon):
        return lon * lat_count + lat

    first_pairs, second_pairs = [], []
    for lon in range(lon_count):
        for lat in range(lat_count):
            first_pairs.append((place(lat, lon), place(lat ^ 1, lon)))
            if lat == lat_count - 1:
                second_pairs.append((place(lat, lon), place(lat, lon_count - 1 - lon)))
            elif lat:
                second_pairs.append((place(lat, lon), place(((lat + 1) ^ 1) - 1, lon)))
    first, second = pack_rows(arrays, levels, rows, cols, height)
    first = lax.ppermute(first, ("lon", "lat"), first_pairs)
    second = lax.ppermute(second, ("lon", "lat"), second_pairs)
    east_msg, west_msg = pack_columns(arrays, levels, rows, cols)
    halo, east_msg, west_msg = merge_halo(first, second, east_msg, west_msg, levels)
    eastward = [(i, (i + 1) % lon_count) for i in range(lon_count)]
    from_west = lax.ppermute(east_msg, "lon", eastward)
    from_east = lax.ppermute(west_msg, "lon", [(b, a) for a, b in eastward])
    temp_raw, salt_raw = advect(arrays, halo, levels, rows, cols)
    return ice_and_edges(arrays, halo, east_msg, west_msg, from_west, from_east, temp_raw, salt_raw,
                         levels, rows, cols, rows * lat_count)


def solution(mesh):
    deep, flat = P(None, "lat", "lon"), P("lat", "lon")
    return jax.shard_map(
        per_device,
        mesh=mesh,
        in_specs=(deep,) * 4 + (flat,) * 7,
        out_specs=(deep, deep, flat, flat),
        check_vma=False,
    )
```

```python
import jax
import jax.numpy as jnp
from jax import lax
from jax.experimental import pallas as pl
from jax.experimental.pallas import tpu as pltpu
from jax.sharding import PartitionSpec as P

SUBCYCLES = 4
HEAT_RATE = 0.1
SALT_RATE = 0.5
FREEZE_SLOPE = 0.054
DIAGONAL = 1.5
HALO = 2 * SUBCYCLES
LANES = 128
SUBLANES = 8
ICE = 6
FOLD_SIGN = (-1.0, -1.0, 1.0, 1.0, -1.0, -1.0)
TRACER_LANE = 64
F32 = jnp.float32


def lane_ids():
    return lax.broadcasted_iota(jnp.int32, (SUBLANES, LANES), 1)


def sublane_ids():
    return lax.broadcasted_iota(jnp.int32, (SUBLANES, LANES), 0)


def turn(x, shift, axis=1):
    shift = shift % x.shape[axis]
    return pltpu.roll(x, shift, axis) if shift else x


def ice_fields(land, ice, u, v, pressure, wind_x, wind_y, ocean_u, ocean_v):
    covered = land.astype(F32) * ice.astype(F32)
    return (u * covered, v * covered, pressure, covered, wind_x + ocean_u, wind_y + ocean_v)


def east_columns(fields, lane):
    packed = jnp.zeros((SUBLANES, LANES), F32)
    for f, tile in enumerate(fields):
        start = HALO * f + 2 * HALO
        moved = turn(tile, start - (LANES - HALO))
        packed = jnp.where((lane >= start) & (lane < start + HALO), moved, packed)
    return packed


def west_columns(fields, lane):
    packed = jnp.zeros((SUBLANES, LANES), F32)
    for f, tile in enumerate(fields):
        start = HALO * f
        packed = jnp.where((lane >= start) & (lane < start + HALO), turn(tile, start), packed)
    return packed


def rows_kernel(levels, *refs):
    tops, bottoms = refs[0:12], refs[12:24]
    first_ref, second_ref = refs[24:26]
    even = lax.rem(lax.axis_index("lat"), 2) == 0

    def message(group, row, northward):
        land, ice, u, v, pressure, wind_x, wind_y, east, north, temp, salt = (
            r for r in group[:11]
        )
        fields = ice_fields(
            land[...], ice[...], u[...], v[...], pressure[...], wind_x[...], wind_y[...],
            east[0], north[0],
        )
        sea = land[row : row + 1, :].astype(F32)
        parts = list(fields) + [temp[:, row, :], salt[:, row, :]]
        if northward:
            parts.append(north[:, row, :] * sea)
        else:
            parts.append(jnp.broadcast_to(sea, (levels, sea.shape[1])))
        return parts

    top = message(tops, SUBLANES - 1, True)
    bottom = message(bottoms, 0, False)
    at = 0
    for t, b in zip(top, bottom):
        size = t.shape[0]
        first_ref[at : at + size, :] = jnp.where(even, t, b)
        second_ref[at : at + size, :] = jnp.where(even, b, t)
        at += size
    pad = first_ref.shape[0] - at
    if pad:
        first_ref[at:, :] = jnp.zeros((pad, first_ref.shape[1]), F32)
        second_ref[at:, :] = jnp.zeros((pad, second_ref.shape[1]), F32)


def pack_rows(arrays, levels, rows, cols, height):
    temp, salt, east, north, land, ice, u, v, pressure, wind_x, wind_y = arrays
    operands = [land, ice, u, v, pressure, wind_x, wind_y, east, north, temp, salt, land]
    last = rows // SUBLANES - 1

    def spec(array, block, count):
        if array.ndim == 2:
            return pl.BlockSpec((SUBLANES, cols), lambda _: (block, 0))
        return pl.BlockSpec((count, SUBLANES, cols), lambda _: (0, block, 0))

    counts = [1] * 7 + [1, levels, levels, levels, 1]
    specs = [spec(a, last, c) for a, c in zip(operands, counts)]
    specs += [spec(a, 0, c) for a, c in zip(operands, counts)]
    out = jax.ShapeDtypeStruct((height, cols), F32)
    return pl.pallas_call(
        lambda *refs: rows_kernel(levels, *refs),
        grid=(1,),
        in_specs=specs,
        out_specs=[pl.BlockSpec((height, cols), lambda _: (0, 0))] * 2,
        out_shape=[out, out],
        name="edge_rows",
        compiler_params=pltpu.CompilerParams(vmem_limit_bytes=8 << 20),
        cost_estimate=pl.CostEstimate(flops=100000, bytes_accessed=1 << 20, transcendentals=0),
    )(*[in_hbm(a) for a in operands + operands])


def columns_kernel(levels, land, ice, u, v, pressure, wind_x, wind_y, east, north, temp, salt,
                   tracer_out, speed_out, sea_out, field_out, east_out, west_out,
                   ints, floats, int_sem, float_sem, tracer_sem, speed_sem):
    lane = lane_ids()
    rows = sea_out.shape[1]
    tiles = sea_out.shape[0]
    tracers = 2 * levels
    first_lane = TRACER_LANE
    mask_lane = TRACER_LANE + tracers

    def cut(ref, t):
        return ref.at[..., pl.ds(LANES * t, LANES)]

    surface, loads = [], {}
    for t in range(tiles):
        for n, ref in enumerate((land, ice)):
            surface.append(pltpu.make_async_copy(cut(ref, t), ints.at[n, t], int_sem.at[n, t]))
        for n, ref in enumerate((u, v, pressure, wind_x, wind_y)):
            surface.append(pltpu.make_async_copy(cut(ref, t), floats.at[n, t], float_sem.at[n, t]))
        for n, ref in enumerate((east, north)):
            surface.append(
                pltpu.make_async_copy(
                    cut(ref.at[0], t), speed_out.at[levels * n, t], speed_sem.at[n, 0, t]
                )
            )
    for n, ref in enumerate((temp, salt)):
        loads[n] = [
            pltpu.make_async_copy(
                cut(ref, t), tracer_out.at[pl.ds(levels * n, levels), t], tracer_sem.at[n, t]
            )
            for t in range(tiles)
        ]
    for n, ref in enumerate((east, north)):
        loads[n + 2] = [
            pltpu.make_async_copy(
                cut(ref.at[pl.ds(1, levels - 1)], t),
                speed_out.at[pl.ds(levels * n + 1, levels - 1), t],
                speed_sem.at[n, 1, t],
            )
            for t in range(tiles)
        ]
    for copy in surface + loads[0] + loads[1] + loads[2] + loads[3]:
        copy.start()

    def each_row_tile(body, size):
        def step(n, carry):
            writes = []
            for j in range(size):
                writes += body(pl.multiple_of((n * size + j) * SUBLANES, SUBLANES))
            for ref, where, value in writes:
                ref[where] = value
            return carry

        lax.fori_loop(0, rows // SUBLANES // size, step, 0)

    for copy in surface:
        copy.wait()
    whole = slice(None)

    def ice_part(start):
        at = pl.ds(start, SUBLANES)
        writes, fields = [], []
        for t in range(tiles):
            fields.append(
                ice_fields(
                    ints[0, t, at, :], ints[1, t, at, :], *[floats[n, t, at, :] for n in range(5)],
                    speed_out[0, t, at, :], speed_out[levels, t, at, :],
                )
            )
            writes.append((sea_out, (t, at, whole), ints[0, t, at, :].astype(F32)))
            for f in range(ICE):
                writes.append((field_out, (f, t, pl.ds(start + HALO, SUBLANES), whole), fields[t][f]))
        writes.append((east_out, (at, whole), east_columns(fields[-1], lane)))
        writes.append((west_out, (at, whole), west_columns(fields[0], lane)))
        return writes

    each_row_tile(ice_part, 2)
    for t in range(tiles):
        for f in range(ICE):
            blank = (HALO + rows, field_out.shape[2])
            field_out[f, t, blank[0] : blank[1], :] = jnp.zeros((blank[1] - blank[0], LANES), F32)

    for n in range(2):
        for copy in loads[n]:
            copy.wait()

        def tracer_part(start, n=n):
            at = pl.ds(start, SUBLANES)
            eastward, westward = east_out[at, :], west_out[at, :]
            for f in range(levels * n, levels * (n + 1)):
                to = first_lane + f
                eastward = jnp.where(
                    lane == to, turn(tracer_out[f, tiles - 1, at, :], to - (LANES - 1)), eastward
                )
                westward = jnp.where(lane == to, turn(tracer_out[f, 0, at, :], to), westward)
            return [(east_out, (at, whole), eastward), (west_out, (at, whole), westward)]

        each_row_tile(tracer_part, 4)
    for copy in loads[2]:
        copy.wait()

    def speed_part(start):
        at = pl.ds(start, SUBLANES)
        masked = (lane >= mask_lane) & (lane < mask_lane + tracers)
        speeds = jnp.zeros((SUBLANES, LANES), F32)
        for f in range(levels):
            moved = turn(speed_out[f, tiles - 1, at, :], mask_lane + f - (LANES - 1))
            speeds = jnp.where(lane == mask_lane + f, moved, speeds)
        speeds = speeds + turn(speeds, levels)
        last = sea_out[tiles - 1, at, LANES - 1 : LANES]
        first = sea_out[0, at, 0:1]
        eastward = jnp.where(masked, speeds * last, east_out[at, :])
        westward = jnp.where(masked, jnp.broadcast_to(first, (SUBLANES, LANES)), west_out[at, :])
        return [(east_out, (at, whole), eastward), (west_out, (at, whole), westward)]

    each_row_tile(speed_part, 4)
    for copy in loads[3]:
        copy.wait()


def in_vmem(x):
    return pltpu.with_memory_space_constraint(x, pltpu.VMEM)


def in_hbm(x):
    return pltpu.with_memory_space_constraint(x, pltpu.HBM)


def resident(*shape):
    return pltpu.VMEM(shape, F32)


VMEM_SPEC = pl.BlockSpec(memory_space=pltpu.VMEM)
ANY_SPEC = pl.BlockSpec(memory_space=pl.ANY)


def load_and_pack_columns(arrays, levels, rows, cols):
    temp, salt, east, north, land, ice, u, v, pressure, wind_x, wind_y = arrays
    tiles = cols // LANES
    message = resident(rows + 2 * HALO, LANES)
    deep = resident(2 * levels, tiles, rows, LANES)
    return pl.pallas_call(
        lambda *refs: columns_kernel(levels, *refs),
        in_specs=[ANY_SPEC] * 11,
        out_specs=[VMEM_SPEC] * 6,
        out_shape=[
            deep, deep, resident(tiles, rows, LANES),
            resident(ICE, tiles, sublane_rows(rows) * SUBLANES, LANES), message, message,
        ],
        scratch_shapes=[
            pltpu.VMEM((2, tiles, rows, LANES), jnp.int32),
            pltpu.VMEM((5, tiles, rows, LANES), F32),
            pltpu.SemaphoreType.DMA((2, tiles)),
            pltpu.SemaphoreType.DMA((5, tiles)),
            pltpu.SemaphoreType.DMA((2, tiles)),
            pltpu.SemaphoreType.DMA((2, 2, tiles)),
        ],
        name="edge_columns",
        compiler_params=pltpu.CompilerParams(vmem_limit_bytes=8 << 20),
        cost_estimate=pl.CostEstimate(flops=5000000, bytes_accessed=12 << 20, transcendentals=0),
    )(*[in_hbm(a) for a in (land, ice, u, v, pressure, wind_x, wind_y, east, north, temp, salt)])


def halo_kernel(levels, first, second, field_in, east_in, west_in,
                halo_ref, field_out, east_out, west_out):
    lat = lax.axis_index("lat")
    even = lax.rem(lat, 2) == 0
    top = lat == lax.axis_size("lat") - 1
    lane, sublane = lane_ids(), sublane_ids()
    tiles = field_out.shape[1]
    rows = east_out.shape[0] - 2 * HALO
    south_fields, north_fields = [], []
    for f in range(ICE):
        at = slice(HALO * f, HALO * (f + 1))
        north_row, south_row = [], []
        for t in range(tiles):
            cols = slice(LANES * t, LANES * (t + 1))
            mirror = slice(LANES * (tiles - 1 - t), LANES * (tiles - t))
            south = jnp.where(even, second[at, cols], first[at, cols])
            plain = jnp.where(even, first[at, cols], second[at, cols])
            turned = jnp.take_along_axis(second[at, mirror], LANES - 1 - lane, axis=1)
            turned = jnp.take_along_axis(turned, SUBLANES - 1 - sublane, axis=0)
            north = jnp.where(top, turned * FOLD_SIGN[f], plain)
            field_out[f, t, 0:HALO, :] = south
            field_out[f, t, rows + HALO : rows + 2 * HALO, :] = north
            south_row.append(south)
            north_row.append(north)
        south_fields.append(south_row)
        north_fields.append(north_row)
    rest = slice(HALO * ICE, first.shape[0])
    halo_ref[0] = jnp.where(even, second[rest, :], first[rest, :])
    halo_ref[1] = jnp.where(top, 0.0, jnp.where(even, first[rest, :], second[rest, :]))
    for at, fields in ((rows, south_fields), (rows + HALO, north_fields)):
        east_out[at : at + HALO, :] = east_columns([f[-1] for f in fields], lane)
        west_out[at : at + HALO, :] = west_columns([f[0] for f in fields], lane)


def merge_halo(first, second, fields, east_msg, west_msg, levels):
    height, cols = first.shape
    return pl.pallas_call(
        lambda *refs: halo_kernel(levels, *refs),
        in_specs=[VMEM_SPEC] * 5,
        out_specs=[VMEM_SPEC] * 4,
        out_shape=[
            resident(2, height - HALO * ICE, cols), resident(*fields.shape),
            resident(*east_msg.shape), resident(*west_msg.shape),
        ],
        input_output_aliases={2: 1, 3: 2, 4: 3},
        name="halo_rows",
        compiler_params=pltpu.CompilerParams(vmem_limit_bytes=8 << 20),
        cost_estimate=pl.CostEstimate(flops=100000, bytes_accessed=1 << 19, transcendentals=0),
    )(first, second, in_vmem(fields), in_vmem(east_msg), in_vmem(west_msg))


def advect_kernel(levels, tracer_ref, speed_ref, sea, halo, out, mask_e, mask_n):
    tiles, rows = sea.shape[:2]
    count = rows // SUBLANES
    group = next(c for c in (6, 4, 2) if count % c == 0)
    lane, sublane = lane_ids(), sublane_ids()
    extra_row = 2 * levels
    whole = slice(None)

    def rows_at(k, offset=0):
        start = pl.multiple_of(k * SUBLANES, SUBLANES)
        return pl.ds(start + offset if offset else start, SUBLANES)

    def row(side, index, t):
        cols = slice(LANES * t, LANES * (t + 1))
        return jnp.broadcast_to(halo[side, index : index + 1, cols], (SUBLANES, LANES))

    def from_next(values):
        turned = [turn(v, -1) for v in values]
        return [
            jnp.where(lane == LANES - 1, turned[t + 1], turned[t]) if t + 1 < tiles else turned[t]
            for t in range(tiles)
        ]

    def from_last(values):
        turned = [turn(v, 1) for v in values]
        return [jnp.where(lane == 0, turned[t - 1], turned[t]) for t in range(tiles)]

    def in_groups(body, carry):
        def some(start, carry, last):
            writes = []
            for j in range(group):
                more, carry = body(start + j, last and j == group - 1, carry)
                writes += more
            for ref, where, value in writes:
                ref[where] = value
            return carry

        groups = count // group
        carry = lax.fori_loop(0, groups - 1, lambda n, c: some(n * group, c, False), carry)
        return some((groups - 1) * group, carry, True)

    def row_above(load, k, last, past):
        if not last:
            return load(rows_at(k, 1))
        return jnp.where(sublane == SUBLANES - 1, past, turn(load(rows_at(k)), -1, 0))

    def masks(k, last, carry):
        here = [sea[t, rows_at(k), :] for t in range(tiles)]
        beside = from_next(here)
        writes = []
        for t in range(tiles):
            above = row_above(lambda at, t=t: sea[t, at, :], k, last, row(1, extra_row, t))
            face = here[t] * beside[t]
            if t == tiles - 1:
                face = jnp.where(lane == LANES - 1, 0.0, face)
            writes.append((mask_e, (t, rows_at(k), whole), face))
            writes.append((mask_n, (t, rows_at(k), whole), here[t] * above))
        return writes, carry

    in_groups(masks, 0)
    for level in range(levels):
        entering = []
        for f in (level, levels + level):
            for t in range(tiles):
                speed = row(0, extra_row + level, t) * sea[t, 0:SUBLANES, :]
                start = tracer_ref[f, t, 0:SUBLANES, :]
                entering.append(speed * jnp.where(speed > 0, row(0, f, t), start))

        def body(k, last, carry, level=level):
            at = rows_at(k)
            fast_e = [speed_ref[level, t, at, :] * mask_e[t, at, :] for t in range(tiles)]
            fast_n = [speed_ref[levels + level, t, at, :] * mask_n[t, at, :] for t in range(tiles)]
            writes, result = [], []
            for f in (level, levels + level):
                here = [tracer_ref[f, t, at, :] for t in range(tiles)]
                beside = from_next(here)
                flux_e = [
                    fast_e[t] * jnp.where(fast_e[t] > 0, here[t], beside[t]) for t in range(tiles)
                ]
                before = from_last(flux_e)
                for t in range(tiles):
                    above = row_above(
                        lambda at, f=f, t=t: tracer_ref[f, t, at, :], k, last, row(1, f, t)
                    )
                    flux_n = fast_n[t] * jnp.where(fast_n[t] > 0, here[t], above)
                    turned = turn(flux_n, 1, 0)
                    below = jnp.where(sublane == 0, carry[len(result)], turned)
                    value = here[t] - ((flux_e[t] - before[t]) + (flux_n - below))
                    writes.append((out, (f, t, at, whole), value))
                    result.append(turned)
            return writes, tuple(result)

        in_groups(body, tuple(entering))


def advect(tracers, speeds, sea, halo, levels):
    tiles, rows = sea.shape[:2]
    return pl.pallas_call(
        lambda *refs: advect_kernel(levels, *refs),
        in_specs=[VMEM_SPEC] * 4,
        out_specs=VMEM_SPEC,
        out_shape=resident(*tracers.shape),
        scratch_shapes=[pltpu.VMEM((tiles, rows, LANES), F32)] * 2,
        name="advect",
        compiler_params=pltpu.CompilerParams(vmem_limit_bytes=8 << 20),
        cost_estimate=pl.CostEstimate(flops=30000000, bytes_accessed=16 << 20, transcendentals=0),
    )(in_vmem(tracers), in_vmem(speeds), in_vmem(sea), in_vmem(halo))


def sublane_rows(rows):
    return (rows + 2 * HALO) // SUBLANES | 1


def in_chunks_of(count, body, group):
    size = max(c for c in range(1, 21) if count % c == 0)

    def step(n, carry):
        for start in range(0, size, group):
            seen, writes = {}, []

            def load(ref, j, *where):
                key = (id(ref), j, *[str(w) for w in where])
                if key not in seen:
                    seen[key] = ref[(n * size + j, slice(None), *where)]
                return seen[key]

            for j in range(start, min(start + group, size)):
                writes += body(n * size + j, j, load)
            for ref, where, value in writes:
                ref[where] = value
        return carry

    lax.fori_loop(0, count // size, step, 0)


def ice_kernel(levels, rows, row_total, *refs):
    (fields_in, tracers_in, speeds_in, east_own, west_own, from_west, from_east,
     temp_out, salt_out, u_out, v_out,
     messages, moved, done, vel_u, vel_v, str_a, str_b, str_c,
     third, force, push_x, push_y, turn_a, turn_b, edge_w, edge_e,
     msg_sem, out_sem, vel_sem) = refs
    tiles = fields_in.shape[1]
    count = sublane_rows(rows)
    tracers = 2 * levels
    lane, sublane = lane_ids(), sublane_ids()
    own = pl.ds(HALO, rows)
    wide = tiles + 1
    whole = slice(None)

    def cut(t):
        return slice(LANES * t, LANES * (t + 1))

    copies = []
    for n, ref in enumerate((from_west, from_east)):
        copies.append((ref.at[pl.ds(0, rows), :], messages.at[n, own, :]))
        copies.append((ref.at[pl.ds(rows, HALO), :], messages.at[n, pl.ds(0, HALO), :]))
        copies.append(
            (ref.at[pl.ds(rows + HALO, HALO), :], messages.at[n, pl.ds(rows + HALO, HALO), :])
        )
    loads = [pltpu.make_async_copy(a, b, msg_sem.at[k]) for k, (a, b) in enumerate(copies)]
    for copy in loads:
        copy.start()
    past = (rows + 2 * HALO, count * SUBLANES)
    if past[0] < past[1]:
        for n in range(2):
            messages[n, past[0] : past[1], :] = jnp.zeros((past[1] - past[0], LANES), F32)
    for copy in loads:
        copy.wait()

    def edge_fluxes(k, carry):
        at = pl.ds(pl.multiple_of(k * SUBLANES + HALO, SUBLANES), SUBLANES)
        put = pl.ds(pl.multiple_of(k * SUBLANES, SUBLANES), SUBLANES)
        west, east_side = messages[0, at, :], messages[1, at, :]
        mine_e, mine_w = east_own[put, :], west_own[put, :]
        speed = turn(west, -tracers)
        edge_w[put, :] = speed * jnp.where(speed > 0, west, mine_w) * turn(mine_w, -tracers)
        speed = turn(mine_e, -tracers)
        edge_e[put, :] = speed * jnp.where(speed > 0, mine_e, east_side) * turn(east_side, -tracers)
        return carry

    lax.fori_loop(0, rows // SUBLANES, edge_fluxes, 0, unroll=8)

    def fixed(f, put):
        low, high = tracers_in[f, 0, put, :], tracers_in[f, tiles - 1, put, :]
        inflow = jnp.where(lane == 0, turn(edge_w[put, :], -(TRACER_LANE + f)), 0.0)
        outflow = jnp.where(
            lane == LANES - 1, turn(edge_e[put, :], LANES - 1 - TRACER_LANE - f), 0.0
        )
        return low + inflow, high - outflow

    def stores(f):
        out = temp_out.at[f] if f < levels else salt_out.at[f - levels]
        return [
            pltpu.make_async_copy(
                moved.at[f, t], out.at[:, pl.ds(LANES * t, LANES)], out_sem.at[f, t]
            )
            for t in range(tiles)
        ]

    pending = []
    for f in [f for f in range(tracers) if f % levels]:

        def fix(n, carry, f=f):
            results = []
            for j in range(8):
                put = pl.ds(pl.multiple_of((n * 8 + j) * SUBLANES, SUBLANES), SUBLANES)
                results.append((put, fixed(f, put)))
            for put, (low, high) in results:
                moved[f, 0, put, :] = low
                moved[f, tiles - 1, put, :] = high
            return carry

        lax.fori_loop(0, rows // SUBLANES // 8, fix, 0)
        for copy in stores(f):
            copy.start()
            pending.append(copy)

    def spread(ref, i, *lead):
        return ref[(*lead, pl.ds(i, SUBLANES, stride=count), whole)]

    lat = lax.axis_index("lat")

    def prepare(i, _, load):
        per_tile = [[spread(fields_in, i, f, t) for f in range(ICE)] for t in range(tiles)]
        west, east_side = spread(messages, i, 0), spread(messages, i, 1)
        extra = []
        for f in range(ICE):
            low, high = per_tile[0][f], per_tile[-1][f]
            middle = turn(jnp.where(lane < LANES // 2, high, low), 48)
            border = turn(high, -24)
            start = HALO * f + 2 * HALO
            beyond = jnp.where((lane >= start) & (lane < start + HALO), west, east_side)
            beyond = turn(beyond, 104 - HALO * f)
            x = jnp.where(lane < 32, low, middle)
            x = jnp.where(lane >= 64, border, x)
            extra.append(jnp.where(lane >= 104, beyond, x))
        writes = []
        for t, fields in enumerate(per_tile + [extra]):
            u0, v0, strength, covered, drive_x, drive_y = fields
            writes.append((vel_u, (i + 1, whole, cut(t)), u0))
            writes.append((vel_v, (i + 1, whole, cut(t)), v0))
            writes.append((third, (i, whole, cut(t)), covered * (1.0 / 3.0)))
            writes.append((force, (i, whole, cut(t)), strength * covered * (1.0 / 12.0)))
            writes.append((push_x, (i, whole, cut(t)), 0.5 * drive_x))
            writes.append((push_y, (i, whole, cut(t)), 0.5 * drive_y))
        y = lat * rows - HALO + sublane * count + i
        y = jnp.where(y >= row_total, 2 * row_total - 1 - y, y)
        coriolis = 0.5 * (2 * y + 1 - row_total).astype(F32) / row_total
        turning = 0.5 * coriolis
        scale = 3.0 / (DIAGONAL * DIAGONAL + turning * turning)
        writes.append((turn_a, (i,), DIAGONAL * scale))
        writes.append((turn_b, (i,), turning * scale))
        return writes

    in_chunks_of(count, prepare, 2)

    def wrap(*fields):
        for ref in fields:
            ref[0] = turn(ref[count], 1, 0)
            ref[count + 1] = turn(ref[1], -1, 0)

    def strain_stress(first):
        def body(i, j, load):
            writes = []
            for t in range(wide):
                c = cut(t)
                u, v = load(vel_u, j + 1, c), load(vel_v, j + 1, c)
                dudx, dvdx = turn(u, -1) - turn(u, 1), turn(v, -1) - turn(v, 1)
                dudy = load(vel_u, j + 2, c) - load(vel_u, j, c)
                dvdy = load(vel_v, j + 2, c) - load(vel_v, j, c)
                div, ten, shr = dudx + dvdy, dudx - dvdy, dudy + dvdx
                square = div * div + 0.25 * (ten * ten + shr * shr) + 1.0
                base = load(force, j, c)
                zeta = base * lax.rsqrt(square)
                quarter = 0.25 * zeta
                even = zeta * div - base
                odd = quarter * ten
                new = [even + odd, even - odd, quarter * shr]
                for n, ref in enumerate((str_a, str_b, str_c)):
                    if not first:
                        new[n] = new[n] + load(third, j, c) * load(ref, j + 1, c)
                    writes.append((ref, (i + 1, whole, c), new[n]))
            return writes

        in_chunks_of(count, body, 3)
        wrap(str_a, str_b, str_c)

    def momentum():
        def body(i, j, load):
            ar, br = load(turn_a, j), load(turn_b, j)
            writes = []
            for t in range(wide):
                c = cut(t)
                a, s = load(str_a, j + 1, c), load(str_c, j + 1, c)
                fx = (turn(a, -1) - turn(a, 1)) + (load(str_c, j + 2, c) - load(str_c, j, c))
                fy = (turn(s, -1) - turn(s, 1)) + (load(str_b, j + 2, c) - load(str_b, j, c))
                ru = (load(vel_u, j + 1, c) + load(push_x, j, c)) + fx
                rv = (load(vel_v, j + 1, c) + load(push_y, j, c)) + fy
                keep = load(third, j, c)
                writes.append((vel_u, (i + 1, whole, c), (ar * ru + br * rv) * keep))
                writes.append((vel_v, (i + 1, whole, c), (ar * rv - br * ru) * keep))
            return writes

        in_chunks_of(count, body, 3)
        wrap(vel_u, vel_v)

    wrap(vel_u, vel_v)
    for subcycle in range(SUBCYCLES):
        strain_stress(subcycle == 0)
        momentum()

    def gather(i, j, load):
        writes = []
        for n, ref in enumerate((vel_u, vel_v)):
            borders = ref[i + 1, :, cut(tiles)]
            middle, outer = turn(borders, -48), turn(borders, 24)
            low, high = ref[i + 1, :, cut(0)], ref[i + 1, :, cut(tiles - 1)]
            low = jnp.where(lane < HALO, borders, jnp.where(lane >= LANES - HALO, middle, low))
            high = jnp.where(lane < HALO, middle, jnp.where(lane >= LANES - HALO, outer, high))
            put = pl.ds(i, SUBLANES, stride=count)
            writes.append((done, (n, 0, put, whole), low))
            writes.append((done, (n, tiles - 1, put, whole), high))
        return writes

    in_chunks_of(count, gather, 4)
    finals = []
    for n, out in enumerate((u_out, v_out)):
        for t in range(tiles):
            finals.append(
                pltpu.make_async_copy(
                    done.at[n, t, own, :], out.at[:, pl.ds(LANES * t, LANES)], vel_sem.at[n, t]
                )
            )
            finals[-1].start()

    def warm(n, carry):
        writes = []
        for j in range(4):
            start = pl.multiple_of((n * 4 + j) * SUBLANES, SUBLANES)
            put, at = pl.ds(start, SUBLANES), pl.ds(start + HALO, SUBLANES)
            sst, sss = fixed(0, put), fixed(levels, put)
            for t in range(tiles):
                slip_u = done[0, t, at, :] - speeds_in[0, t, put, :]
                slip_v = done[1, t, at, :] - speeds_in[levels, t, put, :]
                heat = HEAT_RATE * fields_in[3, t, at, :] * (1.0 + (slip_u * slip_u + slip_v * slip_v))
                heat = heat * (sst[t] + FREEZE_SLOPE * sss[t])
                writes.append((0, t, put, sst[t] - heat))
                writes.append((levels, t, put, sss[t] - SALT_RATE * heat))
        for f, t, put, value in writes:
            moved[f, t, put, :] = value
        return carry

    lax.fori_loop(0, rows // SUBLANES // 4, warm, 0)
    for f in (0, levels):
        copies = stores(f)
        for copy in copies:
            copy.start()
        finals += copies
    for copy in pending + finals:
        copy.wait()


def ice_and_edges(fields, tracers, speeds, east_own, west_own, from_west, from_east,
                  levels, rows, cols, row_total):
    tiles = cols // LANES
    count = sublane_rows(rows)
    extended = count * SUBLANES
    deep = jax.ShapeDtypeStruct((levels, rows, cols), F32)
    flat = jax.ShapeDtypeStruct((rows, cols), F32)
    wide = LANES * (tiles + 1)
    looped = pltpu.VMEM((count + 2, SUBLANES, wide), F32)
    plain = pltpu.VMEM((count, SUBLANES, wide), F32)
    narrow = pltpu.VMEM((count, SUBLANES, LANES), F32)
    edge = pltpu.VMEM((rows, LANES), F32)
    return pl.pallas_call(
        lambda *refs: ice_kernel(levels, rows, row_total, *refs),
        in_specs=[VMEM_SPEC] * 5 + [ANY_SPEC] * 2,
        out_specs=[ANY_SPEC] * 4,
        out_shape=[deep, deep, flat, flat],
        scratch_shapes=[
            pltpu.VMEM((2, extended, LANES), F32),
            pltpu.VMEM((2 * levels, tiles, rows, LANES), F32),
            pltpu.VMEM((2, tiles, extended, LANES), F32),
            looped, looped, looped, looped, looped,
            plain, plain, plain, plain, narrow, narrow, edge, edge,
            pltpu.SemaphoreType.DMA((6,)),
            pltpu.SemaphoreType.DMA((2 * levels, tiles)),
            pltpu.SemaphoreType.DMA((2, tiles)),
        ],
        name="ice",
        compiler_params=pltpu.CompilerParams(vmem_limit_bytes=24 << 20),
        cost_estimate=pl.CostEstimate(flops=60000000, bytes_accessed=16 << 20, transcendentals=0),
    )(*[in_vmem(a) for a in (fields, tracers, speeds, east_own, west_own)], from_west, from_east)


def per_device(*arrays):
    levels, rows, cols = arrays[0].shape
    lon_count, lat_count = lax.axis_size("lon"), lax.axis_size("lat")
    assert cols == 2 * LANES and rows % (2 * HALO) == 0 and lat_count % 2 == 0
    height = -(-(HALO * ICE + 3 * levels) // SUBLANES) * SUBLANES

    def place(lat, lon):
        return lon * lat_count + lat

    first_pairs, second_pairs = [], []
    for lon in range(lon_count):
        for lat in range(lat_count):
            first_pairs.append((place(lat, lon), place(lat ^ 1, lon)))
            if lat == lat_count - 1:
                second_pairs.append((place(lat, lon), place(lat, lon_count - 1 - lon)))
            elif lat:
                second_pairs.append((place(lat, lon), place(((lat + 1) ^ 1) - 1, lon)))
    first, second = pack_rows(arrays, levels, rows, cols, height)
    first = lax.ppermute(first, ("lon", "lat"), first_pairs)
    second = lax.ppermute(second, ("lon", "lat"), second_pairs)
    tracers, speeds, sea, fields, east_msg, west_msg = load_and_pack_columns(
        arrays, levels, rows, cols
    )
    halo, fields, east_msg, west_msg = merge_halo(first, second, fields, east_msg, west_msg, levels)
    eastward = [(i, (i + 1) % lon_count) for i in range(lon_count)]
    from_west = lax.ppermute(east_msg, "lon", eastward)
    from_east = lax.ppermute(west_msg, "lon", [(b, a) for a, b in eastward])
    moved = advect(tracers, speeds, sea, halo, levels)
    return ice_and_edges(fields, moved, speeds, east_msg, west_msg, from_west, from_east,
                         levels, rows, cols, rows * lat_count)


def solution(mesh):
    deep, flat = P(None, "lat", "lon"), P("lat", "lon")
    return jax.shard_map(
        per_device,
        mesh=mesh,
        in_specs=(deep,) * 4 + (flat,) * 7,
        out_specs=(deep, deep, flat, flat),
        check_vma=False,
    )
```

```python
import jax
import jax.numpy as jnp
from jax import lax
from jax.experimental import pallas as pl
from jax.experimental.pallas import tpu as pltpu
from jax.sharding import PartitionSpec as P

SUBCYCLES = 4
HEAT_RATE = 0.1
SALT_RATE = 0.5
FREEZE_SLOPE = 0.054
DIAGONAL = 1.5
HALO = 2 * SUBCYCLES
LANES = 128
SUBLANES = 8
ICE = 6
FOLD_SIGN = (-1.0, -1.0, 1.0, 1.0, -1.0, -1.0)
TRACER_LANE = 64
F32 = jnp.float32


def lane_ids():
    return lax.broadcasted_iota(jnp.int32, (SUBLANES, LANES), 1)


def sublane_ids():
    return lax.broadcasted_iota(jnp.int32, (SUBLANES, LANES), 0)


def turn(x, shift, axis=1):
    shift = shift % x.shape[axis]
    return pltpu.roll(x, shift, axis) if shift else x


def ice_fields(land, ice, u, v, pressure, wind_x, wind_y, ocean_u, ocean_v):
    covered = land.astype(F32) * ice.astype(F32)
    return (u * covered, v * covered, pressure, covered, wind_x + ocean_u, wind_y + ocean_v)


def east_columns(fields, lane):
    packed = jnp.zeros((SUBLANES, LANES), F32)
    for f, tile in enumerate(fields):
        start = HALO * f + 2 * HALO
        moved = turn(tile, start - (LANES - HALO))
        packed = jnp.where((lane >= start) & (lane < start + HALO), moved, packed)
    return packed


def west_columns(fields, lane):
    packed = jnp.zeros((SUBLANES, LANES), F32)
    for f, tile in enumerate(fields):
        start = HALO * f
        packed = jnp.where((lane >= start) & (lane < start + HALO), turn(tile, start), packed)
    return packed


def rows_kernel(levels, *refs):
    tops, bottoms = refs[0:12], refs[12:24]
    first_ref, second_ref = refs[24:26]
    even = lax.rem(lax.axis_index("lat"), 2) == 0

    def message(group, row, northward):
        land, ice, u, v, pressure, wind_x, wind_y, east, north, temp, salt = (
            r for r in group[:11]
        )
        fields = ice_fields(
            land[...], ice[...], u[...], v[...], pressure[...], wind_x[...], wind_y[...],
            east[0], north[0],
        )
        sea = land[row : row + 1, :].astype(F32)
        parts = list(fields) + [temp[:, row, :], salt[:, row, :]]
        if northward:
            parts.append(north[:, row, :] * sea)
        else:
            parts.append(jnp.broadcast_to(sea, (levels, sea.shape[1])))
        return parts

    top = message(tops, SUBLANES - 1, True)
    bottom = message(bottoms, 0, False)
    at = 0
    for t, b in zip(top, bottom):
        size = t.shape[0]
        first_ref[at : at + size, :] = jnp.where(even, t, b)
        second_ref[at : at + size, :] = jnp.where(even, b, t)
        at += size
    pad = first_ref.shape[0] - at
    if pad:
        first_ref[at:, :] = jnp.zeros((pad, first_ref.shape[1]), F32)
        second_ref[at:, :] = jnp.zeros((pad, second_ref.shape[1]), F32)


def pack_rows(arrays, levels, rows, cols, height):
    temp, salt, east, north, land, ice, u, v, pressure, wind_x, wind_y = arrays
    operands = [land, ice, u, v, pressure, wind_x, wind_y, east, north, temp, salt, land]
    last = rows // SUBLANES - 1

    def spec(array, block, count):
        if array.ndim == 2:
            return pl.BlockSpec((SUBLANES, cols), lambda _: (block, 0))
        return pl.BlockSpec((count, SUBLANES, cols), lambda _: (0, block, 0))

    counts = [1] * 7 + [1, levels, levels, levels, 1]
    specs = [spec(a, last, c) for a, c in zip(operands, counts)]
    specs += [spec(a, 0, c) for a, c in zip(operands, counts)]
    out = jax.ShapeDtypeStruct((height, cols), F32)
    return pl.pallas_call(
        lambda *refs: rows_kernel(levels, *refs),
        grid=(1,),
        in_specs=specs,
        out_specs=[pl.BlockSpec((height, cols), lambda _: (0, 0))] * 2,
        out_shape=[out, out],
        name="edge_rows",
        compiler_params=pltpu.CompilerParams(vmem_limit_bytes=8 << 20),
        cost_estimate=pl.CostEstimate(flops=100000, bytes_accessed=1 << 20, transcendentals=0),
    )(*[in_hbm(a) for a in operands + operands])


def columns_kernel(levels, land, ice, u, v, pressure, wind_x, wind_y, east, north, temp, salt,
                   tracer_out, speed_out, sea_out, field_out, east_out, west_out,
                   ints, floats, int_sem, float_sem, tracer_sem, speed_sem):
    lane = lane_ids()
    rows = sea_out.shape[1]
    tiles = sea_out.shape[0]
    tracers = 2 * levels
    first_lane = TRACER_LANE
    mask_lane = TRACER_LANE + tracers

    def cut(ref, t):
        return ref.at[..., pl.ds(LANES * t, LANES)]

    surface, loads = [], {}
    for t in range(tiles):
        for n, ref in enumerate((land, ice)):
            surface.append(pltpu.make_async_copy(cut(ref, t), ints.at[n, t], int_sem.at[n, t]))
        for n, ref in enumerate((u, v, pressure, wind_x, wind_y)):
            surface.append(pltpu.make_async_copy(cut(ref, t), floats.at[n, t], float_sem.at[n, t]))
        for n, ref in enumerate((east, north)):
            surface.append(
                pltpu.make_async_copy(
                    cut(ref.at[0], t), speed_out.at[levels * n, t], speed_sem.at[n, 0, t]
                )
            )
    for n, ref in enumerate((temp, salt)):
        loads[n] = [
            pltpu.make_async_copy(
                cut(ref, t), tracer_out.at[pl.ds(levels * n, levels), t], tracer_sem.at[n, t]
            )
            for t in range(tiles)
        ]
    for n, ref in enumerate((east, north)):
        loads[n + 2] = [
            pltpu.make_async_copy(
                cut(ref.at[pl.ds(1, levels - 1)], t),
                speed_out.at[pl.ds(levels * n + 1, levels - 1), t],
                speed_sem.at[n, 1, t],
            )
            for t in range(tiles)
        ]
    for copy in surface + loads[0] + loads[1] + loads[2] + loads[3]:
        copy.start()

    def each_row_tile(body, size):
        def step(n, carry):
            writes = []
            for j in range(size):
                writes += body(pl.multiple_of((n * size + j) * SUBLANES, SUBLANES))
            for ref, where, value in writes:
                ref[where] = value
            return carry

        lax.fori_loop(0, rows // SUBLANES // size, step, 0)

    for copy in surface:
        copy.wait()
    whole = slice(None)

    def ice_part(start):
        at = pl.ds(start, SUBLANES)
        writes, fields = [], []
        for t in range(tiles):
            fields.append(
                ice_fields(
                    ints[0, t, at, :], ints[1, t, at, :], *[floats[n, t, at, :] for n in range(5)],
                    speed_out[0, t, at, :], speed_out[levels, t, at, :],
                )
            )
            writes.append((sea_out, (t, at, whole), ints[0, t, at, :].astype(F32)))
            for f in range(ICE):
                writes.append((field_out, (f, t, pl.ds(start + HALO, SUBLANES), whole), fields[t][f]))
        writes.append((east_out, (at, whole), east_columns(fields[-1], lane)))
        writes.append((west_out, (at, whole), west_columns(fields[0], lane)))
        return writes

    each_row_tile(ice_part, 4)
    for t in range(tiles):
        for f in range(ICE):
            blank = (HALO + rows, field_out.shape[2])
            field_out[f, t, blank[0] : blank[1], :] = jnp.zeros((blank[1] - blank[0], LANES), F32)

    for n in range(2):
        for copy in loads[n]:
            copy.wait()

        def tracer_part(start, n=n):
            at = pl.ds(start, SUBLANES)
            eastward, westward = east_out[at, :], west_out[at, :]
            for f in range(levels * n, levels * (n + 1)):
                to = first_lane + f
                eastward = jnp.where(
                    lane == to, turn(tracer_out[f, tiles - 1, at, :], to - (LANES - 1)), eastward
                )
                westward = jnp.where(lane == to, turn(tracer_out[f, 0, at, :], to), westward)
            return [(east_out, (at, whole), eastward), (west_out, (at, whole), westward)]

        each_row_tile(tracer_part, 8)
    for copy in loads[2]:
        copy.wait()

    def speed_part(start):
        at = pl.ds(start, SUBLANES)
        masked = (lane >= mask_lane) & (lane < mask_lane + tracers)
        speeds = jnp.zeros((SUBLANES, LANES), F32)
        for f in range(levels):
            moved = turn(speed_out[f, tiles - 1, at, :], mask_lane + f - (LANES - 1))
            speeds = jnp.where(lane == mask_lane + f, moved, speeds)
        speeds = speeds + turn(speeds, levels)
        last = sea_out[tiles - 1, at, LANES - 1 : LANES]
        first = sea_out[0, at, 0:1]
        eastward = jnp.where(masked, speeds * last, east_out[at, :])
        westward = jnp.where(masked, jnp.broadcast_to(first, (SUBLANES, LANES)), west_out[at, :])
        return [(east_out, (at, whole), eastward), (west_out, (at, whole), westward)]

    each_row_tile(speed_part, 8)
    for copy in loads[3]:
        copy.wait()


def in_vmem(x):
    return pltpu.with_memory_space_constraint(x, pltpu.VMEM)


def in_hbm(x):
    return pltpu.with_memory_space_constraint(x, pltpu.HBM)


def resident(*shape):
    return pltpu.VMEM(shape, F32)


VMEM_SPEC = pl.BlockSpec(memory_space=pltpu.VMEM)
ANY_SPEC = pl.BlockSpec(memory_space=pl.ANY)


def load_and_pack_columns(arrays, levels, rows, cols):
    temp, salt, east, north, land, ice, u, v, pressure, wind_x, wind_y = arrays
    tiles = cols // LANES
    message = resident(rows + 2 * HALO, LANES)
    deep = resident(2 * levels, tiles, rows, LANES)
    return pl.pallas_call(
        lambda *refs: columns_kernel(levels, *refs),
        in_specs=[ANY_SPEC] * 11,
        out_specs=[VMEM_SPEC] * 6,
        out_shape=[
            deep, deep, resident(tiles, rows, LANES),
            resident(ICE, tiles, sublane_rows(rows) * SUBLANES, LANES), message, message,
        ],
        scratch_shapes=[
            pltpu.VMEM((2, tiles, rows, LANES), jnp.int32),
            pltpu.VMEM((5, tiles, rows, LANES), F32),
            pltpu.SemaphoreType.DMA((2, tiles)),
            pltpu.SemaphoreType.DMA((5, tiles)),
            pltpu.SemaphoreType.DMA((2, tiles)),
            pltpu.SemaphoreType.DMA((2, 2, tiles)),
        ],
        name="edge_columns",
        compiler_params=pltpu.CompilerParams(vmem_limit_bytes=8 << 20),
        cost_estimate=pl.CostEstimate(flops=5000000, bytes_accessed=12 << 20, transcendentals=0),
    )(*[in_hbm(a) for a in (land, ice, u, v, pressure, wind_x, wind_y, east, north, temp, salt)])


def halo_kernel(levels, first, second, field_in, east_in, west_in,
                halo_ref, field_out, east_out, west_out):
    lat = lax.axis_index("lat")
    even = lax.rem(lat, 2) == 0
    top = lat == lax.axis_size("lat") - 1
    lane, sublane = lane_ids(), sublane_ids()
    tiles = field_out.shape[1]
    rows = east_out.shape[0] - 2 * HALO
    south_fields, north_fields = [], []
    for f in range(ICE):
        at = slice(HALO * f, HALO * (f + 1))
        north_row, south_row = [], []
        for t in range(tiles):
            cols = slice(LANES * t, LANES * (t + 1))
            mirror = slice(LANES * (tiles - 1 - t), LANES * (tiles - t))
            south = jnp.where(even, second[at, cols], first[at, cols])
            plain = jnp.where(even, first[at, cols], second[at, cols])
            turned = jnp.take_along_axis(second[at, mirror], LANES - 1 - lane, axis=1)
            turned = jnp.take_along_axis(turned, SUBLANES - 1 - sublane, axis=0)
            north = jnp.where(top, turned * FOLD_SIGN[f], plain)
            field_out[f, t, 0:HALO, :] = south
            field_out[f, t, rows + HALO : rows + 2 * HALO, :] = north
            south_row.append(south)
            north_row.append(north)
        south_fields.append(south_row)
        north_fields.append(north_row)
    rest = slice(HALO * ICE, first.shape[0])
    halo_ref[0] = jnp.where(even, second[rest, :], first[rest, :])
    halo_ref[1] = jnp.where(top, 0.0, jnp.where(even, first[rest, :], second[rest, :]))
    for at, fields in ((rows, south_fields), (rows + HALO, north_fields)):
        east_out[at : at + HALO, :] = east_columns([f[-1] for f in fields], lane)
        west_out[at : at + HALO, :] = west_columns([f[0] for f in fields], lane)


def merge_halo(first, second, fields, east_msg, west_msg, levels):
    height, cols = first.shape
    return pl.pallas_call(
        lambda *refs: halo_kernel(levels, *refs),
        in_specs=[VMEM_SPEC] * 5,
        out_specs=[VMEM_SPEC] * 4,
        out_shape=[
            resident(2, height - HALO * ICE, cols), resident(*fields.shape),
            resident(*east_msg.shape), resident(*west_msg.shape),
        ],
        input_output_aliases={2: 1, 3: 2, 4: 3},
        name="halo_rows",
        compiler_params=pltpu.CompilerParams(vmem_limit_bytes=8 << 20),
        cost_estimate=pl.CostEstimate(flops=100000, bytes_accessed=1 << 19, transcendentals=0),
    )(first, second, in_vmem(fields), in_vmem(east_msg), in_vmem(west_msg))


def advect_kernel(levels, tracer_ref, speed_ref, sea, halo, out, mask_e, mask_n):
    tiles, rows = sea.shape[:2]
    count = rows // SUBLANES
    group = next(c for c in (12, 8, 4, 2) if count % c == 0)
    lane, sublane = lane_ids(), sublane_ids()
    extra_row = 2 * levels
    whole = slice(None)

    def rows_at(k, offset=0):
        start = pl.multiple_of(k * SUBLANES, SUBLANES)
        return pl.ds(start + offset if offset else start, SUBLANES)

    def row(side, index, t):
        cols = slice(LANES * t, LANES * (t + 1))
        return jnp.broadcast_to(halo[side, index : index + 1, cols], (SUBLANES, LANES))

    def from_next(values):
        turned = [turn(v, -1) for v in values]
        return [
            jnp.where(lane == LANES - 1, turned[t + 1], turned[t]) if t + 1 < tiles else turned[t]
            for t in range(tiles)
        ]

    def from_last(values):
        turned = [turn(v, 1) for v in values]
        return [jnp.where(lane == 0, turned[t - 1], turned[t]) for t in range(tiles)]

    def in_groups(body, carry):
        def some(start, carry, last):
            writes = []
            for j in range(group):
                more, carry = body(start + j, last and j == group - 1, carry)
                writes += more
            for ref, where, value in writes:
                ref[where] = value
            return carry

        groups = count // group
        carry = lax.fori_loop(0, groups - 1, lambda n, c: some(n * group, c, False), carry)
        return some((groups - 1) * group, carry, True)

    def row_above(load, k, last, past):
        if not last:
            return load(rows_at(k, 1))
        return jnp.where(sublane == SUBLANES - 1, past, turn(load(rows_at(k)), -1, 0))

    def masks(k, last, carry):
        here = [sea[t, rows_at(k), :] for t in range(tiles)]
        beside = from_next(here)
        writes = []
        for t in range(tiles):
            above = row_above(lambda at, t=t: sea[t, at, :], k, last, row(1, extra_row, t))
            face = here[t] * beside[t]
            if t == tiles - 1:
                face = jnp.where(lane == LANES - 1, 0.0, face)
            writes.append((mask_e, (t, rows_at(k), whole), face))
            writes.append((mask_n, (t, rows_at(k), whole), here[t] * above))
        return writes, carry

    in_groups(masks, 0)
    for level in range(levels):
        entering = []
        for f in (level, levels + level):
            for t in range(tiles):
                speed = row(0, extra_row + level, t) * sea[t, 0:SUBLANES, :]
                start = tracer_ref[f, t, 0:SUBLANES, :]
                entering.append(speed * jnp.where(speed > 0, row(0, f, t), start))

        def body(k, last, carry, level=level):
            at = rows_at(k)
            fast_e = [speed_ref[level, t, at, :] * mask_e[t, at, :] for t in range(tiles)]
            fast_n = [speed_ref[levels + level, t, at, :] * mask_n[t, at, :] for t in range(tiles)]
            writes, result = [], []
            for f in (level, levels + level):
                here = [tracer_ref[f, t, at, :] for t in range(tiles)]
                beside = from_next(here)
                flux_e = [
                    fast_e[t] * jnp.where(fast_e[t] > 0, here[t], beside[t]) for t in range(tiles)
                ]
                before = from_last(flux_e)
                for t in range(tiles):
                    above = row_above(
                        lambda at, f=f, t=t: tracer_ref[f, t, at, :], k, last, row(1, f, t)
                    )
                    flux_n = fast_n[t] * jnp.where(fast_n[t] > 0, here[t], above)
                    turned = turn(flux_n, 1, 0)
                    below = jnp.where(sublane == 0, carry[len(result)], turned)
                    value = here[t] - ((flux_e[t] - before[t]) + (flux_n - below))
                    writes.append((out, (f, t, at, whole), value))
                    result.append(turned)
            return writes, tuple(result)

        in_groups(body, tuple(entering))


def advect(tracers, speeds, sea, halo, levels):
    tiles, rows = sea.shape[:2]
    return pl.pallas_call(
        lambda *refs: advect_kernel(levels, *refs),
        in_specs=[VMEM_SPEC] * 4,
        out_specs=VMEM_SPEC,
        out_shape=resident(*tracers.shape),
        scratch_shapes=[pltpu.VMEM((tiles, rows, LANES), F32)] * 2,
        name="advect",
        compiler_params=pltpu.CompilerParams(vmem_limit_bytes=8 << 20),
        cost_estimate=pl.CostEstimate(flops=30000000, bytes_accessed=16 << 20, transcendentals=0),
    )(in_vmem(tracers), in_vmem(speeds), in_vmem(sea), in_vmem(halo))


def sublane_rows(rows):
    return (rows + 2 * HALO) // SUBLANES | 1


def in_chunks_of(count, body, group):
    size = max(c for c in range(1, 21) if count % c == 0)

    def step(n, carry):
        seen = {}

        def load(ref, j, *where):
            key = (id(ref), j, *[str(w) for w in where])
            if key not in seen:
                seen[key] = ref[(n * size + j, slice(None), *where)]
            return seen[key]

        for start in range(0, size, group):
            writes = []

            for j in range(start, min(start + group, size)):
                writes += body(n * size + j, j, load)
            for ref, where, value in writes:
                ref[where] = value
        return carry

    lax.fori_loop(0, count // size, step, 0)


def ice_kernel(levels, rows, row_total, *refs):
    (fields_in, tracers_in, speeds_in, east_own, west_own, from_west, from_east,
     temp_out, salt_out, u_out, v_out,
     messages, moved, done, vel_u, vel_v, str_a, str_b, str_c,
     third, force, push_x, push_y, turn_a, turn_b, edge_w, edge_e,
     msg_sem, out_sem, vel_sem) = refs
    tiles = fields_in.shape[1]
    count = sublane_rows(rows)
    tracers = 2 * levels
    lane, sublane = lane_ids(), sublane_ids()
    own = pl.ds(HALO, rows)
    wide = tiles + 1
    whole = slice(None)

    def cut(t):
        return slice(LANES * t, LANES * (t + 1))

    copies = []
    for n, ref in enumerate((from_west, from_east)):
        copies.append((ref.at[pl.ds(0, rows), :], messages.at[n, own, :]))
        copies.append((ref.at[pl.ds(rows, HALO), :], messages.at[n, pl.ds(0, HALO), :]))
        copies.append(
            (ref.at[pl.ds(rows + HALO, HALO), :], messages.at[n, pl.ds(rows + HALO, HALO), :])
        )
    loads = [pltpu.make_async_copy(a, b, msg_sem.at[k]) for k, (a, b) in enumerate(copies)]
    for copy in loads:
        copy.start()
    past = (rows + 2 * HALO, count * SUBLANES)
    if past[0] < past[1]:
        for n in range(2):
            messages[n, past[0] : past[1], :] = jnp.zeros((past[1] - past[0], LANES), F32)
    for copy in loads:
        copy.wait()

    def edge_fluxes(k, carry):
        at = pl.ds(pl.multiple_of(k * SUBLANES + HALO, SUBLANES), SUBLANES)
        put = pl.ds(pl.multiple_of(k * SUBLANES, SUBLANES), SUBLANES)
        west, east_side = messages[0, at, :], messages[1, at, :]
        mine_e, mine_w = east_own[put, :], west_own[put, :]
        speed = turn(west, -tracers)
        edge_w[put, :] = speed * jnp.where(speed > 0, west, mine_w) * turn(mine_w, -tracers)
        speed = turn(mine_e, -tracers)
        edge_e[put, :] = speed * jnp.where(speed > 0, mine_e, east_side) * turn(east_side, -tracers)
        return carry

    lax.fori_loop(0, rows // SUBLANES, edge_fluxes, 0, unroll=8)

    def fixed(f, put):
        low, high = tracers_in[f, 0, put, :], tracers_in[f, tiles - 1, put, :]
        inflow = jnp.where(lane == 0, turn(edge_w[put, :], -(TRACER_LANE + f)), 0.0)
        outflow = jnp.where(
            lane == LANES - 1, turn(edge_e[put, :], LANES - 1 - TRACER_LANE - f), 0.0
        )
        return low + inflow, high - outflow

    def stores(f):
        out = temp_out.at[f] if f < levels else salt_out.at[f - levels]
        return [
            pltpu.make_async_copy(
                moved.at[f, t], out.at[:, pl.ds(LANES * t, LANES)], out_sem.at[f, t]
            )
            for t in range(tiles)
        ]

    pending = []
    for f in [f for f in range(tracers) if f % levels]:

        def fix(n, carry, f=f):
            results = []
            for j in range(8):
                put = pl.ds(pl.multiple_of((n * 8 + j) * SUBLANES, SUBLANES), SUBLANES)
                results.append((put, fixed(f, put)))
            for put, (low, high) in results:
                moved[f, 0, put, :] = low
                moved[f, tiles - 1, put, :] = high
            return carry

        lax.fori_loop(0, rows // SUBLANES // 8, fix, 0)
        for copy in stores(f):
            copy.start()
            pending.append(copy)

    def spread(ref, i, *lead):
        return ref[(*lead, pl.ds(i, SUBLANES, stride=count), whole)]

    lat = lax.axis_index("lat")

    def prepare(i, _, load):
        per_tile = [[spread(fields_in, i, f, t) for f in range(ICE)] for t in range(tiles)]
        west, east_side = spread(messages, i, 0), spread(messages, i, 1)
        extra = []
        for f in range(ICE):
            low, high = per_tile[0][f], per_tile[-1][f]
            middle = turn(jnp.where(lane < LANES // 2, high, low), 48)
            border = turn(high, -24)
            start = HALO * f + 2 * HALO
            beyond = jnp.where((lane >= start) & (lane < start + HALO), west, east_side)
            beyond = turn(beyond, 104 - HALO * f)
            x = jnp.where(lane < 32, low, middle)
            x = jnp.where(lane >= 64, border, x)
            extra.append(jnp.where(lane >= 104, beyond, x))
        writes = []
        for t, fields in enumerate(per_tile + [extra]):
            u0, v0, strength, covered, drive_x, drive_y = fields
            writes.append((vel_u, (i + 1, whole, cut(t)), u0))
            writes.append((vel_v, (i + 1, whole, cut(t)), v0))
            writes.append((third, (i, whole, cut(t)), covered * (1.0 / 3.0)))
            writes.append((force, (i, whole, cut(t)), strength * covered * (1.0 / 12.0)))
            writes.append((push_x, (i, whole, cut(t)), 0.5 * drive_x))
            writes.append((push_y, (i, whole, cut(t)), 0.5 * drive_y))
        y = lat * rows - HALO + sublane * count + i
        y = jnp.where(y >= row_total, 2 * row_total - 1 - y, y)
        coriolis = 0.5 * (2 * y + 1 - row_total).astype(F32) / row_total
        turning = 0.5 * coriolis
        scale = 3.0 / (DIAGONAL * DIAGONAL + turning * turning)
        writes.append((turn_a, (i,), DIAGONAL * scale))
        writes.append((turn_b, (i,), turning * scale))
        return writes

    in_chunks_of(count, prepare, 2)

    def wrap(*fields):
        for ref in fields:
            ref[0] = turn(ref[count], 1, 0)
            ref[count + 1] = turn(ref[1], -1, 0)

    def strain_stress(first):
        def body(i, j, load):
            writes = []
            for t in range(wide):
                c = cut(t)
                u, v = load(vel_u, j + 1, c), load(vel_v, j + 1, c)
                dudx, dvdx = turn(u, -1) - turn(u, 1), turn(v, -1) - turn(v, 1)
                dudy = load(vel_u, j + 2, c) - load(vel_u, j, c)
                dvdy = load(vel_v, j + 2, c) - load(vel_v, j, c)
                div, ten, shr = dudx + dvdy, dudx - dvdy, dudy + dvdx
                square = div * div + 0.25 * (ten * ten + shr * shr) + 1.0
                base = load(force, j, c)
                zeta = base * lax.rsqrt(square)
                quarter = 0.25 * zeta
                even = zeta * div - base
                odd = quarter * ten
                new = [even + odd, even - odd, quarter * shr]
                for n, ref in enumerate((str_a, str_b, str_c)):
                    if not first:
                        new[n] = new[n] + load(third, j, c) * load(ref, j + 1, c)
                    writes.append((ref, (i + 1, whole, c), new[n]))
            return writes

        in_chunks_of(count, body, 1)
        wrap(str_a, str_b, str_c)

    def momentum():
        def body(i, j, load):
            ar, br = load(turn_a, j), load(turn_b, j)
            writes = []
            for t in range(wide):
                c = cut(t)
                a, s = load(str_a, j + 1, c), load(str_c, j + 1, c)
                fx = (turn(a, -1) - turn(a, 1)) + (load(str_c, j + 2, c) - load(str_c, j, c))
                fy = (turn(s, -1) - turn(s, 1)) + (load(str_b, j + 2, c) - load(str_b, j, c))
                ru = (load(vel_u, j + 1, c) + load(push_x, j, c)) + fx
                rv = (load(vel_v, j + 1, c) + load(push_y, j, c)) + fy
                keep = load(third, j, c)
                writes.append((vel_u, (i + 1, whole, c), (ar * ru + br * rv) * keep))
                writes.append((vel_v, (i + 1, whole, c), (ar * rv - br * ru) * keep))
            return writes

        in_chunks_of(count, body, 1)
        wrap(vel_u, vel_v)

    wrap(vel_u, vel_v)
    for subcycle in range(SUBCYCLES):
        strain_stress(subcycle == 0)
        momentum()

    def gather(i, j, load):
        writes = []
        for n, ref in enumerate((vel_u, vel_v)):
            borders = ref[i + 1, :, cut(tiles)]
            middle, outer = turn(borders, -48), turn(borders, 24)
            low, high = ref[i + 1, :, cut(0)], ref[i + 1, :, cut(tiles - 1)]
            low = jnp.where(lane < HALO, borders, jnp.where(lane >= LANES - HALO, middle, low))
            high = jnp.where(lane < HALO, middle, jnp.where(lane >= LANES - HALO, outer, high))
            put = pl.ds(i, SUBLANES, stride=count)
            writes.append((done, (n, 0, put, whole), low))
            writes.append((done, (n, tiles - 1, put, whole), high))
        return writes

    in_chunks_of(count, gather, 4)
    finals = []
    for n, out in enumerate((u_out, v_out)):
        for t in range(tiles):
            finals.append(
                pltpu.make_async_copy(
                    done.at[n, t, own, :], out.at[:, pl.ds(LANES * t, LANES)], vel_sem.at[n, t]
                )
            )
            finals[-1].start()

    def warm(n, carry):
        writes = []
        for j in range(4):
            start = pl.multiple_of((n * 4 + j) * SUBLANES, SUBLANES)
            put, at = pl.ds(start, SUBLANES), pl.ds(start + HALO, SUBLANES)
            sst, sss = fixed(0, put), fixed(levels, put)
            for t in range(tiles):
                slip_u = done[0, t, at, :] - speeds_in[0, t, put, :]
                slip_v = done[1, t, at, :] - speeds_in[levels, t, put, :]
                heat = HEAT_RATE * fields_in[3, t, at, :] * (1.0 + (slip_u * slip_u + slip_v * slip_v))
                heat = heat * (sst[t] + FREEZE_SLOPE * sss[t])
                writes.append((0, t, put, sst[t] - heat))
                writes.append((levels, t, put, sss[t] - SALT_RATE * heat))
        for f, t, put, value in writes:
            moved[f, t, put, :] = value
        return carry

    lax.fori_loop(0, rows // SUBLANES // 4, warm, 0)
    for f in (0, levels):
        copies = stores(f)
        for copy in copies:
            copy.start()
        finals += copies
    for copy in pending + finals:
        copy.wait()


def ice_and_edges(fields, tracers, speeds, east_own, west_own, from_west, from_east,
                  levels, rows, cols, row_total):
    tiles = cols // LANES
    count = sublane_rows(rows)
    extended = count * SUBLANES
    deep = jax.ShapeDtypeStruct((levels, rows, cols), F32)
    flat = jax.ShapeDtypeStruct((rows, cols), F32)
    wide = LANES * (tiles + 1)
    looped = pltpu.VMEM((count + 2, SUBLANES, wide), F32)
    plain = pltpu.VMEM((count, SUBLANES, wide), F32)
    narrow = pltpu.VMEM((count, SUBLANES, LANES), F32)
    edge = pltpu.VMEM((rows, LANES), F32)
    return pl.pallas_call(
        lambda *refs: ice_kernel(levels, rows, row_total, *refs),
        in_specs=[VMEM_SPEC] * 5 + [ANY_SPEC] * 2,
        out_specs=[ANY_SPEC] * 4,
        out_shape=[deep, deep, flat, flat],
        scratch_shapes=[
            pltpu.VMEM((2, extended, LANES), F32),
            pltpu.VMEM((2 * levels, tiles, rows, LANES), F32),
            pltpu.VMEM((2, tiles, extended, LANES), F32),
            looped, looped, looped, looped, looped,
            plain, plain, plain, plain, narrow, narrow, edge, edge,
            pltpu.SemaphoreType.DMA((6,)),
            pltpu.SemaphoreType.DMA((2 * levels, tiles)),
            pltpu.SemaphoreType.DMA((2, tiles)),
        ],
        name="ice",
        compiler_params=pltpu.CompilerParams(vmem_limit_bytes=24 << 20),
        cost_estimate=pl.CostEstimate(flops=60000000, bytes_accessed=16 << 20, transcendentals=0),
    )(*[in_vmem(a) for a in (fields, tracers, speeds, east_own, west_own)], from_west, from_east)


def per_device(*arrays):
    levels, rows, cols = arrays[0].shape
    lon_count, lat_count = lax.axis_size("lon"), lax.axis_size("lat")
    assert cols == 2 * LANES and rows % (2 * HALO) == 0 and lat_count % 2 == 0
    height = -(-(HALO * ICE + 3 * levels) // SUBLANES) * SUBLANES

    def place(lat, lon):
        return lon * lat_count + lat

    first_pairs, second_pairs = [], []
    for lon in range(lon_count):
        for lat in range(lat_count):
            first_pairs.append((place(lat, lon), place(lat ^ 1, lon)))
            if lat == lat_count - 1:
                second_pairs.append((place(lat, lon), place(lat, lon_count - 1 - lon)))
            elif lat:
                second_pairs.append((place(lat, lon), place(((lat + 1) ^ 1) - 1, lon)))
    first, second = pack_rows(arrays, levels, rows, cols, height)
    first = lax.ppermute(first, ("lon", "lat"), first_pairs)
    second = lax.ppermute(second, ("lon", "lat"), second_pairs)
    tracers, speeds, sea, fields, east_msg, west_msg = load_and_pack_columns(
        arrays, levels, rows, cols
    )
    halo, fields, east_msg, west_msg = merge_halo(first, second, fields, east_msg, west_msg, levels)
    eastward = [(i, (i + 1) % lon_count) for i in range(lon_count)]
    from_west = lax.ppermute(east_msg, "lon", eastward)
    from_east = lax.ppermute(west_msg, "lon", [(b, a) for a, b in eastward])
    moved = advect(tracers, speeds, sea, halo, levels)
    return ice_and_edges(fields, moved, speeds, east_msg, west_msg, from_west, from_east,
                         levels, rows, cols, rows * lat_count)


def solution(mesh):
    deep, flat = P(None, "lat", "lon"), P("lat", "lon")
    return jax.shard_map(
        per_device,
        mesh=mesh,
        in_specs=(deep,) * 4 + (flat,) * 7,
        out_specs=(deep, deep, flat, flat),
        check_vma=False,
    )
```

```python
import jax
import jax.numpy as jnp
from jax import lax
from jax.experimental import pallas as pl
from jax.experimental.pallas import tpu as pltpu
from jax.sharding import PartitionSpec as P

SUBCYCLES = 4
HEAT_RATE = 0.1
SALT_RATE = 0.5
FREEZE_SLOPE = 0.054
DIAGONAL = 1.5
HALO = 2 * SUBCYCLES
LANES = 128
SUBLANES = 8
ICE = 6
FOLD_SIGN = (-1.0, -1.0, 1.0, 1.0, -1.0, -1.0)
TRACER_LANE = 64
F32 = jnp.float32


def lane_ids():
    return lax.broadcasted_iota(jnp.int32, (SUBLANES, LANES), 1)


def sublane_ids():
    return lax.broadcasted_iota(jnp.int32, (SUBLANES, LANES), 0)


def turn(x, shift, axis=1):
    shift = shift % x.shape[axis]
    return pltpu.roll(x, shift, axis) if shift else x


def ice_fields(land, ice, u, v, pressure, wind_x, wind_y, ocean_u, ocean_v):
    covered = land.astype(F32) * ice.astype(F32)
    return (u * covered, v * covered, pressure, covered, wind_x + ocean_u, wind_y + ocean_v)


def east_columns(fields, lane):
    packed = jnp.zeros((SUBLANES, LANES), F32)
    for f, tile in enumerate(fields):
        start = HALO * f + 2 * HALO
        moved = turn(tile, start - (LANES - HALO))
        packed = jnp.where((lane >= start) & (lane < start + HALO), moved, packed)
    return packed


def west_columns(fields, lane):
    packed = jnp.zeros((SUBLANES, LANES), F32)
    for f, tile in enumerate(fields):
        start = HALO * f
        packed = jnp.where((lane >= start) & (lane < start + HALO), turn(tile, start), packed)
    return packed


def sublane_rows(rows):
    return (rows + 2 * HALO) // SUBLANES | 1


def in_chunks_of(count, body, group):
    size = max(c for c in range(1, 21) if count % c == 0)

    def step(n, carry):
        seen = {}

        def load(ref, j, *where):
            key = (id(ref), j, *[str(w) for w in where])
            if key not in seen:
                seen[key] = ref[(n * size + j, slice(None), *where)]
            return seen[key]

        for start in range(0, size, group):
            writes = []

            for j in range(start, min(start + group, size)):
                writes += body(n * size + j, j, load)
            for ref, where, value in writes:
                ref[where] = value
        return carry

    lax.fori_loop(0, count // size, step, 0)


def rows_kernel(levels, *refs):
    tops, bottoms = refs[0:12], refs[12:24]
    first_ref, second_ref = refs[24:26]
    even = lax.rem(lax.axis_index("lat"), 2) == 0

    def message(group, row, northward):
        land, ice, u, v, pressure, wind_x, wind_y, east, north, temp, salt = (
            r for r in group[:11]
        )
        fields = ice_fields(
            land[...], ice[...], u[...], v[...], pressure[...], wind_x[...], wind_y[...],
            east[0], north[0],
        )
        sea = land[row : row + 1, :].astype(F32)
        parts = list(fields) + [temp[:, row, :], salt[:, row, :]]
        if northward:
            parts.append(north[:, row, :] * sea)
        else:
            parts.append(jnp.broadcast_to(sea, (levels, sea.shape[1])))
        return parts

    top = message(tops, SUBLANES - 1, True)
    bottom = message(bottoms, 0, False)
    at = 0
    for t, b in zip(top, bottom):
        size = t.shape[0]
        first_ref[at : at + size, :] = jnp.where(even, t, b)
        second_ref[at : at + size, :] = jnp.where(even, b, t)
        at += size
    pad = first_ref.shape[0] - at
    if pad:
        first_ref[at:, :] = jnp.zeros((pad, first_ref.shape[1]), F32)
        second_ref[at:, :] = jnp.zeros((pad, second_ref.shape[1]), F32)


def pack_rows(arrays, levels, rows, cols, height):
    temp, salt, east, north, land, ice, u, v, pressure, wind_x, wind_y = arrays
    operands = [land, ice, u, v, pressure, wind_x, wind_y, east, north, temp, salt, land]
    last = rows // SUBLANES - 1

    def spec(array, block, count):
        if array.ndim == 2:
            return pl.BlockSpec((SUBLANES, cols), lambda _: (block, 0))
        return pl.BlockSpec((count, SUBLANES, cols), lambda _: (0, block, 0))

    counts = [1] * 7 + [1, levels, levels, levels, 1]
    specs = [spec(a, last, c) for a, c in zip(operands, counts)]
    specs += [spec(a, 0, c) for a, c in zip(operands, counts)]
    out = jax.ShapeDtypeStruct((height, cols), F32)
    return pl.pallas_call(
        lambda *refs: rows_kernel(levels, *refs),
        grid=(1,),
        in_specs=specs,
        out_specs=[pl.BlockSpec((height, cols), lambda _: (0, 0))] * 2,
        out_shape=[out, out],
        name="edge_rows",
        compiler_params=pltpu.CompilerParams(vmem_limit_bytes=8 << 20),
        cost_estimate=pl.CostEstimate(flops=100000, bytes_accessed=1 << 20, transcendentals=0),
    )(*[in_hbm(a) for a in operands + operands])


def columns_kernel(levels, land, ice, u, v, pressure, wind_x, wind_y, east, north, temp, salt,
                   tracer_out, speed_out, sea_out, field_out, east_out, west_out,
                   ints, floats, int_sem, float_sem, tracer_sem, speed_sem):
    lane = lane_ids()
    rows = sea_out.shape[1]
    tiles = sea_out.shape[0]
    tracers = 2 * levels
    first_lane = TRACER_LANE
    mask_lane = TRACER_LANE + tracers

    def cut(ref, t):
        return ref.at[..., pl.ds(LANES * t, LANES)]

    surface, loads = [], {}
    for t in range(tiles):
        for n, ref in enumerate((land, ice)):
            surface.append(pltpu.make_async_copy(cut(ref, t), ints.at[n, t], int_sem.at[n, t]))
        for n, ref in enumerate((u, v, pressure, wind_x, wind_y)):
            surface.append(pltpu.make_async_copy(cut(ref, t), floats.at[n, t], float_sem.at[n, t]))
        for n, ref in enumerate((east, north)):
            surface.append(
                pltpu.make_async_copy(
                    cut(ref.at[0], t), speed_out.at[levels * n, t], speed_sem.at[n, 0, t]
                )
            )
    for n, ref in enumerate((temp, salt)):
        loads[n] = [
            pltpu.make_async_copy(
                cut(ref, t), tracer_out.at[pl.ds(levels * n, levels), t], tracer_sem.at[n, t]
            )
            for t in range(tiles)
        ]
    for n, ref in enumerate((east, north)):
        loads[n + 2] = [
            pltpu.make_async_copy(
                cut(ref.at[pl.ds(1, levels - 1)], t),
                speed_out.at[pl.ds(levels * n + 1, levels - 1), t],
                speed_sem.at[n, 1, t],
            )
            for t in range(tiles)
        ]
    for copy in surface + loads[0] + loads[1] + loads[2] + loads[3]:
        copy.start()

    def each_row_tile(body, size):
        def step(n, carry):
            writes = []
            for j in range(size):
                writes += body(pl.multiple_of((n * size + j) * SUBLANES, SUBLANES))
            for ref, where, value in writes:
                ref[where] = value
            return carry

        lax.fori_loop(0, rows // SUBLANES // size, step, 0)

    for copy in surface:
        copy.wait()
    whole = slice(None)

    def ice_part(start):
        at = pl.ds(start, SUBLANES)
        writes, fields = [], []
        for t in range(tiles):
            fields.append(
                ice_fields(
                    ints[0, t, at, :], ints[1, t, at, :], *[floats[n, t, at, :] for n in range(5)],
                    speed_out[0, t, at, :], speed_out[levels, t, at, :],
                )
            )
            writes.append((sea_out, (t, at, whole), ints[0, t, at, :].astype(F32)))
            for f in range(ICE):
                writes.append((field_out, (f, t, pl.ds(start + HALO, SUBLANES), whole), fields[t][f]))
        put = pl.ds(start + HALO, SUBLANES)
        writes.append((east_out, (put, whole), east_columns(fields[-1], lane)))
        writes.append((west_out, (put, whole), west_columns(fields[0], lane)))
        return writes

    each_row_tile(ice_part, 4)
    end = HALO + rows
    blank = jnp.zeros((field_out.shape[2] - end, LANES), F32)
    for t in range(tiles):
        for f in range(ICE):
            field_out[f, t, end:, :] = blank
    for ref in (east_out, west_out):
        ref[end:, :] = blank

    for n in range(2):
        for copy in loads[n]:
            copy.wait()

        def tracer_part(start, n=n):
            at, put = pl.ds(start, SUBLANES), pl.ds(start + HALO, SUBLANES)
            eastward, westward = east_out[put, :], west_out[put, :]
            for f in range(levels * n, levels * (n + 1)):
                to = first_lane + f
                eastward = jnp.where(
                    lane == to, turn(tracer_out[f, tiles - 1, at, :], to - (LANES - 1)), eastward
                )
                westward = jnp.where(lane == to, turn(tracer_out[f, 0, at, :], to), westward)
            return [(east_out, (put, whole), eastward), (west_out, (put, whole), westward)]

        each_row_tile(tracer_part, 8)
    for copy in loads[2]:
        copy.wait()

    def speed_part(start):
        at, put = pl.ds(start, SUBLANES), pl.ds(start + HALO, SUBLANES)
        masked = (lane >= mask_lane) & (lane < mask_lane + tracers)
        speeds = jnp.zeros((SUBLANES, LANES), F32)
        for f in range(levels):
            moved = turn(speed_out[f, tiles - 1, at, :], mask_lane + f - (LANES - 1))
            speeds = jnp.where(lane == mask_lane + f, moved, speeds)
        speeds = speeds + turn(speeds, levels)
        last = sea_out[tiles - 1, at, LANES - 1 : LANES]
        first = sea_out[0, at, 0:1]
        eastward = jnp.where(masked, speeds * last, east_out[put, :])
        westward = jnp.where(masked, jnp.broadcast_to(first, (SUBLANES, LANES)), west_out[put, :])
        return [(east_out, (put, whole), eastward), (west_out, (put, whole), westward)]

    each_row_tile(speed_part, 8)
    for copy in loads[3]:
        copy.wait()


def in_vmem(x):
    return pltpu.with_memory_space_constraint(x, pltpu.VMEM)


def in_hbm(x):
    return pltpu.with_memory_space_constraint(x, pltpu.HBM)


def resident(*shape):
    return pltpu.VMEM(shape, F32)


VMEM_SPEC = pl.BlockSpec(memory_space=pltpu.VMEM)
ANY_SPEC = pl.BlockSpec(memory_space=pl.ANY)


def load_and_pack_columns(arrays, levels, rows, cols):
    temp, salt, east, north, land, ice, u, v, pressure, wind_x, wind_y = arrays
    tiles = cols // LANES
    message = resident(sublane_rows(rows) * SUBLANES, LANES)
    deep = resident(2 * levels, tiles, rows, LANES)
    return pl.pallas_call(
        lambda *refs: columns_kernel(levels, *refs),
        in_specs=[ANY_SPEC] * 11,
        out_specs=[VMEM_SPEC] * 6,
        out_shape=[
            deep, deep, resident(tiles, rows, LANES),
            resident(ICE, tiles, sublane_rows(rows) * SUBLANES, LANES), message, message,
        ],
        scratch_shapes=[
            pltpu.VMEM((2, tiles, rows, LANES), jnp.int32),
            pltpu.VMEM((5, tiles, rows, LANES), F32),
            pltpu.SemaphoreType.DMA((2, tiles)),
            pltpu.SemaphoreType.DMA((5, tiles)),
            pltpu.SemaphoreType.DMA((2, tiles)),
            pltpu.SemaphoreType.DMA((2, 2, tiles)),
        ],
        name="edge_columns",
        compiler_params=pltpu.CompilerParams(vmem_limit_bytes=8 << 20),
        cost_estimate=pl.CostEstimate(flops=5000000, bytes_accessed=12 << 20, transcendentals=0),
    )(*[in_hbm(a) for a in (land, ice, u, v, pressure, wind_x, wind_y, east, north, temp, salt)])


def halo_kernel(levels, rows, first, second, field_in, east_in, west_in,
                halo_ref, field_out, east_out, west_out):
    lat = lax.axis_index("lat")
    even = lax.rem(lat, 2) == 0
    top = lat == lax.axis_size("lat") - 1
    lane, sublane = lane_ids(), sublane_ids()
    tiles = field_out.shape[1]
    south_fields, north_fields = [], []
    for f in range(ICE):
        at = slice(HALO * f, HALO * (f + 1))
        north_row, south_row = [], []
        for t in range(tiles):
            cols = slice(LANES * t, LANES * (t + 1))
            mirror = slice(LANES * (tiles - 1 - t), LANES * (tiles - t))
            south = jnp.where(even, second[at, cols], first[at, cols])
            plain = jnp.where(even, first[at, cols], second[at, cols])
            turned = jnp.take_along_axis(second[at, mirror], LANES - 1 - lane, axis=1)
            turned = jnp.take_along_axis(turned, SUBLANES - 1 - sublane, axis=0)
            north = jnp.where(top, turned * FOLD_SIGN[f], plain)
            field_out[f, t, 0:HALO, :] = south
            field_out[f, t, rows + HALO : rows + 2 * HALO, :] = north
            south_row.append(south)
            north_row.append(north)
        south_fields.append(south_row)
        north_fields.append(north_row)
    rest = slice(HALO * ICE, first.shape[0])
    halo_ref[0] = jnp.where(even, second[rest, :], first[rest, :])
    halo_ref[1] = jnp.where(top, 0.0, jnp.where(even, first[rest, :], second[rest, :]))
    for at, fields in ((0, south_fields), (rows + HALO, north_fields)):
        east_out[at : at + HALO, :] = east_columns([f[-1] for f in fields], lane)
        west_out[at : at + HALO, :] = west_columns([f[0] for f in fields], lane)


def merge_halo(first, second, fields, east_msg, west_msg, levels, rows):
    height, cols = first.shape
    return pl.pallas_call(
        lambda *refs: halo_kernel(levels, rows, *refs),
        in_specs=[VMEM_SPEC] * 5,
        out_specs=[VMEM_SPEC] * 4,
        out_shape=[
            resident(2, height - HALO * ICE, cols), resident(*fields.shape),
            resident(*east_msg.shape), resident(*west_msg.shape),
        ],
        input_output_aliases={2: 1, 3: 2, 4: 3},
        name="halo_rows",
        compiler_params=pltpu.CompilerParams(vmem_limit_bytes=8 << 20),
        cost_estimate=pl.CostEstimate(flops=100000, bytes_accessed=1 << 19, transcendentals=0),
    )(first, second, in_vmem(fields), in_vmem(east_msg), in_vmem(west_msg))


def advect_kernel(levels, row_total, tracer_ref, speed_ref, sea, halo, field_ref,
                  out, base_u, base_v, third, force, push_x, push_y, turn_a, turn_b,
                  mask_e, mask_n):
    tiles, rows = sea.shape[:2]
    count = rows // SUBLANES
    group = next(c for c in (12, 8, 4, 2) if count % c == 0)
    lane, sublane = lane_ids(), sublane_ids()
    extra_row = 2 * levels
    whole = slice(None)

    def rows_at(k, offset=0):
        start = pl.multiple_of(k * SUBLANES, SUBLANES)
        return pl.ds(start + offset if offset else start, SUBLANES)

    def row(side, index, t):
        cols = slice(LANES * t, LANES * (t + 1))
        return jnp.broadcast_to(halo[side, index : index + 1, cols], (SUBLANES, LANES))

    def from_next(values):
        turned = [turn(v, -1) for v in values]
        return [
            jnp.where(lane == LANES - 1, turned[t + 1], turned[t]) if t + 1 < tiles else turned[t]
            for t in range(tiles)
        ]

    def from_last(values):
        turned = [turn(v, 1) for v in values]
        return [jnp.where(lane == 0, turned[t - 1], turned[t]) for t in range(tiles)]

    def in_groups(body, carry):
        def some(start, carry, last):
            writes = []
            for j in range(group):
                more, carry = body(start + j, last and j == group - 1, carry)
                writes += more
            for ref, where, value in writes:
                ref[where] = value
            return carry

        groups = count // group
        carry = lax.fori_loop(0, groups - 1, lambda n, c: some(n * group, c, False), carry)
        return some((groups - 1) * group, carry, True)

    def row_above(load, k, last, past):
        if not last:
            return load(rows_at(k, 1))
        return jnp.where(sublane == SUBLANES - 1, past, turn(load(rows_at(k)), -1, 0))

    def masks(k, last, carry):
        here = [sea[t, rows_at(k), :] for t in range(tiles)]
        beside = from_next(here)
        writes = []
        for t in range(tiles):
            above = row_above(lambda at, t=t: sea[t, at, :], k, last, row(1, extra_row, t))
            face = here[t] * beside[t]
            if t == tiles - 1:
                face = jnp.where(lane == LANES - 1, 0.0, face)
            writes.append((mask_e, (t, rows_at(k), whole), face))
            writes.append((mask_n, (t, rows_at(k), whole), here[t] * above))
        return writes, carry

    in_groups(masks, 0)
    for level in range(levels):
        entering = []
        for f in (level, levels + level):
            for t in range(tiles):
                speed = row(0, extra_row + level, t) * sea[t, 0:SUBLANES, :]
                start = tracer_ref[f, t, 0:SUBLANES, :]
                entering.append(speed * jnp.where(speed > 0, row(0, f, t), start))

        def body(k, last, carry, level=level):
            at = rows_at(k)
            fast_e = [speed_ref[level, t, at, :] * mask_e[t, at, :] for t in range(tiles)]
            fast_n = [speed_ref[levels + level, t, at, :] * mask_n[t, at, :] for t in range(tiles)]
            writes, result = [], []
            for f in (level, levels + level):
                here = [tracer_ref[f, t, at, :] for t in range(tiles)]
                beside = from_next(here)
                flux_e = [
                    fast_e[t] * jnp.where(fast_e[t] > 0, here[t], beside[t]) for t in range(tiles)
                ]
                before = from_last(flux_e)
                for t in range(tiles):
                    above = row_above(
                        lambda at, f=f, t=t: tracer_ref[f, t, at, :], k, last, row(1, f, t)
                    )
                    flux_n = fast_n[t] * jnp.where(fast_n[t] > 0, here[t], above)
                    turned = turn(flux_n, 1, 0)
                    below = jnp.where(sublane == 0, carry[len(result)], turned)
                    value = here[t] - ((flux_e[t] - before[t]) + (flux_n - below))
                    writes.append((out, (f, t, at, whole), value))
                    result.append(turned)
            return writes, tuple(result)

        in_groups(body, tuple(entering))
    spread_fields(rows, row_total, field_ref, base_u, base_v, third, force, push_x, push_y,
                  turn_a, turn_b)


def cut(t):
    return slice(LANES * t, LANES * (t + 1))


def spread(ref, i, count, *lead):
    return ref[(*lead, pl.ds(i, SUBLANES, stride=count), slice(None))]


def wrap(ref, count, lanes=slice(None)):
    ref[0, :, lanes] = turn(ref[count, :, lanes], 1, 0)
    ref[count + 1, :, lanes] = turn(ref[1, :, lanes], -1, 0)


def spread_fields(rows, row_total, field_ref, base_u, base_v, third, force, push_x, push_y,
                  turn_a, turn_b):
    tiles = field_ref.shape[1]
    count = sublane_rows(rows)
    lane, sublane = lane_ids(), sublane_ids()
    lat = lax.axis_index("lat")

    def body(i, _, load):
        per_tile = [[spread(field_ref, i, count, f, t) for f in range(ICE)] for t in range(tiles)]
        extra = []
        for f in range(ICE):
            low, high = per_tile[0][f], per_tile[-1][f]
            middle = turn(jnp.where(lane < LANES // 2, high, low), 48)
            x = jnp.where(lane < 32, low, middle)
            extra.append(jnp.where(lane >= 64, turn(high, -24), x))
        writes = []
        for t, fields in enumerate(per_tile + [extra]):
            u0, v0, strength, covered, drive_x, drive_y = fields
            writes.append((base_u, (i + 1, slice(None), cut(t)), u0))
            writes.append((base_v, (i + 1, slice(None), cut(t)), v0))
            writes.append((third, (i, slice(None), cut(t)), covered * (1.0 / 3.0)))
            writes.append((force, (i, slice(None), cut(t)), strength * covered * (1.0 / 12.0)))
            writes.append((push_x, (i, slice(None), cut(t)), 0.5 * drive_x))
            writes.append((push_y, (i, slice(None), cut(t)), 0.5 * drive_y))
        y = lat * rows - HALO + sublane * count + i
        y = jnp.where(y >= row_total, 2 * row_total - 1 - y, y)
        coriolis = 0.5 * (2 * y + 1 - row_total).astype(F32) / row_total
        turning = 0.5 * coriolis
        scale = 3.0 / (DIAGONAL * DIAGONAL + turning * turning)
        writes.append((turn_a, (i,), DIAGONAL * scale))
        writes.append((turn_b, (i,), turning * scale))
        return writes

    in_chunks_of(count, body, 3)
    wrap(base_u, count)
    wrap(base_v, count)


def advect(tracers, speeds, sea, halo, fields, levels, row_total):
    tiles, rows = sea.shape[:2]
    count = sublane_rows(rows)
    wide = LANES * (tiles + 1)
    looped = resident(count + 2, SUBLANES, wide)
    plain = resident(count, SUBLANES, wide)
    narrow = resident(count, SUBLANES, LANES)
    return pl.pallas_call(
        lambda *refs: advect_kernel(levels, row_total, *refs),
        in_specs=[VMEM_SPEC] * 5,
        out_specs=[VMEM_SPEC] * 9,
        out_shape=[
            resident(*tracers.shape), looped, looped, plain, plain, plain, plain, narrow, narrow,
        ],
        scratch_shapes=[pltpu.VMEM((tiles, rows, LANES), F32)] * 2,
        name="advect",
        compiler_params=pltpu.CompilerParams(vmem_limit_bytes=8 << 20),
        cost_estimate=pl.CostEstimate(flops=30000000, bytes_accessed=16 << 20, transcendentals=0),
    )(*[in_vmem(a) for a in (tracers, speeds, sea, halo, fields)])


def ice_kernel(levels, rows, *refs):
    (covered_in, tracers_in, speeds_in, east_own, west_own, from_west, from_east,
     base_u, base_v, third, force, push_x, push_y, turn_a, turn_b,
     temp_out, salt_out, u_out, v_out,
     moved, done, vel_u, vel_v, str_a, str_b, str_c,
     third_x, force_x, push_x_x, push_y_x, edge_w, edge_e,
     out_sem, vel_sem) = refs
    tiles = tracers_in.shape[1]
    count = sublane_rows(rows)
    tracers = 2 * levels
    lane = lane_ids()
    own = pl.ds(HALO, rows)
    wide = tiles + 1
    whole = slice(None)

    def edge_fluxes(k, carry):
        at = pl.ds(pl.multiple_of(k * SUBLANES + HALO, SUBLANES), SUBLANES)
        put = pl.ds(pl.multiple_of(k * SUBLANES, SUBLANES), SUBLANES)
        west, east_side = from_west[at, :], from_east[at, :]
        mine_e, mine_w = east_own[at, :], west_own[at, :]
        speed = turn(west, -tracers)
        edge_w[put, :] = speed * jnp.where(speed > 0, west, mine_w) * turn(mine_w, -tracers)
        speed = turn(mine_e, -tracers)
        edge_e[put, :] = speed * jnp.where(speed > 0, mine_e, east_side) * turn(east_side, -tracers)
        return carry

    lax.fori_loop(0, rows // SUBLANES, edge_fluxes, 0, unroll=8)

    def fixed(f, put):
        low, high = tracers_in[f, 0, put, :], tracers_in[f, tiles - 1, put, :]
        inflow = jnp.where(lane == 0, turn(edge_w[put, :], -(TRACER_LANE + f)), 0.0)
        outflow = jnp.where(
            lane == LANES - 1, turn(edge_e[put, :], LANES - 1 - TRACER_LANE - f), 0.0
        )
        return low + inflow, high - outflow

    def stores(f):
        out = temp_out.at[f] if f < levels else salt_out.at[f - levels]
        return [
            pltpu.make_async_copy(
                moved.at[f, t], out.at[:, pl.ds(LANES * t, LANES)], out_sem.at[f, t]
            )
            for t in range(tiles)
        ]

    deep = [f for f in range(tracers) if f % levels]
    size = next(c for c in (16, 8, 4, 2) if rows // SUBLANES % c == 0)

    def fix(n, carry):
        puts = [
            pl.ds(pl.multiple_of((n * size + j) * SUBLANES, SUBLANES), SUBLANES)
            for j in range(size)
        ]
        for f in deep:
            results = [fixed(f, put) for put in puts]
            for put, (low, high) in zip(puts, results):
                moved[f, 0, put, :] = low
                moved[f, tiles - 1, put, :] = high
        return carry

    lax.fori_loop(0, rows // SUBLANES // size, fix, 0)
    pending = [copy for f in deep for copy in stores(f)]
    for copy in pending:
        copy.start()

    def insert(i, j, load):
        west, east_side = spread(from_west, i, count), spread(from_east, i, count)
        writes = []
        targets = (
            (base_u, vel_u, 1, tiles, 1.0), (base_v, vel_v, 1, tiles, 1.0),
            (force, force_x, 0, 0, 1.0), (third, third_x, 0, 0, 1.0 / 3.0),
            (push_x, push_x_x, 0, 0, 0.5), (push_y, push_y_x, 0, 0, 0.5),
        )
        beyond = []
        for f in range(ICE):
            start = HALO * f + 2 * HALO
            x = jnp.where((lane >= start) & (lane < start + HALO), west, east_side)
            beyond.append(turn(x, 104 - HALO * f))
        beyond[2] = beyond[2] * beyond[3] * (1.0 / 12.0)
        for x, (source, target, shift, t, factor) in zip(beyond, targets):
            x = x if factor == 1.0 else x * factor
            x = jnp.where(lane >= 104, x, source[i + shift, :, cut(tiles)])
            writes.append((target, (i + shift, whole, cut(t)), x))
        return writes

    in_chunks_of(count, insert, 6)
    wrap(vel_u, count, cut(tiles))
    wrap(vel_v, count, cut(tiles))
    extras = {id(third): third_x, id(force): force_x, id(push_x): push_x_x, id(push_y): push_y_x}

    def constant(load, ref, j, t):
        return load(ref, j, cut(t)) if t < tiles else load(extras[id(ref)], j, cut(0))

    def velocity(load, j, t, first):
        u, v = (base_u, base_v) if first and t < tiles else (vel_u, vel_v)
        return load(u, j, cut(t)), load(v, j, cut(t))

    def strain_stress(first):
        def body(i, j, load):
            writes = []
            for t in range(wide):
                u, v = velocity(load, j + 1, t, first)
                u_above, v_above = velocity(load, j + 2, t, first)
                u_below, v_below = velocity(load, j, t, first)
                dudx, dvdx = turn(u, -1) - turn(u, 1), turn(v, -1) - turn(v, 1)
                dudy, dvdy = u_above - u_below, v_above - v_below
                div, ten, shr = dudx + dvdy, dudx - dvdy, dudy + dvdx
                square = div * div + 0.25 * (ten * ten + shr * shr) + 1.0
                base = constant(load, force, j, t)
                zeta = base * lax.rsqrt(square)
                quarter = 0.25 * zeta
                even = zeta * div - base
                odd = quarter * ten
                new = [even + odd, even - odd, quarter * shr]
                for n, ref in enumerate((str_a, str_b, str_c)):
                    if not first:
                        new[n] = new[n] + constant(load, third, j, t) * load(ref, j + 1, cut(t))
                    writes.append((ref, (i + 1, whole, cut(t)), new[n]))
            return writes

        in_chunks_of(count, body, 1)
        for ref in (str_a, str_b, str_c):
            wrap(ref, count)

    def momentum(first):
        def body(i, j, load):
            ar, br = load(turn_a, j), load(turn_b, j)
            writes = []
            for t in range(wide):
                c = cut(t)
                a, s = load(str_a, j + 1, c), load(str_c, j + 1, c)
                fx = (turn(a, -1) - turn(a, 1)) + (load(str_c, j + 2, c) - load(str_c, j, c))
                fy = (turn(s, -1) - turn(s, 1)) + (load(str_b, j + 2, c) - load(str_b, j, c))
                u, v = velocity(load, j + 1, t, first)
                ru = (u + constant(load, push_x, j, t)) + fx
                rv = (v + constant(load, push_y, j, t)) + fy
                keep = constant(load, third, j, t)
                writes.append((vel_u, (i + 1, whole, c), (ar * ru + br * rv) * keep))
                writes.append((vel_v, (i + 1, whole, c), (ar * rv - br * ru) * keep))
            return writes

        in_chunks_of(count, body, 1)
        wrap(vel_u, count)
        wrap(vel_v, count)

    for subcycle in range(SUBCYCLES):
        strain_stress(subcycle == 0)
        momentum(subcycle == 0)

    def gather(i, j, load):
        writes = []
        for n, ref in enumerate((vel_u, vel_v)):
            borders = ref[i + 1, :, cut(tiles)]
            middle, outer = turn(borders, -48), turn(borders, 24)
            low, high = ref[i + 1, :, cut(0)], ref[i + 1, :, cut(tiles - 1)]
            low = jnp.where(lane < HALO, borders, jnp.where(lane >= LANES - HALO, middle, low))
            high = jnp.where(lane < HALO, middle, jnp.where(lane >= LANES - HALO, outer, high))
            put = pl.ds(i, SUBLANES, stride=count)
            writes.append((done, (n, 0, put, whole), low))
            writes.append((done, (n, tiles - 1, put, whole), high))
        return writes

    in_chunks_of(count, gather, 8)
    finals = []
    for n, out in enumerate((u_out, v_out)):
        for t in range(tiles):
            finals.append(
                pltpu.make_async_copy(
                    done.at[n, t, own, :], out.at[:, pl.ds(LANES * t, LANES)], vel_sem.at[n, t]
                )
            )
            finals[-1].start()

    def warm(n, carry):
        writes = []
        for j in range(size):
            start = pl.multiple_of((n * size + j) * SUBLANES, SUBLANES)
            put, at = pl.ds(start, SUBLANES), pl.ds(start + HALO, SUBLANES)
            sst, sss = fixed(0, put), fixed(levels, put)
            for t in range(tiles):
                slip_u = done[0, t, at, :] - speeds_in[0, t, put, :]
                slip_v = done[1, t, at, :] - speeds_in[levels, t, put, :]
                heat = HEAT_RATE * covered_in[3, t, at, :] * (1.0 + (slip_u * slip_u + slip_v * slip_v))
                heat = heat * (sst[t] + FREEZE_SLOPE * sss[t])
                writes.append((0, t, put, sst[t] - heat))
                writes.append((levels, t, put, sss[t] - SALT_RATE * heat))
        for f, t, put, value in writes:
            moved[f, t, put, :] = value
        return carry

    lax.fori_loop(0, rows // SUBLANES // size, warm, 0)
    for f in (0, levels):
        copies = stores(f)
        for copy in copies:
            copy.start()
        finals += copies
    for copy in pending + finals:
        copy.wait()


def ice_and_edges(operands, levels, rows, cols):
    tiles = cols // LANES
    count = sublane_rows(rows)
    deep = jax.ShapeDtypeStruct((levels, rows, cols), F32)
    flat = jax.ShapeDtypeStruct((rows, cols), F32)
    looped = pltpu.VMEM((count + 2, SUBLANES, LANES * (tiles + 1)), F32)
    narrow = pltpu.VMEM((count, SUBLANES, LANES), F32)
    edge = pltpu.VMEM((rows, LANES), F32)
    return pl.pallas_call(
        lambda *refs: ice_kernel(levels, rows, *refs),
        in_specs=[VMEM_SPEC] * len(operands),
        out_specs=[ANY_SPEC] * 4,
        out_shape=[deep, deep, flat, flat],
        scratch_shapes=[
            pltpu.VMEM((2 * levels, tiles, rows, LANES), F32),
            pltpu.VMEM((2, tiles, count * SUBLANES, LANES), F32),
            looped, looped, looped, looped, looped,
            narrow, narrow, narrow, narrow, edge, edge,
            pltpu.SemaphoreType.DMA((2 * levels, tiles)),
            pltpu.SemaphoreType.DMA((2, tiles)),
        ],
        name="ice",
        compiler_params=pltpu.CompilerParams(vmem_limit_bytes=20 << 20),
        cost_estimate=pl.CostEstimate(flops=60000000, bytes_accessed=16 << 20, transcendentals=0),
    )(*[in_vmem(a) for a in operands])


def per_device(*arrays):
    levels, rows, cols = arrays[0].shape
    lon_count, lat_count = lax.axis_size("lon"), lax.axis_size("lat")
    assert cols == 2 * LANES and rows % (2 * HALO) == 0 and lat_count % 2 == 0
    height = -(-(HALO * ICE + 3 * levels) // SUBLANES) * SUBLANES

    def place(lat, lon):
        return lon * lat_count + lat

    first_pairs, second_pairs = [], []
    for lon in range(lon_count):
        for lat in range(lat_count):
            first_pairs.append((place(lat, lon), place(lat ^ 1, lon)))
            if lat == lat_count - 1:
                second_pairs.append((place(lat, lon), place(lat, lon_count - 1 - lon)))
            elif lat:
                second_pairs.append((place(lat, lon), place(((lat + 1) ^ 1) - 1, lon)))
    first, second = pack_rows(arrays, levels, rows, cols, height)
    first = lax.ppermute(first, ("lon", "lat"), first_pairs)
    second = lax.ppermute(second, ("lon", "lat"), second_pairs)
    tracers, speeds, sea, fields, east_msg, west_msg = load_and_pack_columns(
        arrays, levels, rows, cols
    )
    halo, fields, east_msg, west_msg = merge_halo(
        first, second, fields, east_msg, west_msg, levels, rows
    )
    eastward = [(i, (i + 1) % lon_count) for i in range(lon_count)]
    from_west = lax.ppermute(east_msg, "lon", eastward)
    from_east = lax.ppermute(west_msg, "lon", [(b, a) for a, b in eastward])
    moved, *state = advect(tracers, speeds, sea, halo, fields, levels, rows * lat_count)
    return ice_and_edges(
        [fields, moved, speeds, east_msg, west_msg, from_west, from_east, *state], levels, rows, cols
    )


def solution(mesh):
    deep, flat = P(None, "lat", "lon"), P("lat", "lon")
    return jax.shard_map(
        per_device,
        mesh=mesh,
        in_specs=(deep,) * 4 + (flat,) * 7,
        out_specs=(deep, deep, flat, flat),
        check_vma=False,
    )
```

```python
import jax
import jax.numpy as jnp
from jax import lax
from jax.experimental import pallas as pl
from jax.experimental.pallas import tpu as pltpu
from jax.sharding import PartitionSpec as P

SUBCYCLES = 4
HEAT_RATE = 0.1
SALT_RATE = 0.5
FREEZE_SLOPE = 0.054
DIAGONAL = 1.5
HALO = 2 * SUBCYCLES
LANES = 128
SUBLANES = 8
ICE = 6
FOLD_SIGN = (-1.0, -1.0, 1.0, 1.0, -1.0, -1.0)
TRACER_LANE = 64
F32 = jnp.float32


def lane_ids():
    return lax.broadcasted_iota(jnp.int32, (SUBLANES, LANES), 1)


def sublane_ids():
    return lax.broadcasted_iota(jnp.int32, (SUBLANES, LANES), 0)


def turn(x, shift, axis=1):
    shift = shift % x.shape[axis]
    return pltpu.roll(x, shift, axis) if shift else x


def cut(t):
    return slice(LANES * t, LANES * (t + 1))


def ice_fields(land, ice, u, v, pressure, wind_x, wind_y, ocean_u, ocean_v):
    covered = land.astype(F32) * ice.astype(F32)
    return (u * covered, v * covered, pressure, covered, wind_x + ocean_u, wind_y + ocean_v)


def east_columns(fields, lane):
    packed = jnp.zeros((SUBLANES, LANES), F32)
    for f, tile in enumerate(fields):
        start = HALO * f + 2 * HALO
        moved = turn(tile, start - (LANES - HALO))
        packed = jnp.where((lane >= start) & (lane < start + HALO), moved, packed)
    return packed


def west_columns(fields, lane):
    packed = jnp.zeros((SUBLANES, LANES), F32)
    for f, tile in enumerate(fields):
        start = HALO * f
        packed = jnp.where((lane >= start) & (lane < start + HALO), turn(tile, start), packed)
    return packed


def sublane_rows(rows):
    return (rows + 2 * HALO) // SUBLANES | 1


def in_chunks_of(count, body, group):
    size = max(c for c in range(1, 21) if count % c == 0)

    def step(n, carry):
        seen = {}

        def load(ref, j, *where):
            key = (id(ref), j, *[str(w) for w in where])
            if key not in seen:
                seen[key] = ref[(n * size + j, slice(None), *where)]
            return seen[key]

        for start in range(0, size, group):
            writes = []

            for j in range(start, min(start + group, size)):
                writes += body(n * size + j, j, load)
            for ref, where, value in writes:
                ref[where] = value
        return carry

    lax.fori_loop(0, count // size, step, 0)


def rows_kernel(levels, *refs):
    tops, bottoms = refs[0:12], refs[12:24]
    first_ref, second_ref = refs[24:26]
    even = lax.rem(lax.axis_index("lat"), 2) == 0

    def message(group, row, northward):
        land, ice, u, v, pressure, wind_x, wind_y, east, north, temp, salt = (
            r for r in group[:11]
        )
        fields = ice_fields(
            land[...], ice[...], u[...], v[...], pressure[...], wind_x[...], wind_y[...],
            east[0], north[0],
        )
        sea = land[row : row + 1, :].astype(F32)
        parts = list(fields) + [temp[:, row, :], salt[:, row, :]]
        if northward:
            parts.append(north[:, row, :] * sea)
        else:
            parts.append(jnp.broadcast_to(sea, (levels, sea.shape[1])))
        return parts

    top = message(tops, SUBLANES - 1, True)
    bottom = message(bottoms, 0, False)
    at = 0
    for t, b in zip(top, bottom):
        size = t.shape[0]
        first_ref[at : at + size, :] = jnp.where(even, t, b)
        second_ref[at : at + size, :] = jnp.where(even, b, t)
        at += size
    pad = first_ref.shape[0] - at
    if pad:
        first_ref[at:, :] = jnp.zeros((pad, first_ref.shape[1]), F32)
        second_ref[at:, :] = jnp.zeros((pad, second_ref.shape[1]), F32)


def pack_rows(arrays, levels, rows, cols, height):
    temp, salt, east, north, land, ice, u, v, pressure, wind_x, wind_y = arrays
    operands = [land, ice, u, v, pressure, wind_x, wind_y, east, north, temp, salt, land]
    last = rows // SUBLANES - 1

    def spec(array, block, count):
        if array.ndim == 2:
            return pl.BlockSpec((SUBLANES, cols), lambda _: (block, 0))
        return pl.BlockSpec((count, SUBLANES, cols), lambda _: (0, block, 0))

    counts = [1] * 7 + [1, levels, levels, levels, 1]
    specs = [spec(a, last, c) for a, c in zip(operands, counts)]
    specs += [spec(a, 0, c) for a, c in zip(operands, counts)]
    out = jax.ShapeDtypeStruct((height, cols), F32)
    return pl.pallas_call(
        lambda *refs: rows_kernel(levels, *refs),
        grid=(1,),
        in_specs=specs,
        out_specs=[pl.BlockSpec((height, cols), lambda _: (0, 0))] * 2,
        out_shape=[out, out],
        name="edge_rows",
        compiler_params=pltpu.CompilerParams(vmem_limit_bytes=8 << 20),
        cost_estimate=pl.CostEstimate(flops=100000, bytes_accessed=1 << 20, transcendentals=0),
    )(*[in_hbm(a) for a in operands + operands])


def columns_kernel(levels, land, ice, u, v, pressure, wind_x, wind_y, east, north, temp, salt,
                   tracer_out, speed_out, sea_out, field_out, east_out, west_out, sem):
    lane = lane_ids()
    rows = sea_out.shape[1]
    tiles = sea_out.shape[0]
    tracers = 2 * levels
    first_lane = TRACER_LANE
    mask_lane = TRACER_LANE + tracers

    copies = []
    for n, ref in enumerate((temp, salt, east, north)):
        out = tracer_out if n < 2 else speed_out
        for t in range(tiles):
            copies.append(
                pltpu.make_async_copy(
                    ref.at[..., pl.ds(LANES * t, LANES)],
                    out.at[pl.ds(levels * (n % 2), levels), t],
                    sem.at[n, t],
                )
            )
    for copy in copies:
        copy.start()

    def each_row_tile(body, size):
        def step(n, carry):
            writes = []
            for j in range(size):
                writes += body(pl.multiple_of((n * size + j) * SUBLANES, SUBLANES))
            for ref, where, value in writes:
                ref[where] = value
            return carry

        lax.fori_loop(0, rows // SUBLANES // size, step, 0)

    whole = slice(None)

    def ice_part(start):
        at = pl.ds(start, SUBLANES)
        writes, fields = [], []
        for t in range(tiles):
            c = cut(t)
            fields.append(
                ice_fields(
                    *[r[at, c] for r in (land, ice, u, v, pressure, wind_x, wind_y)],
                    east[0, at, c], north[0, at, c],
                )
            )
            writes.append((sea_out, (t, at, whole), land[at, c].astype(F32)))
            for f in range(ICE):
                writes.append((field_out, (f, t, pl.ds(start + HALO, SUBLANES), whole), fields[t][f]))
        put = pl.ds(start + HALO, SUBLANES)
        writes.append((east_out, (put, whole), east_columns(fields[-1], lane)))
        writes.append((west_out, (put, whole), west_columns(fields[0], lane)))
        return writes

    each_row_tile(ice_part, 4)
    end = HALO + rows
    blank = jnp.zeros((field_out.shape[2] - end, LANES), F32)
    for t in range(tiles):
        for f in range(ICE):
            field_out[f, t, end:, :] = blank
    for ref in (east_out, west_out):
        ref[end:, :] = blank

    for n, ref in enumerate((temp, salt)):

        def tracer_part(start, n=n, ref=ref):
            at, put = pl.ds(start, SUBLANES), pl.ds(start + HALO, SUBLANES)
            eastward, westward = east_out[put, :], west_out[put, :]
            for f in range(levels):
                to = first_lane + levels * n + f
                eastward = jnp.where(
                    lane == to, turn(ref[f, at, cut(tiles - 1)], to - (LANES - 1)), eastward
                )
                westward = jnp.where(lane == to, turn(ref[f, at, cut(0)], to), westward)
            return [(east_out, (put, whole), eastward), (west_out, (put, whole), westward)]

        each_row_tile(tracer_part, 8)
    def speed_part(start):
        at, put = pl.ds(start, SUBLANES), pl.ds(start + HALO, SUBLANES)
        masked = (lane >= mask_lane) & (lane < mask_lane + tracers)
        speeds = jnp.zeros((SUBLANES, LANES), F32)
        for f in range(levels):
            moved = turn(east[f, at, cut(tiles - 1)], mask_lane + f - (LANES - 1))
            speeds = jnp.where(lane == mask_lane + f, moved, speeds)
        speeds = speeds + turn(speeds, levels)
        last = land[at, LANES * tiles - 1 : LANES * tiles].astype(F32)
        first = land[at, 0:1].astype(F32)
        eastward = jnp.where(masked, speeds * last, east_out[put, :])
        westward = jnp.where(masked, jnp.broadcast_to(first, (SUBLANES, LANES)), west_out[put, :])
        return [(east_out, (put, whole), eastward), (west_out, (put, whole), westward)]

    each_row_tile(speed_part, 8)
    for copy in copies:
        copy.wait()


def in_vmem(x):
    return pltpu.with_memory_space_constraint(x, pltpu.VMEM)


def in_hbm(x):
    return pltpu.with_memory_space_constraint(x, pltpu.HBM)


def resident(*shape):
    return pltpu.VMEM(shape, F32)


VMEM_SPEC = pl.BlockSpec(memory_space=pltpu.VMEM)
ANY_SPEC = pl.BlockSpec(memory_space=pl.ANY)


def load_and_pack_columns(arrays, levels, rows, cols):
    temp, salt, east, north, land, ice, u, v, pressure, wind_x, wind_y = arrays
    tiles = cols // LANES
    message = resident(sublane_rows(rows) * SUBLANES, LANES)
    deep = resident(2 * levels, tiles, rows, LANES)
    return pl.pallas_call(
        lambda *refs: columns_kernel(levels, *refs),
        in_specs=[VMEM_SPEC] * 11,
        out_specs=[VMEM_SPEC] * 6,
        out_shape=[
            deep, deep, resident(tiles, rows, LANES),
            resident(ICE, tiles, sublane_rows(rows) * SUBLANES, LANES), message, message,
        ],
        scratch_shapes=[pltpu.SemaphoreType.DMA((4, tiles))],
        name="edge_columns",
        compiler_params=pltpu.CompilerParams(vmem_limit_bytes=4 << 20),
        cost_estimate=pl.CostEstimate(flops=5000000, bytes_accessed=12 << 20, transcendentals=0),
    )(*[in_vmem(a) for a in (land, ice, u, v, pressure, wind_x, wind_y, east, north, temp, salt)])


def halo_kernel(levels, rows, first, second, field_in, east_in, west_in,
                halo_ref, field_out, east_out, west_out):
    lat = lax.axis_index("lat")
    even = lax.rem(lat, 2) == 0
    top = lat == lax.axis_size("lat") - 1
    lane, sublane = lane_ids(), sublane_ids()
    tiles = field_out.shape[1]
    south_fields, north_fields = [], []
    for f in range(ICE):
        at = slice(HALO * f, HALO * (f + 1))
        north_row, south_row = [], []
        for t in range(tiles):
            cols = slice(LANES * t, LANES * (t + 1))
            mirror = slice(LANES * (tiles - 1 - t), LANES * (tiles - t))
            south = jnp.where(even, second[at, cols], first[at, cols])
            plain = jnp.where(even, first[at, cols], second[at, cols])
            turned = jnp.take_along_axis(second[at, mirror], LANES - 1 - lane, axis=1)
            turned = jnp.take_along_axis(turned, SUBLANES - 1 - sublane, axis=0)
            north = jnp.where(top, turned * FOLD_SIGN[f], plain)
            field_out[f, t, 0:HALO, :] = south
            field_out[f, t, rows + HALO : rows + 2 * HALO, :] = north
            south_row.append(south)
            north_row.append(north)
        south_fields.append(south_row)
        north_fields.append(north_row)
    rest = slice(HALO * ICE, first.shape[0])
    halo_ref[0] = jnp.where(even, second[rest, :], first[rest, :])
    halo_ref[1] = jnp.where(top, 0.0, jnp.where(even, first[rest, :], second[rest, :]))
    for at, fields in ((0, south_fields), (rows + HALO, north_fields)):
        east_out[at : at + HALO, :] = east_columns([f[-1] for f in fields], lane)
        west_out[at : at + HALO, :] = west_columns([f[0] for f in fields], lane)


def merge_halo(first, second, fields, east_msg, west_msg, levels, rows):
    height, cols = first.shape
    return pl.pallas_call(
        lambda *refs: halo_kernel(levels, rows, *refs),
        in_specs=[VMEM_SPEC] * 5,
        out_specs=[VMEM_SPEC] * 4,
        out_shape=[
            resident(2, height - HALO * ICE, cols), resident(*fields.shape),
            resident(*east_msg.shape), resident(*west_msg.shape),
        ],
        input_output_aliases={2: 1, 3: 2, 4: 3},
        name="halo_rows",
        compiler_params=pltpu.CompilerParams(vmem_limit_bytes=8 << 20),
        cost_estimate=pl.CostEstimate(flops=100000, bytes_accessed=1 << 19, transcendentals=0),
    )(first, second, in_vmem(fields), in_vmem(east_msg), in_vmem(west_msg))


def advect_kernel(levels, row_total, tracer_ref, speed_ref, sea, halo, field_ref,
                  out, base_u, base_v, third, force, push_x, push_y, turn_a, turn_b,
                  mask_e, mask_n):
    tiles, rows = sea.shape[:2]
    count = rows // SUBLANES
    group = next(c for c in (12, 8, 4, 2) if count % c == 0)
    lane, sublane = lane_ids(), sublane_ids()
    extra_row = 2 * levels
    whole = slice(None)

    def rows_at(k, offset=0):
        start = pl.multiple_of(k * SUBLANES, SUBLANES)
        return pl.ds(start + offset if offset else start, SUBLANES)

    def row(side, index, t):
        cols = slice(LANES * t, LANES * (t + 1))
        return jnp.broadcast_to(halo[side, index : index + 1, cols], (SUBLANES, LANES))

    def from_next(values):
        turned = [turn(v, -1) for v in values]
        return [
            jnp.where(lane == LANES - 1, turned[t + 1], turned[t]) if t + 1 < tiles else turned[t]
            for t in range(tiles)
        ]

    def from_last(values):
        turned = [turn(v, 1) for v in values]
        return [jnp.where(lane == 0, turned[t - 1], turned[t]) for t in range(tiles)]

    def in_groups(body, carry):
        def some(start, carry, last):
            writes = []
            for j in range(group):
                more, carry = body(start + j, last and j == group - 1, carry)
                writes += more
            for ref, where, value in writes:
                ref[where] = value
            return carry

        groups = count // group
        carry = lax.fori_loop(0, groups - 1, lambda n, c: some(n * group, c, False), carry)
        return some((groups - 1) * group, carry, True)

    def row_above(load, k, last, past):
        if not last:
            return load(rows_at(k, 1))
        return jnp.where(sublane == SUBLANES - 1, past, turn(load(rows_at(k)), -1, 0))

    def masks(k, last, carry):
        here = [sea[t, rows_at(k), :] for t in range(tiles)]
        beside = from_next(here)
        writes = []
        for t in range(tiles):
            above = row_above(lambda at, t=t: sea[t, at, :], k, last, row(1, extra_row, t))
            face = here[t] * beside[t]
            if t == tiles - 1:
                face = jnp.where(lane == LANES - 1, 0.0, face)
            writes.append((mask_e, (t, rows_at(k), whole), face))
            writes.append((mask_n, (t, rows_at(k), whole), here[t] * above))
        return writes, carry

    in_groups(masks, 0)
    for level in range(levels):
        entering = []
        for f in (level, levels + level):
            for t in range(tiles):
                speed = row(0, extra_row + level, t) * sea[t, 0:SUBLANES, :]
                start = tracer_ref[f, t, 0:SUBLANES, :]
                entering.append(speed * jnp.where(speed > 0, row(0, f, t), start))

        def body(k, last, carry, level=level):
            at = rows_at(k)
            fast_e = [speed_ref[level, t, at, :] * mask_e[t, at, :] for t in range(tiles)]
            fast_n = [speed_ref[levels + level, t, at, :] * mask_n[t, at, :] for t in range(tiles)]
            writes, result = [], []
            for f in (level, levels + level):
                here = [tracer_ref[f, t, at, :] for t in range(tiles)]
                beside = from_next(here)
                flux_e = [
                    fast_e[t] * jnp.where(fast_e[t] > 0, here[t], beside[t]) for t in range(tiles)
                ]
                before = from_last(flux_e)
                for t in range(tiles):
                    above = row_above(
                        lambda at, f=f, t=t: tracer_ref[f, t, at, :], k, last, row(1, f, t)
                    )
                    flux_n = fast_n[t] * jnp.where(fast_n[t] > 0, here[t], above)
                    turned = turn(flux_n, 1, 0)
                    below = jnp.where(sublane == 0, carry[len(result)], turned)
                    value = here[t] - ((flux_e[t] - before[t]) + (flux_n - below))
                    writes.append((out, (f, t, at, whole), value))
                    result.append(turned)
            return writes, tuple(result)

        in_groups(body, tuple(entering))
    spread_fields(rows, row_total, field_ref, base_u, base_v, third, force, push_x, push_y,
                  turn_a, turn_b)


def spread(ref, i, count, *lead):
    return ref[(*lead, pl.ds(i, SUBLANES, stride=count), slice(None))]


def wrap(ref, count, lanes=slice(None)):
    ref[0, :, lanes] = turn(ref[count, :, lanes], 1, 0)
    ref[count + 1, :, lanes] = turn(ref[1, :, lanes], -1, 0)


def spread_fields(rows, row_total, field_ref, base_u, base_v, third, force, push_x, push_y,
                  turn_a, turn_b):
    tiles = field_ref.shape[1]
    count = sublane_rows(rows)
    lane, sublane = lane_ids(), sublane_ids()
    lat = lax.axis_index("lat")

    def body(i, _, load):
        per_tile = [[spread(field_ref, i, count, f, t) for f in range(ICE)] for t in range(tiles)]
        extra = []
        for f in range(ICE):
            low, high = per_tile[0][f], per_tile[-1][f]
            middle = turn(jnp.where(lane < LANES // 2, high, low), 48)
            x = jnp.where(lane < 32, low, middle)
            extra.append(jnp.where(lane >= 64, turn(high, -24), x))
        writes = []
        for t, fields in enumerate(per_tile + [extra]):
            u0, v0, strength, covered, drive_x, drive_y = fields
            writes.append((base_u, (i + 1, slice(None), cut(t)), u0))
            writes.append((base_v, (i + 1, slice(None), cut(t)), v0))
            writes.append((third, (i, slice(None), cut(t)), covered * (1.0 / 3.0)))
            writes.append((force, (i, slice(None), cut(t)), strength * covered * (1.0 / 12.0)))
            writes.append((push_x, (i, slice(None), cut(t)), 0.5 * drive_x))
            writes.append((push_y, (i, slice(None), cut(t)), 0.5 * drive_y))
        y = lat * rows - HALO + sublane * count + i
        y = jnp.where(y >= row_total, 2 * row_total - 1 - y, y)
        coriolis = 0.5 * (2 * y + 1 - row_total).astype(F32) / row_total
        turning = 0.5 * coriolis
        scale = 3.0 / (DIAGONAL * DIAGONAL + turning * turning)
        writes.append((turn_a, (i,), DIAGONAL * scale))
        writes.append((turn_b, (i,), turning * scale))
        return writes

    in_chunks_of(count, body, 3)
    wrap(base_u, count)
    wrap(base_v, count)


def advect(tracers, speeds, sea, halo, fields, levels, row_total):
    tiles, rows = sea.shape[:2]
    count = sublane_rows(rows)
    wide = LANES * (tiles + 1)
    looped = resident(count + 2, SUBLANES, wide)
    plain = resident(count, SUBLANES, wide)
    narrow = resident(count, SUBLANES, LANES)
    return pl.pallas_call(
        lambda *refs: advect_kernel(levels, row_total, *refs),
        in_specs=[VMEM_SPEC] * 5,
        out_specs=[VMEM_SPEC] * 9,
        out_shape=[
            resident(*tracers.shape), looped, looped, plain, plain, plain, plain, narrow, narrow,
        ],
        scratch_shapes=[pltpu.VMEM((tiles, rows, LANES), F32)] * 2,
        name="advect",
        compiler_params=pltpu.CompilerParams(vmem_limit_bytes=8 << 20),
        cost_estimate=pl.CostEstimate(flops=30000000, bytes_accessed=16 << 20, transcendentals=0),
    )(*[in_vmem(a) for a in (tracers, speeds, sea, halo, fields)])


def ice_kernel(levels, rows, *refs):
    (covered_in, tracers_in, speeds_in, east_own, west_own, from_west, from_east,
     base_u, base_v, third, force, push_x, push_y, turn_a, turn_b,
     temp_out, salt_out, u_out, v_out,
     moved, done, vel_u, vel_v, str_a, str_b, str_c,
     third_x, force_x, push_x_x, push_y_x, edge_w, edge_e,
     out_sem, vel_sem) = refs
    tiles = tracers_in.shape[1]
    count = sublane_rows(rows)
    tracers = 2 * levels
    lane = lane_ids()
    own = pl.ds(HALO, rows)
    wide = tiles + 1
    whole = slice(None)

    def edge_fluxes(k, carry):
        at = pl.ds(pl.multiple_of(k * SUBLANES + HALO, SUBLANES), SUBLANES)
        put = pl.ds(pl.multiple_of(k * SUBLANES, SUBLANES), SUBLANES)
        west, east_side = from_west[at, :], from_east[at, :]
        mine_e, mine_w = east_own[at, :], west_own[at, :]
        speed = turn(west, -tracers)
        edge_w[put, :] = speed * jnp.where(speed > 0, west, mine_w) * turn(mine_w, -tracers)
        speed = turn(mine_e, -tracers)
        edge_e[put, :] = speed * jnp.where(speed > 0, mine_e, east_side) * turn(east_side, -tracers)
        return carry

    lax.fori_loop(0, rows // SUBLANES, edge_fluxes, 0, unroll=8)

    def fixed(f, put):
        low, high = tracers_in[f, 0, put, :], tracers_in[f, tiles - 1, put, :]
        inflow = jnp.where(lane == 0, turn(edge_w[put, :], -(TRACER_LANE + f)), 0.0)
        outflow = jnp.where(
            lane == LANES - 1, turn(edge_e[put, :], LANES - 1 - TRACER_LANE - f), 0.0
        )
        return low + inflow, high - outflow

    def stores(f):
        out = temp_out.at[f] if f < levels else salt_out.at[f - levels]
        return [
            pltpu.make_async_copy(
                moved.at[f, t], out.at[:, pl.ds(LANES * t, LANES)], out_sem.at[f, t]
            )
            for t in range(tiles)
        ]

    deep = [f for f in range(tracers) if f % levels]
    size = next(c for c in (16, 8, 4, 2) if rows // SUBLANES % c == 0)

    def fix(n, carry):
        puts = [
            pl.ds(pl.multiple_of((n * size + j) * SUBLANES, SUBLANES), SUBLANES)
            for j in range(size)
        ]
        for f in deep:
            results = [fixed(f, put) for put in puts]
            for put, (low, high) in zip(puts, results):
                moved[f, 0, put, :] = low
                moved[f, tiles - 1, put, :] = high
        return carry

    lax.fori_loop(0, rows // SUBLANES // size, fix, 0)
    pending = [copy for f in deep for copy in stores(f)]
    for copy in pending:
        copy.start()

    def insert(i, j, load):
        west, east_side = spread(from_west, i, count), spread(from_east, i, count)
        writes = []
        targets = (
            (base_u, vel_u, 1, tiles, 1.0), (base_v, vel_v, 1, tiles, 1.0),
            (force, force_x, 0, 0, 1.0), (third, third_x, 0, 0, 1.0 / 3.0),
            (push_x, push_x_x, 0, 0, 0.5), (push_y, push_y_x, 0, 0, 0.5),
        )
        beyond = []
        for f in range(ICE):
            start = HALO * f + 2 * HALO
            x = jnp.where((lane >= start) & (lane < start + HALO), west, east_side)
            beyond.append(turn(x, 104 - HALO * f))
        beyond[2] = beyond[2] * beyond[3] * (1.0 / 12.0)
        for x, (source, target, shift, t, factor) in zip(beyond, targets):
            x = x if factor == 1.0 else x * factor
            x = jnp.where(lane >= 104, x, source[i + shift, :, cut(tiles)])
            writes.append((target, (i + shift, whole, cut(t)), x))
        return writes

    in_chunks_of(count, insert, 6)
    wrap(vel_u, count, cut(tiles))
    wrap(vel_v, count, cut(tiles))
    extras = {id(third): third_x, id(force): force_x, id(push_x): push_x_x, id(push_y): push_y_x}

    def constant(load, ref, j, t):
        return load(ref, j, cut(t)) if t < tiles else load(extras[id(ref)], j, cut(0))

    def velocity(load, j, t, first):
        u, v = (base_u, base_v) if first and t < tiles else (vel_u, vel_v)
        return load(u, j, cut(t)), load(v, j, cut(t))

    def strain_stress(first):
        def body(i, j, load):
            writes = []
            for t in range(wide):
                u, v = velocity(load, j + 1, t, first)
                u_above, v_above = velocity(load, j + 2, t, first)
                u_below, v_below = velocity(load, j, t, first)
                dudx, dvdx = turn(u, -1) - turn(u, 1), turn(v, -1) - turn(v, 1)
                dudy, dvdy = u_above - u_below, v_above - v_below
                div, ten, shr = dudx + dvdy, dudx - dvdy, dudy + dvdx
                square = div * div + 0.25 * (ten * ten + shr * shr) + 1.0
                base = constant(load, force, j, t)
                zeta = base * lax.rsqrt(square)
                quarter = 0.25 * zeta
                even = zeta * div - base
                odd = quarter * ten
                new = [even + odd, even - odd, quarter * shr]
                for n, ref in enumerate((str_a, str_b, str_c)):
                    if not first:
                        new[n] = new[n] + constant(load, third, j, t) * load(ref, j + 1, cut(t))
                    writes.append((ref, (i + 1, whole, cut(t)), new[n]))
            return writes

        in_chunks_of(count, body, 1)
        for ref in (str_a, str_b, str_c):
            wrap(ref, count)

    def momentum(first):
        def body(i, j, load):
            ar, br = load(turn_a, j), load(turn_b, j)
            writes = []
            for t in range(wide):
                c = cut(t)
                a, s = load(str_a, j + 1, c), load(str_c, j + 1, c)
                fx = (turn(a, -1) - turn(a, 1)) + (load(str_c, j + 2, c) - load(str_c, j, c))
                fy = (turn(s, -1) - turn(s, 1)) + (load(str_b, j + 2, c) - load(str_b, j, c))
                u, v = velocity(load, j + 1, t, first)
                ru = (u + constant(load, push_x, j, t)) + fx
                rv = (v + constant(load, push_y, j, t)) + fy
                keep = constant(load, third, j, t)
                writes.append((vel_u, (i + 1, whole, c), (ar * ru + br * rv) * keep))
                writes.append((vel_v, (i + 1, whole, c), (ar * rv - br * ru) * keep))
            return writes

        in_chunks_of(count, body, 1)
        wrap(vel_u, count)
        wrap(vel_v, count)

    for subcycle in range(SUBCYCLES):
        strain_stress(subcycle == 0)
        momentum(subcycle == 0)

    def gather(i, j, load):
        writes = []
        for n, ref in enumerate((vel_u, vel_v)):
            borders = ref[i + 1, :, cut(tiles)]
            middle, outer = turn(borders, -48), turn(borders, 24)
            low, high = ref[i + 1, :, cut(0)], ref[i + 1, :, cut(tiles - 1)]
            low = jnp.where(lane < HALO, borders, jnp.where(lane >= LANES - HALO, middle, low))
            high = jnp.where(lane < HALO, middle, jnp.where(lane >= LANES - HALO, outer, high))
            put = pl.ds(i, SUBLANES, stride=count)
            writes.append((done, (n, 0, put, whole), low))
            writes.append((done, (n, tiles - 1, put, whole), high))
        return writes

    in_chunks_of(count, gather, 8)
    finals = []
    for n, out in enumerate((u_out, v_out)):
        for t in range(tiles):
            finals.append(
                pltpu.make_async_copy(
                    done.at[n, t, own, :], out.at[:, pl.ds(LANES * t, LANES)], vel_sem.at[n, t]
                )
            )
            finals[-1].start()

    def warm(n, carry):
        writes = []
        for j in range(size):
            start = pl.multiple_of((n * size + j) * SUBLANES, SUBLANES)
            put, at = pl.ds(start, SUBLANES), pl.ds(start + HALO, SUBLANES)
            sst, sss = fixed(0, put), fixed(levels, put)
            for t in range(tiles):
                slip_u = done[0, t, at, :] - speeds_in[0, t, put, :]
                slip_v = done[1, t, at, :] - speeds_in[levels, t, put, :]
                heat = HEAT_RATE * covered_in[3, t, at, :] * (1.0 + (slip_u * slip_u + slip_v * slip_v))
                heat = heat * (sst[t] + FREEZE_SLOPE * sss[t])
                writes.append((0, t, put, sst[t] - heat))
                writes.append((levels, t, put, sss[t] - SALT_RATE * heat))
        for f, t, put, value in writes:
            moved[f, t, put, :] = value
        return carry

    lax.fori_loop(0, rows // SUBLANES // size, warm, 0)
    for f in (0, levels):
        copies = stores(f)
        for copy in copies:
            copy.start()
        finals += copies
    for copy in pending + finals:
        copy.wait()


def ice_and_edges(operands, levels, rows, cols):
    tiles = cols // LANES
    count = sublane_rows(rows)
    deep = jax.ShapeDtypeStruct((levels, rows, cols), F32)
    flat = jax.ShapeDtypeStruct((rows, cols), F32)
    looped = pltpu.VMEM((count + 2, SUBLANES, LANES * (tiles + 1)), F32)
    narrow = pltpu.VMEM((count, SUBLANES, LANES), F32)
    edge = pltpu.VMEM((rows, LANES), F32)
    return pl.pallas_call(
        lambda *refs: ice_kernel(levels, rows, *refs),
        in_specs=[VMEM_SPEC] * len(operands),
        out_specs=[ANY_SPEC] * 4,
        out_shape=[deep, deep, flat, flat],
        scratch_shapes=[
            pltpu.VMEM((2 * levels, tiles, rows, LANES), F32),
            pltpu.VMEM((2, tiles, count * SUBLANES, LANES), F32),
            looped, looped, looped, looped, looped,
            narrow, narrow, narrow, narrow, edge, edge,
            pltpu.SemaphoreType.DMA((2 * levels, tiles)),
            pltpu.SemaphoreType.DMA((2, tiles)),
        ],
        name="ice",
        compiler_params=pltpu.CompilerParams(vmem_limit_bytes=20 << 20),
        cost_estimate=pl.CostEstimate(flops=60000000, bytes_accessed=16 << 20, transcendentals=0),
    )(*[in_vmem(a) for a in operands])


def per_device(*arrays):
    levels, rows, cols = arrays[0].shape
    lon_count, lat_count = lax.axis_size("lon"), lax.axis_size("lat")
    assert cols == 2 * LANES and rows % (2 * HALO) == 0 and lat_count % 2 == 0
    height = -(-(HALO * ICE + 3 * levels) // SUBLANES) * SUBLANES

    def place(lat, lon):
        return lon * lat_count + lat

    first_pairs, second_pairs = [], []
    for lon in range(lon_count):
        for lat in range(lat_count):
            first_pairs.append((place(lat, lon), place(lat ^ 1, lon)))
            if lat == lat_count - 1:
                second_pairs.append((place(lat, lon), place(lat, lon_count - 1 - lon)))
            elif lat:
                second_pairs.append((place(lat, lon), place(((lat + 1) ^ 1) - 1, lon)))
    first, second = pack_rows(arrays, levels, rows, cols, height)
    first = lax.ppermute(first, ("lon", "lat"), first_pairs)
    second = lax.ppermute(second, ("lon", "lat"), second_pairs)
    tracers, speeds, sea, fields, east_msg, west_msg = load_and_pack_columns(
        arrays, levels, rows, cols
    )
    halo, fields, east_msg, west_msg = merge_halo(
        first, second, fields, east_msg, west_msg, levels, rows
    )
    eastward = [(i, (i + 1) % lon_count) for i in range(lon_count)]
    from_west = lax.ppermute(east_msg, "lon", eastward)
    from_east = lax.ppermute(west_msg, "lon", [(b, a) for a, b in eastward])
    moved, *state = advect(tracers, speeds, sea, halo, fields, levels, rows * lat_count)
    return ice_and_edges(
        [fields, moved, speeds, east_msg, west_msg, from_west, from_east, *state], levels, rows, cols
    )


def solution(mesh):
    deep, flat = P(None, "lat", "lon"), P("lat", "lon")
    return jax.shard_map(
        per_device,
        mesh=mesh,
        in_specs=(deep,) * 4 + (flat,) * 7,
        out_specs=(deep, deep, flat, flat),
        check_vma=False,
    )
```

```python
import jax
import jax.numpy as jnp
from jax import lax
from jax.experimental import pallas as pl
from jax.experimental.pallas import tpu as pltpu
from jax.sharding import PartitionSpec as P

SUBCYCLES = 4
HEAT_RATE = 0.1
SALT_RATE = 0.5
FREEZE_SLOPE = 0.054
DIAGONAL = 1.5
HALO = 2 * SUBCYCLES
LANES = 128
SUBLANES = 8
ICE = 6
FOLD_SIGN = (-1.0, -1.0, 1.0, 1.0, -1.0, -1.0)
TRACER_LANE = 64
F32 = jnp.float32


def lane_ids():
    return lax.broadcasted_iota(jnp.int32, (SUBLANES, LANES), 1)


def sublane_ids():
    return lax.broadcasted_iota(jnp.int32, (SUBLANES, LANES), 0)


def turn(x, shift, axis=1):
    shift = shift % x.shape[axis]
    return pltpu.roll(x, shift, axis) if shift else x


def cut(t):
    return slice(LANES * t, LANES * (t + 1))


def ice_fields(land, ice, u, v, pressure, wind_x, wind_y, ocean_u, ocean_v):
    covered = land.astype(F32) * ice.astype(F32)
    return (u * covered, v * covered, pressure, covered, wind_x + ocean_u, wind_y + ocean_v)


def east_columns(fields, lane):
    packed = jnp.zeros((SUBLANES, LANES), F32)
    for f, tile in enumerate(fields):
        start = HALO * f + 2 * HALO
        moved = turn(tile, start - (LANES - HALO))
        packed = jnp.where((lane >= start) & (lane < start + HALO), moved, packed)
    return packed


def west_columns(fields, lane):
    packed = jnp.zeros((SUBLANES, LANES), F32)
    for f, tile in enumerate(fields):
        start = HALO * f
        packed = jnp.where((lane >= start) & (lane < start + HALO), turn(tile, start), packed)
    return packed


def sublane_rows(rows):
    return (rows + 2 * HALO) // SUBLANES | 1


def in_chunks_of(count, body, group):
    size = max(c for c in range(1, 21) if count % c == 0)

    def step(n, carry):
        seen = {}

        def load(ref, j, *where):
            key = (id(ref), j, *[str(w) for w in where])
            if key not in seen:
                seen[key] = ref[(n * size + j, slice(None), *where)]
            return seen[key]

        for start in range(0, size, group):
            writes = []

            for j in range(start, min(start + group, size)):
                writes += body(n * size + j, j, load)
            for ref, where, value in writes:
                ref[where] = value
        return carry

    lax.fori_loop(0, count // size, step, 0)


def rows_kernel(levels, *refs):
    tops, bottoms = refs[0:12], refs[12:24]
    first_ref, second_ref = refs[24:26]
    even = lax.rem(lax.axis_index("lat"), 2) == 0

    def message(group, row, northward):
        land, ice, u, v, pressure, wind_x, wind_y, east, north, temp, salt = (
            r for r in group[:11]
        )
        fields = ice_fields(
            land[...], ice[...], u[...], v[...], pressure[...], wind_x[...], wind_y[...],
            east[0], north[0],
        )
        sea = land[row : row + 1, :].astype(F32)
        parts = list(fields) + [temp[:, row, :], salt[:, row, :]]
        if northward:
            parts.append(north[:, row, :] * sea)
        else:
            parts.append(jnp.broadcast_to(sea, (levels, sea.shape[1])))
        return parts

    top = message(tops, SUBLANES - 1, True)
    bottom = message(bottoms, 0, False)
    at = 0
    for t, b in zip(top, bottom):
        size = t.shape[0]
        first_ref[at : at + size, :] = jnp.where(even, t, b)
        second_ref[at : at + size, :] = jnp.where(even, b, t)
        at += size
    pad = first_ref.shape[0] - at
    if pad:
        first_ref[at:, :] = jnp.zeros((pad, first_ref.shape[1]), F32)
        second_ref[at:, :] = jnp.zeros((pad, second_ref.shape[1]), F32)


def pack_rows(arrays, levels, rows, cols, height):
    temp, salt, east, north, land, ice, u, v, pressure, wind_x, wind_y = arrays
    operands = [land, ice, u, v, pressure, wind_x, wind_y, east, north, temp, salt, land]
    last = rows // SUBLANES - 1

    def spec(array, block, count):
        if array.ndim == 2:
            return pl.BlockSpec((SUBLANES, cols), lambda _: (block, 0))
        return pl.BlockSpec((count, SUBLANES, cols), lambda _: (0, block, 0))

    counts = [1] * 7 + [1, levels, levels, levels, 1]
    specs = [spec(a, last, c) for a, c in zip(operands, counts)]
    specs += [spec(a, 0, c) for a, c in zip(operands, counts)]
    out = jax.ShapeDtypeStruct((height, cols), F32)
    return pl.pallas_call(
        lambda *refs: rows_kernel(levels, *refs),
        grid=(1,),
        in_specs=specs,
        out_specs=[pl.BlockSpec((height, cols), lambda _: (0, 0))] * 2,
        out_shape=[out, out],
        name="edge_rows",
        compiler_params=pltpu.CompilerParams(vmem_limit_bytes=8 << 20),
        cost_estimate=pl.CostEstimate(flops=100000, bytes_accessed=1 << 20, transcendentals=0),
    )(*[in_hbm(a) for a in operands + operands])


def columns_kernel(levels, land, ice, u, v, pressure, wind_x, wind_y, east, north, temp, salt,
                   tracer_out, speed_out, sea_out, field_out, east_out, west_out, sem):
    lane = lane_ids()
    rows = sea_out.shape[1]
    tiles = sea_out.shape[0]
    tracers = 2 * levels
    first_lane = TRACER_LANE
    mask_lane = TRACER_LANE + 2 * tracers

    copies = []
    for n, ref in enumerate((temp, salt, east, north)):
        out = tracer_out if n < 2 else speed_out
        for t in range(tiles):
            copies.append(
                pltpu.make_async_copy(
                    ref.at[..., pl.ds(LANES * t, LANES)],
                    out.at[pl.ds(levels * (n % 2), levels), t],
                    sem.at[n, t],
                )
            )
    for copy in copies:
        copy.start()

    def each_row_tile(body, size):
        size = next(c for c in range(size, 0, -1) if rows // SUBLANES % c == 0)

        def step(n, carry):
            writes = []
            for j in range(size):
                writes += body(pl.multiple_of((n * size + j) * SUBLANES, SUBLANES))
            for ref, where, value in writes:
                ref[where] = value
            return carry

        lax.fori_loop(0, rows // SUBLANES // size, step, 0)

    whole = slice(None)

    def pack(start):
        at, put = pl.ds(start, SUBLANES), pl.ds(start + HALO, SUBLANES)
        writes, fields = [], []
        for t in range(tiles):
            c = cut(t)
            fields.append(
                ice_fields(
                    *[r[at, c] for r in (land, ice, u, v, pressure, wind_x, wind_y)],
                    east[0, at, c], north[0, at, c],
                )
            )
            writes.append((sea_out, (t, at, whole), land[at, c].astype(F32)))
            for f in range(ICE):
                writes.append((field_out, (f, t, put, whole), fields[t][f]))
        eastward = east_columns(fields[-1], lane)
        westward = west_columns(fields[0], lane)
        for f in range(tracers):
            ref, l, to = (temp, salt)[f // levels], f % levels, first_lane + 2 * f
            eastward = jnp.where(
                lane == to, turn(ref[l, at, cut(tiles - 1)], to - (LANES - 1)), eastward
            )
            westward = jnp.where(lane == to, turn(ref[l, at, cut(0)], to), westward)
        masked = (lane >= mask_lane) & (lane < mask_lane + 2 * tracers)
        speeds = jnp.zeros((SUBLANES, LANES), F32)
        for f in range(levels):
            to = mask_lane + 2 * f
            speeds = jnp.where(
                lane == to, turn(east[f, at, cut(tiles - 1)], to - (LANES - 1)), speeds
            )
        speeds = speeds + turn(speeds, 2 * levels)
        last = land[at, LANES * tiles - 1 : LANES * tiles].astype(F32)
        first = jnp.broadcast_to(land[at, 0:1].astype(F32), (SUBLANES, LANES))
        writes.append((east_out, (put, whole), jnp.where(masked, speeds * last, eastward)))
        writes.append((west_out, (put, whole), jnp.where(masked, first, westward)))
        return writes

    each_row_tile(pack, 6)
    end = HALO + rows
    blank = jnp.zeros((field_out.shape[2] - end, LANES), F32)
    for t in range(tiles):
        for f in range(ICE):
            field_out[f, t, end:, :] = blank
    for ref in (east_out, west_out):
        ref[end:, :] = blank
    for copy in copies:
        copy.wait()


def in_vmem(x):
    return pltpu.with_memory_space_constraint(x, pltpu.VMEM)


def in_hbm(x):
    return pltpu.with_memory_space_constraint(x, pltpu.HBM)


def resident(*shape):
    return pltpu.VMEM(shape, F32)


VMEM_SPEC = pl.BlockSpec(memory_space=pltpu.VMEM)
ANY_SPEC = pl.BlockSpec(memory_space=pl.ANY)


def load_and_pack_columns(arrays, levels, rows, cols):
    temp, salt, east, north, land, ice, u, v, pressure, wind_x, wind_y = arrays
    tiles = cols // LANES
    message = resident(sublane_rows(rows) * SUBLANES, LANES)
    deep = resident(2 * levels, tiles, rows, LANES)
    return pl.pallas_call(
        lambda *refs: columns_kernel(levels, *refs),
        in_specs=[VMEM_SPEC] * 11,
        out_specs=[VMEM_SPEC] * 6,
        out_shape=[
            deep, deep, resident(tiles, rows, LANES),
            resident(ICE, tiles, sublane_rows(rows) * SUBLANES, LANES), message, message,
        ],
        scratch_shapes=[pltpu.SemaphoreType.DMA((4, tiles))],
        name="edge_columns",
        compiler_params=pltpu.CompilerParams(vmem_limit_bytes=4 << 20),
        cost_estimate=pl.CostEstimate(flops=5000000, bytes_accessed=12 << 20, transcendentals=0),
    )(*[in_vmem(a) for a in (land, ice, u, v, pressure, wind_x, wind_y, east, north, temp, salt)])


def halo_kernel(levels, rows, first, second, field_in, east_in, west_in,
                halo_ref, field_out, east_out, west_out):
    lat = lax.axis_index("lat")
    even = lax.rem(lat, 2) == 0
    top = lat == lax.axis_size("lat") - 1
    lane, sublane = lane_ids(), sublane_ids()
    tiles = field_out.shape[1]
    south_fields, north_fields = [], []
    for f in range(ICE):
        at = slice(HALO * f, HALO * (f + 1))
        north_row, south_row = [], []
        for t in range(tiles):
            cols = slice(LANES * t, LANES * (t + 1))
            mirror = slice(LANES * (tiles - 1 - t), LANES * (tiles - t))
            south = jnp.where(even, second[at, cols], first[at, cols])
            plain = jnp.where(even, first[at, cols], second[at, cols])
            turned = jnp.take_along_axis(second[at, mirror], LANES - 1 - lane, axis=1)
            turned = jnp.take_along_axis(turned, SUBLANES - 1 - sublane, axis=0)
            north = jnp.where(top, turned * FOLD_SIGN[f], plain)
            field_out[f, t, 0:HALO, :] = south
            field_out[f, t, rows + HALO : rows + 2 * HALO, :] = north
            south_row.append(south)
            north_row.append(north)
        south_fields.append(south_row)
        north_fields.append(north_row)
    rest = slice(HALO * ICE, first.shape[0])
    halo_ref[0] = jnp.where(even, second[rest, :], first[rest, :])
    halo_ref[1] = jnp.where(top, 0.0, jnp.where(even, first[rest, :], second[rest, :]))
    for at, fields in ((0, south_fields), (rows + HALO, north_fields)):
        east_out[at : at + HALO, :] = east_columns([f[-1] for f in fields], lane)
        west_out[at : at + HALO, :] = west_columns([f[0] for f in fields], lane)


def merge_halo(first, second, fields, east_msg, west_msg, levels, rows):
    height, cols = first.shape
    return pl.pallas_call(
        lambda *refs: halo_kernel(levels, rows, *refs),
        in_specs=[VMEM_SPEC] * 5,
        out_specs=[VMEM_SPEC] * 4,
        out_shape=[
            resident(2, height - HALO * ICE, cols), resident(*fields.shape),
            resident(*east_msg.shape), resident(*west_msg.shape),
        ],
        input_output_aliases={2: 1, 3: 2, 4: 3},
        name="halo_rows",
        compiler_params=pltpu.CompilerParams(vmem_limit_bytes=8 << 20),
        cost_estimate=pl.CostEstimate(flops=100000, bytes_accessed=1 << 19, transcendentals=0),
    )(first, second, in_vmem(fields), in_vmem(east_msg), in_vmem(west_msg))


def advect_kernel(levels, row_total, tracer_ref, speed_ref, sea, halo, field_ref,
                  out, base_u, base_v, third, force, push_x, push_y, turn_a, turn_b,
                  mask_e, mask_n):
    tiles, rows = sea.shape[:2]
    count = rows // SUBLANES
    group = next(c for c in (12, 8, 4, 2) if count % c == 0)
    lane, sublane = lane_ids(), sublane_ids()
    extra_row = 2 * levels
    whole = slice(None)

    def rows_at(k, offset=0):
        start = pl.multiple_of(k * SUBLANES, SUBLANES)
        return pl.ds(start + offset if offset else start, SUBLANES)

    def row(side, index, t):
        cols = slice(LANES * t, LANES * (t + 1))
        return jnp.broadcast_to(halo[side, index : index + 1, cols], (SUBLANES, LANES))

    def from_next(values):
        turned = [turn(v, -1) for v in values]
        return [
            jnp.where(lane == LANES - 1, turned[t + 1], turned[t]) if t + 1 < tiles else turned[t]
            for t in range(tiles)
        ]

    def from_last(values):
        turned = [turn(v, 1) for v in values]
        return [jnp.where(lane == 0, turned[t - 1], turned[t]) for t in range(tiles)]

    def in_groups(body, carry):
        def some(start, carry, last):
            writes = []
            for j in range(group):
                more, carry = body(start + j, last and j == group - 1, carry)
                writes += more
            for ref, where, value in writes:
                ref[where] = value
            return carry

        groups = count // group
        carry = lax.fori_loop(0, groups - 1, lambda n, c: some(n * group, c, False), carry)
        return some((groups - 1) * group, carry, True)

    def row_above(load, k, last, past):
        if not last:
            return load(rows_at(k, 1))
        return jnp.where(sublane == SUBLANES - 1, past, turn(load(rows_at(k)), -1, 0))

    def masks(k, last, carry):
        here = [sea[t, rows_at(k), :] for t in range(tiles)]
        beside = from_next(here)
        writes = []
        for t in range(tiles):
            above = row_above(lambda at, t=t: sea[t, at, :], k, last, row(1, extra_row, t))
            face = here[t] * beside[t]
            if t == tiles - 1:
                face = jnp.where(lane == LANES - 1, 0.0, face)
            writes.append((mask_e, (t, rows_at(k), whole), face))
            writes.append((mask_n, (t, rows_at(k), whole), here[t] * above))
        return writes, carry

    in_groups(masks, 0)
    for level in range(levels):
        entering = []
        for f in (level, levels + level):
            for t in range(tiles):
                speed = row(0, extra_row + level, t) * sea[t, 0:SUBLANES, :]
                start = tracer_ref[f, t, 0:SUBLANES, :]
                entering.append(speed * jnp.where(speed > 0, row(0, f, t), start))

        def body(k, last, carry, level=level):
            at = rows_at(k)
            fast_e = [speed_ref[level, t, at, :] * mask_e[t, at, :] for t in range(tiles)]
            fast_n = [speed_ref[levels + level, t, at, :] * mask_n[t, at, :] for t in range(tiles)]
            writes, result = [], []
            for f in (level, levels + level):
                here = [tracer_ref[f, t, at, :] for t in range(tiles)]
                beside = from_next(here)
                flux_e = [
                    fast_e[t] * jnp.where(fast_e[t] > 0, here[t], beside[t]) for t in range(tiles)
                ]
                before = from_last(flux_e)
                for t in range(tiles):
                    above = row_above(
                        lambda at, f=f, t=t: tracer_ref[f, t, at, :], k, last, row(1, f, t)
                    )
                    flux_n = fast_n[t] * jnp.where(fast_n[t] > 0, here[t], above)
                    turned = turn(flux_n, 1, 0)
                    below = jnp.where(sublane == 0, carry[len(result)], turned)
                    value = here[t] - ((flux_e[t] - before[t]) + (flux_n - below))
                    writes.append((out, (f, t, at, whole), value))
                    result.append(turned)
            return writes, tuple(result)

        in_groups(body, tuple(entering))
    spread_fields(rows, row_total, field_ref, base_u, base_v, third, force, push_x, push_y,
                  turn_a, turn_b)


def spread(ref, i, count, *lead):
    return ref[(*lead, pl.ds(i, SUBLANES, stride=count), slice(None))]


def wrap(ref, count, lanes=slice(None)):
    ref[0, :, lanes] = turn(ref[count, :, lanes], 1, 0)
    ref[count + 1, :, lanes] = turn(ref[1, :, lanes], -1, 0)


def spread_fields(rows, row_total, field_ref, base_u, base_v, third, force, push_x, push_y,
                  turn_a, turn_b):
    tiles = field_ref.shape[1]
    count = sublane_rows(rows)
    lane, sublane = lane_ids(), sublane_ids()
    lat = lax.axis_index("lat")

    def body(i, _, load):
        per_tile = [[spread(field_ref, i, count, f, t) for f in range(ICE)] for t in range(tiles)]
        extra = []
        for f in range(ICE):
            low, high = per_tile[0][f], per_tile[-1][f]
            middle = turn(jnp.where(lane < LANES // 2, high, low), 48)
            x = jnp.where(lane < 32, low, middle)
            extra.append(jnp.where(lane >= 64, turn(high, -24), x))
        writes = []
        for t, fields in enumerate(per_tile + [extra]):
            u0, v0, strength, covered, drive_x, drive_y = fields
            writes.append((base_u, (i + 1, slice(None), cut(t)), u0))
            writes.append((base_v, (i + 1, slice(None), cut(t)), v0))
            writes.append((third, (i, slice(None), cut(t)), covered * (1.0 / 3.0)))
            writes.append((force, (i, slice(None), cut(t)), strength * covered * (1.0 / 12.0)))
            writes.append((push_x, (i, slice(None), cut(t)), 0.5 * drive_x))
            writes.append((push_y, (i, slice(None), cut(t)), 0.5 * drive_y))
        y = lat * rows - HALO + sublane * count + i
        y = jnp.where(y >= row_total, 2 * row_total - 1 - y, y)
        coriolis = 0.5 * (2 * y + 1 - row_total).astype(F32) / row_total
        turning = 0.5 * coriolis
        scale = 3.0 / (DIAGONAL * DIAGONAL + turning * turning)
        writes.append((turn_a, (i,), DIAGONAL * scale))
        writes.append((turn_b, (i,), turning * scale))
        return writes

    in_chunks_of(count, body, 3)
    wrap(base_u, count)
    wrap(base_v, count)


def advect(tracers, speeds, sea, halo, fields, levels, row_total):
    tiles, rows = sea.shape[:2]
    count = sublane_rows(rows)
    wide = LANES * (tiles + 1)
    looped = resident(count + 2, SUBLANES, wide)
    plain = resident(count, SUBLANES, wide)
    narrow = resident(count, SUBLANES, LANES)
    return pl.pallas_call(
        lambda *refs: advect_kernel(levels, row_total, *refs),
        in_specs=[VMEM_SPEC] * 5,
        out_specs=[VMEM_SPEC] * 9,
        out_shape=[
            resident(*tracers.shape), looped, looped, plain, plain, plain, plain, narrow, narrow,
        ],
        scratch_shapes=[pltpu.VMEM((tiles, rows, LANES), F32)] * 2,
        name="advect",
        compiler_params=pltpu.CompilerParams(vmem_limit_bytes=8 << 20),
        cost_estimate=pl.CostEstimate(flops=30000000, bytes_accessed=16 << 20, transcendentals=0),
    )(*[in_vmem(a) for a in (tracers, speeds, sea, halo, fields)])


def ice_kernel(levels, rows, *refs):
    (covered_in, tracers_in, speeds_in, east_own, west_own, from_west, from_east,
     base_u, base_v, third, force, push_x, push_y, turn_a, turn_b,
     temp_out, salt_out, u_out, v_out,
     moved, done, vel_u, vel_v, str_a, str_b, str_c,
     third_x, force_x, push_x_x, push_y_x, edges,
     out_sem, vel_sem) = refs
    tiles = tracers_in.shape[1]
    count = sublane_rows(rows)
    tracers = 2 * levels
    lane = lane_ids()
    own = pl.ds(HALO, rows)
    wide = tiles + 1
    whole = slice(None)

    def edge_fluxes(k, carry):
        at = pl.ds(pl.multiple_of(k * SUBLANES + HALO, SUBLANES), SUBLANES)
        put = pl.ds(pl.multiple_of(k * SUBLANES, SUBLANES), SUBLANES)
        west, east_side = from_west[at, :], from_east[at, :]
        mine_e, mine_w = east_own[at, :], west_own[at, :]
        speed = turn(west, -2 * tracers)
        inflow = speed * jnp.where(speed > 0, west, mine_w) * turn(mine_w, -2 * tracers)
        speed = turn(mine_e, -2 * tracers)
        outflow = speed * jnp.where(speed > 0, mine_e, east_side) * turn(east_side, -2 * tracers)
        edges[put, :] = jnp.where(lane % 2 == TRACER_LANE % 2, inflow, turn(outflow, -1))
        return carry

    lax.fori_loop(0, rows // SUBLANES, edge_fluxes, 0, unroll=8)

    def fixed(f, put):
        flux = turn(edges[put, :], -(TRACER_LANE + 2 * f))
        low = tracers_in[f, 0, put, :] + jnp.where(lane == 0, flux, 0.0)
        return low, tracers_in[f, tiles - 1, put, :] - jnp.where(lane == LANES - 1, flux, 0.0)

    def stores(f):
        out = temp_out.at[f] if f < levels else salt_out.at[f - levels]
        return [
            pltpu.make_async_copy(
                moved.at[f, t], out.at[:, pl.ds(LANES * t, LANES)], out_sem.at[f, t]
            )
            for t in range(tiles)
        ]

    deep = [f for f in range(tracers) if f % levels]
    size = next(c for c in (16, 8, 4, 2) if rows // SUBLANES % c == 0)

    def fix(n, carry):
        puts = [
            pl.ds(pl.multiple_of((n * size + j) * SUBLANES, SUBLANES), SUBLANES)
            for j in range(size)
        ]
        for f in deep:
            results = [fixed(f, put) for put in puts]
            for put, (low, high) in zip(puts, results):
                moved[f, 0, put, :] = low
                moved[f, tiles - 1, put, :] = high
        return carry

    lax.fori_loop(0, rows // SUBLANES // size, fix, 0)
    pending = [copy for f in deep for copy in stores(f)]
    for copy in pending:
        copy.start()

    def insert(i, j, load):
        west, east_side = spread(from_west, i, count), spread(from_east, i, count)
        writes = []
        targets = (
            (base_u, vel_u, 1, tiles, 1.0), (base_v, vel_v, 1, tiles, 1.0),
            (force, force_x, 0, 0, 1.0), (third, third_x, 0, 0, 1.0 / 3.0),
            (push_x, push_x_x, 0, 0, 0.5), (push_y, push_y_x, 0, 0, 0.5),
        )
        beyond = []
        for f in range(ICE):
            start = HALO * f + 2 * HALO
            x = jnp.where((lane >= start) & (lane < start + HALO), west, east_side)
            beyond.append(turn(x, 104 - HALO * f))
        beyond[2] = beyond[2] * beyond[3] * (1.0 / 12.0)
        for x, (source, target, shift, t, factor) in zip(beyond, targets):
            x = x if factor == 1.0 else x * factor
            x = jnp.where(lane >= 104, x, source[i + shift, :, cut(tiles)])
            writes.append((target, (i + shift, whole, cut(t)), x))
        return writes

    in_chunks_of(count, insert, 6)
    wrap(vel_u, count, cut(tiles))
    wrap(vel_v, count, cut(tiles))
    extras = {id(third): third_x, id(force): force_x, id(push_x): push_x_x, id(push_y): push_y_x}

    def constant(load, ref, j, t):
        return load(ref, j, cut(t)) if t < tiles else load(extras[id(ref)], j, cut(0))

    def velocity(load, j, t, first):
        u, v = (base_u, base_v) if first and t < tiles else (vel_u, vel_v)
        return load(u, j, cut(t)), load(v, j, cut(t))

    stresses = (str_a, str_b, str_c)

    def stress(i, j, load, fresh, first):
        writes = []
        for t in range(wide):
            u, v = velocity(load, j + 1, t, first)
            u_above, v_above = velocity(load, j + 2, t, first)
            u_below, v_below = velocity(load, j, t, first)
            dudx, dvdx = turn(u, -1) - turn(u, 1), turn(v, -1) - turn(v, 1)
            dudy, dvdy = u_above - u_below, v_above - v_below
            div, ten, shr = dudx + dvdy, dudx - dvdy, dudy + dvdx
            square = div * div + 0.25 * (ten * ten + shr * shr) + 1.0
            base = constant(load, force, j, t)
            zeta = base * lax.rsqrt(square)
            quarter = 0.25 * zeta
            even = zeta * div - base
            odd = quarter * ten
            new = [even + odd, even - odd, quarter * shr]
            for n, ref in enumerate(stresses):
                if not first:
                    new[n] = new[n] + constant(load, third, j, t) * load(ref, j + 1, cut(t))
                writes.append((ref, (i + 1, whole, cut(t)), new[n]))
                fresh[n, j + 1, t] = new[n]
        return writes

    def momentum(i, j, load, fresh, first):
        def now(n, row, t):
            if (n, row, t) in fresh:
                return fresh[n, row, t]
            return load(stresses[n], row, cut(t))

        ar, br = load(turn_a, j), load(turn_b, j)
        writes = []
        for t in range(wide):
            a, s = now(0, j + 1, t), now(2, j + 1, t)
            fx = (turn(a, -1) - turn(a, 1)) + (now(2, j + 2, t) - now(2, j, t))
            fy = (turn(s, -1) - turn(s, 1)) + (now(1, j + 2, t) - now(1, j, t))
            u, v = velocity(load, j + 1, t, first)
            ru = (u + constant(load, push_x, j, t)) + fx
            rv = (v + constant(load, push_y, j, t)) + fy
            keep = constant(load, third, j, t)
            writes.append((vel_u, (i + 1, whole, cut(t)), (ar * ru + br * rv) * keep))
            writes.append((vel_v, (i + 1, whole, cut(t)), (ar * rv - br * ru) * keep))
        return writes

    def store(writes):
        for ref, where, value in writes:
            ref[where] = value

    def loader(base):
        seen = {}

        def load(ref, j, *where):
            key = (id(ref), j, *[str(w) for w in where])
            if key not in seen:
                seen[key] = ref[(base + j, whole, *where)]
            return seen[key]

        return load

    chunk = max(c for c in range(1, 21) if count % c == 0)

    def sweep(n, first, from_start):
        base = n * chunk
        load, fresh = loader(base), {}
        for j in range(chunk):
            store(stress(base + j, j, load, fresh, first))
            if not from_start or j >= 2:
                store(momentum(base + j - 1, j - 1, load, fresh, first))

    def subcycle(first):
        sweep(0, first, True)

        def rest(n, carry):
            sweep(n, first, False)
            return carry

        lax.fori_loop(1, count // chunk, rest, 0)
        wrap(str_b, count)
        wrap(str_c, count)
        for i in (0, count - 1):
            store(momentum(i, i, loader(0), {}, first))
        wrap(vel_u, count)
        wrap(vel_v, count)

    subcycle(True)

    def later(_, carry):
        subcycle(False)
        return carry

    lax.fori_loop(1, SUBCYCLES, later, 0)

    def gather(i, j, load):
        writes = []
        for n, ref in enumerate((vel_u, vel_v)):
            borders = ref[i + 1, :, cut(tiles)]
            middle, outer = turn(borders, -48), turn(borders, 24)
            low, high = ref[i + 1, :, cut(0)], ref[i + 1, :, cut(tiles - 1)]
            low = jnp.where(lane < HALO, borders, jnp.where(lane >= LANES - HALO, middle, low))
            high = jnp.where(lane < HALO, middle, jnp.where(lane >= LANES - HALO, outer, high))
            put = pl.ds(i, SUBLANES, stride=count)
            writes.append((done, (n, 0, put, whole), low))
            writes.append((done, (n, tiles - 1, put, whole), high))
        return writes

    in_chunks_of(count, gather, 8)
    finals = []
    for n, out in enumerate((u_out, v_out)):
        for t in range(tiles):
            finals.append(
                pltpu.make_async_copy(
                    done.at[n, t, own, :], out.at[:, pl.ds(LANES * t, LANES)], vel_sem.at[n, t]
                )
            )
            finals[-1].start()

    def warm(n, carry):
        writes = []
        for j in range(size):
            start = pl.multiple_of((n * size + j) * SUBLANES, SUBLANES)
            put, at = pl.ds(start, SUBLANES), pl.ds(start + HALO, SUBLANES)
            sst, sss = fixed(0, put), fixed(levels, put)
            for t in range(tiles):
                slip_u = done[0, t, at, :] - speeds_in[0, t, put, :]
                slip_v = done[1, t, at, :] - speeds_in[levels, t, put, :]
                heat = HEAT_RATE * covered_in[3, t, at, :] * (1.0 + (slip_u * slip_u + slip_v * slip_v))
                heat = heat * (sst[t] + FREEZE_SLOPE * sss[t])
                writes.append((0, t, put, sst[t] - heat))
                writes.append((levels, t, put, sss[t] - SALT_RATE * heat))
        for f, t, put, value in writes:
            moved[f, t, put, :] = value
        return carry

    lax.fori_loop(0, rows // SUBLANES // size, warm, 0)
    for f in (0, levels):
        copies = stores(f)
        for copy in copies:
            copy.start()
        finals += copies
    for copy in pending + finals:
        copy.wait()


def ice_and_edges(operands, levels, rows, cols):
    tiles = cols // LANES
    count = sublane_rows(rows)
    deep = jax.ShapeDtypeStruct((levels, rows, cols), F32)
    flat = jax.ShapeDtypeStruct((rows, cols), F32)
    looped = pltpu.VMEM((count + 2, SUBLANES, LANES * (tiles + 1)), F32)
    narrow = pltpu.VMEM((count, SUBLANES, LANES), F32)
    return pl.pallas_call(
        lambda *refs: ice_kernel(levels, rows, *refs),
        in_specs=[VMEM_SPEC] * len(operands),
        out_specs=[ANY_SPEC] * 4,
        out_shape=[deep, deep, flat, flat],
        scratch_shapes=[
            pltpu.VMEM((2 * levels, tiles, rows, LANES), F32),
            pltpu.VMEM((2, tiles, count * SUBLANES, LANES), F32),
            looped, looped, looped, looped, looped,
            narrow, narrow, narrow, narrow, pltpu.VMEM((rows, LANES), F32),
            pltpu.SemaphoreType.DMA((2 * levels, tiles)),
            pltpu.SemaphoreType.DMA((2, tiles)),
        ],
        name="ice",
        compiler_params=pltpu.CompilerParams(vmem_limit_bytes=20 << 20),
        cost_estimate=pl.CostEstimate(flops=60000000, bytes_accessed=16 << 20, transcendentals=0),
    )(*[in_vmem(a) for a in operands])


def per_device(*arrays):
    levels, rows, cols = arrays[0].shape
    lon_count, lat_count = lax.axis_size("lon"), lax.axis_size("lat")
    assert cols == 2 * LANES and rows % (2 * HALO) == 0 and lat_count % 2 == 0
    height = -(-(HALO * ICE + 3 * levels) // SUBLANES) * SUBLANES

    def place(lat, lon):
        return lon * lat_count + lat

    first_pairs, second_pairs = [], []
    for lon in range(lon_count):
        for lat in range(lat_count):
            first_pairs.append((place(lat, lon), place(lat ^ 1, lon)))
            if lat == lat_count - 1:
                second_pairs.append((place(lat, lon), place(lat, lon_count - 1 - lon)))
            elif lat:
                second_pairs.append((place(lat, lon), place(((lat + 1) ^ 1) - 1, lon)))
    first, second = pack_rows(arrays, levels, rows, cols, height)
    first = lax.ppermute(first, ("lon", "lat"), first_pairs)
    second = lax.ppermute(second, ("lon", "lat"), second_pairs)
    tracers, speeds, sea, fields, east_msg, west_msg = load_and_pack_columns(
        arrays, levels, rows, cols
    )
    halo, fields, east_msg, west_msg = merge_halo(
        first, second, fields, east_msg, west_msg, levels, rows
    )
    eastward = [(i, (i + 1) % lon_count) for i in range(lon_count)]
    from_west = lax.ppermute(east_msg, "lon", eastward)
    from_east = lax.ppermute(west_msg, "lon", [(b, a) for a, b in eastward])
    moved, *state = advect(tracers, speeds, sea, halo, fields, levels, rows * lat_count)
    return ice_and_edges(
        [fields, moved, speeds, east_msg, west_msg, from_west, from_east, *state], levels, rows, cols
    )


def solution(mesh):
    deep, flat = P(None, "lat", "lon"), P("lat", "lon")
    return jax.shard_map(
        per_device,
        mesh=mesh,
        in_specs=(deep,) * 4 + (flat,) * 7,
        out_specs=(deep, deep, flat, flat),
        check_vma=False,
    )
```

```python
import jax
import jax.numpy as jnp
from jax import lax
from jax.experimental import pallas as pl
from jax.experimental.pallas import tpu as pltpu
from jax.sharding import PartitionSpec as P

SUBCYCLES = 4
HEAT_RATE = 0.1
SALT_RATE = 0.5
FREEZE_SLOPE = 0.054
DIAGONAL = 1.5
HALO = 2 * SUBCYCLES
LANES = 128
SUBLANES = 8
ICE = 6
FOLD_SIGN = (-1.0, -1.0, 1.0, 1.0, -1.0, -1.0)
TRACER_LANE = 64
F32 = jnp.float32


def lane_ids():
    return lax.broadcasted_iota(jnp.int32, (SUBLANES, LANES), 1)


def sublane_ids():
    return lax.broadcasted_iota(jnp.int32, (SUBLANES, LANES), 0)


def turn(x, shift, axis=1):
    shift = shift % x.shape[axis]
    return pltpu.roll(x, shift, axis) if shift else x


def cut(t):
    return slice(LANES * t, LANES * (t + 1))


def ice_fields(land, ice, u, v, pressure, wind_x, wind_y, ocean_u, ocean_v):
    covered = land.astype(F32) * ice.astype(F32)
    return (u * covered, v * covered, pressure, covered, wind_x + ocean_u, wind_y + ocean_v)


def east_columns(fields, lane):
    packed = jnp.zeros((SUBLANES, LANES), F32)
    for f, tile in enumerate(fields):
        start = HALO * f + 2 * HALO
        moved = turn(tile, start - (LANES - HALO))
        packed = jnp.where((lane >= start) & (lane < start + HALO), moved, packed)
    return packed


def west_columns(fields, lane):
    packed = jnp.zeros((SUBLANES, LANES), F32)
    for f, tile in enumerate(fields):
        start = HALO * f
        packed = jnp.where((lane >= start) & (lane < start + HALO), turn(tile, start), packed)
    return packed


def sublane_rows(rows):
    return (rows + 2 * HALO) // SUBLANES | 1


def in_chunks_of(count, body, group):
    size = max(c for c in range(1, 21) if count % c == 0)

    def step(n, carry):
        seen = {}

        def load(ref, name, j, *where):
            key = (name, j, *[str(w) for w in where])
            if key not in seen:
                seen[key] = ref[(n * size + j, slice(None), *where)]
            return seen[key]

        for start in range(0, size, group):
            writes = []

            for j in range(start, min(start + group, size)):
                writes += body(n * size + j, j, load)
            for ref, where, value in writes:
                ref[where] = value
        return carry

    lax.fori_loop(0, count // size, step, 0)


def rows_kernel(levels, *refs):
    tops, bottoms = refs[0:12], refs[12:24]
    first_ref, second_ref = refs[24:26]
    even = lax.rem(lax.axis_index("lat"), 2) == 0

    def message(group, row, northward):
        land, ice, u, v, pressure, wind_x, wind_y, east, north, temp, salt = (
            r for r in group[:11]
        )
        fields = ice_fields(
            land[...], ice[...], u[...], v[...], pressure[...], wind_x[...], wind_y[...],
            east[0], north[0],
        )
        sea = land[row : row + 1, :].astype(F32)
        parts = list(fields) + [temp[:, row, :], salt[:, row, :]]
        if northward:
            parts.append(north[:, row, :] * sea)
        else:
            parts.append(jnp.broadcast_to(sea, (levels, sea.shape[1])))
        return parts

    top = message(tops, SUBLANES - 1, True)
    bottom = message(bottoms, 0, False)
    at = 0
    for t, b in zip(top, bottom):
        size = t.shape[0]
        first_ref[at : at + size, :] = jnp.where(even, t, b)
        second_ref[at : at + size, :] = jnp.where(even, b, t)
        at += size
    pad = first_ref.shape[0] - at
    if pad:
        first_ref[at:, :] = jnp.zeros((pad, first_ref.shape[1]), F32)
        second_ref[at:, :] = jnp.zeros((pad, second_ref.shape[1]), F32)


def pack_rows(arrays, levels, rows, cols, height):
    temp, salt, east, north, land, ice, u, v, pressure, wind_x, wind_y = arrays
    operands = [land, ice, u, v, pressure, wind_x, wind_y, east, north, temp, salt, land]
    last = rows // SUBLANES - 1

    def spec(array, block, count):
        if array.ndim == 2:
            return pl.BlockSpec((SUBLANES, cols), lambda _: (block, 0))
        return pl.BlockSpec((count, SUBLANES, cols), lambda _: (0, block, 0))

    counts = [1] * 7 + [1, levels, levels, levels, 1]
    specs = [spec(a, last, c) for a, c in zip(operands, counts)]
    specs += [spec(a, 0, c) for a, c in zip(operands, counts)]
    out = jax.ShapeDtypeStruct((height, cols), F32)
    return pl.pallas_call(
        lambda *refs: rows_kernel(levels, *refs),
        grid=(1,),
        in_specs=specs,
        out_specs=[pl.BlockSpec((height, cols), lambda _: (0, 0))] * 2,
        out_shape=[out, out],
        name="edge_rows",
        compiler_params=pltpu.CompilerParams(vmem_limit_bytes=8 << 20),
        cost_estimate=pl.CostEstimate(flops=100000, bytes_accessed=1 << 20, transcendentals=0),
    )(*[in_hbm(a) for a in operands + operands])


def columns_kernel(levels, land, ice, u, v, pressure, wind_x, wind_y, east, north, temp, salt,
                   tracer_out, speed_out, sea_out, field_out, east_out, west_out, sem):
    lane = lane_ids()
    rows = sea_out.shape[1]
    tiles = sea_out.shape[0]
    tracers = 2 * levels
    first_lane = TRACER_LANE
    mask_lane = TRACER_LANE + 2 * tracers

    copies = []
    for n, ref in enumerate((temp, salt, east, north)):
        out = tracer_out if n < 2 else speed_out
        for t in range(tiles):
            copies.append(
                pltpu.make_async_copy(
                    ref.at[..., pl.ds(LANES * t, LANES)],
                    out.at[pl.ds(levels * (n % 2), levels), t],
                    sem.at[n, t],
                )
            )
    for copy in copies:
        copy.start()

    def each_row_tile(body, size):
        size = next(c for c in range(size, 0, -1) if rows // SUBLANES % c == 0)

        def step(n, carry):
            writes = []
            for j in range(size):
                writes += body(pl.multiple_of((n * size + j) * SUBLANES, SUBLANES))
            for ref, where, value in writes:
                ref[where] = value
            return carry

        lax.fori_loop(0, rows // SUBLANES // size, step, 0)

    whole = slice(None)

    def ice_part(start):
        at, put = pl.ds(start, SUBLANES), pl.ds(start + HALO, SUBLANES)
        writes, fields = [], []
        for t in range(tiles):
            c = cut(t)
            fields.append(
                ice_fields(
                    *[r[at, c] for r in (land, ice, u, v, pressure, wind_x, wind_y)],
                    east[0, at, c], north[0, at, c],
                )
            )
            writes.append((sea_out, (t, at, whole), land[at, c].astype(F32)))
            for f in range(ICE):
                writes.append((field_out, (f, t, put, whole), fields[t][f]))
        writes.append((east_out, (put, whole), east_columns(fields[-1], lane)))
        writes.append((west_out, (put, whole), west_columns(fields[0], lane)))
        return writes

    each_row_tile(ice_part, 4)

    def tracer_part(start):
        at, put = pl.ds(start, SUBLANES), pl.ds(start + HALO, SUBLANES)
        eastward, westward = east_out[put, :], west_out[put, :]
        for f in range(tracers):
            ref, l, to = (temp, salt)[f // levels], f % levels, first_lane + 2 * f
            eastward = jnp.where(
                lane == to, turn(ref[l, at, cut(tiles - 1)], to - (LANES - 1)), eastward
            )
            westward = jnp.where(lane == to, turn(ref[l, at, cut(0)], to), westward)
        return [(east_out, (put, whole), eastward), (west_out, (put, whole), westward)]

    each_row_tile(tracer_part, 8)

    def speed_part(start):
        at, put = pl.ds(start, SUBLANES), pl.ds(start + HALO, SUBLANES)
        masked = (lane >= mask_lane) & (lane < mask_lane + 2 * tracers)
        speeds = jnp.zeros((SUBLANES, LANES), F32)
        for f in range(levels):
            to = mask_lane + 2 * f
            speeds = jnp.where(
                lane == to, turn(east[f, at, cut(tiles - 1)], to - (LANES - 1)), speeds
            )
        speeds = speeds + turn(speeds, 2 * levels)
        last = land[at, LANES * tiles - 1 : LANES * tiles].astype(F32)
        first = jnp.broadcast_to(land[at, 0:1].astype(F32), (SUBLANES, LANES))
        eastward = jnp.where(masked, speeds * last, east_out[put, :])
        westward = jnp.where(masked, first, west_out[put, :])
        return [(east_out, (put, whole), eastward), (west_out, (put, whole), westward)]

    each_row_tile(speed_part, 8)
    end = HALO + rows
    blank = jnp.zeros((field_out.shape[2] - end, LANES), F32)
    for t in range(tiles):
        for f in range(ICE):
            field_out[f, t, end:, :] = blank
    for ref in (east_out, west_out):
        ref[end:, :] = blank
    for copy in copies:
        copy.wait()


def in_vmem(x):
    return pltpu.with_memory_space_constraint(x, pltpu.VMEM)


def in_hbm(x):
    return pltpu.with_memory_space_constraint(x, pltpu.HBM)


def resident(*shape):
    return pltpu.VMEM(shape, F32)


VMEM_SPEC = pl.BlockSpec(memory_space=pltpu.VMEM)
ANY_SPEC = pl.BlockSpec(memory_space=pl.ANY)


def load_and_pack_columns(arrays, levels, rows, cols):
    temp, salt, east, north, land, ice, u, v, pressure, wind_x, wind_y = arrays
    tiles = cols // LANES
    message = resident(sublane_rows(rows) * SUBLANES, LANES)
    deep = resident(2 * levels, tiles, rows, LANES)
    return pl.pallas_call(
        lambda *refs: columns_kernel(levels, *refs),
        in_specs=[VMEM_SPEC] * 11,
        out_specs=[VMEM_SPEC] * 6,
        out_shape=[
            deep, deep, resident(tiles, rows, LANES),
            resident(ICE, tiles, sublane_rows(rows) * SUBLANES, LANES), message, message,
        ],
        scratch_shapes=[pltpu.SemaphoreType.DMA((4, tiles))],
        name="edge_columns",
        compiler_params=pltpu.CompilerParams(vmem_limit_bytes=4 << 20),
        cost_estimate=pl.CostEstimate(flops=5000000, bytes_accessed=12 << 20, transcendentals=0),
    )(*[in_vmem(a) for a in (land, ice, u, v, pressure, wind_x, wind_y, east, north, temp, salt)])


def halo_kernel(levels, rows, first, second, field_in, east_in, west_in,
                halo_ref, field_out, east_out, west_out):
    lat = lax.axis_index("lat")
    even = lax.rem(lat, 2) == 0
    top = lat == lax.axis_size("lat") - 1
    lane, sublane = lane_ids(), sublane_ids()
    tiles = field_out.shape[1]
    south_fields, north_fields = [], []
    for f in range(ICE):
        at = slice(HALO * f, HALO * (f + 1))
        north_row, south_row = [], []
        for t in range(tiles):
            cols = slice(LANES * t, LANES * (t + 1))
            mirror = slice(LANES * (tiles - 1 - t), LANES * (tiles - t))
            south = jnp.where(even, second[at, cols], first[at, cols])
            plain = jnp.where(even, first[at, cols], second[at, cols])
            turned = jnp.take_along_axis(second[at, mirror], LANES - 1 - lane, axis=1)
            turned = jnp.take_along_axis(turned, SUBLANES - 1 - sublane, axis=0)
            north = jnp.where(top, turned * FOLD_SIGN[f], plain)
            field_out[f, t, 0:HALO, :] = south
            field_out[f, t, rows + HALO : rows + 2 * HALO, :] = north
            south_row.append(south)
            north_row.append(north)
        south_fields.append(south_row)
        north_fields.append(north_row)
    rest = slice(HALO * ICE, first.shape[0])
    halo_ref[0] = jnp.where(even, second[rest, :], first[rest, :])
    halo_ref[1] = jnp.where(top, 0.0, jnp.where(even, first[rest, :], second[rest, :]))
    for at, fields in ((0, south_fields), (rows + HALO, north_fields)):
        east_out[at : at + HALO, :] = east_columns([f[-1] for f in fields], lane)
        west_out[at : at + HALO, :] = west_columns([f[0] for f in fields], lane)


def merge_halo(first, second, fields, east_msg, west_msg, levels, rows):
    height, cols = first.shape
    return pl.pallas_call(
        lambda *refs: halo_kernel(levels, rows, *refs),
        in_specs=[VMEM_SPEC] * 5,
        out_specs=[VMEM_SPEC] * 4,
        out_shape=[
            resident(2, height - HALO * ICE, cols), resident(*fields.shape),
            resident(*east_msg.shape), resident(*west_msg.shape),
        ],
        input_output_aliases={2: 1, 3: 2, 4: 3},
        name="halo_rows",
        compiler_params=pltpu.CompilerParams(vmem_limit_bytes=8 << 20),
        cost_estimate=pl.CostEstimate(flops=100000, bytes_accessed=1 << 19, transcendentals=0),
    )(first, second, in_vmem(fields), in_vmem(east_msg), in_vmem(west_msg))


def advect_kernel(levels, row_total, tracer_ref, speed_ref, sea, halo, field_ref,
                  out, base_u, base_v, third, force, push_x, push_y, turn_a, turn_b,
                  mask_e, mask_n):
    tiles, rows = sea.shape[:2]
    count = rows // SUBLANES
    group = next(c for c in (12, 8, 4, 2) if count % c == 0)
    lane, sublane = lane_ids(), sublane_ids()
    extra_row = 2 * levels
    whole = slice(None)

    def rows_at(k, offset=0):
        start = pl.multiple_of(k * SUBLANES, SUBLANES)
        return pl.ds(start + offset if offset else start, SUBLANES)

    def row(side, index, t):
        cols = slice(LANES * t, LANES * (t + 1))
        return jnp.broadcast_to(halo[side, index : index + 1, cols], (SUBLANES, LANES))

    def from_next(values):
        turned = [turn(v, -1) for v in values]
        return [
            jnp.where(lane == LANES - 1, turned[t + 1], turned[t]) if t + 1 < tiles else turned[t]
            for t in range(tiles)
        ]

    def from_last(values):
        turned = [turn(v, 1) for v in values]
        return [jnp.where(lane == 0, turned[t - 1], turned[t]) for t in range(tiles)]

    def in_groups(body, carry):
        def some(start, carry, last):
            writes = []
            for j in range(group):
                more, carry = body(start + j, last and j == group - 1, carry)
                writes += more
            for ref, where, value in writes:
                ref[where] = value
            return carry

        groups = count // group
        carry = lax.fori_loop(0, groups - 1, lambda n, c: some(n * group, c, False), carry)
        return some((groups - 1) * group, carry, True)

    def row_above(load, k, last, past):
        if not last:
            return load(rows_at(k, 1))
        return jnp.where(sublane == SUBLANES - 1, past, turn(load(rows_at(k)), -1, 0))

    def masks(k, last, carry):
        here = [sea[t, rows_at(k), :] for t in range(tiles)]
        beside = from_next(here)
        writes = []
        for t in range(tiles):
            above = row_above(lambda at, t=t: sea[t, at, :], k, last, row(1, extra_row, t))
            face = here[t] * beside[t]
            if t == tiles - 1:
                face = jnp.where(lane == LANES - 1, 0.0, face)
            writes.append((mask_e, (t, rows_at(k), whole), face))
            writes.append((mask_n, (t, rows_at(k), whole), here[t] * above))
        return writes, carry

    in_groups(masks, 0)
    for level in range(levels):
        entering = []
        for f in (level, levels + level):
            for t in range(tiles):
                speed = row(0, extra_row + level, t) * sea[t, 0:SUBLANES, :]
                start = tracer_ref[f, t, 0:SUBLANES, :]
                entering.append(speed * jnp.where(speed > 0, row(0, f, t), start))

        def body(k, last, carry, level=level):
            at = rows_at(k)
            fast_e = [speed_ref[level, t, at, :] * mask_e[t, at, :] for t in range(tiles)]
            fast_n = [speed_ref[levels + level, t, at, :] * mask_n[t, at, :] for t in range(tiles)]
            writes, result = [], []
            for f in (level, levels + level):
                here = [tracer_ref[f, t, at, :] for t in range(tiles)]
                beside = from_next(here)
                flux_e = [
                    fast_e[t] * jnp.where(fast_e[t] > 0, here[t], beside[t]) for t in range(tiles)
                ]
                before = from_last(flux_e)
                for t in range(tiles):
                    above = row_above(
                        lambda at, f=f, t=t: tracer_ref[f, t, at, :], k, last, row(1, f, t)
                    )
                    flux_n = fast_n[t] * jnp.where(fast_n[t] > 0, here[t], above)
                    turned = turn(flux_n, 1, 0)
                    below = jnp.where(sublane == 0, carry[len(result)], turned)
                    value = here[t] - ((flux_e[t] - before[t]) + (flux_n - below))
                    writes.append((out, (f, t, at, whole), value))
                    result.append(turned)
            return writes, tuple(result)

        in_groups(body, tuple(entering))
    spread_fields(rows, row_total, field_ref, base_u, base_v, third, force, push_x, push_y,
                  turn_a, turn_b)


def spread(ref, i, count, *lead):
    return ref[(*lead, pl.ds(i, SUBLANES, stride=count), slice(None))]


def wrap(ref, count, lanes=slice(None)):
    ref[0, :, lanes] = turn(ref[count, :, lanes], 1, 0)
    ref[count + 1, :, lanes] = turn(ref[1, :, lanes], -1, 0)


def spread_fields(rows, row_total, field_ref, base_u, base_v, third, force, push_x, push_y,
                  turn_a, turn_b):
    tiles = field_ref.shape[1]
    count = sublane_rows(rows)
    lane, sublane = lane_ids(), sublane_ids()
    lat = lax.axis_index("lat")

    def body(i, _, load):
        per_tile = [[spread(field_ref, i, count, f, t) for f in range(ICE)] for t in range(tiles)]
        extra = []
        for f in range(ICE):
            low, high = per_tile[0][f], per_tile[-1][f]
            middle = turn(jnp.where(lane < LANES // 2, high, low), 48)
            x = jnp.where(lane < 32, low, middle)
            extra.append(jnp.where(lane >= 64, turn(high, -24), x))
        writes = []
        for t, fields in enumerate(per_tile + [extra]):
            u0, v0, strength, covered, drive_x, drive_y = fields
            writes.append((base_u, (i + 1, slice(None), cut(t)), u0))
            writes.append((base_v, (i + 1, slice(None), cut(t)), v0))
            writes.append((third, (i, slice(None), cut(t)), covered * (1.0 / 3.0)))
            writes.append((force, (i, slice(None), cut(t)), strength * covered * (1.0 / 12.0)))
            writes.append((push_x, (i, slice(None), cut(t)), 0.5 * drive_x))
            writes.append((push_y, (i, slice(None), cut(t)), 0.5 * drive_y))
        y = lat * rows - HALO + sublane * count + i
        y = jnp.where(y >= row_total, 2 * row_total - 1 - y, y)
        coriolis = 0.5 * (2 * y + 1 - row_total).astype(F32) / row_total
        turning = 0.5 * coriolis
        scale = 3.0 / (DIAGONAL * DIAGONAL + turning * turning)
        writes.append((turn_a, (i,), DIAGONAL * scale))
        writes.append((turn_b, (i,), turning * scale))
        return writes

    in_chunks_of(count, body, 3)
    wrap(base_u, count)
    wrap(base_v, count)


def advect(tracers, speeds, sea, halo, fields, levels, row_total):
    tiles, rows = sea.shape[:2]
    count = sublane_rows(rows)
    wide = LANES * (tiles + 1)
    looped = resident(count + 2, SUBLANES, wide)
    plain = resident(count, SUBLANES, wide)
    narrow = resident(count, SUBLANES, LANES)
    return pl.pallas_call(
        lambda *refs: advect_kernel(levels, row_total, *refs),
        in_specs=[VMEM_SPEC] * 5,
        out_specs=[VMEM_SPEC] * 9,
        out_shape=[
            resident(*tracers.shape), looped, looped, plain, plain, plain, plain, narrow, narrow,
        ],
        scratch_shapes=[pltpu.VMEM((tiles, rows, LANES), F32)] * 2,
        name="advect",
        compiler_params=pltpu.CompilerParams(vmem_limit_bytes=8 << 20),
        cost_estimate=pl.CostEstimate(flops=30000000, bytes_accessed=16 << 20, transcendentals=0),
    )(*[in_vmem(a) for a in (tracers, speeds, sea, halo, fields)])


def ice_kernel(levels, rows, *refs):
    (covered_in, tracers_in, speeds_in, east_own, west_own, from_west, from_east,
     base_u, base_v, third, force, push_x, push_y, turn_a, turn_b,
     temp_out, salt_out, u_out, v_out,
     moved, done, vel_u, vel_v, str_a, str_b, str_c,
     third_x, force_x, push_x_x, push_y_x, edges,
     out_sem, vel_sem) = refs
    tiles = tracers_in.shape[1]
    count = sublane_rows(rows)
    tracers = 2 * levels
    lane = lane_ids()
    own = pl.ds(HALO, rows)
    wide = tiles + 1
    whole = slice(None)

    def edge_fluxes(k, carry):
        at = pl.ds(pl.multiple_of(k * SUBLANES + HALO, SUBLANES), SUBLANES)
        put = pl.ds(pl.multiple_of(k * SUBLANES, SUBLANES), SUBLANES)
        west, east_side = from_west[at, :], from_east[at, :]
        mine_e, mine_w = east_own[at, :], west_own[at, :]
        speed = turn(west, -2 * tracers)
        inflow = speed * jnp.where(speed > 0, west, mine_w) * turn(mine_w, -2 * tracers)
        speed = turn(mine_e, -2 * tracers)
        outflow = speed * jnp.where(speed > 0, mine_e, east_side) * turn(east_side, -2 * tracers)
        edges[put, :] = jnp.where(lane % 2 == TRACER_LANE % 2, inflow, turn(outflow, -1))
        return carry

    lax.fori_loop(0, rows // SUBLANES, edge_fluxes, 0, unroll=8)

    def fixed(f, put):
        flux = turn(edges[put, :], -(TRACER_LANE + 2 * f))
        low = tracers_in[f, 0, put, :] + jnp.where(lane == 0, flux, 0.0)
        return low, tracers_in[f, tiles - 1, put, :] - jnp.where(lane == LANES - 1, flux, 0.0)

    def stores(f):
        out = temp_out.at[f] if f < levels else salt_out.at[f - levels]
        return [
            pltpu.make_async_copy(
                moved.at[f, t], out.at[:, pl.ds(LANES * t, LANES)], out_sem.at[f, t]
            )
            for t in range(tiles)
        ]

    deep = [f for f in range(tracers) if f % levels]
    size = next(c for c in (16, 8, 4, 2) if rows // SUBLANES % c == 0)

    def fix(n, carry):
        puts = [
            pl.ds(pl.multiple_of((n * size + j) * SUBLANES, SUBLANES), SUBLANES)
            for j in range(size)
        ]
        for f in deep:
            results = [fixed(f, put) for put in puts]
            for put, (low, high) in zip(puts, results):
                moved[f, 0, put, :] = low
                moved[f, tiles - 1, put, :] = high
        return carry

    lax.fori_loop(0, rows // SUBLANES // size, fix, 0)
    pending = [copy for f in deep for copy in stores(f)]
    for copy in pending:
        copy.start()

    def insert(i, j, load):
        west, east_side = spread(from_west, i, count), spread(from_east, i, count)
        writes = []
        targets = (
            (base_u, vel_u.at[0], 1, tiles, 1.0), (base_v, vel_v.at[0], 1, tiles, 1.0),
            (force, force_x, 0, 0, 1.0), (third, third_x, 0, 0, 1.0 / 3.0),
            (push_x, push_x_x, 0, 0, 0.5), (push_y, push_y_x, 0, 0, 0.5),
        )
        beyond = []
        for f in range(ICE):
            start = HALO * f + 2 * HALO
            x = jnp.where((lane >= start) & (lane < start + HALO), west, east_side)
            beyond.append(turn(x, 104 - HALO * f))
        beyond[2] = beyond[2] * beyond[3] * (1.0 / 12.0)
        for x, (source, target, shift, t, factor) in zip(beyond, targets):
            x = x if factor == 1.0 else x * factor
            x = jnp.where(lane >= 104, x, source[i + shift, :, cut(tiles)])
            writes.append((target, (i + shift, whole, cut(t)), x))
        return writes

    in_chunks_of(count, insert, 6)
    wrap(vel_u.at[0], count, cut(tiles))
    wrap(vel_v.at[0], count, cut(tiles))
    extras = {id(third): third_x, id(force): force_x, id(push_x): push_x_x, id(push_y): push_y_x}

    def constant(load, ref, j, t):
        name = id(ref)
        return load(ref, name, j, cut(t)) if t < tiles else load(extras[name], (name, 1), j, cut(0))

    def velocity(load, step, j, t):
        own = step == 0 and t < tiles
        u, v = (base_u, base_v) if own else (vel_u.at[step % 2], vel_v.at[step % 2])
        tag = -1 if own else step % 2
        return load(u, (tag, 0), j, cut(t)), load(v, (tag, 1), j, cut(t))

    def strain_stress(step):
        new_set, old_set = (step + 1) % 2, step % 2

        def body(i, j, load):
            writes = []
            for t in range(wide):
                u, v = velocity(load, step, j + 1, t)
                u_above, v_above = velocity(load, step, j + 2, t)
                u_below, v_below = velocity(load, step, j, t)
                dudx, dvdx = turn(u, -1) - turn(u, 1), turn(v, -1) - turn(v, 1)
                dudy, dvdy = u_above - u_below, v_above - v_below
                div, ten, shr = dudx + dvdy, dudx - dvdy, dudy + dvdx
                square = div * div + 0.25 * (ten * ten + shr * shr) + 1.0
                base = constant(load, force, j, t)
                zeta = base * lax.rsqrt(square)
                quarter = 0.25 * zeta
                even = zeta * div - base
                odd = quarter * ten
                new = [even + odd, even - odd, quarter * shr]
                for n, ref in enumerate((str_a, str_b, str_c)):
                    if step:
                        old = load(ref.at[old_set], (n, 2), j + 1, cut(t))
                        new[n] = new[n] + constant(load, third, j, t) * old
                    writes.append((ref, (new_set, i + 1, whole, cut(t)), new[n]))
            return writes

        in_chunks_of(count, body, 1)
        for ref in (str_b, str_c):
            wrap(ref.at[new_set], count)

    def momentum(step):
        new_set = (step + 1) % 2

        def body(i, j, load):
            ar, br = load(turn_a, "ar", j), load(turn_b, "br", j)
            writes = []
            for t in range(wide):
                c = cut(t)

                def now(n, row):
                    return load((str_a, str_b, str_c)[n].at[new_set], (n, 3), row, c)

                a, s = now(0, j + 1), now(2, j + 1)
                fx = (turn(a, -1) - turn(a, 1)) + (now(2, j + 2) - now(2, j))
                fy = (turn(s, -1) - turn(s, 1)) + (now(1, j + 2) - now(1, j))
                u, v = velocity(load, step, j + 1, t)
                ru = (u + constant(load, push_x, j, t)) + fx
                rv = (v + constant(load, push_y, j, t)) + fy
                keep = constant(load, third, j, t)
                writes.append((vel_u, (new_set, i + 1, whole, c), (ar * ru + br * rv) * keep))
                writes.append((vel_v, (new_set, i + 1, whole, c), (ar * rv - br * ru) * keep))
            return writes

        in_chunks_of(count, body, 1)
        wrap(vel_u.at[new_set], count)
        wrap(vel_v.at[new_set], count)

    for step in range(SUBCYCLES):
        strain_stress(step)
        momentum(step)

    def gather(i, j, load):
        writes = []
        for n, ref in enumerate((vel_u.at[SUBCYCLES % 2], vel_v.at[SUBCYCLES % 2])):
            borders = ref[i + 1, :, cut(tiles)]
            middle, outer = turn(borders, -48), turn(borders, 24)
            low, high = ref[i + 1, :, cut(0)], ref[i + 1, :, cut(tiles - 1)]
            low = jnp.where(lane < HALO, borders, jnp.where(lane >= LANES - HALO, middle, low))
            high = jnp.where(lane < HALO, middle, jnp.where(lane >= LANES - HALO, outer, high))
            put = pl.ds(i, SUBLANES, stride=count)
            writes.append((done, (n, 0, put, whole), low))
            writes.append((done, (n, tiles - 1, put, whole), high))
        return writes

    in_chunks_of(count, gather, 8)
    finals = []
    for n, out in enumerate((u_out, v_out)):
        for t in range(tiles):
            finals.append(
                pltpu.make_async_copy(
                    done.at[n, t, own, :], out.at[:, pl.ds(LANES * t, LANES)], vel_sem.at[n, t]
                )
            )
            finals[-1].start()

    def warm(n, carry):
        writes = []
        for j in range(size):
            start = pl.multiple_of((n * size + j) * SUBLANES, SUBLANES)
            put, at = pl.ds(start, SUBLANES), pl.ds(start + HALO, SUBLANES)
            sst, sss = fixed(0, put), fixed(levels, put)
            for t in range(tiles):
                slip_u = done[0, t, at, :] - speeds_in[0, t, put, :]
                slip_v = done[1, t, at, :] - speeds_in[levels, t, put, :]
                heat = HEAT_RATE * covered_in[3, t, at, :] * (1.0 + (slip_u * slip_u + slip_v * slip_v))
                heat = heat * (sst[t] + FREEZE_SLOPE * sss[t])
                writes.append((0, t, put, sst[t] - heat))
                writes.append((levels, t, put, sss[t] - SALT_RATE * heat))
        for f, t, put, value in writes:
            moved[f, t, put, :] = value
        return carry

    lax.fori_loop(0, rows // SUBLANES // size, warm, 0)
    for f in (0, levels):
        copies = stores(f)
        for copy in copies:
            copy.start()
        finals += copies
    for copy in pending + finals:
        copy.wait()


def ice_and_edges(operands, levels, rows, cols):
    tiles = cols // LANES
    count = sublane_rows(rows)
    deep = jax.ShapeDtypeStruct((levels, rows, cols), F32)
    flat = jax.ShapeDtypeStruct((rows, cols), F32)
    looped = pltpu.VMEM((2, count + 2, SUBLANES, LANES * (tiles + 1)), F32)
    narrow = pltpu.VMEM((count, SUBLANES, LANES), F32)
    return pl.pallas_call(
        lambda *refs: ice_kernel(levels, rows, *refs),
        in_specs=[VMEM_SPEC] * len(operands),
        out_specs=[ANY_SPEC] * 4,
        out_shape=[deep, deep, flat, flat],
        scratch_shapes=[
            pltpu.VMEM((2 * levels, tiles, rows, LANES), F32),
            pltpu.VMEM((2, tiles, count * SUBLANES, LANES), F32),
            looped, looped, looped, looped, looped,
            narrow, narrow, narrow, narrow, pltpu.VMEM((rows, LANES), F32),
            pltpu.SemaphoreType.DMA((2 * levels, tiles)),
            pltpu.SemaphoreType.DMA((2, tiles)),
        ],
        name="ice",
        compiler_params=pltpu.CompilerParams(vmem_limit_bytes=20 << 20),
        cost_estimate=pl.CostEstimate(flops=60000000, bytes_accessed=16 << 20, transcendentals=0),
    )(*[in_vmem(a) for a in operands])


def per_device(*arrays):
    levels, rows, cols = arrays[0].shape
    lon_count, lat_count = lax.axis_size("lon"), lax.axis_size("lat")
    assert cols == 2 * LANES and rows % (2 * HALO) == 0 and lat_count % 2 == 0
    height = -(-(HALO * ICE + 3 * levels) // SUBLANES) * SUBLANES

    def place(lat, lon):
        return lon * lat_count + lat

    first_pairs, second_pairs = [], []
    for lon in range(lon_count):
        for lat in range(lat_count):
            first_pairs.append((place(lat, lon), place(lat ^ 1, lon)))
            if lat == lat_count - 1:
                second_pairs.append((place(lat, lon), place(lat, lon_count - 1 - lon)))
            elif lat:
                second_pairs.append((place(lat, lon), place(((lat + 1) ^ 1) - 1, lon)))
    first, second = pack_rows(arrays, levels, rows, cols, height)
    first = lax.ppermute(first, ("lon", "lat"), first_pairs)
    second = lax.ppermute(second, ("lon", "lat"), second_pairs)
    tracers, speeds, sea, fields, east_msg, west_msg = load_and_pack_columns(
        arrays, levels, rows, cols
    )
    halo, fields, east_msg, west_msg = merge_halo(
        first, second, fields, east_msg, west_msg, levels, rows
    )
    eastward = [(i, (i + 1) % lon_count) for i in range(lon_count)]
    from_west = lax.ppermute(east_msg, "lon", eastward)
    from_east = lax.ppermute(west_msg, "lon", [(b, a) for a, b in eastward])
    moved, *state = advect(tracers, speeds, sea, halo, fields, levels, rows * lat_count)
    return ice_and_edges(
        [fields, moved, speeds, east_msg, west_msg, from_west, from_east, *state], levels, rows, cols
    )


def solution(mesh):
    deep, flat = P(None, "lat", "lon"), P("lat", "lon")
    return jax.shard_map(
        per_device,
        mesh=mesh,
        in_specs=(deep,) * 4 + (flat,) * 7,
        out_specs=(deep, deep, flat, flat),
        check_vma=False,
    )
```

```python
import jax
import jax.numpy as jnp
from jax import lax
from jax.experimental import pallas as pl
from jax.experimental.pallas import tpu as pltpu
from jax.sharding import PartitionSpec as P

SUBCYCLES = 4
HEAT_RATE = 0.1
SALT_RATE = 0.5
FREEZE_SLOPE = 0.054
DIAGONAL = 1.5
HALO = 2 * SUBCYCLES
LANES = 128
SUBLANES = 8
ICE = 6
FOLD_SIGN = (-1.0, -1.0, 1.0, 1.0, -1.0, -1.0)
TRACER_LANE = 64
F32 = jnp.float32


def lane_ids():
    return lax.broadcasted_iota(jnp.int32, (SUBLANES, LANES), 1)


def sublane_ids():
    return lax.broadcasted_iota(jnp.int32, (SUBLANES, LANES), 0)


def turn(x, shift, axis=1):
    shift = shift % x.shape[axis]
    return pltpu.roll(x, shift, axis) if shift else x


def cut(t):
    return slice(LANES * t, LANES * (t + 1))


def ice_fields(land, ice, u, v, pressure, wind_x, wind_y, ocean_u, ocean_v):
    covered = land.astype(F32) * ice.astype(F32)
    return (u * covered, v * covered, pressure, covered, wind_x + ocean_u, wind_y + ocean_v)


def east_columns(fields, lane):
    packed = jnp.zeros((SUBLANES, LANES), F32)
    for f, tile in enumerate(fields):
        start = HALO * f + 2 * HALO
        moved = turn(tile, start - (LANES - HALO))
        packed = jnp.where((lane >= start) & (lane < start + HALO), moved, packed)
    return packed


def west_columns(fields, lane):
    packed = jnp.zeros((SUBLANES, LANES), F32)
    for f, tile in enumerate(fields):
        start = HALO * f
        packed = jnp.where((lane >= start) & (lane < start + HALO), turn(tile, start), packed)
    return packed


def sublane_rows(rows):
    return (rows + 2 * HALO) // SUBLANES | 1


def in_chunks_of(count, body, group):
    size = max(c for c in range(1, 21) if count % c == 0)

    def step(n, carry):
        seen = {}

        def load(ref, name, j, *where):
            key = (name, j, *[str(w) for w in where])
            if key not in seen:
                seen[key] = ref[(n * size + j, slice(None), *where)]
            return seen[key]

        for start in range(0, size, group):
            writes = []

            for j in range(start, min(start + group, size)):
                writes += body(n * size + j, j, load)
            for ref, where, value in writes:
                ref[where] = value
        return carry

    lax.fori_loop(0, count // size, step, 0)


def rows_kernel(levels, *refs):
    tops, bottoms = refs[0:12], refs[12:24]
    first_ref, second_ref = refs[24:26]
    even = lax.rem(lax.axis_index("lat"), 2) == 0

    def message(group, row, northward):
        land, ice, u, v, pressure, wind_x, wind_y, east, north, temp, salt = (
            r for r in group[:11]
        )
        fields = ice_fields(
            land[...], ice[...], u[...], v[...], pressure[...], wind_x[...], wind_y[...],
            east[0], north[0],
        )
        sea = land[row : row + 1, :].astype(F32)
        parts = list(fields) + [temp[:, row, :], salt[:, row, :]]
        if northward:
            parts.append(north[:, row, :] * sea)
        else:
            parts.append(jnp.broadcast_to(sea, (levels, sea.shape[1])))
        return parts

    top = message(tops, SUBLANES - 1, True)
    bottom = message(bottoms, 0, False)
    at = 0
    for t, b in zip(top, bottom):
        size = t.shape[0]
        first_ref[at : at + size, :] = jnp.where(even, t, b)
        second_ref[at : at + size, :] = jnp.where(even, b, t)
        at += size
    pad = first_ref.shape[0] - at
    if pad:
        first_ref[at:, :] = jnp.zeros((pad, first_ref.shape[1]), F32)
        second_ref[at:, :] = jnp.zeros((pad, second_ref.shape[1]), F32)


def pack_rows(arrays, levels, rows, cols, height):
    temp, salt, east, north, land, ice, u, v, pressure, wind_x, wind_y = arrays
    operands = [land, ice, u, v, pressure, wind_x, wind_y, east, north, temp, salt, land]
    last = rows // SUBLANES - 1

    def spec(array, block, count):
        if array.ndim == 2:
            return pl.BlockSpec((SUBLANES, cols), lambda _: (block, 0))
        return pl.BlockSpec((count, SUBLANES, cols), lambda _: (0, block, 0))

    counts = [1] * 7 + [1, levels, levels, levels, 1]
    specs = [spec(a, last, c) for a, c in zip(operands, counts)]
    specs += [spec(a, 0, c) for a, c in zip(operands, counts)]
    out = jax.ShapeDtypeStruct((height, cols), F32)
    return pl.pallas_call(
        lambda *refs: rows_kernel(levels, *refs),
        grid=(1,),
        in_specs=specs,
        out_specs=[pl.BlockSpec((height, cols), lambda _: (0, 0))] * 2,
        out_shape=[out, out],
        name="edge_rows",
        compiler_params=pltpu.CompilerParams(vmem_limit_bytes=8 << 20),
        cost_estimate=pl.CostEstimate(flops=100000, bytes_accessed=1 << 20, transcendentals=0),
    )(*[in_hbm(a) for a in operands + operands])


def columns_kernel(levels, land, ice, u, v, pressure, wind_x, wind_y, east, north, temp, salt,
                   tracer_out, speed_out, sea_out, field_out, east_out, west_out, sem):
    lane = lane_ids()
    rows = sea_out.shape[1]
    tiles = sea_out.shape[0]
    tracers = 2 * levels
    first_lane = TRACER_LANE
    mask_lane = TRACER_LANE + 2 * tracers

    copies = []
    for n, ref in enumerate((temp, salt, east, north)):
        out = tracer_out if n < 2 else speed_out
        for t in range(tiles):
            copies.append(
                pltpu.make_async_copy(
                    ref.at[..., pl.ds(LANES * t, LANES)],
                    out.at[pl.ds(levels * (n % 2), levels), t],
                    sem.at[n, t],
                )
            )
    for copy in copies:
        copy.start()

    def each_row_tile(body, size):
        size = next(c for c in range(size, 0, -1) if rows // SUBLANES % c == 0)

        def step(n, carry):
            writes = []
            for j in range(size):
                writes += body(pl.multiple_of((n * size + j) * SUBLANES, SUBLANES))
            for ref, where, value in writes:
                ref[where] = value
            return carry

        lax.fori_loop(0, rows // SUBLANES // size, step, 0)

    whole = slice(None)

    def ice_part(start):
        at, put = pl.ds(start, SUBLANES), pl.ds(start + HALO, SUBLANES)
        writes, fields = [], []
        for t in range(tiles):
            c = cut(t)
            fields.append(
                ice_fields(
                    *[r[at, c] for r in (land, ice, u, v, pressure, wind_x, wind_y)],
                    east[0, at, c], north[0, at, c],
                )
            )
            writes.append((sea_out, (t, at, whole), land[at, c].astype(F32)))
            for f in range(ICE):
                writes.append((field_out, (f, t, put, whole), fields[t][f]))
        writes.append((east_out, (put, whole), east_columns(fields[-1], lane)))
        writes.append((west_out, (put, whole), west_columns(fields[0], lane)))
        return writes

    each_row_tile(ice_part, 4)

    def tracer_part(start):
        at, put = pl.ds(start, SUBLANES), pl.ds(start + HALO, SUBLANES)
        eastward, westward = east_out[put, :], west_out[put, :]
        for f in range(tracers):
            ref, l, to = (temp, salt)[f // levels], f % levels, first_lane + 2 * f
            eastward = jnp.where(
                lane == to, turn(ref[l, at, cut(tiles - 1)], to - (LANES - 1)), eastward
            )
            westward = jnp.where(lane == to, turn(ref[l, at, cut(0)], to), westward)
        return [(east_out, (put, whole), eastward), (west_out, (put, whole), westward)]

    each_row_tile(tracer_part, 8)

    def speed_part(start):
        at, put = pl.ds(start, SUBLANES), pl.ds(start + HALO, SUBLANES)
        masked = (lane >= mask_lane) & (lane < mask_lane + 2 * tracers)
        speeds = jnp.zeros((SUBLANES, LANES), F32)
        for f in range(levels):
            to = mask_lane + 2 * f
            speeds = jnp.where(
                lane == to, turn(east[f, at, cut(tiles - 1)], to - (LANES - 1)), speeds
            )
        speeds = speeds + turn(speeds, 2 * levels)
        last = land[at, LANES * tiles - 1 : LANES * tiles].astype(F32)
        first = jnp.broadcast_to(land[at, 0:1].astype(F32), (SUBLANES, LANES))
        eastward = jnp.where(masked, speeds * last, east_out[put, :])
        westward = jnp.where(masked, first, west_out[put, :])
        return [(east_out, (put, whole), eastward), (west_out, (put, whole), westward)]

    each_row_tile(speed_part, 8)
    end = HALO + rows
    blank = jnp.zeros((field_out.shape[2] - end, LANES), F32)
    for t in range(tiles):
        for f in range(ICE):
            field_out[f, t, end:, :] = blank
    for ref in (east_out, west_out):
        ref[end:, :] = blank
    for copy in copies:
        copy.wait()


def in_vmem(x):
    return pltpu.with_memory_space_constraint(x, pltpu.VMEM)


def in_hbm(x):
    return pltpu.with_memory_space_constraint(x, pltpu.HBM)


def resident(*shape):
    return pltpu.VMEM(shape, F32)


VMEM_SPEC = pl.BlockSpec(memory_space=pltpu.VMEM)
ANY_SPEC = pl.BlockSpec(memory_space=pl.ANY)


def load_and_pack_columns(arrays, levels, rows, cols):
    temp, salt, east, north, land, ice, u, v, pressure, wind_x, wind_y = arrays
    tiles = cols // LANES
    message = resident(sublane_rows(rows) * SUBLANES, LANES)
    deep = resident(2 * levels, tiles, rows, LANES)
    return pl.pallas_call(
        lambda *refs: columns_kernel(levels, *refs),
        in_specs=[VMEM_SPEC] * 11,
        out_specs=[VMEM_SPEC] * 6,
        out_shape=[
            deep, deep, resident(tiles, rows, LANES),
            resident(ICE, tiles, sublane_rows(rows) * SUBLANES, LANES), message, message,
        ],
        scratch_shapes=[pltpu.SemaphoreType.DMA((4, tiles))],
        name="edge_columns",
        compiler_params=pltpu.CompilerParams(vmem_limit_bytes=4 << 20),
        cost_estimate=pl.CostEstimate(flops=5000000, bytes_accessed=12 << 20, transcendentals=0),
    )(*[in_vmem(a) for a in (land, ice, u, v, pressure, wind_x, wind_y, east, north, temp, salt)])


def halo_kernel(levels, rows, first, second, field_in, east_in, west_in,
                halo_ref, field_out, east_out, west_out):
    lat = lax.axis_index("lat")
    even = lax.rem(lat, 2) == 0
    top = lat == lax.axis_size("lat") - 1
    lane, sublane = lane_ids(), sublane_ids()
    tiles = field_out.shape[1]
    south_fields, north_fields = [], []
    for f in range(ICE):
        at = slice(HALO * f, HALO * (f + 1))
        north_row, south_row = [], []
        for t in range(tiles):
            cols = slice(LANES * t, LANES * (t + 1))
            mirror = slice(LANES * (tiles - 1 - t), LANES * (tiles - t))
            south = jnp.where(even, second[at, cols], first[at, cols])
            plain = jnp.where(even, first[at, cols], second[at, cols])
            turned = jnp.take_along_axis(second[at, mirror], LANES - 1 - lane, axis=1)
            turned = jnp.take_along_axis(turned, SUBLANES - 1 - sublane, axis=0)
            north = jnp.where(top, turned * FOLD_SIGN[f], plain)
            field_out[f, t, 0:HALO, :] = south
            field_out[f, t, rows + HALO : rows + 2 * HALO, :] = north
            south_row.append(south)
            north_row.append(north)
        south_fields.append(south_row)
        north_fields.append(north_row)
    rest = slice(HALO * ICE, first.shape[0])
    halo_ref[0] = jnp.where(even, second[rest, :], first[rest, :])
    halo_ref[1] = jnp.where(top, 0.0, jnp.where(even, first[rest, :], second[rest, :]))
    for at, fields in ((0, south_fields), (rows + HALO, north_fields)):
        east_out[at : at + HALO, :] = east_columns([f[-1] for f in fields], lane)
        west_out[at : at + HALO, :] = west_columns([f[0] for f in fields], lane)


def merge_halo(first, second, fields, east_msg, west_msg, levels, rows):
    height, cols = first.shape
    return pl.pallas_call(
        lambda *refs: halo_kernel(levels, rows, *refs),
        in_specs=[VMEM_SPEC] * 5,
        out_specs=[VMEM_SPEC] * 4,
        out_shape=[
            resident(2, height - HALO * ICE, cols), resident(*fields.shape),
            resident(*east_msg.shape), resident(*west_msg.shape),
        ],
        input_output_aliases={2: 1, 3: 2, 4: 3},
        name="halo_rows",
        compiler_params=pltpu.CompilerParams(vmem_limit_bytes=8 << 20),
        cost_estimate=pl.CostEstimate(flops=100000, bytes_accessed=1 << 19, transcendentals=0),
    )(first, second, in_vmem(fields), in_vmem(east_msg), in_vmem(west_msg))


def advect_kernel(levels, row_total, tracer_ref, speed_ref, sea, halo, field_ref,
                  out, base_u, base_v, third, force, push_x, push_y, turn_a, turn_b,
                  mask_e, mask_n):
    tiles, rows = sea.shape[:2]
    count = rows // SUBLANES
    group = next(c for c in (12, 8, 4, 2) if count % c == 0)
    lane, sublane = lane_ids(), sublane_ids()
    extra_row = 2 * levels
    whole = slice(None)

    def rows_at(k, offset=0):
        start = pl.multiple_of(k * SUBLANES, SUBLANES)
        return pl.ds(start + offset if offset else start, SUBLANES)

    def row(side, index, t):
        cols = slice(LANES * t, LANES * (t + 1))
        return jnp.broadcast_to(halo[side, index : index + 1, cols], (SUBLANES, LANES))

    def from_next(values):
        turned = [turn(v, -1) for v in values]
        return [
            jnp.where(lane == LANES - 1, turned[t + 1], turned[t]) if t + 1 < tiles else turned[t]
            for t in range(tiles)
        ]

    def from_last(values):
        turned = [turn(v, 1) for v in values]
        return [jnp.where(lane == 0, turned[t - 1], turned[t]) for t in range(tiles)]

    def in_groups(body, carry):
        def some(start, carry, last):
            writes = []
            for j in range(group):
                more, carry = body(start + j, last and j == group - 1, carry)
                writes += more
            for ref, where, value in writes:
                ref[where] = value
            return carry

        groups = count // group
        carry = lax.fori_loop(0, groups - 1, lambda n, c: some(n * group, c, False), carry)
        return some((groups - 1) * group, carry, True)

    def row_above(load, k, last, past):
        if not last:
            return load(rows_at(k, 1))
        return jnp.where(sublane == SUBLANES - 1, past, turn(load(rows_at(k)), -1, 0))

    def masks(k, last, carry):
        here = [sea[t, rows_at(k), :] for t in range(tiles)]
        beside = from_next(here)
        writes = []
        for t in range(tiles):
            above = row_above(lambda at, t=t: sea[t, at, :], k, last, row(1, extra_row, t))
            face = here[t] * beside[t]
            if t == tiles - 1:
                face = jnp.where(lane == LANES - 1, 0.0, face)
            writes.append((mask_e, (t, rows_at(k), whole), face))
            writes.append((mask_n, (t, rows_at(k), whole), here[t] * above))
        return writes, carry

    in_groups(masks, 0)
    for level in range(levels):
        entering = []
        for f in (level, levels + level):
            for t in range(tiles):
                speed = row(0, extra_row + level, t) * sea[t, 0:SUBLANES, :]
                start = tracer_ref[f, t, 0:SUBLANES, :]
                entering.append(speed * jnp.where(speed > 0, row(0, f, t), start))

        def body(k, last, carry, level=level):
            at = rows_at(k)
            fast_e = [speed_ref[level, t, at, :] * mask_e[t, at, :] for t in range(tiles)]
            fast_n = [speed_ref[levels + level, t, at, :] * mask_n[t, at, :] for t in range(tiles)]
            writes, result = [], []
            for f in (level, levels + level):
                here = [tracer_ref[f, t, at, :] for t in range(tiles)]
                beside = from_next(here)
                flux_e = [
                    fast_e[t] * jnp.where(fast_e[t] > 0, here[t], beside[t]) for t in range(tiles)
                ]
                before = from_last(flux_e)
                for t in range(tiles):
                    above = row_above(
                        lambda at, f=f, t=t: tracer_ref[f, t, at, :], k, last, row(1, f, t)
                    )
                    flux_n = fast_n[t] * jnp.where(fast_n[t] > 0, here[t], above)
                    turned = turn(flux_n, 1, 0)
                    below = jnp.where(sublane == 0, carry[len(result)], turned)
                    value = here[t] - ((flux_e[t] - before[t]) + (flux_n - below))
                    writes.append((out, (f, t, at, whole), value))
                    result.append(turned)
            return writes, tuple(result)

        in_groups(body, tuple(entering))
    spread_fields(rows, row_total, field_ref, base_u, base_v, third, force, push_x, push_y,
                  turn_a, turn_b)


def spread(ref, i, count, *lead):
    return ref[(*lead, pl.ds(i, SUBLANES, stride=count), slice(None))]


def wrap(ref, count, lanes=slice(None)):
    ref[0, :, lanes] = turn(ref[count, :, lanes], 1, 0)
    ref[count + 1, :, lanes] = turn(ref[1, :, lanes], -1, 0)


def spread_fields(rows, row_total, field_ref, base_u, base_v, third, force, push_x, push_y,
                  turn_a, turn_b):
    tiles = field_ref.shape[1]
    count = sublane_rows(rows)
    lane, sublane = lane_ids(), sublane_ids()
    lat = lax.axis_index("lat")

    def body(i, _, load):
        per_tile = [[spread(field_ref, i, count, f, t) for f in range(ICE)] for t in range(tiles)]
        extra = []
        for f in range(ICE):
            low, high = per_tile[0][f], per_tile[-1][f]
            middle = turn(jnp.where(lane < LANES // 2, high, low), 48)
            x = jnp.where(lane < 32, low, middle)
            extra.append(jnp.where(lane >= 64, turn(high, -24), x))
        writes = []
        for t, fields in enumerate(per_tile + [extra]):
            u0, v0, strength, covered, drive_x, drive_y = fields
            writes.append((base_u, (i + 1, slice(None), cut(t)), u0))
            writes.append((base_v, (i + 1, slice(None), cut(t)), v0))
            writes.append((third, (i, slice(None), cut(t)), covered * (1.0 / 3.0)))
            writes.append((force, (i, slice(None), cut(t)), strength * covered * (1.0 / 12.0)))
            writes.append((push_x, (i, slice(None), cut(t)), 0.5 * drive_x))
            writes.append((push_y, (i, slice(None), cut(t)), 0.5 * drive_y))
        y = lat * rows - HALO + sublane * count + i
        y = jnp.where(y >= row_total, 2 * row_total - 1 - y, y)
        coriolis = 0.5 * (2 * y + 1 - row_total).astype(F32) / row_total
        turning = 0.5 * coriolis
        scale = 3.0 / (DIAGONAL * DIAGONAL + turning * turning)
        writes.append((turn_a, (i,), DIAGONAL * scale))
        writes.append((turn_b, (i,), turning * scale))
        return writes

    in_chunks_of(count, body, 3)
    wrap(base_u, count)
    wrap(base_v, count)


def advect(tracers, speeds, sea, halo, fields, levels, row_total):
    tiles, rows = sea.shape[:2]
    count = sublane_rows(rows)
    wide = LANES * (tiles + 1)
    looped = resident(count + 2, SUBLANES, wide)
    plain = resident(count, SUBLANES, wide)
    narrow = resident(count, SUBLANES, LANES)
    return pl.pallas_call(
        lambda *refs: advect_kernel(levels, row_total, *refs),
        in_specs=[VMEM_SPEC] * 5,
        out_specs=[VMEM_SPEC] * 9,
        out_shape=[
            resident(*tracers.shape), looped, looped, plain, plain, plain, plain, narrow, narrow,
        ],
        scratch_shapes=[pltpu.VMEM((tiles, rows, LANES), F32)] * 2,
        name="advect",
        compiler_params=pltpu.CompilerParams(vmem_limit_bytes=8 << 20),
        cost_estimate=pl.CostEstimate(flops=30000000, bytes_accessed=16 << 20, transcendentals=0),
    )(*[in_vmem(a) for a in (tracers, speeds, sea, halo, fields)])


def ice_kernel(levels, rows, *refs):
    (covered_in, tracers_in, speeds_in, east_own, west_own, from_west, from_east,
     base_u, base_v, third, force, push_x, push_y, turn_a, turn_b,
     temp_out, salt_out, u_out, v_out,
     moved, done, vel_u, vel_v, str_a, str_b, str_c,
     third_x, force_x, push_x_x, push_y_x, edges,
     out_sem, vel_sem) = refs
    tiles = tracers_in.shape[1]
    count = sublane_rows(rows)
    tracers = 2 * levels
    lane = lane_ids()
    own = pl.ds(HALO, rows)
    wide = tiles + 1
    whole = slice(None)

    def edge_fluxes(k, carry):
        at = pl.ds(pl.multiple_of(k * SUBLANES + HALO, SUBLANES), SUBLANES)
        put = pl.ds(pl.multiple_of(k * SUBLANES, SUBLANES), SUBLANES)
        west, east_side = from_west[at, :], from_east[at, :]
        mine_e, mine_w = east_own[at, :], west_own[at, :]
        speed = turn(west, -2 * tracers)
        inflow = speed * jnp.where(speed > 0, west, mine_w) * turn(mine_w, -2 * tracers)
        speed = turn(mine_e, -2 * tracers)
        outflow = speed * jnp.where(speed > 0, mine_e, east_side) * turn(east_side, -2 * tracers)
        edges[put, :] = jnp.where(lane % 2 == TRACER_LANE % 2, inflow, turn(outflow, -1))
        return carry

    lax.fori_loop(0, rows // SUBLANES, edge_fluxes, 0, unroll=8)

    def fixed(f, put):
        flux = turn(edges[put, :], -(TRACER_LANE + 2 * f))
        low = tracers_in[f, 0, put, :] + jnp.where(lane == 0, flux, 0.0)
        return low, tracers_in[f, tiles - 1, put, :] - jnp.where(lane == LANES - 1, flux, 0.0)

    def insert(i, j, load):
        west, east_side = spread(from_west, i, count), spread(from_east, i, count)
        writes = []
        targets = (
            (base_u, vel_u, 1, tiles, 1.0), (base_v, vel_v, 1, tiles, 1.0),
            (force, force_x, 0, 0, 1.0), (third, third_x, 0, 0, 1.0 / 3.0),
            (push_x, push_x_x, 0, 0, 0.5), (push_y, push_y_x, 0, 0, 0.5),
        )
        beyond = []
        for f in range(ICE):
            start = HALO * f + 2 * HALO
            x = jnp.where((lane >= start) & (lane < start + HALO), west, east_side)
            beyond.append(turn(x, 104 - HALO * f))
        beyond[2] = beyond[2] * beyond[3] * (1.0 / 12.0)
        for x, (source, target, shift, t, factor) in zip(beyond, targets):
            x = x if factor == 1.0 else x * factor
            x = jnp.where(lane >= 104, x, source[i + shift, :, cut(tiles)])
            writes.append((target, (i + shift, whole, cut(t)), x))
        own_lanes = slice(0, LANES * tiles)
        for source, target in ((base_u, vel_u), (base_v, vel_v)):
            writes.append((target, (i + 1, whole, own_lanes), source[i + 1, :, own_lanes]))
        for ref in (str_a, str_b, str_c):
            writes.append((ref, (i + 1,), jnp.zeros(ref.shape[1:], F32)))
        return writes

    in_chunks_of(count, insert, 6)
    wrap(vel_u, count)
    wrap(vel_v, count)

    def constant(ref, extra, i, t):
        return ref[i, :, cut(t)] if t < tiles else extra[i]

    def load_once(ref, name, seen, j, t):
        if (name, j, t) not in seen:
            seen[name, j, t] = ref[(j, whole) if t is None else (j, whole, cut(t))]
        return seen[name, j, t]

    share = rows // SUBLANES // SUBCYCLES
    items = [(k, f) for k in range(share) for f in range(tracers)]

    def fix(step, i):
        for k, f in items[len(items) * i // count : len(items) * (i + 1) // count]:
            put = pl.ds(pl.multiple_of((step * share + k) * SUBLANES, SUBLANES), SUBLANES)
            low, high = fixed(f, put)
            moved[f, 0, put, :] = low
            moved[f, tiles - 1, put, :] = high

    def fixed_rows(step):
        part = pl.ds(pl.multiple_of(step * share * SUBLANES, SUBLANES), share * SUBLANES)
        return [
            pltpu.make_async_copy(
                moved.at[pl.ds(levels * n + 1, levels - 1), t, part, :],
                out.at[pl.ds(1, levels - 1), part, pl.ds(LANES * t, LANES)],
                out_sem.at[step, n, t],
            )
            for n, out in enumerate((temp_out, salt_out))
            for t in range(tiles)
        ]

    def strain_stress(step):
        seen = {}
        for i in range(count):
            for t in range(wide):
                u, v = (load_once(r, n, seen, i + 1, t) for n, r in enumerate((vel_u, vel_v)))
                dudx, dvdx = turn(u, -1) - turn(u, 1), turn(v, -1) - turn(v, 1)
                dudy, dvdy = (
                    load_once(r, n, seen, i + 2, t) - load_once(r, n, seen, i, t)
                    for n, r in enumerate((vel_u, vel_v))
                )
                div, ten, shr = dudx + dvdy, dudx - dvdy, dudy + dvdx
                square = div * div + 0.25 * (ten * ten + shr * shr) + 1.0
                base = constant(force, force_x, i, t)
                zeta = base * lax.rsqrt(square)
                quarter = 0.25 * zeta
                even = zeta * div - base
                odd = quarter * ten
                keep = constant(third, third_x, i, t)
                for ref, new in (
                    (str_a, even + odd), (str_b, even - odd), (str_c, quarter * shr)
                ):
                    ref[i + 1, :, cut(t)] = new + keep * ref[i + 1, :, cut(t)]
            fix(step, i)
        wrap(str_b, count)
        wrap(str_c, count)

    def momentum():
        seen = {}
        for i in range(count):
            ar, br = turn_a[i], turn_b[i]
            for t in range(wide):
                a = str_a[i + 1, :, cut(t)]
                s = load_once(str_c, 2, seen, i + 1, t)
                fx = (turn(a, -1) - turn(a, 1)) + (
                    load_once(str_c, 2, seen, i + 2, t) - load_once(str_c, 2, seen, i, t)
                )
                fy = (turn(s, -1) - turn(s, 1)) + (
                    load_once(str_b, 1, seen, i + 2, t) - load_once(str_b, 1, seen, i, t)
                )
                ru = (vel_u[i + 1, :, cut(t)] + constant(push_x, push_x_x, i, t)) + fx
                rv = (vel_v[i + 1, :, cut(t)] + constant(push_y, push_y_x, i, t)) + fy
                keep = constant(third, third_x, i, t)
                vel_u[i + 1, :, cut(t)] = (ar * ru + br * rv) * keep
                vel_v[i + 1, :, cut(t)] = (ar * rv - br * ru) * keep
        wrap(vel_u, count)
        wrap(vel_v, count)

    def subcycle(step, carry):
        strain_stress(step)
        for copy in fixed_rows(step):
            copy.start()
        momentum()
        return carry

    lax.fori_loop(0, SUBCYCLES, subcycle, 0)

    def gather(i, j, load):
        writes = []
        for n, ref in enumerate((vel_u, vel_v)):
            borders = ref[i + 1, :, cut(tiles)]
            middle, outer = turn(borders, -48), turn(borders, 24)
            low, high = ref[i + 1, :, cut(0)], ref[i + 1, :, cut(tiles - 1)]
            low = jnp.where(lane < HALO, borders, jnp.where(lane >= LANES - HALO, middle, low))
            high = jnp.where(lane < HALO, middle, jnp.where(lane >= LANES - HALO, outer, high))
            put = pl.ds(i, SUBLANES, stride=count)
            writes.append((done, (n, 0, put, whole), low))
            writes.append((done, (n, tiles - 1, put, whole), high))
        return writes

    in_chunks_of(count, gather, 8)
    finals = []
    for n, out in enumerate((u_out, v_out)):
        for t in range(tiles):
            finals.append(
                pltpu.make_async_copy(
                    done.at[n, t, own, :], out.at[:, pl.ds(LANES * t, LANES)], vel_sem.at[n, t]
                )
            )
            finals[-1].start()

    size = next(c for c in (16, 8, 4, 2) if rows // SUBLANES % c == 0)

    def warm(n, carry):
        writes = []
        for j in range(size):
            start = pl.multiple_of((n * size + j) * SUBLANES, SUBLANES)
            put, at = pl.ds(start, SUBLANES), pl.ds(start + HALO, SUBLANES)
            for t in range(tiles):
                sst, sss = moved[0, t, put, :], moved[levels, t, put, :]
                slip_u = done[0, t, at, :] - speeds_in[0, t, put, :]
                slip_v = done[1, t, at, :] - speeds_in[levels, t, put, :]
                heat = HEAT_RATE * covered_in[3, t, at, :] * (1.0 + (slip_u * slip_u + slip_v * slip_v))
                heat = heat * (sst + FREEZE_SLOPE * sss)
                writes.append((0, t, put, sst - heat))
                writes.append((levels, t, put, sss - SALT_RATE * heat))
        for f, t, put, value in writes:
            moved[f, t, put, :] = value
        return carry

    lax.fori_loop(0, rows // SUBLANES // size, warm, 0)
    for n, out in enumerate((temp_out, salt_out)):
        for t in range(tiles):
            finals.append(
                pltpu.make_async_copy(
                    moved.at[levels * n, t],
                    out.at[0, :, pl.ds(LANES * t, LANES)],
                    out_sem.at[SUBCYCLES, n, t],
                )
            )
            finals[-1].start()
    for step in range(SUBCYCLES):
        finals += fixed_rows(step)
    for copy in finals:
        copy.wait()


def ice_and_edges(operands, levels, rows, cols):
    tiles = cols // LANES
    count = sublane_rows(rows)
    deep = jax.ShapeDtypeStruct((levels, rows, cols), F32)
    flat = jax.ShapeDtypeStruct((rows, cols), F32)
    looped = pltpu.VMEM((count + 2, SUBLANES, LANES * (tiles + 1)), F32)
    narrow = pltpu.VMEM((count, SUBLANES, LANES), F32)
    return pl.pallas_call(
        lambda *refs: ice_kernel(levels, rows, *refs),
        in_specs=[VMEM_SPEC] * len(operands),
        out_specs=[ANY_SPEC] * 4,
        out_shape=[deep, deep, flat, flat],
        scratch_shapes=[
            pltpu.VMEM((2 * levels, tiles, rows, LANES), F32),
            pltpu.VMEM((2, tiles, count * SUBLANES, LANES), F32),
            looped, looped, looped, looped, looped,
            narrow, narrow, narrow, narrow, pltpu.VMEM((rows, LANES), F32),
            pltpu.SemaphoreType.DMA((SUBCYCLES + 1, 2, tiles)),
            pltpu.SemaphoreType.DMA((2, tiles)),
        ],
        name="ice",
        compiler_params=pltpu.CompilerParams(vmem_limit_bytes=20 << 20),
        cost_estimate=pl.CostEstimate(flops=60000000, bytes_accessed=16 << 20, transcendentals=0),
    )(*[in_vmem(a) for a in operands])


def per_device(*arrays):
    levels, rows, cols = arrays[0].shape
    lon_count, lat_count = lax.axis_size("lon"), lax.axis_size("lat")
    assert cols == 2 * LANES and rows % (SUBLANES * SUBCYCLES) == 0 and lat_count % 2 == 0
    height = -(-(HALO * ICE + 3 * levels) // SUBLANES) * SUBLANES

    def place(lat, lon):
        return lon * lat_count + lat

    first_pairs, second_pairs = [], []
    for lon in range(lon_count):
        for lat in range(lat_count):
            first_pairs.append((place(lat, lon), place(lat ^ 1, lon)))
            if lat == lat_count - 1:
                second_pairs.append((place(lat, lon), place(lat, lon_count - 1 - lon)))
            elif lat:
                second_pairs.append((place(lat, lon), place(((lat + 1) ^ 1) - 1, lon)))
    first, second = pack_rows(arrays, levels, rows, cols, height)
    first = lax.ppermute(first, ("lon", "lat"), first_pairs)
    second = lax.ppermute(second, ("lon", "lat"), second_pairs)
    tracers, speeds, sea, fields, east_msg, west_msg = load_and_pack_columns(
        arrays, levels, rows, cols
    )
    halo, fields, east_msg, west_msg = merge_halo(
        first, second, fields, east_msg, west_msg, levels, rows
    )
    eastward = [(i, (i + 1) % lon_count) for i in range(lon_count)]
    from_west = lax.ppermute(east_msg, "lon", eastward)
    from_east = lax.ppermute(west_msg, "lon", [(b, a) for a, b in eastward])
    moved, *state = advect(tracers, speeds, sea, halo, fields, levels, rows * lat_count)
    return ice_and_edges(
        [fields, moved, speeds, east_msg, west_msg, from_west, from_east, *state], levels, rows, cols
    )


def solution(mesh):
    deep, flat = P(None, "lat", "lon"), P("lat", "lon")
    return jax.shard_map(
        per_device,
        mesh=mesh,
        in_specs=(deep,) * 4 + (flat,) * 7,
        out_specs=(deep, deep, flat, flat),
        check_vma=False,
    )
```

```python
import jax
import jax.numpy as jnp
from jax import lax
from jax.experimental import pallas as pl
from jax.experimental.pallas import tpu as pltpu
from jax.sharding import PartitionSpec as P

SUBCYCLES = 4
HEAT_RATE = 0.1
SALT_RATE = 0.5
FREEZE_SLOPE = 0.054
DIAGONAL = 1.5
HALO = 2 * SUBCYCLES
LANES = 128
SUBLANES = 8
ICE = 6
FOLD_SIGN = (-1.0, -1.0, 1.0, 1.0, -1.0, -1.0)
TRACER_LANE = 64
F32 = jnp.float32


def lane_ids():
    return lax.broadcasted_iota(jnp.int32, (SUBLANES, LANES), 1)


def sublane_ids():
    return lax.broadcasted_iota(jnp.int32, (SUBLANES, LANES), 0)


def turn(x, shift, axis=1):
    shift = shift % x.shape[axis]
    return pltpu.roll(x, shift, axis) if shift else x


def cut(t):
    return slice(LANES * t, LANES * (t + 1))


def ice_fields(land, ice, u, v, pressure, wind_x, wind_y, ocean_u, ocean_v):
    covered = land.astype(F32) * ice.astype(F32)
    return (u * covered, v * covered, pressure, covered, wind_x + ocean_u, wind_y + ocean_v)


def east_columns(fields, lane):
    packed = jnp.zeros((SUBLANES, LANES), F32)
    for f, tile in enumerate(fields):
        start = HALO * f + 2 * HALO
        moved = turn(tile, start - (LANES - HALO))
        packed = jnp.where((lane >= start) & (lane < start + HALO), moved, packed)
    return packed


def west_columns(fields, lane):
    packed = jnp.zeros((SUBLANES, LANES), F32)
    for f, tile in enumerate(fields):
        start = HALO * f
        packed = jnp.where((lane >= start) & (lane < start + HALO), turn(tile, start), packed)
    return packed


def sublane_rows(rows):
    return (rows + 2 * HALO) // SUBLANES | 1


class Trailing:
    def __init__(self, window):
        self.window, self.waiting = window, []

    def add(self, writes):
        self.waiting.append(writes)
        while len(self.waiting) > self.window:
            self.flush(self.waiting.pop(0))

    def finish(self):
        for writes in self.waiting:
            self.flush(writes)

    @staticmethod
    def flush(writes):
        for ref, where, value in writes:
            ref[where] = value


def straight(steps, body, window, size):
    size = max(c for c in range(1, size + 1) if steps % c == 0)

    def run(n, carry):
        pending = Trailing(window)
        for j in range(size):
            pending.add(body(n * size + j))
        pending.finish()
        return carry

    if size == steps:
        run(0, 0)
    else:
        lax.fori_loop(0, steps // size, run, 0)


def tile_rows(k, offset=0):
    start = k * SUBLANES
    if not isinstance(k, int):
        start = pl.multiple_of(start, SUBLANES)
    return pl.ds(start + offset if offset else start, SUBLANES)


def rows_kernel(levels, *refs):
    tops, bottoms = refs[0:12], refs[12:24]
    first_ref, second_ref = refs[24:26]
    even = lax.rem(lax.axis_index("lat"), 2) == 0

    def message(group, row, northward):
        land, ice, u, v, pressure, wind_x, wind_y, east, north, temp, salt = (
            r for r in group[:11]
        )
        fields = ice_fields(
            land[...], ice[...], u[...], v[...], pressure[...], wind_x[...], wind_y[...],
            east[0], north[0],
        )
        sea = land[row : row + 1, :].astype(F32)
        parts = list(fields) + [temp[:, row, :], salt[:, row, :]]
        if northward:
            parts.append(north[:, row, :] * sea)
        else:
            parts.append(jnp.broadcast_to(sea, (levels, sea.shape[1])))
        return parts

    top = message(tops, SUBLANES - 1, True)
    bottom = message(bottoms, 0, False)
    at = 0
    for t, b in zip(top, bottom):
        size = t.shape[0]
        first_ref[at : at + size, :] = jnp.where(even, t, b)
        second_ref[at : at + size, :] = jnp.where(even, b, t)
        at += size
    pad = first_ref.shape[0] - at
    if pad:
        first_ref[at:, :] = jnp.zeros((pad, first_ref.shape[1]), F32)
        second_ref[at:, :] = jnp.zeros((pad, second_ref.shape[1]), F32)


def pack_rows(arrays, levels, rows, cols, height):
    temp, salt, east, north, land, ice, u, v, pressure, wind_x, wind_y = arrays
    operands = [land, ice, u, v, pressure, wind_x, wind_y, east, north, temp, salt, land]
    last = rows // SUBLANES - 1

    def spec(array, block, count):
        if array.ndim == 2:
            return pl.BlockSpec((SUBLANES, cols), lambda _: (block, 0))
        return pl.BlockSpec((count, SUBLANES, cols), lambda _: (0, block, 0))

    counts = [1] * 7 + [1, levels, levels, levels, 1]
    specs = [spec(a, last, c) for a, c in zip(operands, counts)]
    specs += [spec(a, 0, c) for a, c in zip(operands, counts)]
    out = jax.ShapeDtypeStruct((height, cols), F32)
    return pl.pallas_call(
        lambda *refs: rows_kernel(levels, *refs),
        grid=(1,),
        in_specs=specs,
        out_specs=[pl.BlockSpec((height, cols), lambda _: (0, 0))] * 2,
        out_shape=[out, out],
        name="edge_rows",
        compiler_params=pltpu.CompilerParams(vmem_limit_bytes=8 << 20),
        cost_estimate=pl.CostEstimate(flops=100000, bytes_accessed=1 << 20, transcendentals=0),
    )(*[in_hbm(a) for a in operands + operands])


def columns_kernel(levels, land, ice, u, v, pressure, wind_x, wind_y, east, north, temp, salt,
                   tracer_out, speed_out, sea_out, field_out, east_out, west_out, sem):
    lane = lane_ids()
    rows = sea_out.shape[1]
    tiles = sea_out.shape[0]
    tracers = 2 * levels
    first_lane = TRACER_LANE
    mask_lane = TRACER_LANE + 2 * tracers

    copies = []
    for n, ref in enumerate((temp, salt, east, north)):
        out = tracer_out if n < 2 else speed_out
        for t in range(tiles):
            copies.append(
                pltpu.make_async_copy(
                    ref.at[..., pl.ds(LANES * t, LANES)],
                    out.at[pl.ds(levels * (n % 2), levels), t],
                    sem.at[n, t],
                )
            )
    for copy in copies:
        copy.start()

    whole = slice(None)

    def ice_part(k):
        at, put = tile_rows(k), tile_rows(k + 1)
        writes, fields = [], []
        for t in range(tiles):
            c = cut(t)
            fields.append(
                ice_fields(
                    *[r[at, c] for r in (land, ice, u, v, pressure, wind_x, wind_y)],
                    east[0, at, c], north[0, at, c],
                )
            )
            writes.append((sea_out, (t, at, whole), land[at, c].astype(F32)))
            for f in range(ICE):
                writes.append((field_out, (f, t, put, whole), fields[t][f]))
        writes.append((east_out, (put, whole), east_columns(fields[-1], lane)))
        writes.append((west_out, (put, whole), west_columns(fields[0], lane)))
        return writes

    straight(rows // SUBLANES, ice_part, 2, 12)

    def tracer_part(k):
        at, put = tile_rows(k), tile_rows(k + 1)
        eastward, westward = east_out[put, :], west_out[put, :]
        for f in range(tracers):
            ref, l, to = (temp, salt)[f // levels], f % levels, first_lane + 2 * f
            eastward = jnp.where(
                lane == to, turn(ref[l, at, cut(tiles - 1)], to - (LANES - 1)), eastward
            )
            westward = jnp.where(lane == to, turn(ref[l, at, cut(0)], to), westward)
        return [(east_out, (put, whole), eastward), (west_out, (put, whole), westward)]

    straight(rows // SUBLANES, tracer_part, 6, 24)

    def speed_part(k):
        at, put = tile_rows(k), tile_rows(k + 1)
        masked = (lane >= mask_lane) & (lane < mask_lane + 2 * tracers)
        speeds = jnp.zeros((SUBLANES, LANES), F32)
        for f in range(levels):
            to = mask_lane + 2 * f
            speeds = jnp.where(
                lane == to, turn(east[f, at, cut(tiles - 1)], to - (LANES - 1)), speeds
            )
        speeds = speeds + turn(speeds, 2 * levels)
        last = land[at, LANES * tiles - 1 : LANES * tiles].astype(F32)
        first = jnp.broadcast_to(land[at, 0:1].astype(F32), (SUBLANES, LANES))
        eastward = jnp.where(masked, speeds * last, east_out[put, :])
        westward = jnp.where(masked, first, west_out[put, :])
        return [(east_out, (put, whole), eastward), (west_out, (put, whole), westward)]

    straight(rows // SUBLANES, speed_part, 6, 24)
    end = HALO + rows
    blank = jnp.zeros((field_out.shape[2] - end, LANES), F32)
    for t in range(tiles):
        for f in range(ICE):
            field_out[f, t, end:, :] = blank
    for ref in (east_out, west_out):
        ref[end:, :] = blank
    for copy in copies:
        copy.wait()


def in_vmem(x):
    return pltpu.with_memory_space_constraint(x, pltpu.VMEM)


def in_hbm(x):
    return pltpu.with_memory_space_constraint(x, pltpu.HBM)


def resident(*shape):
    return pltpu.VMEM(shape, F32)


VMEM_SPEC = pl.BlockSpec(memory_space=pltpu.VMEM)
ANY_SPEC = pl.BlockSpec(memory_space=pl.ANY)


def load_and_pack_columns(arrays, levels, rows, cols):
    temp, salt, east, north, land, ice, u, v, pressure, wind_x, wind_y = arrays
    tiles = cols // LANES
    message = resident(sublane_rows(rows) * SUBLANES, LANES)
    deep = resident(2 * levels, tiles, rows, LANES)
    return pl.pallas_call(
        lambda *refs: columns_kernel(levels, *refs),
        in_specs=[VMEM_SPEC] * 11,
        out_specs=[VMEM_SPEC] * 6,
        out_shape=[
            deep, deep, resident(tiles, rows, LANES),
            resident(ICE, tiles, sublane_rows(rows) * SUBLANES, LANES), message, message,
        ],
        scratch_shapes=[pltpu.SemaphoreType.DMA((4, tiles))],
        name="edge_columns",
        compiler_params=pltpu.CompilerParams(vmem_limit_bytes=4 << 20),
        cost_estimate=pl.CostEstimate(flops=5000000, bytes_accessed=12 << 20, transcendentals=0),
    )(*[in_vmem(a) for a in (land, ice, u, v, pressure, wind_x, wind_y, east, north, temp, salt)])


def halo_kernel(levels, rows, first, second, field_in, east_in, west_in,
                halo_ref, field_out, east_out, west_out):
    lat = lax.axis_index("lat")
    even = lax.rem(lat, 2) == 0
    top = lat == lax.axis_size("lat") - 1
    lane, sublane = lane_ids(), sublane_ids()
    tiles = field_out.shape[1]
    south_fields, north_fields = [], []
    for f in range(ICE):
        at = slice(HALO * f, HALO * (f + 1))
        north_row, south_row = [], []
        for t in range(tiles):
            cols = slice(LANES * t, LANES * (t + 1))
            mirror = slice(LANES * (tiles - 1 - t), LANES * (tiles - t))
            south = jnp.where(even, second[at, cols], first[at, cols])
            plain = jnp.where(even, first[at, cols], second[at, cols])
            turned = jnp.take_along_axis(second[at, mirror], LANES - 1 - lane, axis=1)
            turned = jnp.take_along_axis(turned, SUBLANES - 1 - sublane, axis=0)
            north = jnp.where(top, turned * FOLD_SIGN[f], plain)
            field_out[f, t, 0:HALO, :] = south
            field_out[f, t, rows + HALO : rows + 2 * HALO, :] = north
            south_row.append(south)
            north_row.append(north)
        south_fields.append(south_row)
        north_fields.append(north_row)
    rest = slice(HALO * ICE, first.shape[0])
    for t in range(tiles):
        c = cut(t)
        halo_ref[0, t] = jnp.where(even, second[rest, c], first[rest, c])
        halo_ref[1, t] = jnp.where(top, 0.0, jnp.where(even, first[rest, c], second[rest, c]))
    for at, fields in ((0, south_fields), (rows + HALO, north_fields)):
        east_out[at : at + HALO, :] = east_columns([f[-1] for f in fields], lane)
        west_out[at : at + HALO, :] = west_columns([f[0] for f in fields], lane)


def merge_halo(first, second, fields, east_msg, west_msg, levels, rows):
    height, cols = first.shape
    return pl.pallas_call(
        lambda *refs: halo_kernel(levels, rows, *refs),
        in_specs=[VMEM_SPEC] * 5,
        out_specs=[VMEM_SPEC] * 4,
        out_shape=[
            resident(2, cols // LANES, height - HALO * ICE, LANES), resident(*fields.shape),
            resident(*east_msg.shape), resident(*west_msg.shape),
        ],
        input_output_aliases={2: 1, 3: 2, 4: 3},
        name="halo_rows",
        compiler_params=pltpu.CompilerParams(vmem_limit_bytes=8 << 20),
        cost_estimate=pl.CostEstimate(flops=100000, bytes_accessed=1 << 19, transcendentals=0),
    )(first, second, in_vmem(fields), in_vmem(east_msg), in_vmem(west_msg))


def advect_kernel(levels, row_total, tracer_ref, speed_ref, sea, halo, field_ref,
                  out, base_u, base_v, third, force, push_x, push_y, turn_a, turn_b,
                  mask_e, mask_n):
    tiles, rows = sea.shape[:2]
    count = rows // SUBLANES
    lane, sublane = lane_ids(), sublane_ids()
    extra_row = 2 * levels
    whole = slice(None)

    def row(side, index, t):
        return jnp.broadcast_to(halo[side, t, pl.ds(index, 1), :], (SUBLANES, LANES))

    def from_next(values):
        turned = [turn(v, -1) for v in values]
        return [
            jnp.where(lane == LANES - 1, turned[t + 1], turned[t]) if t + 1 < tiles else turned[t]
            for t in range(tiles)
        ]

    def from_last(values):
        turned = [turn(v, 1) for v in values]
        return [jnp.where(lane == 0, turned[t - 1], turned[t]) for t in range(tiles)]

    def row_above(load, k, past):
        if k + 1 < count:
            return load(tile_rows(k, 1))
        return jnp.where(sublane == SUBLANES - 1, past(), turn(load(tile_rows(k)), -1, 0))

    def masks(k):
        here = [sea[t, tile_rows(k), :] for t in range(tiles)]
        beside = from_next(here)
        writes = []
        for t in range(tiles):
            above = row_above(lambda at: sea[t, at, :], k, lambda: row(1, extra_row, t))
            face = here[t] * beside[t]
            if t == tiles - 1:
                face = jnp.where(lane == LANES - 1, 0.0, face)
            writes.append((mask_e, (t, tile_rows(k), whole), face))
            writes.append((mask_n, (t, tile_rows(k), whole), here[t] * above))
        return writes

    straight(count, masks, 4, count)

    def one_level(level, nothing):
        entering = []
        for n in range(2):
            f = levels * n + level
            for t in range(tiles):
                speed = row(0, extra_row + level, t) * sea[t, 0:SUBLANES, :]
                start = tracer_ref[f, t, 0:SUBLANES, :]
                entering.append(speed * jnp.where(speed > 0, row(0, f, t), start))

        def body(k):
            at = tile_rows(k)
            fast_e = [speed_ref[level, t, at, :] * mask_e[t, at, :] for t in range(tiles)]
            fast_n = [speed_ref[levels + level, t, at, :] * mask_n[t, at, :] for t in range(tiles)]
            writes = []
            for n in range(2):
                f = levels * n + level
                here = [tracer_ref[f, t, at, :] for t in range(tiles)]
                beside = from_next(here)
                flux_e = [
                    fast_e[t] * jnp.where(fast_e[t] > 0, here[t], beside[t]) for t in range(tiles)
                ]
                before = from_last(flux_e)
                for t in range(tiles):
                    above = row_above(
                        lambda at: tracer_ref[f, t, at, :], k, lambda: row(1, f, t)
                    )
                    flux_n = fast_n[t] * jnp.where(fast_n[t] > 0, here[t], above)
                    turned = turn(flux_n, 1, 0)
                    below = jnp.where(sublane == 0, entering[n * tiles + t], turned)
                    entering[n * tiles + t] = turned
                    value = here[t] - ((flux_e[t] - before[t]) + (flux_n - below))
                    writes.append((out, (f, t, at, whole), value))
            return writes

        straight(count, body, 6, count)
        return nothing

    lax.fori_loop(0, levels, one_level, 0)
    spread_fields(rows, row_total, field_ref, base_u, base_v, third, force, push_x, push_y,
                  turn_a, turn_b)


def spread(ref, i, count, *lead):
    return ref[(*lead, pl.ds(i, SUBLANES, stride=count), slice(None))]


def wrap(ref, count, lanes=slice(None)):
    ref[0, :, lanes] = turn(ref[count, :, lanes], 1, 0)
    ref[count + 1, :, lanes] = turn(ref[1, :, lanes], -1, 0)


def spread_fields(rows, row_total, field_ref, base_u, base_v, third, force, push_x, push_y,
                  turn_a, turn_b):
    tiles = field_ref.shape[1]
    count = sublane_rows(rows)
    lane, sublane = lane_ids(), sublane_ids()
    lat = lax.axis_index("lat")

    def body(i):
        per_tile = [[spread(field_ref, i, count, f, t) for f in range(ICE)] for t in range(tiles)]
        extra = []
        for f in range(ICE):
            low, high = per_tile[0][f], per_tile[-1][f]
            middle = turn(jnp.where(lane < LANES // 2, high, low), 48)
            x = jnp.where(lane < 32, low, middle)
            extra.append(jnp.where(lane >= 64, turn(high, -24), x))
        writes = []
        for t, fields in enumerate(per_tile + [extra]):
            u0, v0, strength, covered, drive_x, drive_y = fields
            writes.append((base_u, (i + 1, slice(None), cut(t)), u0))
            writes.append((base_v, (i + 1, slice(None), cut(t)), v0))
            writes.append((third, (i, slice(None), cut(t)), covered * (1.0 / 3.0)))
            writes.append((force, (i, slice(None), cut(t)), strength * covered * (1.0 / 12.0)))
            writes.append((push_x, (i, slice(None), cut(t)), 0.5 * drive_x))
            writes.append((push_y, (i, slice(None), cut(t)), 0.5 * drive_y))
        y = lat * rows - HALO + sublane * count + i
        y = jnp.where(y >= row_total, 2 * row_total - 1 - y, y)
        coriolis = 0.5 * (2 * y + 1 - row_total).astype(F32) / row_total
        turning = 0.5 * coriolis
        scale = 3.0 / (DIAGONAL * DIAGONAL + turning * turning)
        writes.append((turn_a, (i,), DIAGONAL * scale))
        writes.append((turn_b, (i,), turning * scale))
        return writes

    straight(count, body, 2, 17)
    wrap(base_u, count)
    wrap(base_v, count)


def advect(tracers, speeds, sea, halo, fields, levels, row_total):
    tiles, rows = sea.shape[:2]
    count = sublane_rows(rows)
    wide = LANES * (tiles + 1)
    looped = resident(count + 2, SUBLANES, wide)
    plain = resident(count, SUBLANES, wide)
    narrow = resident(count, SUBLANES, LANES)
    return pl.pallas_call(
        lambda *refs: advect_kernel(levels, row_total, *refs),
        in_specs=[VMEM_SPEC] * 5,
        out_specs=[VMEM_SPEC] * 9,
        out_shape=[
            resident(*tracers.shape), looped, looped, plain, plain, plain, plain, narrow, narrow,
        ],
        scratch_shapes=[pltpu.VMEM((tiles, rows, LANES), F32)] * 2,
        name="advect",
        compiler_params=pltpu.CompilerParams(vmem_limit_bytes=8 << 20),
        cost_estimate=pl.CostEstimate(flops=30000000, bytes_accessed=16 << 20, transcendentals=0),
    )(*[in_vmem(a) for a in (tracers, speeds, sea, halo, fields)])


def ice_kernel(levels, rows, *refs):
    (covered_in, tracers_in, speeds_in, east_own, west_own, from_west, from_east,
     base_u, base_v, third, force, push_x, push_y, turn_a, turn_b,
     temp_out, salt_out, u_out, v_out,
     moved, done, vel_u, vel_v, str_a, str_b, str_c,
     third_x, force_x, push_x_x, push_y_x, edges,
     out_sem, vel_sem) = refs
    tiles = tracers_in.shape[1]
    count = sublane_rows(rows)
    tracers = 2 * levels
    lane = lane_ids()
    own = pl.ds(HALO, rows)
    wide = tiles + 1
    whole = slice(None)

    def edge_fluxes(k):
        at, put = tile_rows(k + 1), tile_rows(k)
        west, east_side = from_west[at, :], from_east[at, :]
        mine_e, mine_w = east_own[at, :], west_own[at, :]
        speed = turn(west, -2 * tracers)
        inflow = speed * jnp.where(speed > 0, west, mine_w) * turn(mine_w, -2 * tracers)
        speed = turn(mine_e, -2 * tracers)
        outflow = speed * jnp.where(speed > 0, mine_e, east_side) * turn(east_side, -2 * tracers)
        flux = jnp.where(lane % 2 == TRACER_LANE % 2, inflow, turn(outflow, -1))
        return [(edges, (put, whole), flux)]

    straight(rows // SUBLANES, edge_fluxes, 8, 24)

    def fixed(f, put):
        flux = turn(edges[put, :], -(TRACER_LANE + 2 * f))
        low = tracers_in[f, 0, put, :] + jnp.where(lane == 0, flux, 0.0)
        return low, tracers_in[f, tiles - 1, put, :] - jnp.where(lane == LANES - 1, flux, 0.0)

    def insert(i):
        west, east_side = spread(from_west, i, count), spread(from_east, i, count)
        writes = []
        targets = (
            (base_u, vel_u, 1, tiles, 1.0), (base_v, vel_v, 1, tiles, 1.0),
            (force, force_x, 0, 0, 1.0), (third, third_x, 0, 0, 1.0 / 3.0),
            (push_x, push_x_x, 0, 0, 0.5), (push_y, push_y_x, 0, 0, 0.5),
        )
        beyond = []
        for f in range(ICE):
            start = HALO * f + 2 * HALO
            x = jnp.where((lane >= start) & (lane < start + HALO), west, east_side)
            beyond.append(turn(x, 104 - HALO * f))
        beyond[2] = beyond[2] * beyond[3] * (1.0 / 12.0)
        for x, (source, target, shift, t, factor) in zip(beyond, targets):
            x = x if factor == 1.0 else x * factor
            x = jnp.where(lane >= 104, x, source[i + shift, :, cut(tiles)])
            writes.append((target, (i + shift, whole, cut(t)), x))
        own_lanes = slice(0, LANES * tiles)
        for source, target in ((base_u, vel_u), (base_v, vel_v)):
            writes.append((target, (i + 1, whole, own_lanes), source[i + 1, :, own_lanes]))
        for ref in (str_a, str_b, str_c):
            writes.append((ref, (i + 1,), jnp.zeros(ref.shape[1:], F32)))
        return writes

    straight(count, insert, 3, 17)
    wrap(vel_u, count)
    wrap(vel_v, count)

    def constant(ref, extra, i, t):
        return ref[i, :, cut(t)] if t < tiles else extra[i]

    def load_once(ref, name, seen, j, t):
        if (name, j, t) not in seen:
            seen[name, j, t] = ref[(j, whole) if t is None else (j, whole, cut(t))]
        return seen[name, j, t]

    share = rows // SUBLANES // SUBCYCLES
    items = [(k, f) for k in range(share) for f in range(tracers)]

    def fix(step, i):
        for k, f in items[len(items) * i // count : len(items) * (i + 1) // count]:
            put = pl.ds(pl.multiple_of((step * share + k) * SUBLANES, SUBLANES), SUBLANES)
            low, high = fixed(f, put)
            moved[f, 0, put, :] = low
            moved[f, tiles - 1, put, :] = high

    def fixed_rows(step):
        part = pl.ds(pl.multiple_of(step * share * SUBLANES, SUBLANES), share * SUBLANES)
        return [
            pltpu.make_async_copy(
                moved.at[pl.ds(levels * n + 1, levels - 1), t, part, :],
                out.at[pl.ds(1, levels - 1), part, pl.ds(LANES * t, LANES)],
                out_sem.at[step, n, t],
            )
            for n, out in enumerate((temp_out, salt_out))
            for t in range(tiles)
        ]

    def strain_stress(step):
        seen = {}
        for i in range(count):
            for t in range(wide):
                u, v = (load_once(r, n, seen, i + 1, t) for n, r in enumerate((vel_u, vel_v)))
                dudx, dvdx = turn(u, -1) - turn(u, 1), turn(v, -1) - turn(v, 1)
                dudy, dvdy = (
                    load_once(r, n, seen, i + 2, t) - load_once(r, n, seen, i, t)
                    for n, r in enumerate((vel_u, vel_v))
                )
                div, ten, shr = dudx + dvdy, dudx - dvdy, dudy + dvdx
                square = div * div + 0.25 * (ten * ten + shr * shr) + 1.0
                base = constant(force, force_x, i, t)
                zeta = base * lax.rsqrt(square)
                quarter = 0.25 * zeta
                even = zeta * div - base
                odd = quarter * ten
                keep = constant(third, third_x, i, t)
                for ref, new in (
                    (str_a, even + odd), (str_b, even - odd), (str_c, quarter * shr)
                ):
                    ref[i + 1, :, cut(t)] = new + keep * ref[i + 1, :, cut(t)]
            fix(step, i)
        wrap(str_b, count)
        wrap(str_c, count)

    def momentum():
        seen = {}
        for i in range(count):
            ar, br = turn_a[i], turn_b[i]
            for t in range(wide):
                a = str_a[i + 1, :, cut(t)]
                s = load_once(str_c, 2, seen, i + 1, t)
                fx = (turn(a, -1) - turn(a, 1)) + (
                    load_once(str_c, 2, seen, i + 2, t) - load_once(str_c, 2, seen, i, t)
                )
                fy = (turn(s, -1) - turn(s, 1)) + (
                    load_once(str_b, 1, seen, i + 2, t) - load_once(str_b, 1, seen, i, t)
                )
                ru = (vel_u[i + 1, :, cut(t)] + constant(push_x, push_x_x, i, t)) + fx
                rv = (vel_v[i + 1, :, cut(t)] + constant(push_y, push_y_x, i, t)) + fy
                keep = constant(third, third_x, i, t)
                vel_u[i + 1, :, cut(t)] = (ar * ru + br * rv) * keep
                vel_v[i + 1, :, cut(t)] = (ar * rv - br * ru) * keep
        wrap(vel_u, count)
        wrap(vel_v, count)

    def subcycle(step, carry):
        strain_stress(step)
        for copy in fixed_rows(step):
            copy.start()
        momentum()
        return carry

    lax.fori_loop(0, SUBCYCLES, subcycle, 0)

    def gather(i):
        writes = []
        for n, ref in enumerate((vel_u, vel_v)):
            borders = ref[i + 1, :, cut(tiles)]
            middle, outer = turn(borders, -48), turn(borders, 24)
            low, high = ref[i + 1, :, cut(0)], ref[i + 1, :, cut(tiles - 1)]
            low = jnp.where(lane < HALO, borders, jnp.where(lane >= LANES - HALO, middle, low))
            high = jnp.where(lane < HALO, middle, jnp.where(lane >= LANES - HALO, outer, high))
            put = pl.ds(i, SUBLANES, stride=count)
            writes.append((done, (n, 0, put, whole), low))
            writes.append((done, (n, tiles - 1, put, whole), high))
        return writes

    straight(count, gather, 6, 51)
    finals = []
    for n, out in enumerate((u_out, v_out)):
        for t in range(tiles):
            finals.append(
                pltpu.make_async_copy(
                    done.at[n, t, own, :], out.at[:, pl.ds(LANES * t, LANES)], vel_sem.at[n, t]
                )
            )
            finals[-1].start()

    def warm(k):
        put, at = tile_rows(k), tile_rows(k + 1)
        writes = []
        for t in range(tiles):
            sst, sss = moved[0, t, put, :], moved[levels, t, put, :]
            slip_u = done[0, t, at, :] - speeds_in[0, t, put, :]
            slip_v = done[1, t, at, :] - speeds_in[levels, t, put, :]
            heat = HEAT_RATE * covered_in[3, t, at, :] * (1.0 + (slip_u * slip_u + slip_v * slip_v))
            heat = heat * (sst + FREEZE_SLOPE * sss)
            writes.append((moved, (0, t, put, whole), sst - heat))
            writes.append((moved, (levels, t, put, whole), sss - SALT_RATE * heat))
        return writes

    straight(rows // SUBLANES, warm, 6, 24)
    for n, out in enumerate((temp_out, salt_out)):
        for t in range(tiles):
            finals.append(
                pltpu.make_async_copy(
                    moved.at[levels * n, t],
                    out.at[0, :, pl.ds(LANES * t, LANES)],
                    out_sem.at[SUBCYCLES, n, t],
                )
            )
            finals[-1].start()
    for step in range(SUBCYCLES):
        finals += fixed_rows(step)
    for copy in finals:
        copy.wait()


def ice_and_edges(operands, levels, rows, cols):
    tiles = cols // LANES
    count = sublane_rows(rows)
    deep = jax.ShapeDtypeStruct((levels, rows, cols), F32)
    flat = jax.ShapeDtypeStruct((rows, cols), F32)
    looped = pltpu.VMEM((count + 2, SUBLANES, LANES * (tiles + 1)), F32)
    narrow = pltpu.VMEM((count, SUBLANES, LANES), F32)
    return pl.pallas_call(
        lambda *refs: ice_kernel(levels, rows, *refs),
        in_specs=[VMEM_SPEC] * len(operands),
        out_specs=[ANY_SPEC] * 4,
        out_shape=[deep, deep, flat, flat],
        scratch_shapes=[
            pltpu.VMEM((2 * levels, tiles, rows, LANES), F32),
            pltpu.VMEM((2, tiles, count * SUBLANES, LANES), F32),
            looped, looped, looped, looped, looped,
            narrow, narrow, narrow, narrow, pltpu.VMEM((rows, LANES), F32),
            pltpu.SemaphoreType.DMA((SUBCYCLES + 1, 2, tiles)),
            pltpu.SemaphoreType.DMA((2, tiles)),
        ],
        name="ice",
        compiler_params=pltpu.CompilerParams(vmem_limit_bytes=20 << 20),
        cost_estimate=pl.CostEstimate(flops=60000000, bytes_accessed=16 << 20, transcendentals=0),
    )(*[in_vmem(a) for a in operands])


def per_device(*arrays):
    levels, rows, cols = arrays[0].shape
    lon_count, lat_count = lax.axis_size("lon"), lax.axis_size("lat")
    assert cols == 2 * LANES and rows % (SUBLANES * SUBCYCLES) == 0 and lat_count % 2 == 0
    height = -(-(HALO * ICE + 3 * levels) // SUBLANES) * SUBLANES

    def place(lat, lon):
        return lon * lat_count + lat

    first_pairs, second_pairs = [], []
    for lon in range(lon_count):
        for lat in range(lat_count):
            first_pairs.append((place(lat, lon), place(lat ^ 1, lon)))
            if lat == lat_count - 1:
                second_pairs.append((place(lat, lon), place(lat, lon_count - 1 - lon)))
            elif lat:
                second_pairs.append((place(lat, lon), place(((lat + 1) ^ 1) - 1, lon)))
    first, second = pack_rows(arrays, levels, rows, cols, height)
    first = lax.ppermute(first, ("lon", "lat"), first_pairs)
    second = lax.ppermute(second, ("lon", "lat"), second_pairs)
    tracers, speeds, sea, fields, east_msg, west_msg = load_and_pack_columns(
        arrays, levels, rows, cols
    )
    halo, fields, east_msg, west_msg = merge_halo(
        first, second, fields, east_msg, west_msg, levels, rows
    )
    eastward = [(i, (i + 1) % lon_count) for i in range(lon_count)]
    from_west = lax.ppermute(east_msg, "lon", eastward)
    from_east = lax.ppermute(west_msg, "lon", [(b, a) for a, b in eastward])
    moved, *state = advect(tracers, speeds, sea, halo, fields, levels, rows * lat_count)
    return ice_and_edges(
        [fields, moved, speeds, east_msg, west_msg, from_west, from_east, *state], levels, rows, cols
    )


def solution(mesh):
    deep, flat = P(None, "lat", "lon"), P("lat", "lon")
    return jax.shard_map(
        per_device,
        mesh=mesh,
        in_specs=(deep,) * 4 + (flat,) * 7,
        out_specs=(deep, deep, flat, flat),
        check_vma=False,
    )
```

```python
import jax
import jax.numpy as jnp
from jax import lax
from jax.experimental import pallas as pl
from jax.experimental.pallas import tpu as pltpu
from jax.sharding import PartitionSpec as P

SUBCYCLES = 4
HEAT_RATE = 0.1
SALT_RATE = 0.5
FREEZE_SLOPE = 0.054
DIAGONAL = 1.5
HALO = 2 * SUBCYCLES
LANES = 128
SUBLANES = 8
ICE = 6
FOLD_SIGN = (-1.0, -1.0, 1.0, 1.0, -1.0, -1.0)
TRACER_LANE = 64
F32 = jnp.float32


def lane_ids():
    return lax.broadcasted_iota(jnp.int32, (SUBLANES, LANES), 1)


def sublane_ids():
    return lax.broadcasted_iota(jnp.int32, (SUBLANES, LANES), 0)


def turn(x, shift, axis=1):
    shift = shift % x.shape[axis]
    return pltpu.roll(x, shift, axis) if shift else x


def cut(t):
    return slice(LANES * t, LANES * (t + 1))


def ice_fields(land, ice, u, v, pressure, wind_x, wind_y, ocean_u, ocean_v):
    covered = land.astype(F32) * ice.astype(F32)
    return (u * covered, v * covered, pressure, covered, wind_x + ocean_u, wind_y + ocean_v)


def east_columns(fields, lane):
    packed = jnp.zeros((SUBLANES, LANES), F32)
    for f, tile in enumerate(fields):
        start = HALO * f + 2 * HALO
        moved = turn(tile, start - (LANES - HALO))
        packed = jnp.where((lane >= start) & (lane < start + HALO), moved, packed)
    return packed


def west_columns(fields, lane):
    packed = jnp.zeros((SUBLANES, LANES), F32)
    for f, tile in enumerate(fields):
        start = HALO * f
        packed = jnp.where((lane >= start) & (lane < start + HALO), turn(tile, start), packed)
    return packed


def sublane_rows(rows):
    return (rows + 2 * HALO) // SUBLANES | 1


class Trailing:
    def __init__(self, window):
        self.window, self.waiting = window, []

    def add(self, writes):
        self.waiting.append(writes)
        while len(self.waiting) > self.window:
            self.flush(self.waiting.pop(0))

    def finish(self):
        for writes in self.waiting:
            self.flush(writes)

    @staticmethod
    def flush(writes):
        for ref, where, value in writes:
            ref[where] = value


def straight(steps, body, window, size):
    size = max(c for c in range(1, size + 1) if steps % c == 0)

    def run(n, carry):
        pending = Trailing(window)
        for j in range(size):
            pending.add(body(n * size + j))
        pending.finish()
        return carry

    if size == steps:
        run(0, 0)
    else:
        lax.fori_loop(0, steps // size, run, 0)


def in_groups_of(group, steps, body):
    group = max(c for c in range(1, group + 1) if steps % c == 0)

    def run(n, carry):
        writes = []
        for j in range(group):
            writes += body(n * group + j)
        Trailing.flush(writes)
        return carry

    lax.fori_loop(0, steps // group, run, 0)


def tile_rows(k, offset=0):
    start = k * SUBLANES
    if not isinstance(k, int):
        start = pl.multiple_of(start, SUBLANES)
    return pl.ds(start + offset if offset else start, SUBLANES)


def rows_kernel(levels, *refs):
    tops, bottoms = refs[0:12], refs[12:24]
    first_ref, second_ref = refs[24:26]
    even = lax.rem(lax.axis_index("lat"), 2) == 0

    def message(group, row, northward):
        land, ice, u, v, pressure, wind_x, wind_y, east, north, temp, salt = (
            r for r in group[:11]
        )
        fields = ice_fields(
            land[...], ice[...], u[...], v[...], pressure[...], wind_x[...], wind_y[...],
            east[0], north[0],
        )
        sea = land[row : row + 1, :].astype(F32)
        parts = list(fields) + [temp[:, row, :], salt[:, row, :]]
        if northward:
            parts.append(north[:, row, :] * sea)
        else:
            parts.append(jnp.broadcast_to(sea, (levels, sea.shape[1])))
        return parts

    top = message(tops, SUBLANES - 1, True)
    bottom = message(bottoms, 0, False)
    at = 0
    for t, b in zip(top, bottom):
        size = t.shape[0]
        first_ref[at : at + size, :] = jnp.where(even, t, b)
        second_ref[at : at + size, :] = jnp.where(even, b, t)
        at += size
    pad = first_ref.shape[0] - at
    if pad:
        first_ref[at:, :] = jnp.zeros((pad, first_ref.shape[1]), F32)
        second_ref[at:, :] = jnp.zeros((pad, second_ref.shape[1]), F32)


def pack_rows(arrays, levels, rows, cols, height):
    temp, salt, east, north, land, ice, u, v, pressure, wind_x, wind_y = arrays
    operands = [land, ice, u, v, pressure, wind_x, wind_y, east, north, temp, salt, land]
    last = rows // SUBLANES - 1

    def spec(array, block, count):
        if array.ndim == 2:
            return pl.BlockSpec((SUBLANES, cols), lambda _: (block, 0))
        return pl.BlockSpec((count, SUBLANES, cols), lambda _: (0, block, 0))

    counts = [1] * 7 + [1, levels, levels, levels, 1]
    specs = [spec(a, last, c) for a, c in zip(operands, counts)]
    specs += [spec(a, 0, c) for a, c in zip(operands, counts)]
    out = jax.ShapeDtypeStruct((height, cols), F32)
    return pl.pallas_call(
        lambda *refs: rows_kernel(levels, *refs),
        grid=(1,),
        in_specs=specs,
        out_specs=[pl.BlockSpec((height, cols), lambda _: (0, 0))] * 2,
        out_shape=[out, out],
        name="edge_rows",
        compiler_params=pltpu.CompilerParams(vmem_limit_bytes=8 << 20),
        cost_estimate=pl.CostEstimate(flops=100000, bytes_accessed=1 << 20, transcendentals=0),
    )(*[in_hbm(a) for a in operands + operands])


def columns_kernel(levels, land, ice, u, v, pressure, wind_x, wind_y, east, north, temp, salt,
                   tracer_out, speed_out, sea_out, field_out, east_out, west_out, sem):
    lane = lane_ids()
    rows = sea_out.shape[1]
    tiles = sea_out.shape[0]
    tracers = 2 * levels
    first_lane = TRACER_LANE
    mask_lane = TRACER_LANE + 2 * tracers

    copies = []
    for n, ref in enumerate((temp, salt, east, north)):
        out = tracer_out if n < 2 else speed_out
        for t in range(tiles):
            copies.append(
                pltpu.make_async_copy(
                    ref.at[..., pl.ds(LANES * t, LANES)],
                    out.at[pl.ds(levels * (n % 2), levels), t],
                    sem.at[n, t],
                )
            )
    for copy in copies:
        copy.start()

    whole = slice(None)

    def ice_part(k):
        at, put = tile_rows(k), tile_rows(k + 1)
        writes, fields = [], []
        for t in range(tiles):
            c = cut(t)
            fields.append(
                ice_fields(
                    *[r[at, c] for r in (land, ice, u, v, pressure, wind_x, wind_y)],
                    east[0, at, c], north[0, at, c],
                )
            )
            writes.append((sea_out, (t, at, whole), land[at, c].astype(F32)))
            for f in range(ICE):
                writes.append((field_out, (f, t, put, whole), fields[t][f]))
        writes.append((east_out, (put, whole), east_columns(fields[-1], lane)))
        writes.append((west_out, (put, whole), west_columns(fields[0], lane)))
        return writes

    in_groups_of(4, rows // SUBLANES, ice_part)

    def tracer_part(k):
        at, put = tile_rows(k), tile_rows(k + 1)
        eastward, westward = east_out[put, :], west_out[put, :]
        for f in range(tracers):
            ref, l, to = (temp, salt)[f // levels], f % levels, first_lane + 2 * f
            eastward = jnp.where(
                lane == to, turn(ref[l, at, cut(tiles - 1)], to - (LANES - 1)), eastward
            )
            westward = jnp.where(lane == to, turn(ref[l, at, cut(0)], to), westward)
        return [(east_out, (put, whole), eastward), (west_out, (put, whole), westward)]

    in_groups_of(12, rows // SUBLANES, tracer_part)

    def speed_part(k):
        at, put = tile_rows(k), tile_rows(k + 1)
        masked = (lane >= mask_lane) & (lane < mask_lane + 2 * tracers)
        speeds = jnp.zeros((SUBLANES, LANES), F32)
        for f in range(levels):
            to = mask_lane + 2 * f
            speeds = jnp.where(
                lane == to, turn(east[f, at, cut(tiles - 1)], to - (LANES - 1)), speeds
            )
        speeds = speeds + turn(speeds, 2 * levels)
        last = land[at, LANES * tiles - 1 : LANES * tiles].astype(F32)
        first = jnp.broadcast_to(land[at, 0:1].astype(F32), (SUBLANES, LANES))
        eastward = jnp.where(masked, speeds * last, east_out[put, :])
        westward = jnp.where(masked, first, west_out[put, :])
        return [(east_out, (put, whole), eastward), (west_out, (put, whole), westward)]

    in_groups_of(12, rows // SUBLANES, speed_part)
    end = HALO + rows
    blank = jnp.zeros((field_out.shape[2] - end, LANES), F32)
    for t in range(tiles):
        for f in range(ICE):
            field_out[f, t, end:, :] = blank
    for ref in (east_out, west_out):
        ref[end:, :] = blank
    for copy in copies:
        copy.wait()


def in_vmem(x):
    return pltpu.with_memory_space_constraint(x, pltpu.VMEM)


def in_hbm(x):
    return pltpu.with_memory_space_constraint(x, pltpu.HBM)


def resident(*shape):
    return pltpu.VMEM(shape, F32)


VMEM_SPEC = pl.BlockSpec(memory_space=pltpu.VMEM)
ANY_SPEC = pl.BlockSpec(memory_space=pl.ANY)


def load_and_pack_columns(arrays, levels, rows, cols):
    temp, salt, east, north, land, ice, u, v, pressure, wind_x, wind_y = arrays
    tiles = cols // LANES
    message = resident(sublane_rows(rows) * SUBLANES, LANES)
    deep = resident(2 * levels, tiles, rows, LANES)
    return pl.pallas_call(
        lambda *refs: columns_kernel(levels, *refs),
        in_specs=[VMEM_SPEC] * 11,
        out_specs=[VMEM_SPEC] * 6,
        out_shape=[
            deep, deep, resident(tiles, rows, LANES),
            resident(ICE, tiles, sublane_rows(rows) * SUBLANES, LANES), message, message,
        ],
        scratch_shapes=[pltpu.SemaphoreType.DMA((4, tiles))],
        name="edge_columns",
        compiler_params=pltpu.CompilerParams(vmem_limit_bytes=4 << 20),
        cost_estimate=pl.CostEstimate(flops=5000000, bytes_accessed=12 << 20, transcendentals=0),
    )(*[in_vmem(a) for a in (land, ice, u, v, pressure, wind_x, wind_y, east, north, temp, salt)])


def halo_kernel(levels, rows, first, second, field_in, east_in, west_in,
                halo_ref, field_out, east_out, west_out):
    lat = lax.axis_index("lat")
    even = lax.rem(lat, 2) == 0
    top = lat == lax.axis_size("lat") - 1
    lane, sublane = lane_ids(), sublane_ids()
    tiles = field_out.shape[1]
    south_fields, north_fields = [], []
    for f in range(ICE):
        at = slice(HALO * f, HALO * (f + 1))
        north_row, south_row = [], []
        for t in range(tiles):
            cols = slice(LANES * t, LANES * (t + 1))
            mirror = slice(LANES * (tiles - 1 - t), LANES * (tiles - t))
            south = jnp.where(even, second[at, cols], first[at, cols])
            plain = jnp.where(even, first[at, cols], second[at, cols])
            turned = jnp.take_along_axis(second[at, mirror], LANES - 1 - lane, axis=1)
            turned = jnp.take_along_axis(turned, SUBLANES - 1 - sublane, axis=0)
            north = jnp.where(top, turned * FOLD_SIGN[f], plain)
            field_out[f, t, 0:HALO, :] = south
            field_out[f, t, rows + HALO : rows + 2 * HALO, :] = north
            south_row.append(south)
            north_row.append(north)
        south_fields.append(south_row)
        north_fields.append(north_row)
    rest = slice(HALO * ICE, first.shape[0])
    for t in range(tiles):
        c = cut(t)
        halo_ref[0, t] = jnp.where(even, second[rest, c], first[rest, c])
        halo_ref[1, t] = jnp.where(top, 0.0, jnp.where(even, first[rest, c], second[rest, c]))
    for at, fields in ((0, south_fields), (rows + HALO, north_fields)):
        east_out[at : at + HALO, :] = east_columns([f[-1] for f in fields], lane)
        west_out[at : at + HALO, :] = west_columns([f[0] for f in fields], lane)


def merge_halo(first, second, fields, east_msg, west_msg, levels, rows):
    height, cols = first.shape
    return pl.pallas_call(
        lambda *refs: halo_kernel(levels, rows, *refs),
        in_specs=[VMEM_SPEC] * 5,
        out_specs=[VMEM_SPEC] * 4,
        out_shape=[
            resident(2, cols // LANES, height - HALO * ICE, LANES), resident(*fields.shape),
            resident(*east_msg.shape), resident(*west_msg.shape),
        ],
        input_output_aliases={2: 1, 3: 2, 4: 3},
        name="halo_rows",
        compiler_params=pltpu.CompilerParams(vmem_limit_bytes=8 << 20),
        cost_estimate=pl.CostEstimate(flops=100000, bytes_accessed=1 << 19, transcendentals=0),
    )(first, second, in_vmem(fields), in_vmem(east_msg), in_vmem(west_msg))


def advect_kernel(levels, row_total, tracer_ref, speed_ref, sea, halo, field_ref,
                  out, base_u, base_v, third, force, push_x, push_y, turn_a, turn_b,
                  mask_e, mask_n):
    tiles, rows = sea.shape[:2]
    count = rows // SUBLANES
    group = next(c for c in (16, 8, 4, 2) if count % c == 0)
    lane, sublane = lane_ids(), sublane_ids()
    extra_row = 2 * levels
    whole = slice(None)

    def rows_at(k, offset=0):
        start = pl.multiple_of(k * SUBLANES, SUBLANES)
        return pl.ds(start + offset if offset else start, SUBLANES)

    def row(side, index, t):
        return jnp.broadcast_to(halo[side, t, index : index + 1, :], (SUBLANES, LANES))

    def from_next(values):
        turned = [turn(v, -1) for v in values]
        return [
            jnp.where(lane == LANES - 1, turned[t + 1], turned[t]) if t + 1 < tiles else turned[t]
            for t in range(tiles)
        ]

    def from_last(values):
        turned = [turn(v, 1) for v in values]
        return [jnp.where(lane == 0, turned[t - 1], turned[t]) for t in range(tiles)]

    def in_groups(body, carry):
        def some(start, carry, last):
            writes = []
            for j in range(group):
                more, carry = body(start + j, last and j == group - 1, carry)
                writes += more
            for ref, where, value in writes:
                ref[where] = value
            return carry

        groups = count // group
        carry = lax.fori_loop(0, groups - 1, lambda n, c: some(n * group, c, False), carry)
        return some((groups - 1) * group, carry, True)

    def row_above(load, k, last, past):
        if not last:
            return load(rows_at(k, 1))
        return jnp.where(sublane == SUBLANES - 1, past, turn(load(rows_at(k)), -1, 0))

    def masks(k, last, carry):
        here = [sea[t, rows_at(k), :] for t in range(tiles)]
        beside = from_next(here)
        writes = []
        for t in range(tiles):
            above = row_above(lambda at, t=t: sea[t, at, :], k, last, row(1, extra_row, t))
            face = here[t] * beside[t]
            if t == tiles - 1:
                face = jnp.where(lane == LANES - 1, 0.0, face)
            writes.append((mask_e, (t, rows_at(k), whole), face))
            writes.append((mask_n, (t, rows_at(k), whole), here[t] * above))
        return writes, carry

    in_groups(masks, 0)
    for level in range(levels):
        entering = []
        for f in (level, levels + level):
            for t in range(tiles):
                speed = row(0, extra_row + level, t) * sea[t, 0:SUBLANES, :]
                start = tracer_ref[f, t, 0:SUBLANES, :]
                entering.append(speed * jnp.where(speed > 0, row(0, f, t), start))

        def body(k, last, carry, level=level):
            at = rows_at(k)
            fast_e = [speed_ref[level, t, at, :] * mask_e[t, at, :] for t in range(tiles)]
            fast_n = [speed_ref[levels + level, t, at, :] * mask_n[t, at, :] for t in range(tiles)]
            writes, result = [], []
            for f in (level, levels + level):
                here = [tracer_ref[f, t, at, :] for t in range(tiles)]
                beside = from_next(here)
                flux_e = [
                    fast_e[t] * jnp.where(fast_e[t] > 0, here[t], beside[t]) for t in range(tiles)
                ]
                before = from_last(flux_e)
                for t in range(tiles):
                    above = row_above(
                        lambda at, f=f, t=t: tracer_ref[f, t, at, :], k, last, row(1, f, t)
                    )
                    flux_n = fast_n[t] * jnp.where(fast_n[t] > 0, here[t], above)
                    turned = turn(flux_n, 1, 0)
                    below = jnp.where(sublane == 0, carry[len(result)], turned)
                    value = here[t] - ((flux_e[t] - before[t]) + (flux_n - below))
                    writes.append((out, (f, t, at, whole), value))
                    result.append(turned)
            return writes, tuple(result)

        in_groups(body, tuple(entering))
    spread_fields(rows, row_total, field_ref, base_u, base_v, third, force, push_x, push_y,
                  turn_a, turn_b)


def spread(ref, i, count, *lead):
    return ref[(*lead, pl.ds(i, SUBLANES, stride=count), slice(None))]


def wrap(ref, count, lanes=slice(None)):
    ref[0, :, lanes] = turn(ref[count, :, lanes], 1, 0)
    ref[count + 1, :, lanes] = turn(ref[1, :, lanes], -1, 0)


def spread_fields(rows, row_total, field_ref, base_u, base_v, third, force, push_x, push_y,
                  turn_a, turn_b):
    tiles = field_ref.shape[1]
    count = sublane_rows(rows)
    lane, sublane = lane_ids(), sublane_ids()
    lat = lax.axis_index("lat")

    def body(i):
        per_tile = [[spread(field_ref, i, count, f, t) for f in range(ICE)] for t in range(tiles)]
        extra = []
        for f in range(ICE):
            low, high = per_tile[0][f], per_tile[-1][f]
            middle = turn(jnp.where(lane < LANES // 2, high, low), 48)
            x = jnp.where(lane < 32, low, middle)
            extra.append(jnp.where(lane >= 64, turn(high, -24), x))
        writes = []
        for t, fields in enumerate(per_tile + [extra]):
            u0, v0, strength, covered, drive_x, drive_y = fields
            writes.append((base_u, (i + 1, slice(None), cut(t)), u0))
            writes.append((base_v, (i + 1, slice(None), cut(t)), v0))
            writes.append((third, (i, slice(None), cut(t)), covered * (1.0 / 3.0)))
            writes.append((force, (i, slice(None), cut(t)), strength * covered * (1.0 / 12.0)))
            writes.append((push_x, (i, slice(None), cut(t)), 0.5 * drive_x))
            writes.append((push_y, (i, slice(None), cut(t)), 0.5 * drive_y))
        y = lat * rows - HALO + sublane * count + i
        y = jnp.where(y >= row_total, 2 * row_total - 1 - y, y)
        coriolis = 0.5 * (2 * y + 1 - row_total).astype(F32) / row_total
        turning = 0.5 * coriolis
        scale = 3.0 / (DIAGONAL * DIAGONAL + turning * turning)
        writes.append((turn_a, (i,), DIAGONAL * scale))
        writes.append((turn_b, (i,), turning * scale))
        return writes

    in_groups_of(3, count, body)
    wrap(base_u, count)
    wrap(base_v, count)


def advect(tracers, speeds, sea, halo, fields, levels, row_total):
    tiles, rows = sea.shape[:2]
    count = sublane_rows(rows)
    wide = LANES * (tiles + 1)
    looped = resident(count + 2, SUBLANES, wide)
    plain = resident(count, SUBLANES, wide)
    narrow = resident(count, SUBLANES, LANES)
    return pl.pallas_call(
        lambda *refs: advect_kernel(levels, row_total, *refs),
        in_specs=[VMEM_SPEC] * 5,
        out_specs=[VMEM_SPEC] * 9,
        out_shape=[
            resident(*tracers.shape), looped, looped, plain, plain, plain, plain, narrow, narrow,
        ],
        scratch_shapes=[pltpu.VMEM((tiles, rows, LANES), F32)] * 2,
        name="advect",
        compiler_params=pltpu.CompilerParams(vmem_limit_bytes=8 << 20),
        cost_estimate=pl.CostEstimate(flops=30000000, bytes_accessed=16 << 20, transcendentals=0),
    )(*[in_vmem(a) for a in (tracers, speeds, sea, halo, fields)])


def ice_kernel(levels, rows, *refs):
    (covered_in, tracers_in, speeds_in, east_own, west_own, from_west, from_east,
     base_u, base_v, third, force, push_x, push_y, turn_a, turn_b,
     temp_out, salt_out, u_out, v_out,
     moved, done, vel_u, vel_v, str_a, str_b, str_c,
     third_x, force_x, push_x_x, push_y_x, edges,
     out_sem, vel_sem) = refs
    tiles = tracers_in.shape[1]
    count = sublane_rows(rows)
    tracers = 2 * levels
    lane = lane_ids()
    own = pl.ds(HALO, rows)
    wide = tiles + 1
    whole = slice(None)

    def edge_fluxes(k):
        at, put = tile_rows(k + 1), tile_rows(k)
        west, east_side = from_west[at, :], from_east[at, :]
        mine_e, mine_w = east_own[at, :], west_own[at, :]
        speed = turn(west, -2 * tracers)
        inflow = speed * jnp.where(speed > 0, west, mine_w) * turn(mine_w, -2 * tracers)
        speed = turn(mine_e, -2 * tracers)
        outflow = speed * jnp.where(speed > 0, mine_e, east_side) * turn(east_side, -2 * tracers)
        flux = jnp.where(lane % 2 == TRACER_LANE % 2, inflow, turn(outflow, -1))
        return [(edges, (put, whole), flux)]

    straight(rows // SUBLANES, edge_fluxes, 8, 24)

    def fixed(f, put):
        flux = turn(edges[put, :], -(TRACER_LANE + 2 * f))
        low = tracers_in[f, 0, put, :] + jnp.where(lane == 0, flux, 0.0)
        return low, tracers_in[f, tiles - 1, put, :] - jnp.where(lane == LANES - 1, flux, 0.0)

    def insert(i):
        west, east_side = spread(from_west, i, count), spread(from_east, i, count)
        writes = []
        targets = (
            (base_u, vel_u, 1, tiles, 1.0), (base_v, vel_v, 1, tiles, 1.0),
            (force, force_x, 0, 0, 1.0), (third, third_x, 0, 0, 1.0 / 3.0),
            (push_x, push_x_x, 0, 0, 0.5), (push_y, push_y_x, 0, 0, 0.5),
        )
        beyond = []
        for f in range(ICE):
            start = HALO * f + 2 * HALO
            x = jnp.where((lane >= start) & (lane < start + HALO), west, east_side)
            beyond.append(turn(x, 104 - HALO * f))
        beyond[2] = beyond[2] * beyond[3] * (1.0 / 12.0)
        for x, (source, target, shift, t, factor) in zip(beyond, targets):
            x = x if factor == 1.0 else x * factor
            x = jnp.where(lane >= 104, x, source[i + shift, :, cut(tiles)])
            writes.append((target, (i + shift, whole, cut(t)), x))
        own_lanes = slice(0, LANES * tiles)
        for source, target in ((base_u, vel_u), (base_v, vel_v)):
            writes.append((target, (i + 1, whole, own_lanes), source[i + 1, :, own_lanes]))
        for ref in (str_a, str_b, str_c):
            writes.append((ref, (i + 1,), jnp.zeros(ref.shape[1:], F32)))
        return writes

    straight(count, insert, 3, 17)
    wrap(vel_u, count)
    wrap(vel_v, count)

    def constant(ref, extra, i, t):
        return ref[i, :, cut(t)] if t < tiles else extra[i]

    def load_once(ref, name, seen, j, t):
        if (name, j, t) not in seen:
            seen[name, j, t] = ref[(j, whole) if t is None else (j, whole, cut(t))]
        return seen[name, j, t]

    share = rows // SUBLANES // SUBCYCLES
    items = [(k, f) for k in range(share) for f in range(tracers)]

    def fix(step, i):
        for k, f in items[len(items) * i // count : len(items) * (i + 1) // count]:
            put = pl.ds(pl.multiple_of((step * share + k) * SUBLANES, SUBLANES), SUBLANES)
            low, high = fixed(f, put)
            moved[f, 0, put, :] = low
            moved[f, tiles - 1, put, :] = high

    def fixed_rows(step):
        part = pl.ds(pl.multiple_of(step * share * SUBLANES, SUBLANES), share * SUBLANES)
        return [
            pltpu.make_async_copy(
                moved.at[pl.ds(levels * n + 1, levels - 1), t, part, :],
                out.at[pl.ds(1, levels - 1), part, pl.ds(LANES * t, LANES)],
                out_sem.at[step, n, t],
            )
            for n, out in enumerate((temp_out, salt_out))
            for t in range(tiles)
        ]

    def strain_stress(step):
        seen = {}
        for i in range(count):
            for t in range(wide):
                u, v = (load_once(r, n, seen, i + 1, t) for n, r in enumerate((vel_u, vel_v)))
                dudx, dvdx = turn(u, -1) - turn(u, 1), turn(v, -1) - turn(v, 1)
                dudy, dvdy = (
                    load_once(r, n, seen, i + 2, t) - load_once(r, n, seen, i, t)
                    for n, r in enumerate((vel_u, vel_v))
                )
                div, ten, shr = dudx + dvdy, dudx - dvdy, dudy + dvdx
                square = div * div + 0.25 * (ten * ten + shr * shr) + 1.0
                base = constant(force, force_x, i, t)
                zeta = base * lax.rsqrt(square)
                quarter = 0.25 * zeta
                even = zeta * div - base
                odd = quarter * ten
                keep = constant(third, third_x, i, t)
                for ref, new in (
                    (str_a, even + odd), (str_b, even - odd), (str_c, quarter * shr)
                ):
                    ref[i + 1, :, cut(t)] = new + keep * ref[i + 1, :, cut(t)]
            fix(step, i)
        wrap(str_b, count)
        wrap(str_c, count)

    def momentum():
        seen = {}
        for i in range(count):
            ar, br = turn_a[i], turn_b[i]
            for t in range(wide):
                a = str_a[i + 1, :, cut(t)]
                s = load_once(str_c, 2, seen, i + 1, t)
                fx = (turn(a, -1) - turn(a, 1)) + (
                    load_once(str_c, 2, seen, i + 2, t) - load_once(str_c, 2, seen, i, t)
                )
                fy = (turn(s, -1) - turn(s, 1)) + (
                    load_once(str_b, 1, seen, i + 2, t) - load_once(str_b, 1, seen, i, t)
                )
                ru = (vel_u[i + 1, :, cut(t)] + constant(push_x, push_x_x, i, t)) + fx
                rv = (vel_v[i + 1, :, cut(t)] + constant(push_y, push_y_x, i, t)) + fy
                keep = constant(third, third_x, i, t)
                vel_u[i + 1, :, cut(t)] = (ar * ru + br * rv) * keep
                vel_v[i + 1, :, cut(t)] = (ar * rv - br * ru) * keep
        wrap(vel_u, count)
        wrap(vel_v, count)

    def subcycle(step, carry):
        strain_stress(step)
        for copy in fixed_rows(step):
            copy.start()
        momentum()
        return carry

    lax.fori_loop(0, SUBCYCLES, subcycle, 0)

    def gather(i):
        writes = []
        for n, ref in enumerate((vel_u, vel_v)):
            borders = ref[i + 1, :, cut(tiles)]
            middle, outer = turn(borders, -48), turn(borders, 24)
            low, high = ref[i + 1, :, cut(0)], ref[i + 1, :, cut(tiles - 1)]
            low = jnp.where(lane < HALO, borders, jnp.where(lane >= LANES - HALO, middle, low))
            high = jnp.where(lane < HALO, middle, jnp.where(lane >= LANES - HALO, outer, high))
            put = pl.ds(i, SUBLANES, stride=count)
            writes.append((done, (n, 0, put, whole), low))
            writes.append((done, (n, tiles - 1, put, whole), high))
        return writes

    straight(count, gather, 6, 51)
    finals = []
    for n, out in enumerate((u_out, v_out)):
        for t in range(tiles):
            finals.append(
                pltpu.make_async_copy(
                    done.at[n, t, own, :], out.at[:, pl.ds(LANES * t, LANES)], vel_sem.at[n, t]
                )
            )
            finals[-1].start()

    def warm(k):
        put, at = tile_rows(k), tile_rows(k + 1)
        writes = []
        for t in range(tiles):
            sst, sss = moved[0, t, put, :], moved[levels, t, put, :]
            slip_u = done[0, t, at, :] - speeds_in[0, t, put, :]
            slip_v = done[1, t, at, :] - speeds_in[levels, t, put, :]
            heat = HEAT_RATE * covered_in[3, t, at, :] * (1.0 + (slip_u * slip_u + slip_v * slip_v))
            heat = heat * (sst + FREEZE_SLOPE * sss)
            writes.append((moved, (0, t, put, whole), sst - heat))
            writes.append((moved, (levels, t, put, whole), sss - SALT_RATE * heat))
        return writes

    straight(rows // SUBLANES, warm, 6, 24)
    for n, out in enumerate((temp_out, salt_out)):
        for t in range(tiles):
            finals.append(
                pltpu.make_async_copy(
                    moved.at[levels * n, t],
                    out.at[0, :, pl.ds(LANES * t, LANES)],
                    out_sem.at[SUBCYCLES, n, t],
                )
            )
            finals[-1].start()
    for step in range(SUBCYCLES):
        finals += fixed_rows(step)
    for copy in finals:
        copy.wait()


def ice_and_edges(operands, levels, rows, cols):
    tiles = cols // LANES
    count = sublane_rows(rows)
    deep = jax.ShapeDtypeStruct((levels, rows, cols), F32)
    flat = jax.ShapeDtypeStruct((rows, cols), F32)
    looped = pltpu.VMEM((count + 2, SUBLANES, LANES * (tiles + 1)), F32)
    narrow = pltpu.VMEM((count, SUBLANES, LANES), F32)
    return pl.pallas_call(
        lambda *refs: ice_kernel(levels, rows, *refs),
        in_specs=[VMEM_SPEC] * len(operands),
        out_specs=[ANY_SPEC] * 4,
        out_shape=[deep, deep, flat, flat],
        scratch_shapes=[
            pltpu.VMEM((2 * levels, tiles, rows, LANES), F32),
            pltpu.VMEM((2, tiles, count * SUBLANES, LANES), F32),
            looped, looped, looped, looped, looped,
            narrow, narrow, narrow, narrow, pltpu.VMEM((rows, LANES), F32),
            pltpu.SemaphoreType.DMA((SUBCYCLES + 1, 2, tiles)),
            pltpu.SemaphoreType.DMA((2, tiles)),
        ],
        name="ice",
        compiler_params=pltpu.CompilerParams(vmem_limit_bytes=20 << 20),
        cost_estimate=pl.CostEstimate(flops=60000000, bytes_accessed=16 << 20, transcendentals=0),
    )(*[in_vmem(a) for a in operands])


def per_device(*arrays):
    levels, rows, cols = arrays[0].shape
    lon_count, lat_count = lax.axis_size("lon"), lax.axis_size("lat")
    assert cols == 2 * LANES and rows % (SUBLANES * SUBCYCLES) == 0 and lat_count % 2 == 0
    height = -(-(HALO * ICE + 3 * levels) // SUBLANES) * SUBLANES

    def place(lat, lon):
        return lon * lat_count + lat

    first_pairs, second_pairs = [], []
    for lon in range(lon_count):
        for lat in range(lat_count):
            first_pairs.append((place(lat, lon), place(lat ^ 1, lon)))
            if lat == lat_count - 1:
                second_pairs.append((place(lat, lon), place(lat, lon_count - 1 - lon)))
            elif lat:
                second_pairs.append((place(lat, lon), place(((lat + 1) ^ 1) - 1, lon)))
    first, second = pack_rows(arrays, levels, rows, cols, height)
    first = lax.ppermute(first, ("lon", "lat"), first_pairs)
    second = lax.ppermute(second, ("lon", "lat"), second_pairs)
    tracers, speeds, sea, fields, east_msg, west_msg = load_and_pack_columns(
        arrays, levels, rows, cols
    )
    halo, fields, east_msg, west_msg = merge_halo(
        first, second, fields, east_msg, west_msg, levels, rows
    )
    eastward = [(i, (i + 1) % lon_count) for i in range(lon_count)]
    from_west = lax.ppermute(east_msg, "lon", eastward)
    from_east = lax.ppermute(west_msg, "lon", [(b, a) for a, b in eastward])
    moved, *state = advect(tracers, speeds, sea, halo, fields, levels, rows * lat_count)
    return ice_and_edges(
        [fields, moved, speeds, east_msg, west_msg, from_west, from_east, *state], levels, rows, cols
    )


def solution(mesh):
    deep, flat = P(None, "lat", "lon"), P("lat", "lon")
    return jax.shard_map(
        per_device,
        mesh=mesh,
        in_specs=(deep,) * 4 + (flat,) * 7,
        out_specs=(deep, deep, flat, flat),
        check_vma=False,
    )
```

```python
import jax
import jax.numpy as jnp
from jax import lax
from jax.experimental import pallas as pl
from jax.experimental.pallas import tpu as pltpu
from jax.sharding import PartitionSpec as P

SUBCYCLES = 4
HEAT_RATE = 0.1
SALT_RATE = 0.5
FREEZE_SLOPE = 0.054
DIAGONAL = 1.5
HALO = 2 * SUBCYCLES
LANES = 128
SUBLANES = 8
ICE = 6
FOLD_SIGN = (-1.0, -1.0, 1.0, 1.0, -1.0, -1.0)
TRACER_LANE = 64
F32 = jnp.float32


def lane_ids():
    return lax.broadcasted_iota(jnp.int32, (SUBLANES, LANES), 1)


def sublane_ids():
    return lax.broadcasted_iota(jnp.int32, (SUBLANES, LANES), 0)


def turn(x, shift, axis=1):
    shift = shift % x.shape[axis]
    return pltpu.roll(x, shift, axis) if shift else x


def cut(t):
    return slice(LANES * t, LANES * (t + 1))


def ice_fields(land, ice, u, v, pressure, wind_x, wind_y, ocean_u, ocean_v):
    covered = land.astype(F32) * ice.astype(F32)
    return (u * covered, v * covered, pressure, covered, wind_x + ocean_u, wind_y + ocean_v)


def east_columns(fields, lane):
    packed = jnp.zeros((SUBLANES, LANES), F32)
    for f, tile in enumerate(fields):
        start = HALO * f + 2 * HALO
        moved = turn(tile, start - (LANES - HALO))
        packed = jnp.where((lane >= start) & (lane < start + HALO), moved, packed)
    return packed


def west_columns(fields, lane):
    packed = jnp.zeros((SUBLANES, LANES), F32)
    for f, tile in enumerate(fields):
        start = HALO * f
        packed = jnp.where((lane >= start) & (lane < start + HALO), turn(tile, start), packed)
    return packed


def sublane_rows(rows):
    return (rows + 2 * HALO) // SUBLANES | 1


class Trailing:
    def __init__(self, window):
        self.window, self.waiting = window, []

    def add(self, writes):
        self.waiting.append(writes)
        while len(self.waiting) > self.window:
            self.flush(self.waiting.pop(0))

    def finish(self):
        for writes in self.waiting:
            self.flush(writes)

    @staticmethod
    def flush(writes):
        for ref, where, value in writes:
            ref[where] = value


def straight(steps, body, window, size):
    size = max(c for c in range(1, size + 1) if steps % c == 0)

    def run(n, carry):
        pending = Trailing(window)
        for j in range(size):
            pending.add(body(n * size + j))
        pending.finish()
        return carry

    if size == steps:
        run(0, 0)
    else:
        lax.fori_loop(0, steps // size, run, 0)


def in_groups_of(group, steps, body):
    group = max(c for c in range(1, group + 1) if steps % c == 0)

    def run(n, carry):
        writes = []
        for j in range(group):
            writes += body(n * group + j)
        Trailing.flush(writes)
        return carry

    lax.fori_loop(0, steps // group, run, 0)


def tile_rows(k, offset=0):
    start = k * SUBLANES
    if not isinstance(k, int):
        start = pl.multiple_of(start, SUBLANES)
    return pl.ds(start + offset if offset else start, SUBLANES)


def rows_kernel(levels, *refs):
    tops, bottoms = refs[0:12], refs[12:24]
    first_ref, second_ref = refs[24:26]
    even = lax.rem(lax.axis_index("lat"), 2) == 0

    def message(group, row, northward):
        land, ice, u, v, pressure, wind_x, wind_y, east, north, temp, salt = (
            r for r in group[:11]
        )
        fields = ice_fields(
            land[...], ice[...], u[...], v[...], pressure[...], wind_x[...], wind_y[...],
            east[0], north[0],
        )
        sea = land[row : row + 1, :].astype(F32)
        parts = list(fields) + [temp[:, row, :], salt[:, row, :]]
        if northward:
            parts.append(north[:, row, :] * sea)
        else:
            parts.append(jnp.broadcast_to(sea, (levels, sea.shape[1])))
        return parts

    top = message(tops, SUBLANES - 1, True)
    bottom = message(bottoms, 0, False)
    at = 0
    for t, b in zip(top, bottom):
        size = t.shape[0]
        first_ref[at : at + size, :] = jnp.where(even, t, b)
        second_ref[at : at + size, :] = jnp.where(even, b, t)
        at += size
    pad = first_ref.shape[0] - at
    if pad:
        first_ref[at:, :] = jnp.zeros((pad, first_ref.shape[1]), F32)
        second_ref[at:, :] = jnp.zeros((pad, second_ref.shape[1]), F32)


def pack_rows(arrays, levels, rows, cols, height):
    temp, salt, east, north, land, ice, u, v, pressure, wind_x, wind_y = arrays
    operands = [land, ice, u, v, pressure, wind_x, wind_y, east, north, temp, salt, land]
    last = rows // SUBLANES - 1

    def spec(array, block, count):
        if array.ndim == 2:
            return pl.BlockSpec((SUBLANES, cols), lambda _: (block, 0))
        return pl.BlockSpec((count, SUBLANES, cols), lambda _: (0, block, 0))

    counts = [1] * 7 + [1, levels, levels, levels, 1]
    specs = [spec(a, last, c) for a, c in zip(operands, counts)]
    specs += [spec(a, 0, c) for a, c in zip(operands, counts)]
    out = jax.ShapeDtypeStruct((height, cols), F32)
    return pl.pallas_call(
        lambda *refs: rows_kernel(levels, *refs),
        grid=(1,),
        in_specs=specs,
        out_specs=[pl.BlockSpec((height, cols), lambda _: (0, 0))] * 2,
        out_shape=[out, out],
        name="edge_rows",
        compiler_params=pltpu.CompilerParams(vmem_limit_bytes=8 << 20),
        cost_estimate=pl.CostEstimate(flops=100000, bytes_accessed=1 << 20, transcendentals=0),
    )(*[in_hbm(a) for a in operands + operands])


def on_even_lon():
    return lax.rem(lax.axis_index("lon"), 2) == 0


def local_copies(refs, outs, sem):
    return [
        pltpu.make_async_copy(ref.at[..., pl.ds(LANES * t, LANES)], out.at[:, t], sem.at[n, t])
        for n, (ref, out) in enumerate(zip(refs, outs))
        for t in range(ref.shape[-1] // LANES)
    ]


def surface_kernel(levels, land, ice, u, v, pressure, wind_x, wind_y, east, north,
                   speed_out, sea_out, field_out, east_out, west_out, sem):
    lane = lane_ids()
    tiles, rows = sea_out.shape[:2]
    whole = slice(None)
    copies = local_copies(
        (east, north), [speed_out.at[pl.ds(levels * n, levels)] for n in range(2)], sem
    )
    for copy in copies:
        copy.start()

    def ice_part(k):
        at, put = tile_rows(k), tile_rows(k + 1)
        writes, fields = [], []
        for t in range(tiles):
            c = cut(t)
            fields.append(
                ice_fields(
                    *[r[at, c] for r in (land, ice, u, v, pressure, wind_x, wind_y)],
                    east[0, at, c], north[0, at, c],
                )
            )
            writes.append((sea_out, (t, at, whole), land[at, c].astype(F32)))
            for f in range(ICE):
                writes.append((field_out, (f, t, put, whole), fields[t][f]))
        writes.append((east_out, (at, whole), east_columns(fields[-1], lane)))
        writes.append((west_out, (at, whole), west_columns(fields[0], lane)))
        return writes

    in_groups_of(4, rows // SUBLANES, ice_part)
    end = HALO + rows
    blank = jnp.zeros((field_out.shape[2] - end, LANES), F32)
    for t in range(tiles):
        for f in range(ICE):
            field_out[f, t, end:, :] = blank
    for copy in copies:
        copy.wait()


def tracer_kernel(levels, temp, salt, east, sea, east_ice, west_ice,
                  tracer_out, inter_out, intra_out, sem):
    lane = lane_ids()
    even = on_even_lon()
    tiles, rows = sea.shape[:2]
    tracers = 2 * levels
    first_lane = TRACER_LANE
    mask_lane = TRACER_LANE + 2 * tracers
    whole = slice(None)
    copies = local_copies(
        (temp, salt), [tracer_out.at[pl.ds(levels * n, levels)] for n in range(2)], sem
    )
    for copy in copies:
        copy.start()

    def tracer_part(k):
        at, put = tile_rows(k), tile_rows(k + 1)
        eastward, westward = east_ice[at, :], west_ice[at, :]
        for f in range(tracers):
            ref, l, to = (temp, salt)[f // levels], f % levels, first_lane + 2 * f
            eastward = jnp.where(
                lane == to, turn(ref[l, at, cut(tiles - 1)], to - (LANES - 1)), eastward
            )
            westward = jnp.where(lane == to, turn(ref[l, at, cut(0)], to), westward)
        masked = (lane >= mask_lane) & (lane < mask_lane + 2 * tracers)
        speeds = jnp.zeros((SUBLANES, LANES), F32)
        for f in range(levels):
            to = mask_lane + 2 * f
            moved = turn(east[f, tiles - 1, at, :], to - (LANES - 1))
            speeds = jnp.where(lane == to, moved, speeds)
        speeds = speeds + turn(speeds, 2 * levels)
        last = sea[tiles - 1, at, LANES - 1 : LANES]
        first = jnp.broadcast_to(sea[0, at, 0:1], (SUBLANES, LANES))
        eastward = jnp.where(masked, speeds * last, eastward)
        westward = jnp.where(masked, first, westward)
        return [
            (inter_out, (put, whole), jnp.where(even, westward, eastward)),
            (intra_out, (put, whole), jnp.where(even, eastward, westward)),
        ]

    in_groups_of(8, rows // SUBLANES, tracer_part)
    end = HALO + rows
    for ref in (inter_out, intra_out):
        ref[end:, :] = jnp.zeros((ref.shape[0] - end, LANES), F32)
    for copy in copies:
        copy.wait()


def in_vmem(x):
    return pltpu.with_memory_space_constraint(x, pltpu.VMEM)


def in_hbm(x):
    return pltpu.with_memory_space_constraint(x, pltpu.HBM)


def resident(*shape):
    return pltpu.VMEM(shape, F32)


VMEM_SPEC = pl.BlockSpec(memory_space=pltpu.VMEM)
ANY_SPEC = pl.BlockSpec(memory_space=pl.ANY)


def prepare_surface(arrays, levels, rows, cols):
    temp, salt, east, north, land, ice, u, v, pressure, wind_x, wind_y = arrays
    tiles = cols // LANES
    message = resident(rows, LANES)
    return pl.pallas_call(
        lambda *refs: surface_kernel(levels, *refs),
        in_specs=[VMEM_SPEC] * 9,
        out_specs=[VMEM_SPEC] * 5,
        out_shape=[
            resident(2 * levels, tiles, rows, LANES), resident(tiles, rows, LANES),
            resident(ICE, tiles, sublane_rows(rows) * SUBLANES, LANES), message, message,
        ],
        scratch_shapes=[pltpu.SemaphoreType.DMA((2, tiles))],
        name="surface",
        compiler_params=pltpu.CompilerParams(vmem_limit_bytes=4 << 20),
        cost_estimate=pl.CostEstimate(flops=5000000, bytes_accessed=8 << 20, transcendentals=0),
    )(*[in_vmem(a) for a in (land, ice, u, v, pressure, wind_x, wind_y, east, north)])


def pack_columns(temp, salt, speeds, sea, east_ice, west_ice, levels):
    tiles, rows = sea.shape[:2]
    message = resident(sublane_rows(rows) * SUBLANES, LANES)
    return pl.pallas_call(
        lambda *refs: tracer_kernel(levels, *refs),
        in_specs=[VMEM_SPEC] * 6,
        out_specs=[VMEM_SPEC] * 3,
        out_shape=[resident(2 * levels, tiles, rows, LANES), message, message],
        scratch_shapes=[pltpu.SemaphoreType.DMA((2, tiles))],
        name="edge_columns",
        compiler_params=pltpu.CompilerParams(vmem_limit_bytes=4 << 20),
        cost_estimate=pl.CostEstimate(flops=5000000, bytes_accessed=8 << 20, transcendentals=0),
    )(*[in_vmem(a) for a in (temp, salt, speeds, sea, east_ice, west_ice)])


def halo_kernel(levels, rows, first, second, field_in, inter_in, intra_in,
                halo_ref, field_out, inter_out, intra_out):
    lat = lax.axis_index("lat")
    even = lax.rem(lat, 2) == 0
    top = lat == lax.axis_size("lat") - 1
    lane, sublane = lane_ids(), sublane_ids()
    tiles = field_out.shape[1]
    south_fields, north_fields = [], []
    for f in range(ICE):
        at = slice(HALO * f, HALO * (f + 1))
        north_row, south_row = [], []
        for t in range(tiles):
            cols = slice(LANES * t, LANES * (t + 1))
            mirror = slice(LANES * (tiles - 1 - t), LANES * (tiles - t))
            south = jnp.where(even, second[at, cols], first[at, cols])
            plain = jnp.where(even, first[at, cols], second[at, cols])
            turned = jnp.take_along_axis(second[at, mirror], LANES - 1 - lane, axis=1)
            turned = jnp.take_along_axis(turned, SUBLANES - 1 - sublane, axis=0)
            north = jnp.where(top, turned * FOLD_SIGN[f], plain)
            field_out[f, t, 0:HALO, :] = south
            field_out[f, t, rows + HALO : rows + 2 * HALO, :] = north
            south_row.append(south)
            north_row.append(north)
        south_fields.append(south_row)
        north_fields.append(north_row)
    rest = slice(HALO * ICE, first.shape[0])
    for t in range(tiles):
        c = cut(t)
        halo_ref[0, t] = jnp.where(even, second[rest, c], first[rest, c])
        halo_ref[1, t] = jnp.where(top, 0.0, jnp.where(even, first[rest, c], second[rest, c]))
    for at, fields in ((0, south_fields), (rows + HALO, north_fields)):
        eastward = east_columns([f[-1] for f in fields], lane)
        westward = west_columns([f[0] for f in fields], lane)
        inter_out[at : at + HALO, :] = jnp.where(on_even_lon(), westward, eastward)
        intra_out[at : at + HALO, :] = jnp.where(on_even_lon(), eastward, westward)


def merge_halo(first, second, fields, inter_msg, intra_msg, levels, rows):
    height, cols = first.shape
    return pl.pallas_call(
        lambda *refs: halo_kernel(levels, rows, *refs),
        in_specs=[VMEM_SPEC] * 5,
        out_specs=[VMEM_SPEC] * 4,
        out_shape=[
            resident(2, cols // LANES, height - HALO * ICE, LANES), resident(*fields.shape),
            resident(*inter_msg.shape), resident(*intra_msg.shape),
        ],
        input_output_aliases={2: 1, 3: 2, 4: 3},
        name="halo_rows",
        compiler_params=pltpu.CompilerParams(vmem_limit_bytes=8 << 20),
        cost_estimate=pl.CostEstimate(flops=100000, bytes_accessed=1 << 19, transcendentals=0),
    )(first, second, in_vmem(fields), in_vmem(inter_msg), in_vmem(intra_msg))


def advect_kernel(levels, row_total, tracer_ref, speed_ref, sea, halo, field_ref,
                  out, base_u, base_v, third, force, push_x, push_y, turn_a, turn_b,
                  mask_e, mask_n):
    tiles, rows = sea.shape[:2]
    count = rows // SUBLANES
    group = next(c for c in (12, 8, 4, 2) if count % c == 0)
    lane, sublane = lane_ids(), sublane_ids()
    extra_row = 2 * levels
    whole = slice(None)

    def rows_at(k, offset=0):
        start = pl.multiple_of(k * SUBLANES, SUBLANES)
        return pl.ds(start + offset if offset else start, SUBLANES)

    def row(side, index, t):
        return jnp.broadcast_to(halo[side, t, index : index + 1, :], (SUBLANES, LANES))

    def from_next(values):
        turned = [turn(v, -1) for v in values]
        return [
            jnp.where(lane == LANES - 1, turned[t + 1], turned[t]) if t + 1 < tiles else turned[t]
            for t in range(tiles)
        ]

    def from_last(values):
        turned = [turn(v, 1) for v in values]
        return [jnp.where(lane == 0, turned[t - 1], turned[t]) for t in range(tiles)]

    def in_groups(body, carry):
        def some(start, carry, last):
            writes = []
            for j in range(group):
                more, carry = body(start + j, last and j == group - 1, carry)
                writes += more
            for ref, where, value in writes:
                ref[where] = value
            return carry

        groups = count // group
        carry = lax.fori_loop(0, groups - 1, lambda n, c: some(n * group, c, False), carry)
        return some((groups - 1) * group, carry, True)

    def row_above(load, k, last, past):
        if not last:
            return load(rows_at(k, 1))
        return jnp.where(sublane == SUBLANES - 1, past, turn(load(rows_at(k)), -1, 0))

    def masks(k, last, carry):
        here = [sea[t, rows_at(k), :] for t in range(tiles)]
        beside = from_next(here)
        writes = []
        for t in range(tiles):
            above = row_above(lambda at, t=t: sea[t, at, :], k, last, row(1, extra_row, t))
            face = here[t] * beside[t]
            if t == tiles - 1:
                face = jnp.where(lane == LANES - 1, 0.0, face)
            writes.append((mask_e, (t, rows_at(k), whole), face))
            writes.append((mask_n, (t, rows_at(k), whole), here[t] * above))
        return writes, carry

    in_groups(masks, 0)
    for level in range(levels):
        entering = []
        for f in (level, levels + level):
            for t in range(tiles):
                speed = row(0, extra_row + level, t) * sea[t, 0:SUBLANES, :]
                start = tracer_ref[f, t, 0:SUBLANES, :]
                entering.append(speed * jnp.where(speed > 0, row(0, f, t), start))

        def body(k, last, carry, level=level):
            at = rows_at(k)
            fast_e = [speed_ref[level, t, at, :] * mask_e[t, at, :] for t in range(tiles)]
            fast_n = [speed_ref[levels + level, t, at, :] * mask_n[t, at, :] for t in range(tiles)]
            writes, result = [], []
            for f in (level, levels + level):
                here = [tracer_ref[f, t, at, :] for t in range(tiles)]
                beside = from_next(here)
                flux_e = [
                    fast_e[t] * jnp.where(fast_e[t] > 0, here[t], beside[t]) for t in range(tiles)
                ]
                before = from_last(flux_e)
                for t in range(tiles):
                    above = row_above(
                        lambda at, f=f, t=t: tracer_ref[f, t, at, :], k, last, row(1, f, t)
                    )
                    flux_n = fast_n[t] * jnp.where(fast_n[t] > 0, here[t], above)
                    turned = turn(flux_n, 1, 0)
                    below = jnp.where(sublane == 0, carry[len(result)], turned)
                    value = here[t] - ((flux_e[t] - before[t]) + (flux_n - below))
                    writes.append((out, (f, t, at, whole), value))
                    result.append(turned)
            return writes, tuple(result)

        in_groups(body, tuple(entering))
    spread_fields(rows, row_total, field_ref, base_u, base_v, third, force, push_x, push_y,
                  turn_a, turn_b)


def spread(ref, i, count, *lead):
    return ref[(*lead, pl.ds(i, SUBLANES, stride=count), slice(None))]


def wrap(ref, count, lanes=slice(None)):
    ref[0, :, lanes] = turn(ref[count, :, lanes], 1, 0)
    ref[count + 1, :, lanes] = turn(ref[1, :, lanes], -1, 0)


def spread_fields(rows, row_total, field_ref, base_u, base_v, third, force, push_x, push_y,
                  turn_a, turn_b):
    tiles = field_ref.shape[1]
    count = sublane_rows(rows)
    lane, sublane = lane_ids(), sublane_ids()
    lat = lax.axis_index("lat")

    def body(i):
        per_tile = [[spread(field_ref, i, count, f, t) for f in range(ICE)] for t in range(tiles)]
        extra = []
        for f in range(ICE):
            low, high = per_tile[0][f], per_tile[-1][f]
            middle = turn(jnp.where(lane < LANES // 2, high, low), 48)
            x = jnp.where(lane < 32, low, middle)
            extra.append(jnp.where(lane >= 64, turn(high, -24), x))
        writes = []
        for t, fields in enumerate(per_tile + [extra]):
            u0, v0, strength, covered, drive_x, drive_y = fields
            writes.append((base_u, (i + 1, slice(None), cut(t)), u0))
            writes.append((base_v, (i + 1, slice(None), cut(t)), v0))
            writes.append((third, (i, slice(None), cut(t)), covered * (1.0 / 3.0)))
            writes.append((force, (i, slice(None), cut(t)), strength * covered * (1.0 / 12.0)))
            writes.append((push_x, (i, slice(None), cut(t)), 0.5 * drive_x))
            writes.append((push_y, (i, slice(None), cut(t)), 0.5 * drive_y))
        y = lat * rows - HALO + sublane * count + i
        y = jnp.where(y >= row_total, 2 * row_total - 1 - y, y)
        coriolis = 0.5 * (2 * y + 1 - row_total).astype(F32) / row_total
        turning = 0.5 * coriolis
        scale = 3.0 / (DIAGONAL * DIAGONAL + turning * turning)
        writes.append((turn_a, (i,), DIAGONAL * scale))
        writes.append((turn_b, (i,), turning * scale))
        return writes

    in_groups_of(3, count, body)
    wrap(base_u, count)
    wrap(base_v, count)


def advect(tracers, speeds, sea, halo, fields, levels, row_total):
    tiles, rows = sea.shape[:2]
    count = sublane_rows(rows)
    wide = LANES * (tiles + 1)
    looped = resident(count + 2, SUBLANES, wide)
    plain = resident(count, SUBLANES, wide)
    narrow = resident(count, SUBLANES, LANES)
    return pl.pallas_call(
        lambda *refs: advect_kernel(levels, row_total, *refs),
        in_specs=[VMEM_SPEC] * 5,
        out_specs=[VMEM_SPEC] * 9,
        out_shape=[
            resident(*tracers.shape), looped, looped, plain, plain, plain, plain, narrow, narrow,
        ],
        scratch_shapes=[pltpu.VMEM((tiles, rows, LANES), F32)] * 2,
        name="advect",
        compiler_params=pltpu.CompilerParams(vmem_limit_bytes=8 << 20),
        cost_estimate=pl.CostEstimate(flops=30000000, bytes_accessed=16 << 20, transcendentals=0),
    )(*[in_vmem(a) for a in (tracers, speeds, sea, halo, fields)])


def ice_kernel(levels, rows, *refs):
    (covered_in, tracers_in, speeds_in, inter_own, intra_own, inter_in, intra_in,
     base_u, base_v, third, force, push_x, push_y, turn_a, turn_b,
     temp_out, salt_out, u_out, v_out,
     moved, done, vel_u, vel_v, str_a, str_b, str_c,
     third_x, force_x, push_x_x, push_y_x, edges,
     out_sem, vel_sem) = refs
    tiles = tracers_in.shape[1]
    count = sublane_rows(rows)
    tracers = 2 * levels
    lane = lane_ids()
    own = pl.ds(HALO, rows)
    wide = tiles + 1
    whole = slice(None)

    even = on_even_lon()

    def sides(inter, intra):
        return jnp.where(even, inter, intra), jnp.where(even, intra, inter)

    def edge_fluxes(k):
        at, put = tile_rows(k + 1), tile_rows(k)
        west, east_side = sides(inter_in[at, :], intra_in[at, :])
        mine_w, mine_e = sides(inter_own[at, :], intra_own[at, :])
        speed = turn(west, -2 * tracers)
        inflow = speed * jnp.where(speed > 0, west, mine_w) * turn(mine_w, -2 * tracers)
        speed = turn(mine_e, -2 * tracers)
        outflow = speed * jnp.where(speed > 0, mine_e, east_side) * turn(east_side, -2 * tracers)
        flux = jnp.where(lane % 2 == TRACER_LANE % 2, inflow, turn(outflow, -1))
        return [(edges, (put, whole), flux)]

    straight(rows // SUBLANES, edge_fluxes, 8, 24)

    def fixed(f, put):
        flux = turn(edges[put, :], -(TRACER_LANE + 2 * f))
        low = tracers_in[f, 0, put, :] + jnp.where(lane == 0, flux, 0.0)
        return low, tracers_in[f, tiles - 1, put, :] - jnp.where(lane == LANES - 1, flux, 0.0)

    def insert(i):
        west, east_side = sides(spread(inter_in, i, count), spread(intra_in, i, count))
        writes = []
        targets = (
            (base_u, vel_u, 1, tiles, 1.0), (base_v, vel_v, 1, tiles, 1.0),
            (force, force_x, 0, 0, 1.0), (third, third_x, 0, 0, 1.0 / 3.0),
            (push_x, push_x_x, 0, 0, 0.5), (push_y, push_y_x, 0, 0, 0.5),
        )
        beyond = []
        for f in range(ICE):
            start = HALO * f + 2 * HALO
            x = jnp.where((lane >= start) & (lane < start + HALO), west, east_side)
            beyond.append(turn(x, 104 - HALO * f))
        beyond[2] = beyond[2] * beyond[3] * (1.0 / 12.0)
        for x, (source, target, shift, t, factor) in zip(beyond, targets):
            x = x if factor == 1.0 else x * factor
            x = jnp.where(lane >= 104, x, source[i + shift, :, cut(tiles)])
            writes.append((target, (i + shift, whole, cut(t)), x))
        own_lanes = slice(0, LANES * tiles)
        for source, target in ((base_u, vel_u), (base_v, vel_v)):
            writes.append((target, (i + 1, whole, own_lanes), source[i + 1, :, own_lanes]))
        for ref in (str_a, str_b, str_c):
            writes.append((ref, (i + 1,), jnp.zeros(ref.shape[1:], F32)))
        return writes

    straight(count, insert, 3, 17)
    wrap(vel_u, count)
    wrap(vel_v, count)

    def constant(ref, extra, i, t):
        return ref[i, :, cut(t)] if t < tiles else extra[i]

    def load_once(ref, name, seen, j, t):
        if (name, j, t) not in seen:
            seen[name, j, t] = ref[(j, whole) if t is None else (j, whole, cut(t))]
        return seen[name, j, t]

    share = rows // SUBLANES // SUBCYCLES
    items = [(k, f) for k in range(share) for f in range(tracers)]

    def fix(step, i):
        for k, f in items[len(items) * i // count : len(items) * (i + 1) // count]:
            put = pl.ds(pl.multiple_of((step * share + k) * SUBLANES, SUBLANES), SUBLANES)
            low, high = fixed(f, put)
            moved[f, 0, put, :] = low
            moved[f, tiles - 1, put, :] = high

    def fixed_rows(step):
        part = pl.ds(pl.multiple_of(step * share * SUBLANES, SUBLANES), share * SUBLANES)
        return [
            pltpu.make_async_copy(
                moved.at[pl.ds(levels * n + 1, levels - 1), t, part, :],
                out.at[pl.ds(1, levels - 1), part, pl.ds(LANES * t, LANES)],
                out_sem.at[step, n, t],
            )
            for n, out in enumerate((temp_out, salt_out))
            for t in range(tiles)
        ]

    def strain_stress(step):
        seen = {}
        for i in range(count):
            for t in range(wide):
                u, v = (load_once(r, n, seen, i + 1, t) for n, r in enumerate((vel_u, vel_v)))
                dudx, dvdx = turn(u, -1) - turn(u, 1), turn(v, -1) - turn(v, 1)
                dudy, dvdy = (
                    load_once(r, n, seen, i + 2, t) - load_once(r, n, seen, i, t)
                    for n, r in enumerate((vel_u, vel_v))
                )
                div, ten, shr = dudx + dvdy, dudx - dvdy, dudy + dvdx
                square = div * div + 0.25 * (ten * ten + shr * shr) + 1.0
                base = constant(force, force_x, i, t)
                zeta = base * lax.rsqrt(square)
                quarter = 0.25 * zeta
                even = zeta * div - base
                odd = quarter * ten
                keep = constant(third, third_x, i, t)
                for ref, new in (
                    (str_a, even + odd), (str_b, even - odd), (str_c, quarter * shr)
                ):
                    ref[i + 1, :, cut(t)] = new + keep * ref[i + 1, :, cut(t)]
            fix(step, i)
        wrap(str_b, count)
        wrap(str_c, count)

    def momentum():
        seen = {}
        for i in range(count):
            ar, br = turn_a[i], turn_b[i]
            for t in range(wide):
                a = str_a[i + 1, :, cut(t)]
                s = load_once(str_c, 2, seen, i + 1, t)
                fx = (turn(a, -1) - turn(a, 1)) + (
                    load_once(str_c, 2, seen, i + 2, t) - load_once(str_c, 2, seen, i, t)
                )
                fy = (turn(s, -1) - turn(s, 1)) + (
                    load_once(str_b, 1, seen, i + 2, t) - load_once(str_b, 1, seen, i, t)
                )
                ru = (vel_u[i + 1, :, cut(t)] + constant(push_x, push_x_x, i, t)) + fx
                rv = (vel_v[i + 1, :, cut(t)] + constant(push_y, push_y_x, i, t)) + fy
                keep = constant(third, third_x, i, t)
                vel_u[i + 1, :, cut(t)] = (ar * ru + br * rv) * keep
                vel_v[i + 1, :, cut(t)] = (ar * rv - br * ru) * keep
        wrap(vel_u, count)
        wrap(vel_v, count)

    def subcycle(step, carry):
        strain_stress(step)
        for copy in fixed_rows(step):
            copy.start()
        momentum()
        return carry

    lax.fori_loop(0, SUBCYCLES, subcycle, 0)

    def gather(i):
        writes = []
        for n, ref in enumerate((vel_u, vel_v)):
            borders = ref[i + 1, :, cut(tiles)]
            middle, outer = turn(borders, -48), turn(borders, 24)
            low, high = ref[i + 1, :, cut(0)], ref[i + 1, :, cut(tiles - 1)]
            low = jnp.where(lane < HALO, borders, jnp.where(lane >= LANES - HALO, middle, low))
            high = jnp.where(lane < HALO, middle, jnp.where(lane >= LANES - HALO, outer, high))
            put = pl.ds(i, SUBLANES, stride=count)
            writes.append((done, (n, 0, put, whole), low))
            writes.append((done, (n, tiles - 1, put, whole), high))
        return writes

    straight(count, gather, 6, 51)
    finals = []
    for n, out in enumerate((u_out, v_out)):
        for t in range(tiles):
            finals.append(
                pltpu.make_async_copy(
                    done.at[n, t, own, :], out.at[:, pl.ds(LANES * t, LANES)], vel_sem.at[n, t]
                )
            )
            finals[-1].start()

    def warm(k):
        put, at = tile_rows(k), tile_rows(k + 1)
        writes = []
        for t in range(tiles):
            sst, sss = moved[0, t, put, :], moved[levels, t, put, :]
            slip_u = done[0, t, at, :] - speeds_in[0, t, put, :]
            slip_v = done[1, t, at, :] - speeds_in[levels, t, put, :]
            heat = HEAT_RATE * covered_in[3, t, at, :] * (1.0 + (slip_u * slip_u + slip_v * slip_v))
            heat = heat * (sst + FREEZE_SLOPE * sss)
            writes.append((moved, (0, t, put, whole), sst - heat))
            writes.append((moved, (levels, t, put, whole), sss - SALT_RATE * heat))
        return writes

    straight(rows // SUBLANES, warm, 6, 24)
    for n, out in enumerate((temp_out, salt_out)):
        for t in range(tiles):
            finals.append(
                pltpu.make_async_copy(
                    moved.at[levels * n, t],
                    out.at[0, :, pl.ds(LANES * t, LANES)],
                    out_sem.at[SUBCYCLES, n, t],
                )
            )
            finals[-1].start()
    for step in range(SUBCYCLES):
        finals += fixed_rows(step)
    for copy in finals:
        copy.wait()


def ice_and_edges(operands, levels, rows, cols):
    tiles = cols // LANES
    count = sublane_rows(rows)
    deep = jax.ShapeDtypeStruct((levels, rows, cols), F32)
    flat = jax.ShapeDtypeStruct((rows, cols), F32)
    looped = pltpu.VMEM((count + 2, SUBLANES, LANES * (tiles + 1)), F32)
    narrow = pltpu.VMEM((count, SUBLANES, LANES), F32)
    return pl.pallas_call(
        lambda *refs: ice_kernel(levels, rows, *refs),
        in_specs=[VMEM_SPEC] * len(operands),
        out_specs=[ANY_SPEC] * 4,
        out_shape=[deep, deep, flat, flat],
        scratch_shapes=[
            pltpu.VMEM((2 * levels, tiles, rows, LANES), F32),
            pltpu.VMEM((2, tiles, count * SUBLANES, LANES), F32),
            looped, looped, looped, looped, looped,
            narrow, narrow, narrow, narrow, pltpu.VMEM((rows, LANES), F32),
            pltpu.SemaphoreType.DMA((SUBCYCLES + 1, 2, tiles)),
            pltpu.SemaphoreType.DMA((2, tiles)),
        ],
        name="ice",
        compiler_params=pltpu.CompilerParams(vmem_limit_bytes=20 << 20),
        cost_estimate=pl.CostEstimate(flops=60000000, bytes_accessed=16 << 20, transcendentals=0),
    )(*[in_vmem(a) for a in operands])


def per_device(*arrays):
    levels, rows, cols = arrays[0].shape
    lon_count, lat_count = lax.axis_size("lon"), lax.axis_size("lat")
    assert cols == 2 * LANES and rows % (SUBLANES * SUBCYCLES) == 0
    assert lat_count % 2 == 0 and lon_count % 2 == 0
    height = -(-(HALO * ICE + 3 * levels) // SUBLANES) * SUBLANES

    def place(lat, lon):
        return lon * lat_count + lat

    first_pairs, second_pairs = [], []
    for lon in range(lon_count):
        for lat in range(lat_count):
            first_pairs.append((place(lat, lon), place(lat ^ 1, lon)))
            if lat == lat_count - 1:
                second_pairs.append((place(lat, lon), place(lat, lon_count - 1 - lon)))
            elif lat:
                second_pairs.append((place(lat, lon), place(((lat + 1) ^ 1) - 1, lon)))
    inter_pairs = [(i, (i - 1 if i % 2 == 0 else i + 1) % lon_count) for i in range(lon_count)]
    intra_pairs = [(i, i ^ 1) for i in range(lon_count)]
    first, second = pack_rows(arrays, levels, rows, cols, height)
    first = lax.ppermute(first, ("lon", "lat"), first_pairs)
    speeds, sea, fields, east_ice, west_ice = prepare_surface(arrays, levels, rows, cols)
    second, east_ice = lax.optimization_barrier((second, east_ice))
    second = lax.ppermute(second, ("lon", "lat"), second_pairs)
    tracers, inter, intra = pack_columns(
        arrays[0], arrays[1], speeds, sea, east_ice, west_ice, levels
    )
    halo, fields, inter, intra = merge_halo(first, second, fields, inter, intra, levels, rows)
    intra_in = lax.ppermute(intra, "lon", intra_pairs)
    inter_in = lax.ppermute(inter, "lon", inter_pairs)
    moved, *state = advect(tracers, speeds, sea, halo, fields, levels, rows * lat_count)
    return ice_and_edges(
        [fields, moved, speeds, inter, intra, inter_in, intra_in, *state], levels, rows, cols
    )


def solution(mesh):
    deep, flat = P(None, "lat", "lon"), P("lat", "lon")
    return jax.shard_map(
        per_device,
        mesh=mesh,
        in_specs=(deep,) * 4 + (flat,) * 7,
        out_specs=(deep, deep, flat, flat),
        check_vma=False,
    )
```

```python
import jax
import jax.numpy as jnp
from jax import lax
from jax.experimental import pallas as pl
from jax.experimental.pallas import tpu as pltpu
from jax.sharding import PartitionSpec as P

SUBCYCLES = 4
HEAT_RATE = 0.1
SALT_RATE = 0.5
FREEZE_SLOPE = 0.054
DIAGONAL = 1.5
HALO = 2 * SUBCYCLES
LANES = 128
SUBLANES = 8
ICE = 6
FOLD_SIGN = (-1.0, -1.0, 1.0, 1.0, -1.0, -1.0)
TRACER_LANE = 64
F32 = jnp.float32


def lane_ids():
    return lax.broadcasted_iota(jnp.int32, (SUBLANES, LANES), 1)


def sublane_ids():
    return lax.broadcasted_iota(jnp.int32, (SUBLANES, LANES), 0)


def turn(x, shift, axis=1):
    shift = shift % x.shape[axis]
    return pltpu.roll(x, shift, axis) if shift else x


def cut(t):
    return slice(LANES * t, LANES * (t + 1))


def ice_fields(land, ice, u, v, pressure, wind_x, wind_y, ocean_u, ocean_v):
    covered = land.astype(F32) * ice.astype(F32)
    return (u * covered, v * covered, pressure, covered, wind_x + ocean_u, wind_y + ocean_v)


def east_columns(fields, lane):
    packed = jnp.zeros((SUBLANES, LANES), F32)
    for f, tile in enumerate(fields):
        start = HALO * f + 2 * HALO
        moved = turn(tile, start - (LANES - HALO))
        packed = jnp.where((lane >= start) & (lane < start + HALO), moved, packed)
    return packed


def west_columns(fields, lane):
    packed = jnp.zeros((SUBLANES, LANES), F32)
    for f, tile in enumerate(fields):
        start = HALO * f
        packed = jnp.where((lane >= start) & (lane < start + HALO), turn(tile, start), packed)
    return packed


def sublane_rows(rows):
    return (rows + 2 * HALO) // SUBLANES | 1


class Trailing:
    def __init__(self, window):
        self.window, self.waiting = window, []

    def add(self, writes):
        self.waiting.append(writes)
        while len(self.waiting) > self.window:
            self.flush(self.waiting.pop(0))

    def finish(self):
        for writes in self.waiting:
            self.flush(writes)

    @staticmethod
    def flush(writes):
        for ref, where, value in writes:
            ref[where] = value


def straight(steps, body, window, size):
    size = max(c for c in range(1, size + 1) if steps % c == 0)

    def run(n, carry):
        pending = Trailing(window)
        for j in range(size):
            pending.add(body(n * size + j))
        pending.finish()
        return carry

    if size == steps:
        run(0, 0)
    else:
        lax.fori_loop(0, steps // size, run, 0)


def in_groups_of(group, steps, body, size=0):
    size = max(c for c in range(1, (size or group) + 1) if steps % c == 0)

    def run(n, carry):
        for start in range(0, size, group):
            writes = []
            for j in range(start, min(start + group, size)):
                writes += body(n * size + j)
            Trailing.flush(writes)
        return carry

    lax.fori_loop(0, steps // size, run, 0)


def tile_rows(k, offset=0):
    start = k * SUBLANES
    if not isinstance(k, int):
        start = pl.multiple_of(start, SUBLANES)
    return pl.ds(start + offset if offset else start, SUBLANES)


def rows_kernel(levels, *refs):
    tops, bottoms = refs[0:12], refs[12:24]
    second_ref, first_ref = refs[24:26]
    even = lax.rem(lax.axis_index("lat"), 2) == 0

    def message(group, row, northward):
        land, ice, u, v, pressure, wind_x, wind_y, east, north, temp, salt = (
            r for r in group[:11]
        )
        fields = ice_fields(
            land[...], ice[...], u[...], v[...], pressure[...], wind_x[...], wind_y[...],
            east[0], north[0],
        )
        sea = land[row : row + 1, :].astype(F32)
        parts = list(fields) + [temp[:, row, :], salt[:, row, :]]
        if northward:
            parts.append(north[:, row, :] * sea)
        else:
            parts.append(jnp.broadcast_to(sea, (levels, sea.shape[1])))
        return parts

    top = message(tops, SUBLANES - 1, True)
    bottom = message(bottoms, 0, False)
    at = 0
    for t, b in zip(top, bottom):
        size = t.shape[0]
        first_ref[at : at + size, :] = jnp.where(even, t, b)
        second_ref[at : at + size, :] = jnp.where(even, b, t)
        at += size
    pad = first_ref.shape[0] - at
    if pad:
        first_ref[at:, :] = jnp.zeros((pad, first_ref.shape[1]), F32)
        second_ref[at:, :] = jnp.zeros((pad, second_ref.shape[1]), F32)


def pack_rows(arrays, levels, rows, cols, height):
    temp, salt, east, north, land, ice, u, v, pressure, wind_x, wind_y = arrays
    operands = [land, ice, u, v, pressure, wind_x, wind_y, east, north, temp, salt, land]
    last = rows // SUBLANES - 1

    def spec(array, block, count):
        if array.ndim == 2:
            return pl.BlockSpec((SUBLANES, cols), lambda _: (block, 0))
        return pl.BlockSpec((count, SUBLANES, cols), lambda _: (0, block, 0))

    counts = [1] * 7 + [1, levels, levels, levels, 1]
    specs = [spec(a, last, c) for a, c in zip(operands, counts)]
    specs += [spec(a, 0, c) for a, c in zip(operands, counts)]
    out = jax.ShapeDtypeStruct((height, cols), F32)
    return pl.pallas_call(
        lambda *refs: rows_kernel(levels, *refs),
        grid=(1,),
        in_specs=specs,
        out_specs=[pl.BlockSpec((height, cols), lambda _: (0, 0))] * 2,
        out_shape=[out, out],
        name="edge_rows",
        compiler_params=pltpu.CompilerParams(vmem_limit_bytes=8 << 20),
        cost_estimate=pl.CostEstimate(flops=100000, bytes_accessed=1 << 20, transcendentals=0),
    )(*[in_hbm(a) for a in operands + operands])


def on_even_lon():
    return lax.rem(lax.axis_index("lon"), 2) == 0


def columns_kernel(levels, land, ice, u, v, pressure, wind_x, wind_y, east, north, temp, salt,
                   tracer_out, speed_out, sea_out, field_out, inter_out, intra_out, sem):
    lane = lane_ids()
    even = on_even_lon()
    rows = sea_out.shape[1]
    tiles = sea_out.shape[0]
    tracers = 2 * levels
    first_lane = TRACER_LANE
    mask_lane = TRACER_LANE + 2 * tracers

    copies = []
    for n, ref in enumerate((temp, salt, east, north)):
        out = tracer_out if n < 2 else speed_out
        for t in range(tiles):
            copies.append(
                pltpu.make_async_copy(
                    ref.at[..., pl.ds(LANES * t, LANES)],
                    out.at[pl.ds(levels * (n % 2), levels), t],
                    sem.at[n, t],
                )
            )
    for copy in copies:
        copy.start()

    whole = slice(None)

    def messages(put, eastward, westward):
        return [
            (inter_out, (put, whole), jnp.where(even, westward, eastward)),
            (intra_out, (put, whole), jnp.where(even, eastward, westward)),
        ]

    def packed(put):
        inter, intra = inter_out[put, :], intra_out[put, :]
        return jnp.where(even, intra, inter), jnp.where(even, inter, intra)

    def ice_part(k):
        at, put = tile_rows(k), tile_rows(k + 1)
        writes, fields = [], []
        for t in range(tiles):
            c = cut(t)
            fields.append(
                ice_fields(
                    *[r[at, c] for r in (land, ice, u, v, pressure, wind_x, wind_y)],
                    east[0, at, c], north[0, at, c],
                )
            )
            writes.append((sea_out, (t, at, whole), land[at, c].astype(F32)))
            for f in range(ICE):
                writes.append((field_out, (f, t, put, whole), fields[t][f]))
        return writes + messages(
            put, east_columns(fields[-1], lane), west_columns(fields[0], lane)
        )

    in_groups_of(4, rows // SUBLANES, ice_part)

    def tracer_part(k):
        at, put = tile_rows(k), tile_rows(k + 1)
        eastward, westward = packed(put)
        for f in range(tracers):
            ref, l, to = (temp, salt)[f // levels], f % levels, first_lane + 2 * f
            eastward = jnp.where(
                lane == to, turn(ref[l, at, cut(tiles - 1)], to - (LANES - 1)), eastward
            )
            westward = jnp.where(lane == to, turn(ref[l, at, cut(0)], to), westward)
        return messages(put, eastward, westward)

    in_groups_of(12, rows // SUBLANES, tracer_part)

    def speed_part(k):
        at, put = tile_rows(k), tile_rows(k + 1)
        masked = (lane >= mask_lane) & (lane < mask_lane + 2 * tracers)
        speeds = jnp.zeros((SUBLANES, LANES), F32)
        for f in range(levels):
            to = mask_lane + 2 * f
            speeds = jnp.where(
                lane == to, turn(east[f, at, cut(tiles - 1)], to - (LANES - 1)), speeds
            )
        speeds = speeds + turn(speeds, 2 * levels)
        last = land[at, LANES * tiles - 1 : LANES * tiles].astype(F32)
        first = jnp.broadcast_to(land[at, 0:1].astype(F32), (SUBLANES, LANES))
        eastward, westward = packed(put)
        eastward = jnp.where(masked, speeds * last, eastward)
        westward = jnp.where(masked, first, westward)
        return messages(put, eastward, westward)

    in_groups_of(12, rows // SUBLANES, speed_part)
    end = HALO + rows
    blank = jnp.zeros((field_out.shape[2] - end, LANES), F32)
    for t in range(tiles):
        for f in range(ICE):
            field_out[f, t, end:, :] = blank
    for ref in (inter_out, intra_out):
        ref[end:, :] = blank
    for copy in copies:
        copy.wait()


def in_vmem(x):
    return pltpu.with_memory_space_constraint(x, pltpu.VMEM)


def in_hbm(x):
    return pltpu.with_memory_space_constraint(x, pltpu.HBM)


def resident(*shape):
    return pltpu.VMEM(shape, F32)


VMEM_SPEC = pl.BlockSpec(memory_space=pltpu.VMEM)
ANY_SPEC = pl.BlockSpec(memory_space=pl.ANY)


def load_and_pack_columns(arrays, levels, rows, cols):
    temp, salt, east, north, land, ice, u, v, pressure, wind_x, wind_y = arrays
    tiles = cols // LANES
    message = resident(sublane_rows(rows) * SUBLANES, LANES)
    deep = resident(2 * levels, tiles, rows, LANES)
    return pl.pallas_call(
        lambda *refs: columns_kernel(levels, *refs),
        in_specs=[VMEM_SPEC] * 11,
        out_specs=[VMEM_SPEC] * 6,
        out_shape=[
            deep, deep, resident(tiles, rows, LANES),
            resident(ICE, tiles, sublane_rows(rows) * SUBLANES, LANES), message, message,
        ],
        scratch_shapes=[pltpu.SemaphoreType.DMA((4, tiles))],
        name="edge_columns",
        compiler_params=pltpu.CompilerParams(vmem_limit_bytes=4 << 20),
        cost_estimate=pl.CostEstimate(flops=5000000, bytes_accessed=12 << 20, transcendentals=0),
    )(*[in_vmem(a) for a in (land, ice, u, v, pressure, wind_x, wind_y, east, north, temp, salt)])


def halo_kernel(levels, rows, second, first, field_in, inter_in, intra_in,
                halo_ref, field_out, inter_out, intra_out):
    lat = lax.axis_index("lat")
    even = lax.rem(lat, 2) == 0
    top = lat == lax.axis_size("lat") - 1
    lane, sublane = lane_ids(), sublane_ids()
    tiles = field_out.shape[1]
    south_fields, north_fields = [], []
    for f in range(ICE):
        at = slice(HALO * f, HALO * (f + 1))
        north_row, south_row = [], []
        for t in range(tiles):
            cols = slice(LANES * t, LANES * (t + 1))
            mirror = slice(LANES * (tiles - 1 - t), LANES * (tiles - t))
            south = jnp.where(even, second[at, cols], first[at, cols])
            plain = jnp.where(even, first[at, cols], second[at, cols])
            turned = jnp.take_along_axis(second[at, mirror], LANES - 1 - lane, axis=1)
            turned = jnp.take_along_axis(turned, SUBLANES - 1 - sublane, axis=0)
            north = jnp.where(top, turned * FOLD_SIGN[f], plain)
            field_out[f, t, 0:HALO, :] = south
            field_out[f, t, rows + HALO : rows + 2 * HALO, :] = north
            south_row.append(south)
            north_row.append(north)
        south_fields.append(south_row)
        north_fields.append(north_row)
    rest = slice(HALO * ICE, first.shape[0])
    for t in range(tiles):
        c = cut(t)
        halo_ref[0, t] = jnp.where(even, second[rest, c], first[rest, c])
        halo_ref[1, t] = jnp.where(top, 0.0, jnp.where(even, first[rest, c], second[rest, c]))
    for at, fields in ((0, south_fields), (rows + HALO, north_fields)):
        eastward = east_columns([f[-1] for f in fields], lane)
        westward = west_columns([f[0] for f in fields], lane)
        inter_out[at : at + HALO, :] = jnp.where(on_even_lon(), westward, eastward)
        intra_out[at : at + HALO, :] = jnp.where(on_even_lon(), eastward, westward)


def merge_halo(second, first, fields, inter_msg, intra_msg, levels, rows):
    height, cols = first.shape
    return pl.pallas_call(
        lambda *refs: halo_kernel(levels, rows, *refs),
        in_specs=[VMEM_SPEC] * 5,
        out_specs=[VMEM_SPEC] * 4,
        out_shape=[
            resident(2, cols // LANES, height - HALO * ICE, LANES), resident(*fields.shape),
            resident(*inter_msg.shape), resident(*intra_msg.shape),
        ],
        input_output_aliases={2: 1, 3: 2, 4: 3},
        name="halo_rows",
        compiler_params=pltpu.CompilerParams(vmem_limit_bytes=8 << 20),
        cost_estimate=pl.CostEstimate(flops=100000, bytes_accessed=1 << 19, transcendentals=0),
    )(second, first, in_vmem(fields), in_vmem(inter_msg), in_vmem(intra_msg))


def advect_kernel(levels, row_total, tracer_ref, speed_ref, sea, halo, field_ref,
                  out, base_u, base_v, third, force, push_x, push_y, turn_a, turn_b,
                  mask_e, mask_n):
    tiles, rows = sea.shape[:2]
    count = rows // SUBLANES
    group = next(c for c in (12, 8, 4, 2) if count % c == 0)
    lane, sublane = lane_ids(), sublane_ids()
    extra_row = 2 * levels
    whole = slice(None)

    def rows_at(k, offset=0):
        start = pl.multiple_of(k * SUBLANES, SUBLANES)
        return pl.ds(start + offset if offset else start, SUBLANES)

    def row(side, index, t):
        return jnp.broadcast_to(halo[side, t, index : index + 1, :], (SUBLANES, LANES))

    def from_next(values):
        turned = [turn(v, -1) for v in values]
        return [
            jnp.where(lane == LANES - 1, turned[t + 1], turned[t]) if t + 1 < tiles else turned[t]
            for t in range(tiles)
        ]

    def from_last(values):
        turned = [turn(v, 1) for v in values]
        return [jnp.where(lane == 0, turned[t - 1], turned[t]) for t in range(tiles)]

    def in_groups(body, carry):
        def some(start, carry, last):
            writes = []
            for j in range(group):
                more, carry = body(start + j, last and j == group - 1, carry)
                writes += more
            for ref, where, value in writes:
                ref[where] = value
            return carry

        groups = count // group
        carry = lax.fori_loop(0, groups - 1, lambda n, c: some(n * group, c, False), carry)
        return some((groups - 1) * group, carry, True)

    def row_above(load, k, last, past):
        if not last:
            return load(rows_at(k, 1))
        return jnp.where(sublane == SUBLANES - 1, past, turn(load(rows_at(k)), -1, 0))

    def masks(k, last, carry):
        here = [sea[t, rows_at(k), :] for t in range(tiles)]
        beside = from_next(here)
        writes = []
        for t in range(tiles):
            above = row_above(lambda at, t=t: sea[t, at, :], k, last, row(1, extra_row, t))
            face = here[t] * beside[t]
            if t == tiles - 1:
                face = jnp.where(lane == LANES - 1, 0.0, face)
            writes.append((mask_e, (t, rows_at(k), whole), face))
            writes.append((mask_n, (t, rows_at(k), whole), here[t] * above))
        return writes, carry

    in_groups(masks, 0)
    for level in range(levels):
        entering = []
        for f in (level, levels + level):
            for t in range(tiles):
                speed = row(0, extra_row + level, t) * sea[t, 0:SUBLANES, :]
                start = tracer_ref[f, t, 0:SUBLANES, :]
                entering.append(speed * jnp.where(speed > 0, row(0, f, t), start))

        def body(k, last, carry, level=level):
            at = rows_at(k)
            fast_e = [speed_ref[level, t, at, :] * mask_e[t, at, :] for t in range(tiles)]
            fast_n = [speed_ref[levels + level, t, at, :] * mask_n[t, at, :] for t in range(tiles)]
            writes, result = [], []
            for f in (level, levels + level):
                here = [tracer_ref[f, t, at, :] for t in range(tiles)]
                beside = from_next(here)
                flux_e = [
                    fast_e[t] * jnp.where(fast_e[t] > 0, here[t], beside[t]) for t in range(tiles)
                ]
                before = from_last(flux_e)
                for t in range(tiles):
                    above = row_above(
                        lambda at, f=f, t=t: tracer_ref[f, t, at, :], k, last, row(1, f, t)
                    )
                    flux_n = fast_n[t] * jnp.where(fast_n[t] > 0, here[t], above)
                    turned = turn(flux_n, 1, 0)
                    below = jnp.where(sublane == 0, carry[len(result)], turned)
                    value = here[t] - ((flux_e[t] - before[t]) + (flux_n - below))
                    writes.append((out, (f, t, at, whole), value))
                    result.append(turned)
            return writes, tuple(result)

        in_groups(body, tuple(entering))
    spread_fields(rows, row_total, field_ref, base_u, base_v, third, force, push_x, push_y,
                  turn_a, turn_b)


def spread(ref, i, count, *lead):
    return ref[(*lead, pl.ds(i, SUBLANES, stride=count), slice(None))]


def wrap(ref, count, lanes=slice(None)):
    ref[0, :, lanes] = turn(ref[count, :, lanes], 1, 0)
    ref[count + 1, :, lanes] = turn(ref[1, :, lanes], -1, 0)


def spread_fields(rows, row_total, field_ref, base_u, base_v, third, force, push_x, push_y,
                  turn_a, turn_b):
    tiles = field_ref.shape[1]
    count = sublane_rows(rows)
    lane, sublane = lane_ids(), sublane_ids()
    lat = lax.axis_index("lat")

    def body(i):
        per_tile = [[spread(field_ref, i, count, f, t) for f in range(ICE)] for t in range(tiles)]
        extra = []
        for f in range(ICE):
            low, high = per_tile[0][f], per_tile[-1][f]
            middle = turn(jnp.where(lane < LANES // 2, high, low), 48)
            x = jnp.where(lane < 32, low, middle)
            extra.append(jnp.where(lane >= 64, turn(high, -24), x))
        writes = []
        for t, fields in enumerate(per_tile + [extra]):
            u0, v0, strength, covered, drive_x, drive_y = fields
            writes.append((base_u, (i + 1, slice(None), cut(t)), u0))
            writes.append((base_v, (i + 1, slice(None), cut(t)), v0))
            writes.append((third, (i, slice(None), cut(t)), covered * (1.0 / 3.0)))
            writes.append((force, (i, slice(None), cut(t)), strength * covered * (1.0 / 12.0)))
            writes.append((push_x, (i, slice(None), cut(t)), 0.5 * drive_x))
            writes.append((push_y, (i, slice(None), cut(t)), 0.5 * drive_y))
        y = lat * rows - HALO + sublane * count + i
        y = jnp.where(y >= row_total, 2 * row_total - 1 - y, y)
        coriolis = 0.5 * (2 * y + 1 - row_total).astype(F32) / row_total
        turning = 0.5 * coriolis
        scale = 3.0 / (DIAGONAL * DIAGONAL + turning * turning)
        writes.append((turn_a, (i,), DIAGONAL * scale))
        writes.append((turn_b, (i,), turning * scale))
        return writes

    in_groups_of(3, count, body, 17)
    wrap(base_u, count)
    wrap(base_v, count)


def advect(tracers, speeds, sea, halo, fields, levels, row_total):
    tiles, rows = sea.shape[:2]
    count = sublane_rows(rows)
    wide = LANES * (tiles + 1)
    looped = resident(count + 2, SUBLANES, wide)
    plain = resident(count, SUBLANES, wide)
    narrow = resident(count, SUBLANES, LANES)
    return pl.pallas_call(
        lambda *refs: advect_kernel(levels, row_total, *refs),
        in_specs=[VMEM_SPEC] * 5,
        out_specs=[VMEM_SPEC] * 9,
        out_shape=[
            resident(*tracers.shape), looped, looped, plain, plain, plain, plain, narrow, narrow,
        ],
        scratch_shapes=[pltpu.VMEM((tiles, rows, LANES), F32)] * 2,
        name="advect",
        compiler_params=pltpu.CompilerParams(vmem_limit_bytes=8 << 20),
        cost_estimate=pl.CostEstimate(flops=30000000, bytes_accessed=16 << 20, transcendentals=0),
    )(*[in_vmem(a) for a in (tracers, speeds, sea, halo, fields)])


def ice_kernel(levels, rows, *refs):
    (covered_in, tracers_in, speeds_in, inter_own, intra_own, inter_in, intra_in,
     base_u, base_v, third, force, push_x, push_y, turn_a, turn_b,
     temp_out, salt_out, u_out, v_out,
     moved, done, vel_u, vel_v, str_a, str_b, str_c,
     third_x, force_x, push_x_x, push_y_x, edges,
     out_sem, vel_sem) = refs
    tiles = tracers_in.shape[1]
    count = sublane_rows(rows)
    tracers = 2 * levels
    lane = lane_ids()
    own = pl.ds(HALO, rows)
    wide = tiles + 1
    whole = slice(None)

    even = on_even_lon()

    def sides(inter, intra):
        return jnp.where(even, inter, intra), jnp.where(even, intra, inter)

    def edge_fluxes(k):
        at, put = tile_rows(k + 1), tile_rows(k)
        west, east_side = sides(inter_in[at, :], intra_in[at, :])
        mine_w, mine_e = sides(inter_own[at, :], intra_own[at, :])
        speed = turn(west, -2 * tracers)
        inflow = speed * jnp.where(speed > 0, west, mine_w) * turn(mine_w, -2 * tracers)
        speed = turn(mine_e, -2 * tracers)
        outflow = speed * jnp.where(speed > 0, mine_e, east_side) * turn(east_side, -2 * tracers)
        flux = jnp.where(lane % 2 == TRACER_LANE % 2, inflow, turn(outflow, -1))
        return [(edges, (put, whole), flux)]

    straight(rows // SUBLANES, edge_fluxes, 8, 24)

    def fixed(f, put):
        flux = turn(edges[put, :], -(TRACER_LANE + 2 * f))
        low = tracers_in[f, 0, put, :] + jnp.where(lane == 0, flux, 0.0)
        return low, tracers_in[f, tiles - 1, put, :] - jnp.where(lane == LANES - 1, flux, 0.0)

    def insert(i):
        west, east_side = sides(spread(inter_in, i, count), spread(intra_in, i, count))
        writes = []
        targets = (
            (base_u, vel_u, 1, tiles, 1.0), (base_v, vel_v, 1, tiles, 1.0),
            (force, force_x, 0, 0, 1.0), (third, third_x, 0, 0, 1.0 / 3.0),
            (push_x, push_x_x, 0, 0, 0.5), (push_y, push_y_x, 0, 0, 0.5),
        )
        beyond = []
        for f in range(ICE):
            start = HALO * f + 2 * HALO
            x = jnp.where((lane >= start) & (lane < start + HALO), west, east_side)
            beyond.append(turn(x, 104 - HALO * f))
        beyond[2] = beyond[2] * beyond[3] * (1.0 / 12.0)
        for x, (source, target, shift, t, factor) in zip(beyond, targets):
            x = x if factor == 1.0 else x * factor
            x = jnp.where(lane >= 104, x, source[i + shift, :, cut(tiles)])
            writes.append((target, (i + shift, whole, cut(t)), x))
        own_lanes = slice(0, LANES * tiles)
        for source, target in ((base_u, vel_u), (base_v, vel_v)):
            writes.append((target, (i + 1, whole, own_lanes), source[i + 1, :, own_lanes]))
        for ref in (str_a, str_b, str_c):
            writes.append((ref, (i + 1,), jnp.zeros(ref.shape[1:], F32)))
        return writes

    straight(count, insert, 3, 17)
    wrap(vel_u, count)
    wrap(vel_v, count)

    def constant(ref, extra, i, t):
        return ref[i, :, cut(t)] if t < tiles else extra[i]

    def load_once(ref, name, seen, j, t):
        if (name, j, t) not in seen:
            seen[name, j, t] = ref[(j, whole) if t is None else (j, whole, cut(t))]
        return seen[name, j, t]

    share = rows // SUBLANES // SUBCYCLES
    items = [(k, f) for k in range(share) for f in range(tracers)]

    def fix(step, i):
        for k, f in items[len(items) * i // count : len(items) * (i + 1) // count]:
            put = pl.ds(pl.multiple_of((step * share + k) * SUBLANES, SUBLANES), SUBLANES)
            low, high = fixed(f, put)
            moved[f, 0, put, :] = low
            moved[f, tiles - 1, put, :] = high

    def fixed_rows(step):
        part = pl.ds(pl.multiple_of(step * share * SUBLANES, SUBLANES), share * SUBLANES)
        return [
            pltpu.make_async_copy(
                moved.at[pl.ds(levels * n + 1, levels - 1), t, part, :],
                out.at[pl.ds(1, levels - 1), part, pl.ds(LANES * t, LANES)],
                out_sem.at[step, n, t],
            )
            for n, out in enumerate((temp_out, salt_out))
            for t in range(tiles)
        ]

    def strain_stress(step):
        seen = {}
        for i in range(count):
            for t in range(wide):
                u, v = (load_once(r, n, seen, i + 1, t) for n, r in enumerate((vel_u, vel_v)))
                dudx, dvdx = turn(u, -1) - turn(u, 1), turn(v, -1) - turn(v, 1)
                dudy, dvdy = (
                    load_once(r, n, seen, i + 2, t) - load_once(r, n, seen, i, t)
                    for n, r in enumerate((vel_u, vel_v))
                )
                div, ten, shr = dudx + dvdy, dudx - dvdy, dudy + dvdx
                square = div * div + 0.25 * (ten * ten + shr * shr) + 1.0
                base = constant(force, force_x, i, t)
                zeta = base * lax.rsqrt(square)
                quarter = 0.25 * zeta
                even = zeta * div - base
                odd = quarter * ten
                keep = constant(third, third_x, i, t)
                for ref, new in (
                    (str_a, even + odd), (str_b, even - odd), (str_c, quarter * shr)
                ):
                    ref[i + 1, :, cut(t)] = new + keep * ref[i + 1, :, cut(t)]
            fix(step, i)
        wrap(str_b, count)
        wrap(str_c, count)

    def momentum():
        seen = {}
        for i in range(count):
            ar, br = turn_a[i], turn_b[i]
            for t in range(wide):
                a = str_a[i + 1, :, cut(t)]
                s = load_once(str_c, 2, seen, i + 1, t)
                fx = (turn(a, -1) - turn(a, 1)) + (
                    load_once(str_c, 2, seen, i + 2, t) - load_once(str_c, 2, seen, i, t)
                )
                fy = (turn(s, -1) - turn(s, 1)) + (
                    load_once(str_b, 1, seen, i + 2, t) - load_once(str_b, 1, seen, i, t)
                )
                ru = (vel_u[i + 1, :, cut(t)] + constant(push_x, push_x_x, i, t)) + fx
                rv = (vel_v[i + 1, :, cut(t)] + constant(push_y, push_y_x, i, t)) + fy
                keep = constant(third, third_x, i, t)
                vel_u[i + 1, :, cut(t)] = (ar * ru + br * rv) * keep
                vel_v[i + 1, :, cut(t)] = (ar * rv - br * ru) * keep
        wrap(vel_u, count)
        wrap(vel_v, count)

    def subcycle(step, carry):
        strain_stress(step)
        for copy in fixed_rows(step):
            copy.start()
        momentum()
        return carry

    lax.fori_loop(0, SUBCYCLES, subcycle, 0)

    def gather(i):
        writes = []
        for n, ref in enumerate((vel_u, vel_v)):
            borders = ref[i + 1, :, cut(tiles)]
            middle, outer = turn(borders, -48), turn(borders, 24)
            low, high = ref[i + 1, :, cut(0)], ref[i + 1, :, cut(tiles - 1)]
            low = jnp.where(lane < HALO, borders, jnp.where(lane >= LANES - HALO, middle, low))
            high = jnp.where(lane < HALO, middle, jnp.where(lane >= LANES - HALO, outer, high))
            put = pl.ds(i, SUBLANES, stride=count)
            writes.append((done, (n, 0, put, whole), low))
            writes.append((done, (n, tiles - 1, put, whole), high))
        return writes

    straight(count, gather, 6, 51)
    finals = []
    for n, out in enumerate((u_out, v_out)):
        for t in range(tiles):
            finals.append(
                pltpu.make_async_copy(
                    done.at[n, t, own, :], out.at[:, pl.ds(LANES * t, LANES)], vel_sem.at[n, t]
                )
            )
            finals[-1].start()

    def warm(k):
        put, at = tile_rows(k), tile_rows(k + 1)
        writes = []
        for t in range(tiles):
            sst, sss = moved[0, t, put, :], moved[levels, t, put, :]
            slip_u = done[0, t, at, :] - speeds_in[0, t, put, :]
            slip_v = done[1, t, at, :] - speeds_in[levels, t, put, :]
            heat = HEAT_RATE * covered_in[3, t, at, :] * (1.0 + (slip_u * slip_u + slip_v * slip_v))
            heat = heat * (sst + FREEZE_SLOPE * sss)
            writes.append((moved, (0, t, put, whole), sst - heat))
            writes.append((moved, (levels, t, put, whole), sss - SALT_RATE * heat))
        return writes

    straight(rows // SUBLANES, warm, 6, 24)
    for n, out in enumerate((temp_out, salt_out)):
        for t in range(tiles):
            finals.append(
                pltpu.make_async_copy(
                    moved.at[levels * n, t],
                    out.at[0, :, pl.ds(LANES * t, LANES)],
                    out_sem.at[SUBCYCLES, n, t],
                )
            )
            finals[-1].start()
    for step in range(SUBCYCLES):
        finals += fixed_rows(step)
    for copy in finals:
        copy.wait()


def ice_and_edges(operands, levels, rows, cols):
    tiles = cols // LANES
    count = sublane_rows(rows)
    deep = jax.ShapeDtypeStruct((levels, rows, cols), F32)
    flat = jax.ShapeDtypeStruct((rows, cols), F32)
    looped = pltpu.VMEM((count + 2, SUBLANES, LANES * (tiles + 1)), F32)
    narrow = pltpu.VMEM((count, SUBLANES, LANES), F32)
    return pl.pallas_call(
        lambda *refs: ice_kernel(levels, rows, *refs),
        in_specs=[VMEM_SPEC] * len(operands),
        out_specs=[ANY_SPEC] * 4,
        out_shape=[deep, deep, flat, flat],
        scratch_shapes=[
            pltpu.VMEM((2 * levels, tiles, rows, LANES), F32),
            pltpu.VMEM((2, tiles, count * SUBLANES, LANES), F32),
            looped, looped, looped, looped, looped,
            narrow, narrow, narrow, narrow, pltpu.VMEM((rows, LANES), F32),
            pltpu.SemaphoreType.DMA((SUBCYCLES + 1, 2, tiles)),
            pltpu.SemaphoreType.DMA((2, tiles)),
        ],
        name="ice",
        compiler_params=pltpu.CompilerParams(vmem_limit_bytes=20 << 20),
        cost_estimate=pl.CostEstimate(flops=60000000, bytes_accessed=16 << 20, transcendentals=0),
    )(*[in_vmem(a) for a in operands])


def per_device(*arrays):
    levels, rows, cols = arrays[0].shape
    lon_count, lat_count = lax.axis_size("lon"), lax.axis_size("lat")
    assert cols == 2 * LANES and rows % (SUBLANES * SUBCYCLES) == 0
    assert lat_count % 2 == 0 and lon_count % 2 == 0
    height = -(-(HALO * ICE + 3 * levels) // SUBLANES) * SUBLANES

    def place(lat, lon):
        return lon * lat_count + lat

    first_pairs, second_pairs = [], []
    for lon in range(lon_count):
        for lat in range(lat_count):
            first_pairs.append((place(lat, lon), place(lat ^ 1, lon)))
            if lat == lat_count - 1:
                second_pairs.append((place(lat, lon), place(lat, lon_count - 1 - lon)))
            elif lat:
                second_pairs.append((place(lat, lon), place(((lat + 1) ^ 1) - 1, lon)))
    inter_pairs = [(i, (i - 1 if i % 2 == 0 else i + 1) % lon_count) for i in range(lon_count)]
    intra_pairs = [(i, i ^ 1) for i in range(lon_count)]
    second, first = pack_rows(arrays, levels, rows, cols, height)
    second = lax.ppermute(second, ("lon", "lat"), second_pairs)
    first = lax.ppermute(first, ("lon", "lat"), first_pairs)
    tracers, speeds, sea, fields, inter, intra = load_and_pack_columns(arrays, levels, rows, cols)
    halo, fields, inter, intra = merge_halo(second, first, fields, inter, intra, levels, rows)
    intra_in = lax.ppermute(intra, "lon", intra_pairs)
    inter_in = lax.ppermute(inter, "lon", inter_pairs)
    moved, *state = advect(tracers, speeds, sea, halo, fields, levels, rows * lat_count)
    return ice_and_edges(
        [fields, moved, speeds, inter, intra, inter_in, intra_in, *state], levels, rows, cols
    )


def solution(mesh):
    deep, flat = P(None, "lat", "lon"), P("lat", "lon")
    return jax.shard_map(
        per_device,
        mesh=mesh,
        in_specs=(deep,) * 4 + (flat,) * 7,
        out_specs=(deep, deep, flat, flat),
        check_vma=False,
    )
```

```python
import jax
import jax.numpy as jnp
from jax import lax
from jax.experimental import pallas as pl
from jax.experimental.pallas import tpu as pltpu
from jax.sharding import PartitionSpec as P

SUBCYCLES = 4
HEAT_RATE = 0.1
SALT_RATE = 0.5
FREEZE_SLOPE = 0.054
DIAGONAL = 1.5
HALO = 2 * SUBCYCLES
LANES = 128
SUBLANES = 8
ICE = 6
FOLD_SIGN = (-1.0, -1.0, 1.0, 1.0, -1.0, -1.0)
TRACER_LANE = 64
F32 = jnp.float32


def lane_ids():
    return lax.broadcasted_iota(jnp.int32, (SUBLANES, LANES), 1)


def sublane_ids():
    return lax.broadcasted_iota(jnp.int32, (SUBLANES, LANES), 0)


def turn(x, shift, axis=1):
    shift = shift % x.shape[axis]
    return pltpu.roll(x, shift, axis) if shift else x


def cut(t):
    return slice(LANES * t, LANES * (t + 1))


def ice_fields(land, ice, u, v, pressure, wind_x, wind_y, ocean_u, ocean_v):
    covered = land.astype(F32) * ice.astype(F32)
    return (u * covered, v * covered, pressure, covered, wind_x + ocean_u, wind_y + ocean_v)


def east_columns(fields, lane):
    packed = jnp.zeros((SUBLANES, LANES), F32)
    for f, tile in enumerate(fields):
        start = HALO * f + 2 * HALO
        moved = turn(tile, start - (LANES - HALO))
        packed = jnp.where((lane >= start) & (lane < start + HALO), moved, packed)
    return packed


def west_columns(fields, lane):
    packed = jnp.zeros((SUBLANES, LANES), F32)
    for f, tile in enumerate(fields):
        start = HALO * f
        packed = jnp.where((lane >= start) & (lane < start + HALO), turn(tile, start), packed)
    return packed


def sublane_rows(rows):
    return (rows + 2 * HALO) // SUBLANES | 1


class Trailing:
    def __init__(self, window):
        self.window, self.waiting = window, []

    def add(self, writes):
        self.waiting.append(writes)
        while len(self.waiting) > self.window:
            self.flush(self.waiting.pop(0))

    def finish(self):
        for writes in self.waiting:
            self.flush(writes)

    @staticmethod
    def flush(writes):
        for ref, where, value in writes:
            ref[where] = value


def straight(steps, body, window, size):
    size = max(c for c in range(1, size + 1) if steps % c == 0)

    def run(n, carry):
        pending = Trailing(window)
        for j in range(size):
            pending.add(body(n * size + j))
        pending.finish()
        return carry

    if size == steps:
        run(0, 0)
    else:
        lax.fori_loop(0, steps // size, run, 0)


def in_groups_of(group, steps, body, size=0):
    size = max(c for c in range(1, (size or group) + 1) if steps % c == 0)

    def run(n, carry):
        for start in range(0, size, group):
            writes = []
            for j in range(start, min(start + group, size)):
                writes += body(n * size + j)
            Trailing.flush(writes)
        return carry

    lax.fori_loop(0, steps // size, run, 0)


def tile_rows(k, offset=0):
    start = k * SUBLANES
    if not isinstance(k, int):
        start = pl.multiple_of(start, SUBLANES)
    return pl.ds(start + offset if offset else start, SUBLANES)


def rows_kernel(levels, *refs):
    tops, bottoms = refs[0:12], refs[12:24]
    first_ref, second_ref = refs[24:26]
    even = lax.rem(lax.axis_index("lat"), 2) == 0

    def message(group, row, northward):
        land, ice, u, v, pressure, wind_x, wind_y, east, north, temp, salt = (
            r for r in group[:11]
        )
        fields = ice_fields(
            land[...], ice[...], u[...], v[...], pressure[...], wind_x[...], wind_y[...],
            east[0], north[0],
        )
        sea = land[row : row + 1, :].astype(F32)
        parts = list(fields) + [temp[:, row, :], salt[:, row, :]]
        if northward:
            parts.append(north[:, row, :] * sea)
        else:
            parts.append(jnp.broadcast_to(sea, (levels, sea.shape[1])))
        return parts

    top = message(tops, SUBLANES - 1, True)
    bottom = message(bottoms, 0, False)
    at = 0
    for t, b in zip(top, bottom):
        size = t.shape[0]
        first_ref[at : at + size, :] = jnp.where(even, t, b)
        second_ref[at : at + size, :] = jnp.where(even, b, t)
        at += size
    pad = first_ref.shape[0] - at
    if pad:
        first_ref[at:, :] = jnp.zeros((pad, first_ref.shape[1]), F32)
        second_ref[at:, :] = jnp.zeros((pad, second_ref.shape[1]), F32)


def pack_rows(arrays, levels, rows, cols, height):
    temp, salt, east, north, land, ice, u, v, pressure, wind_x, wind_y = arrays
    operands = [land, ice, u, v, pressure, wind_x, wind_y, east, north, temp, salt, land]
    last = rows // SUBLANES - 1

    def spec(array, block, count):
        if array.ndim == 2:
            return pl.BlockSpec((SUBLANES, cols), lambda _: (block, 0))
        return pl.BlockSpec((count, SUBLANES, cols), lambda _: (0, block, 0))

    counts = [1] * 7 + [1, levels, levels, levels, 1]
    specs = [spec(a, last, c) for a, c in zip(operands, counts)]
    specs += [spec(a, 0, c) for a, c in zip(operands, counts)]
    out = jax.ShapeDtypeStruct((height, cols), F32)
    return pl.pallas_call(
        lambda *refs: rows_kernel(levels, *refs),
        grid=(1,),
        in_specs=specs,
        out_specs=[pl.BlockSpec((height, cols), lambda _: (0, 0))] * 2,
        out_shape=[out, out],
        name="edge_rows",
        compiler_params=pltpu.CompilerParams(vmem_limit_bytes=8 << 20),
        cost_estimate=pl.CostEstimate(flops=100000, bytes_accessed=1 << 20, transcendentals=0),
    )(*[in_hbm(a) for a in operands + operands])


def on_even_lon():
    return lax.rem(lax.axis_index("lon"), 2) == 0


def columns_kernel(levels, land, ice, u, v, pressure, wind_x, wind_y, east, north, temp, salt,
                   tracer_out, speed_out, sea_out, field_out, inter_out, intra_out, sem):
    lane = lane_ids()
    even = on_even_lon()
    rows = sea_out.shape[1]
    tiles = sea_out.shape[0]
    tracers = 2 * levels
    first_lane = TRACER_LANE
    mask_lane = TRACER_LANE + 2 * tracers

    copies = []
    for n, ref in enumerate((temp, salt, east, north)):
        out = tracer_out if n < 2 else speed_out
        for t in range(tiles):
            copies.append(
                pltpu.make_async_copy(
                    ref.at[..., pl.ds(LANES * t, LANES)],
                    out.at[pl.ds(levels * (n % 2), levels), t],
                    sem.at[n, t],
                )
            )
    for copy in copies:
        copy.start()

    whole = slice(None)

    def messages(put, eastward, westward):
        return [
            (inter_out, (put, whole), jnp.where(even, westward, eastward)),
            (intra_out, (put, whole), jnp.where(even, eastward, westward)),
        ]

    def packed(put):
        inter, intra = inter_out[put, :], intra_out[put, :]
        return jnp.where(even, intra, inter), jnp.where(even, inter, intra)

    def ice_part(k):
        at, put = tile_rows(k), tile_rows(k + 1)
        writes, fields = [], []
        for t in range(tiles):
            c = cut(t)
            fields.append(
                ice_fields(
                    *[r[at, c] for r in (land, ice, u, v, pressure, wind_x, wind_y)],
                    east[0, at, c], north[0, at, c],
                )
            )
            writes.append((sea_out, (t, at, whole), land[at, c].astype(F32)))
            for f in range(ICE):
                writes.append((field_out, (f, t, put, whole), fields[t][f]))
        return writes + messages(
            put, east_columns(fields[-1], lane), west_columns(fields[0], lane)
        )

    in_groups_of(4, rows // SUBLANES, ice_part)

    def tracer_part(k):
        at, put = tile_rows(k), tile_rows(k + 1)
        eastward, westward = packed(put)
        for f in range(tracers):
            ref, l, to = (temp, salt)[f // levels], f % levels, first_lane + 2 * f
            eastward = jnp.where(
                lane == to, turn(ref[l, at, cut(tiles - 1)], to - (LANES - 1)), eastward
            )
            westward = jnp.where(lane == to, turn(ref[l, at, cut(0)], to), westward)
        return messages(put, eastward, westward)

    in_groups_of(12, rows // SUBLANES, tracer_part)

    def speed_part(k):
        at, put = tile_rows(k), tile_rows(k + 1)
        masked = (lane >= mask_lane) & (lane < mask_lane + 2 * tracers)
        speeds = jnp.zeros((SUBLANES, LANES), F32)
        for f in range(levels):
            to = mask_lane + 2 * f
            speeds = jnp.where(
                lane == to, turn(east[f, at, cut(tiles - 1)], to - (LANES - 1)), speeds
            )
        speeds = speeds + turn(speeds, 2 * levels)
        last = land[at, LANES * tiles - 1 : LANES * tiles].astype(F32)
        first = jnp.broadcast_to(land[at, 0:1].astype(F32), (SUBLANES, LANES))
        eastward, westward = packed(put)
        eastward = jnp.where(masked, speeds * last, eastward)
        westward = jnp.where(masked, first, westward)
        return messages(put, eastward, westward)

    in_groups_of(12, rows // SUBLANES, speed_part)
    end = HALO + rows
    blank = jnp.zeros((field_out.shape[2] - end, LANES), F32)
    for t in range(tiles):
        for f in range(ICE):
            field_out[f, t, end:, :] = blank
    for ref in (inter_out, intra_out):
        ref[end:, :] = blank
    for copy in copies:
        copy.wait()


def in_vmem(x):
    return pltpu.with_memory_space_constraint(x, pltpu.VMEM)


def in_hbm(x):
    return pltpu.with_memory_space_constraint(x, pltpu.HBM)


def resident(*shape):
    return pltpu.VMEM(shape, F32)


VMEM_SPEC = pl.BlockSpec(memory_space=pltpu.VMEM)
ANY_SPEC = pl.BlockSpec(memory_space=pl.ANY)


def load_and_pack_columns(arrays, levels, rows, cols):
    temp, salt, east, north, land, ice, u, v, pressure, wind_x, wind_y = arrays
    tiles = cols // LANES
    message = resident(sublane_rows(rows) * SUBLANES, LANES)
    deep = resident(2 * levels, tiles, rows, LANES)
    return pl.pallas_call(
        lambda *refs: columns_kernel(levels, *refs),
        in_specs=[VMEM_SPEC] * 11,
        out_specs=[VMEM_SPEC] * 6,
        out_shape=[
            deep, deep, resident(tiles, rows, LANES),
            resident(ICE, tiles, sublane_rows(rows) * SUBLANES, LANES), message, message,
        ],
        scratch_shapes=[pltpu.SemaphoreType.DMA((4, tiles))],
        name="edge_columns",
        compiler_params=pltpu.CompilerParams(vmem_limit_bytes=4 << 20),
        cost_estimate=pl.CostEstimate(flops=5000000, bytes_accessed=12 << 20, transcendentals=0),
    )(*[in_vmem(a) for a in (land, ice, u, v, pressure, wind_x, wind_y, east, north, temp, salt)])


def halo_kernel(levels, rows, first, second, field_in, inter_in, intra_in,
                halo_ref, field_out, inter_out, intra_out):
    lat = lax.axis_index("lat")
    even = lax.rem(lat, 2) == 0
    top = lat == lax.axis_size("lat") - 1
    lane, sublane = lane_ids(), sublane_ids()
    tiles = field_out.shape[1]
    south_fields, north_fields = [], []
    for f in range(ICE):
        at = slice(HALO * f, HALO * (f + 1))
        north_row, south_row = [], []
        for t in range(tiles):
            cols = slice(LANES * t, LANES * (t + 1))
            mirror = slice(LANES * (tiles - 1 - t), LANES * (tiles - t))
            south = jnp.where(even, second[at, cols], first[at, cols])
            plain = jnp.where(even, first[at, cols], second[at, cols])
            turned = jnp.take_along_axis(second[at, mirror], LANES - 1 - lane, axis=1)
            turned = jnp.take_along_axis(turned, SUBLANES - 1 - sublane, axis=0)
            north = jnp.where(top, turned * FOLD_SIGN[f], plain)
            field_out[f, t, 0:HALO, :] = south
            field_out[f, t, rows + HALO : rows + 2 * HALO, :] = north
            south_row.append(south)
            north_row.append(north)
        south_fields.append(south_row)
        north_fields.append(north_row)
    rest = slice(HALO * ICE, first.shape[0])
    for t in range(tiles):
        c = cut(t)
        halo_ref[0, t] = jnp.where(even, second[rest, c], first[rest, c])
        halo_ref[1, t] = jnp.where(top, 0.0, jnp.where(even, first[rest, c], second[rest, c]))
    for at, fields in ((0, south_fields), (rows + HALO, north_fields)):
        eastward = east_columns([f[-1] for f in fields], lane)
        westward = west_columns([f[0] for f in fields], lane)
        inter_out[at : at + HALO, :] = jnp.where(on_even_lon(), westward, eastward)
        intra_out[at : at + HALO, :] = jnp.where(on_even_lon(), eastward, westward)


def merge_halo(first, second, fields, inter_msg, intra_msg, levels, rows):
    height, cols = first.shape
    return pl.pallas_call(
        lambda *refs: halo_kernel(levels, rows, *refs),
        in_specs=[VMEM_SPEC] * 5,
        out_specs=[VMEM_SPEC] * 4,
        out_shape=[
            resident(2, cols // LANES, height - HALO * ICE, LANES), resident(*fields.shape),
            resident(*inter_msg.shape), resident(*intra_msg.shape),
        ],
        input_output_aliases={2: 1, 3: 2, 4: 3},
        name="halo_rows",
        compiler_params=pltpu.CompilerParams(vmem_limit_bytes=8 << 20),
        cost_estimate=pl.CostEstimate(flops=100000, bytes_accessed=1 << 19, transcendentals=0),
    )(first, second, in_vmem(fields), in_vmem(inter_msg), in_vmem(intra_msg))


def advect_kernel(levels, row_total, tracer_ref, speed_ref, sea, halo, field_ref,
                  out, base_u, base_v, third, force, push_x, push_y, turn_a, turn_b,
                  mask_e, mask_n):
    tiles, rows = sea.shape[:2]
    count = rows // SUBLANES
    group = next(c for c in (12, 8, 4, 2) if count % c == 0)
    lane, sublane = lane_ids(), sublane_ids()
    extra_row = 2 * levels
    whole = slice(None)

    def rows_at(k, offset=0):
        start = pl.multiple_of(k * SUBLANES, SUBLANES)
        return pl.ds(start + offset if offset else start, SUBLANES)

    def row(side, index, t):
        return jnp.broadcast_to(halo[side, t, index : index + 1, :], (SUBLANES, LANES))

    def from_next(values):
        turned = [turn(v, -1) for v in values]
        return [
            jnp.where(lane == LANES - 1, turned[t + 1], turned[t]) if t + 1 < tiles else turned[t]
            for t in range(tiles)
        ]

    def from_last(values):
        turned = [turn(v, 1) for v in values]
        return [jnp.where(lane == 0, turned[t - 1], turned[t]) for t in range(tiles)]

    def in_groups(body, carry):
        def some(start, carry, last):
            writes = []
            for j in range(group):
                more, carry = body(start + j, last and j == group - 1, carry)
                writes += more
            for ref, where, value in writes:
                ref[where] = value
            return carry

        groups = count // group
        carry = lax.fori_loop(0, groups - 1, lambda n, c: some(n * group, c, False), carry)
        return some((groups - 1) * group, carry, True)

    def row_above(load, k, last, past):
        if not last:
            return load(rows_at(k, 1))
        return jnp.where(sublane == SUBLANES - 1, past, turn(load(rows_at(k)), -1, 0))

    def masks(k, last, carry):
        here = [sea[t, rows_at(k), :] for t in range(tiles)]
        beside = from_next(here)
        writes = []
        for t in range(tiles):
            above = row_above(lambda at, t=t: sea[t, at, :], k, last, row(1, extra_row, t))
            face = here[t] * beside[t]
            if t == tiles - 1:
                face = jnp.where(lane == LANES - 1, 0.0, face)
            writes.append((mask_e, (t, rows_at(k), whole), face))
            writes.append((mask_n, (t, rows_at(k), whole), here[t] * above))
        return writes, carry

    in_groups(masks, 0)
    for level in range(levels):
        entering = []
        for f in (level, levels + level):
            for t in range(tiles):
                speed = row(0, extra_row + level, t) * sea[t, 0:SUBLANES, :]
                start = tracer_ref[f, t, 0:SUBLANES, :]
                entering.append(speed * jnp.where(speed > 0, row(0, f, t), start))

        def body(k, last, carry, level=level):
            at = rows_at(k)
            fast_e = [speed_ref[level, t, at, :] * mask_e[t, at, :] for t in range(tiles)]
            fast_n = [speed_ref[levels + level, t, at, :] * mask_n[t, at, :] for t in range(tiles)]
            writes, result = [], []
            for f in (level, levels + level):
                here = [tracer_ref[f, t, at, :] for t in range(tiles)]
                beside = from_next(here)
                flux_e = [
                    fast_e[t] * jnp.where(fast_e[t] > 0, here[t], beside[t]) for t in range(tiles)
                ]
                before = from_last(flux_e)
                for t in range(tiles):
                    above = row_above(
                        lambda at, f=f, t=t: tracer_ref[f, t, at, :], k, last, row(1, f, t)
                    )
                    flux_n = fast_n[t] * jnp.where(fast_n[t] > 0, here[t], above)
                    turned = turn(flux_n, 1, 0)
                    below = jnp.where(sublane == 0, carry[len(result)], turned)
                    value = here[t] - ((flux_e[t] - before[t]) + (flux_n - below))
                    writes.append((out, (f, t, at, whole), value))
                    result.append(turned)
            return writes, tuple(result)

        in_groups(body, tuple(entering))
    spread_fields(rows, row_total, field_ref, base_u, base_v, third, force, push_x, push_y,
                  turn_a, turn_b)


def spread(ref, i, count, *lead):
    return ref[(*lead, pl.ds(i, SUBLANES, stride=count), slice(None))]


def wrap(ref, count, lanes=slice(None)):
    ref[0, :, lanes] = turn(ref[count, :, lanes], 1, 0)
    ref[count + 1, :, lanes] = turn(ref[1, :, lanes], -1, 0)


def spread_fields(rows, row_total, field_ref, base_u, base_v, third, force, push_x, push_y,
                  turn_a, turn_b):
    tiles = field_ref.shape[1]
    count = sublane_rows(rows)
    lane, sublane = lane_ids(), sublane_ids()
    lat = lax.axis_index("lat")

    def body(i):
        per_tile = [[spread(field_ref, i, count, f, t) for f in range(ICE)] for t in range(tiles)]
        extra = []
        for f in range(ICE):
            low, high = per_tile[0][f], per_tile[-1][f]
            middle = turn(jnp.where(lane < LANES // 2, high, low), 48)
            x = jnp.where(lane < 32, low, middle)
            extra.append(jnp.where(lane >= 64, turn(high, -24), x))
        writes = []
        for t, fields in enumerate(per_tile + [extra]):
            u0, v0, strength, covered, drive_x, drive_y = fields
            writes.append((base_u, (i + 1, slice(None), cut(t)), u0))
            writes.append((base_v, (i + 1, slice(None), cut(t)), v0))
            writes.append((third, (i, slice(None), cut(t)), covered * (1.0 / 3.0)))
            writes.append((force, (i, slice(None), cut(t)), strength * covered * (1.0 / 12.0)))
            writes.append((push_x, (i, slice(None), cut(t)), 0.5 * drive_x))
            writes.append((push_y, (i, slice(None), cut(t)), 0.5 * drive_y))
        y = lat * rows - HALO + sublane * count + i
        y = jnp.where(y >= row_total, 2 * row_total - 1 - y, y)
        coriolis = 0.5 * (2 * y + 1 - row_total).astype(F32) / row_total
        turning = 0.5 * coriolis
        scale = 3.0 / (DIAGONAL * DIAGONAL + turning * turning)
        writes.append((turn_a, (i,), DIAGONAL * scale))
        writes.append((turn_b, (i,), turning * scale))
        return writes

    in_groups_of(3, count, body, 17)
    wrap(base_u, count)
    wrap(base_v, count)


def advect(tracers, speeds, sea, halo, fields, levels, row_total):
    tiles, rows = sea.shape[:2]
    count = sublane_rows(rows)
    wide = LANES * (tiles + 1)
    looped = resident(count + 2, SUBLANES, wide)
    plain = resident(count, SUBLANES, wide)
    narrow = resident(count, SUBLANES, LANES)
    return pl.pallas_call(
        lambda *refs: advect_kernel(levels, row_total, *refs),
        in_specs=[VMEM_SPEC] * 5,
        out_specs=[VMEM_SPEC] * 9,
        out_shape=[
            resident(*tracers.shape), looped, looped, plain, plain, plain, plain, narrow, narrow,
        ],
        scratch_shapes=[pltpu.VMEM((tiles, rows, LANES), F32)] * 2,
        name="advect",
        compiler_params=pltpu.CompilerParams(vmem_limit_bytes=8 << 20),
        cost_estimate=pl.CostEstimate(flops=30000000, bytes_accessed=16 << 20, transcendentals=0),
    )(*[in_vmem(a) for a in (tracers, speeds, sea, halo, fields)])


def ice_kernel(levels, rows, *refs):
    (covered_in, tracers_in, speeds_in, inter_own, intra_own, inter_in, intra_in,
     base_u, base_v, third, force, push_x, push_y, turn_a, turn_b,
     temp_out, salt_out, u_out, v_out,
     moved, done, vel_u, vel_v, str_a, str_b, str_c,
     third_x, force_x, push_x_x, push_y_x, edges,
     out_sem, vel_sem) = refs
    tiles = tracers_in.shape[1]
    count = sublane_rows(rows)
    tracers = 2 * levels
    lane = lane_ids()
    own = pl.ds(HALO, rows)
    wide = tiles + 1
    whole = slice(None)

    even = on_even_lon()

    def sides(inter, intra):
        return jnp.where(even, inter, intra), jnp.where(even, intra, inter)

    def edge_fluxes(k):
        at, put = tile_rows(k + 1), tile_rows(k)
        west, east_side = sides(inter_in[at, :], intra_in[at, :])
        mine_w, mine_e = sides(inter_own[at, :], intra_own[at, :])
        speed = turn(west, -2 * tracers)
        inflow = speed * jnp.where(speed > 0, west, mine_w) * turn(mine_w, -2 * tracers)
        speed = turn(mine_e, -2 * tracers)
        outflow = speed * jnp.where(speed > 0, mine_e, east_side) * turn(east_side, -2 * tracers)
        flux = jnp.where(lane % 2 == TRACER_LANE % 2, inflow, turn(outflow, -1))
        return [(edges, (put, whole), flux)]

    straight(rows // SUBLANES, edge_fluxes, 8, 24)

    def fixed(f, put):
        flux = turn(edges[put, :], -(TRACER_LANE + 2 * f))
        low = tracers_in[f, 0, put, :] + jnp.where(lane == 0, flux, 0.0)
        return low, tracers_in[f, tiles - 1, put, :] - jnp.where(lane == LANES - 1, flux, 0.0)

    def insert(i):
        west, east_side = sides(spread(inter_in, i, count), spread(intra_in, i, count))
        writes = []
        targets = (
            (base_u, vel_u, 1, tiles, 1.0), (base_v, vel_v, 1, tiles, 1.0),
            (force, force_x, 0, 0, 1.0), (third, third_x, 0, 0, 1.0 / 3.0),
            (push_x, push_x_x, 0, 0, 0.5), (push_y, push_y_x, 0, 0, 0.5),
        )
        beyond = []
        for f in range(ICE):
            start = HALO * f + 2 * HALO
            x = jnp.where((lane >= start) & (lane < start + HALO), west, east_side)
            beyond.append(turn(x, 104 - HALO * f))
        beyond[2] = beyond[2] * beyond[3] * (1.0 / 12.0)
        for x, (source, target, shift, t, factor) in zip(beyond, targets):
            x = x if factor == 1.0 else x * factor
            x = jnp.where(lane >= 104, x, source[i + shift, :, cut(tiles)])
            writes.append((target, (i + shift, whole, cut(t)), x))
        own_lanes = slice(0, LANES * tiles)
        for source, target in ((base_u, vel_u), (base_v, vel_v)):
            writes.append((target, (i + 1, whole, own_lanes), source[i + 1, :, own_lanes]))
        for ref in (str_a, str_b, str_c):
            writes.append((ref, (i + 1,), jnp.zeros(ref.shape[1:], F32)))
        return writes

    straight(count, insert, 3, 17)
    wrap(vel_u, count)
    wrap(vel_v, count)

    def constant(ref, extra, i, t):
        return ref[i, :, cut(t)] if t < tiles else extra[i]

    def load_once(ref, name, seen, j, t):
        if (name, j, t) not in seen:
            seen[name, j, t] = ref[(j, whole) if t is None else (j, whole, cut(t))]
        return seen[name, j, t]

    share = rows // SUBLANES // SUBCYCLES
    items = [(k, f) for k in range(share) for f in range(tracers)]

    def fix(step, i):
        for k, f in items[len(items) * i // count : len(items) * (i + 1) // count]:
            put = pl.ds(pl.multiple_of((step * share + k) * SUBLANES, SUBLANES), SUBLANES)
            low, high = fixed(f, put)
            moved[f, 0, put, :] = low
            moved[f, tiles - 1, put, :] = high

    def fixed_rows(step):
        part = pl.ds(pl.multiple_of(step * share * SUBLANES, SUBLANES), share * SUBLANES)
        return [
            pltpu.make_async_copy(
                moved.at[pl.ds(levels * n + 1, levels - 1), t, part, :],
                out.at[pl.ds(1, levels - 1), part, pl.ds(LANES * t, LANES)],
                out_sem.at[step, n, t],
            )
            for n, out in enumerate((temp_out, salt_out))
            for t in range(tiles)
        ]

    def strain_stress(step):
        seen = {}
        for i in range(count):
            for t in range(wide):
                u, v = (load_once(r, n, seen, i + 1, t) for n, r in enumerate((vel_u, vel_v)))
                dudx, dvdx = turn(u, -1) - turn(u, 1), turn(v, -1) - turn(v, 1)
                dudy, dvdy = (
                    load_once(r, n, seen, i + 2, t) - load_once(r, n, seen, i, t)
                    for n, r in enumerate((vel_u, vel_v))
                )
                div, ten, shr = dudx + dvdy, dudx - dvdy, dudy + dvdx
                square = div * div + 0.25 * (ten * ten + shr * shr) + 1.0
                base = constant(force, force_x, i, t)
                zeta = base * lax.rsqrt(square)
                quarter = 0.25 * zeta
                even = zeta * div - base
                odd = quarter * ten
                keep = constant(third, third_x, i, t)
                for ref, new in (
                    (str_a, even + odd), (str_b, even - odd), (str_c, quarter * shr)
                ):
                    ref[i + 1, :, cut(t)] = new + keep * ref[i + 1, :, cut(t)]
            fix(step, i)
        wrap(str_b, count)
        wrap(str_c, count)

    def momentum():
        seen = {}
        for i in range(count):
            ar, br = turn_a[i], turn_b[i]
            for t in range(wide):
                a = str_a[i + 1, :, cut(t)]
                s = load_once(str_c, 2, seen, i + 1, t)
                fx = (turn(a, -1) - turn(a, 1)) + (
                    load_once(str_c, 2, seen, i + 2, t) - load_once(str_c, 2, seen, i, t)
                )
                fy = (turn(s, -1) - turn(s, 1)) + (
                    load_once(str_b, 1, seen, i + 2, t) - load_once(str_b, 1, seen, i, t)
                )
                ru = (vel_u[i + 1, :, cut(t)] + constant(push_x, push_x_x, i, t)) + fx
                rv = (vel_v[i + 1, :, cut(t)] + constant(push_y, push_y_x, i, t)) + fy
                keep = constant(third, third_x, i, t)
                vel_u[i + 1, :, cut(t)] = (ar * ru + br * rv) * keep
                vel_v[i + 1, :, cut(t)] = (ar * rv - br * ru) * keep
        wrap(vel_u, count)
        wrap(vel_v, count)

    def subcycle(step, carry):
        strain_stress(step)
        for copy in fixed_rows(step):
            copy.start()
        momentum()
        return carry

    lax.fori_loop(0, SUBCYCLES, subcycle, 0)

    def gather(i):
        writes = []
        for n, ref in enumerate((vel_u, vel_v)):
            borders = ref[i + 1, :, cut(tiles)]
            middle, outer = turn(borders, -48), turn(borders, 24)
            low, high = ref[i + 1, :, cut(0)], ref[i + 1, :, cut(tiles - 1)]
            low = jnp.where(lane < HALO, borders, jnp.where(lane >= LANES - HALO, middle, low))
            high = jnp.where(lane < HALO, middle, jnp.where(lane >= LANES - HALO, outer, high))
            put = pl.ds(i, SUBLANES, stride=count)
            writes.append((done, (n, 0, put, whole), low))
            writes.append((done, (n, tiles - 1, put, whole), high))
        return writes

    straight(count, gather, 6, 51)
    finals = []
    for n, out in enumerate((u_out, v_out)):
        for t in range(tiles):
            finals.append(
                pltpu.make_async_copy(
                    done.at[n, t, own, :], out.at[:, pl.ds(LANES * t, LANES)], vel_sem.at[n, t]
                )
            )
            finals[-1].start()

    def warm(k):
        put, at = tile_rows(k), tile_rows(k + 1)
        writes = []
        for t in range(tiles):
            sst, sss = moved[0, t, put, :], moved[levels, t, put, :]
            slip_u = done[0, t, at, :] - speeds_in[0, t, put, :]
            slip_v = done[1, t, at, :] - speeds_in[levels, t, put, :]
            heat = HEAT_RATE * covered_in[3, t, at, :] * (1.0 + (slip_u * slip_u + slip_v * slip_v))
            heat = heat * (sst + FREEZE_SLOPE * sss)
            writes.append((moved, (0, t, put, whole), sst - heat))
            writes.append((moved, (levels, t, put, whole), sss - SALT_RATE * heat))
        return writes

    straight(rows // SUBLANES, warm, 6, 24)
    for n, out in enumerate((temp_out, salt_out)):
        for t in range(tiles):
            finals.append(
                pltpu.make_async_copy(
                    moved.at[levels * n, t],
                    out.at[0, :, pl.ds(LANES * t, LANES)],
                    out_sem.at[SUBCYCLES, n, t],
                )
            )
            finals[-1].start()
    for step in range(SUBCYCLES):
        finals += fixed_rows(step)
    for copy in finals:
        copy.wait()


def ice_and_edges(operands, levels, rows, cols):
    tiles = cols // LANES
    count = sublane_rows(rows)
    deep = jax.ShapeDtypeStruct((levels, rows, cols), F32)
    flat = jax.ShapeDtypeStruct((rows, cols), F32)
    looped = pltpu.VMEM((count + 2, SUBLANES, LANES * (tiles + 1)), F32)
    narrow = pltpu.VMEM((count, SUBLANES, LANES), F32)
    return pl.pallas_call(
        lambda *refs: ice_kernel(levels, rows, *refs),
        in_specs=[VMEM_SPEC] * len(operands),
        out_specs=[ANY_SPEC] * 4,
        out_shape=[deep, deep, flat, flat],
        scratch_shapes=[
            pltpu.VMEM((2 * levels, tiles, rows, LANES), F32),
            pltpu.VMEM((2, tiles, count * SUBLANES, LANES), F32),
            looped, looped, looped, looped, looped,
            narrow, narrow, narrow, narrow, pltpu.VMEM((rows, LANES), F32),
            pltpu.SemaphoreType.DMA((SUBCYCLES + 1, 2, tiles)),
            pltpu.SemaphoreType.DMA((2, tiles)),
        ],
        name="ice",
        compiler_params=pltpu.CompilerParams(vmem_limit_bytes=20 << 20),
        cost_estimate=pl.CostEstimate(flops=60000000, bytes_accessed=16 << 20, transcendentals=0),
    )(*[in_vmem(a) for a in operands])


def per_device(*arrays):
    levels, rows, cols = arrays[0].shape
    lon_count, lat_count = lax.axis_size("lon"), lax.axis_size("lat")
    assert cols == 2 * LANES and rows % (SUBLANES * SUBCYCLES) == 0
    assert lat_count % 2 == 0 and lon_count % 2 == 0
    height = -(-(HALO * ICE + 3 * levels) // SUBLANES) * SUBLANES

    def place(lat, lon):
        return lon * lat_count + lat

    first_pairs, second_pairs = [], []
    for lon in range(lon_count):
        for lat in range(lat_count):
            first_pairs.append((place(lat, lon), place(lat ^ 1, lon)))
            if lat == lat_count - 1:
                second_pairs.append((place(lat, lon), place(lat, lon_count - 1 - lon)))
            elif lat:
                second_pairs.append((place(lat, lon), place(((lat + 1) ^ 1) - 1, lon)))
    inter_pairs = [(i, (i - 1 if i % 2 == 0 else i + 1) % lon_count) for i in range(lon_count)]
    intra_pairs = [(i, i ^ 1) for i in range(lon_count)]
    first, second = pack_rows(arrays, levels, rows, cols, height)
    first = lax.ppermute(first, ("lon", "lat"), first_pairs)
    second = lax.ppermute(second, ("lon", "lat"), second_pairs)
    tracers, speeds, sea, fields, inter, intra = load_and_pack_columns(arrays, levels, rows, cols)
    halo, fields, inter, intra = merge_halo(first, second, fields, inter, intra, levels, rows)
    intra_in = lax.ppermute(intra, "lon", intra_pairs)
    inter_in = lax.ppermute(inter, "lon", inter_pairs)
    moved, *state = advect(tracers, speeds, sea, halo, fields, levels, rows * lat_count)
    return ice_and_edges(
        [fields, moved, speeds, inter, intra, inter_in, intra_in, *state], levels, rows, cols
    )


def solution(mesh):
    deep, flat = P(None, "lat", "lon"), P("lat", "lon")
    return jax.shard_map(
        per_device,
        mesh=mesh,
        in_specs=(deep,) * 4 + (flat,) * 7,
        out_specs=(deep, deep, flat, flat),
        check_vma=False,
    )
```

```python
import jax
import jax.numpy as jnp
from jax import lax
from jax.experimental import pallas as pl
from jax.experimental.pallas import tpu as pltpu
from jax.sharding import PartitionSpec as P

SUBCYCLES = 4
HEAT_RATE = 0.1
SALT_RATE = 0.5
FREEZE_SLOPE = 0.054
DIAGONAL = 1.5
HALO = 2 * SUBCYCLES
LANES = 128
SUBLANES = 8
ICE = 6
FOLD_SIGN = (-1.0, -1.0, 1.0, 1.0, -1.0, -1.0)
TRACER_LANE = 64
F32 = jnp.float32


def lane_ids():
    return lax.broadcasted_iota(jnp.int32, (SUBLANES, LANES), 1)


def sublane_ids():
    return lax.broadcasted_iota(jnp.int32, (SUBLANES, LANES), 0)


def turn(x, shift, axis=1):
    shift = shift % x.shape[axis]
    return pltpu.roll(x, shift, axis) if shift else x


def cut(t):
    return slice(LANES * t, LANES * (t + 1))


def ice_fields(land, ice, u, v, pressure, wind_x, wind_y, ocean_u, ocean_v):
    covered = land.astype(F32) * ice.astype(F32)
    return (u * covered, v * covered, pressure, covered, wind_x + ocean_u, wind_y + ocean_v)


def east_columns(fields, lane):
    packed = jnp.zeros((SUBLANES, LANES), F32)
    for f, tile in enumerate(fields):
        start = HALO * f + 2 * HALO
        moved = turn(tile, start - (LANES - HALO))
        packed = jnp.where((lane >= start) & (lane < start + HALO), moved, packed)
    return packed


def west_columns(fields, lane):
    packed = jnp.zeros((SUBLANES, LANES), F32)
    for f, tile in enumerate(fields):
        start = HALO * f
        packed = jnp.where((lane >= start) & (lane < start + HALO), turn(tile, start), packed)
    return packed


def sublane_rows(rows):
    return (rows + 2 * HALO) // SUBLANES | 1


class Trailing:
    def __init__(self, window):
        self.window, self.waiting = window, []

    def add(self, writes):
        self.waiting.append(writes)
        while len(self.waiting) > self.window:
            self.flush(self.waiting.pop(0))

    def finish(self):
        for writes in self.waiting:
            self.flush(writes)

    @staticmethod
    def flush(writes):
        for ref, where, value in writes:
            ref[where] = value


def straight(steps, body, window, size):
    size = max(c for c in range(1, size + 1) if steps % c == 0)

    def run(n, carry):
        pending = Trailing(window)
        for j in range(size):
            pending.add(body(n * size + j))
        pending.finish()
        return carry

    if size == steps:
        run(0, 0)
    else:
        lax.fori_loop(0, steps // size, run, 0)


def in_groups_of(group, steps, body, size=0):
    size = max(c for c in range(1, (size or group) + 1) if steps % c == 0)

    def run(n, carry):
        for start in range(0, size, group):
            writes = []
            for j in range(start, min(start + group, size)):
                writes += body(n * size + j)
            Trailing.flush(writes)
        return carry

    lax.fori_loop(0, steps // size, run, 0)


def tile_rows(k, offset=0):
    start = k * SUBLANES
    if not isinstance(k, int):
        start = pl.multiple_of(start, SUBLANES)
    return pl.ds(start + offset if offset else start, SUBLANES)


def rows_kernel(levels, *refs):
    tops, bottoms = refs[0:12], refs[12:24]
    first_ref, second_ref = refs[24:26]
    even = lax.rem(lax.axis_index("lat"), 2) == 0

    def message(group, row, northward):
        land, ice, u, v, pressure, wind_x, wind_y, east, north, temp, salt = (
            r for r in group[:11]
        )
        fields = ice_fields(
            land[...], ice[...], u[...], v[...], pressure[...], wind_x[...], wind_y[...],
            east[0], north[0],
        )
        sea = land[row : row + 1, :].astype(F32)
        parts = list(fields) + [temp[:, row, :], salt[:, row, :]]
        if northward:
            parts.append(north[:, row, :] * sea)
        else:
            parts.append(jnp.broadcast_to(sea, (levels, sea.shape[1])))
        return parts

    top = message(tops, SUBLANES - 1, True)
    bottom = message(bottoms, 0, False)
    at = 0
    for t, b in zip(top, bottom):
        size = t.shape[0]
        first_ref[at : at + size, :] = jnp.where(even, t, b)
        second_ref[at : at + size, :] = jnp.where(even, b, t)
        at += size
    pad = first_ref.shape[0] - at
    if pad:
        first_ref[at:, :] = jnp.zeros((pad, first_ref.shape[1]), F32)
        second_ref[at:, :] = jnp.zeros((pad, second_ref.shape[1]), F32)


def pack_rows(arrays, levels, rows, cols, height):
    temp, salt, east, north, land, ice, u, v, pressure, wind_x, wind_y = arrays
    operands = [land, ice, u, v, pressure, wind_x, wind_y, east, north, temp, salt, land]
    last = rows // SUBLANES - 1

    def spec(array, block, count):
        if array.ndim == 2:
            return pl.BlockSpec((SUBLANES, cols), lambda _: (block, 0))
        return pl.BlockSpec((count, SUBLANES, cols), lambda _: (0, block, 0))

    counts = [1] * 7 + [1, levels, levels, levels, 1]
    specs = [spec(a, last, c) for a, c in zip(operands, counts)]
    specs += [spec(a, 0, c) for a, c in zip(operands, counts)]
    out = jax.ShapeDtypeStruct((height, cols), F32)
    return pl.pallas_call(
        lambda *refs: rows_kernel(levels, *refs),
        grid=(1,),
        in_specs=specs,
        out_specs=[pl.BlockSpec((height, cols), lambda _: (0, 0))] * 2,
        out_shape=[out, out],
        name="edge_rows",
        compiler_params=pltpu.CompilerParams(vmem_limit_bytes=8 << 20),
        cost_estimate=pl.CostEstimate(flops=100000, bytes_accessed=1 << 20, transcendentals=0),
    )(*[in_hbm(a) for a in operands + operands])


def on_even_lon():
    return lax.rem(lax.axis_index("lon"), 2) == 0


def columns_kernel(levels, land, ice, u, v, pressure, wind_x, wind_y, east, north, temp, salt,
                   tracer_out, speed_out, sea_out, field_out, inter_out, intra_out, sem):
    lane = lane_ids()
    even = on_even_lon()
    rows = sea_out.shape[1]
    tiles = sea_out.shape[0]
    tracers = 2 * levels
    first_lane = TRACER_LANE
    mask_lane = TRACER_LANE + 2 * tracers

    copies = []
    for n, ref in enumerate((temp, salt, east, north)):
        out = tracer_out if n < 2 else speed_out
        for t in range(tiles):
            copies.append(
                pltpu.make_async_copy(
                    ref.at[..., pl.ds(LANES * t, LANES)],
                    out.at[pl.ds(levels * (n % 2), levels), t],
                    sem.at[n, t],
                )
            )
    for copy in copies:
        copy.start()

    whole = slice(None)

    def messages(put, eastward, westward):
        return [
            (inter_out, (put, whole), jnp.where(even, westward, eastward)),
            (intra_out, (put, whole), jnp.where(even, eastward, westward)),
        ]

    def packed(put):
        inter, intra = inter_out[put, :], intra_out[put, :]
        return jnp.where(even, intra, inter), jnp.where(even, inter, intra)

    def ice_part(k):
        at, put = tile_rows(k), tile_rows(k + 1)
        writes, fields = [], []
        for t in range(tiles):
            c = cut(t)
            fields.append(
                ice_fields(
                    *[r[at, c] for r in (land, ice, u, v, pressure, wind_x, wind_y)],
                    east[0, at, c], north[0, at, c],
                )
            )
            writes.append((sea_out, (t, at, whole), land[at, c].astype(F32)))
            for f in range(ICE):
                writes.append((field_out, (f, t, put, whole), fields[t][f]))
        return writes + messages(
            put, east_columns(fields[-1], lane), west_columns(fields[0], lane)
        )

    in_groups_of(4, rows // SUBLANES, ice_part)

    def tracer_part(k):
        at, put = tile_rows(k), tile_rows(k + 1)
        eastward, westward = packed(put)
        for f in range(tracers):
            ref, l, to = (temp, salt)[f // levels], f % levels, first_lane + 2 * f
            eastward = jnp.where(
                lane == to, turn(ref[l, at, cut(tiles - 1)], to - (LANES - 1)), eastward
            )
            westward = jnp.where(lane == to, turn(ref[l, at, cut(0)], to), westward)
        return messages(put, eastward, westward)

    in_groups_of(12, rows // SUBLANES, tracer_part)

    def speed_part(k):
        at, put = tile_rows(k), tile_rows(k + 1)
        masked = (lane >= mask_lane) & (lane < mask_lane + 2 * tracers)
        speeds = jnp.zeros((SUBLANES, LANES), F32)
        for f in range(levels):
            to = mask_lane + 2 * f
            speeds = jnp.where(
                lane == to, turn(east[f, at, cut(tiles - 1)], to - (LANES - 1)), speeds
            )
        speeds = speeds + turn(speeds, 2 * levels)
        last = land[at, LANES * tiles - 1 : LANES * tiles].astype(F32)
        first = jnp.broadcast_to(land[at, 0:1].astype(F32), (SUBLANES, LANES))
        eastward, westward = packed(put)
        eastward = jnp.where(masked, speeds * last, eastward)
        westward = jnp.where(masked, first, westward)
        return messages(put, eastward, westward)

    in_groups_of(12, rows // SUBLANES, speed_part)
    end = HALO + rows
    blank = jnp.zeros((field_out.shape[2] - end, LANES), F32)
    for t in range(tiles):
        for f in range(ICE):
            field_out[f, t, end:, :] = blank
    for ref in (inter_out, intra_out):
        ref[end:, :] = blank
    for copy in copies:
        copy.wait()


def in_vmem(x):
    return pltpu.with_memory_space_constraint(x, pltpu.VMEM)


def in_hbm(x):
    return pltpu.with_memory_space_constraint(x, pltpu.HBM)


def resident(*shape):
    return pltpu.VMEM(shape, F32)


VMEM_SPEC = pl.BlockSpec(memory_space=pltpu.VMEM)
ANY_SPEC = pl.BlockSpec(memory_space=pl.ANY)


def load_and_pack_columns(arrays, levels, rows, cols):
    temp, salt, east, north, land, ice, u, v, pressure, wind_x, wind_y = arrays
    tiles = cols // LANES
    message = resident(sublane_rows(rows) * SUBLANES, LANES)
    deep = resident(2 * levels, tiles, rows, LANES)
    return pl.pallas_call(
        lambda *refs: columns_kernel(levels, *refs),
        in_specs=[VMEM_SPEC] * 11,
        out_specs=[VMEM_SPEC] * 6,
        out_shape=[
            deep, deep, resident(tiles, rows, LANES),
            resident(ICE, tiles, sublane_rows(rows) * SUBLANES, LANES), message, message,
        ],
        scratch_shapes=[pltpu.SemaphoreType.DMA((4, tiles))],
        name="edge_columns",
        compiler_params=pltpu.CompilerParams(vmem_limit_bytes=4 << 20),
        cost_estimate=pl.CostEstimate(flops=5000000, bytes_accessed=12 << 20, transcendentals=0),
    )(*[in_vmem(a) for a in (land, ice, u, v, pressure, wind_x, wind_y, east, north, temp, salt)])


def halo_kernel(levels, rows, first, second, field_in, inter_in, intra_in,
                halo_ref, field_out, inter_out, intra_out):
    lat = lax.axis_index("lat")
    even = lax.rem(lat, 2) == 0
    top = lat == lax.axis_size("lat") - 1
    lane, sublane = lane_ids(), sublane_ids()
    tiles = field_out.shape[1]
    south_fields, north_fields = [], []
    for f in range(ICE):
        at = slice(HALO * f, HALO * (f + 1))
        north_row, south_row = [], []
        for t in range(tiles):
            cols = slice(LANES * t, LANES * (t + 1))
            mirror = slice(LANES * (tiles - 1 - t), LANES * (tiles - t))
            south = jnp.where(even, second[at, cols], first[at, cols])
            plain = jnp.where(even, first[at, cols], second[at, cols])
            turned = jnp.take_along_axis(second[at, mirror], LANES - 1 - lane, axis=1)
            turned = jnp.take_along_axis(turned, SUBLANES - 1 - sublane, axis=0)
            north = jnp.where(top, turned * FOLD_SIGN[f], plain)
            field_out[f, t, 0:HALO, :] = south
            field_out[f, t, rows + HALO : rows + 2 * HALO, :] = north
            south_row.append(south)
            north_row.append(north)
        south_fields.append(south_row)
        north_fields.append(north_row)
    rest = slice(HALO * ICE, first.shape[0])
    for t in range(tiles):
        c = cut(t)
        halo_ref[0, t] = jnp.where(even, second[rest, c], first[rest, c])
        halo_ref[1, t] = jnp.where(top, 0.0, jnp.where(even, first[rest, c], second[rest, c]))
    for at, fields in ((0, south_fields), (rows + HALO, north_fields)):
        eastward = east_columns([f[-1] for f in fields], lane)
        westward = west_columns([f[0] for f in fields], lane)
        inter_out[at : at + HALO, :] = jnp.where(on_even_lon(), westward, eastward)
        intra_out[at : at + HALO, :] = jnp.where(on_even_lon(), eastward, westward)


def merge_halo(first, second, fields, inter_msg, intra_msg, levels, rows):
    height, cols = first.shape
    return pl.pallas_call(
        lambda *refs: halo_kernel(levels, rows, *refs),
        in_specs=[VMEM_SPEC] * 5,
        out_specs=[VMEM_SPEC] * 4,
        out_shape=[
            resident(2, cols // LANES, height - HALO * ICE, LANES), resident(*fields.shape),
            resident(*inter_msg.shape), resident(*intra_msg.shape),
        ],
        input_output_aliases={2: 1, 3: 2, 4: 3},
        name="halo_rows",
        compiler_params=pltpu.CompilerParams(vmem_limit_bytes=8 << 20),
        cost_estimate=pl.CostEstimate(flops=100000, bytes_accessed=1 << 19, transcendentals=0),
    )(first, second, in_vmem(fields), in_vmem(inter_msg), in_vmem(intra_msg))


def advect_kernel(levels, row_total, tracer_ref, speed_ref, sea, halo, field_ref,
                  out, base_u, base_v, third, force, push_x, push_y, turn_a, turn_b,
                  mask_e, mask_n):
    tiles, rows = sea.shape[:2]
    count = rows // SUBLANES
    group = next(c for c in (12, 8, 4, 2) if count % c == 0)
    lane, sublane = lane_ids(), sublane_ids()
    extra_row = 2 * levels
    whole = slice(None)

    def rows_at(k, offset=0):
        start = pl.multiple_of(k * SUBLANES, SUBLANES)
        return pl.ds(start + offset if offset else start, SUBLANES)

    def row(side, index, t):
        return jnp.broadcast_to(halo[side, t, index : index + 1, :], (SUBLANES, LANES))

    def from_next(values):
        turned = [turn(v, -1) for v in values]
        return [
            jnp.where(lane == LANES - 1, turned[t + 1], turned[t]) if t + 1 < tiles else turned[t]
            for t in range(tiles)
        ]

    def from_last(values):
        turned = [turn(v, 1) for v in values]
        return [jnp.where(lane == 0, turned[t - 1], turned[t]) for t in range(tiles)]

    def in_groups(body, carry):
        def some(start, carry, last):
            writes = []
            for j in range(group):
                more, carry = body(start + j, last and j == group - 1, carry)
                writes += more
            for ref, where, value in writes:
                ref[where] = value
            return carry

        groups = count // group
        carry = lax.fori_loop(0, groups - 1, lambda n, c: some(n * group, c, False), carry)
        return some((groups - 1) * group, carry, True)

    def row_above(load, k, last, past):
        if not last:
            return load(rows_at(k, 1))
        return jnp.where(sublane == SUBLANES - 1, past, turn(load(rows_at(k)), -1, 0))

    def masks(k, last, carry):
        here = [sea[t, rows_at(k), :] for t in range(tiles)]
        beside = from_next(here)
        writes = []
        for t in range(tiles):
            above = row_above(lambda at, t=t: sea[t, at, :], k, last, row(1, extra_row, t))
            face = here[t] * beside[t]
            if t == tiles - 1:
                face = jnp.where(lane == LANES - 1, 0.0, face)
            writes.append((mask_e, (t, rows_at(k), whole), face))
            writes.append((mask_n, (t, rows_at(k), whole), here[t] * above))
        return writes, carry

    in_groups(masks, 0)
    for level in range(levels):
        entering = []
        for f in (level, levels + level):
            for t in range(tiles):
                speed = row(0, extra_row + level, t) * sea[t, 0:SUBLANES, :]
                start = tracer_ref[f, t, 0:SUBLANES, :]
                entering.append(speed * jnp.where(speed > 0, row(0, f, t), start))

        def body(k, last, carry, level=level):
            at = rows_at(k)
            fast_e = [speed_ref[level, t, at, :] * mask_e[t, at, :] for t in range(tiles)]
            fast_n = [speed_ref[levels + level, t, at, :] * mask_n[t, at, :] for t in range(tiles)]
            writes, result = [], []
            for f in (level, levels + level):
                here = [tracer_ref[f, t, at, :] for t in range(tiles)]
                beside = from_next(here)
                flux_e = [
                    fast_e[t] * jnp.where(fast_e[t] > 0, here[t], beside[t]) for t in range(tiles)
                ]
                before = from_last(flux_e)
                for t in range(tiles):
                    above = row_above(
                        lambda at, f=f, t=t: tracer_ref[f, t, at, :], k, last, row(1, f, t)
                    )
                    flux_n = fast_n[t] * jnp.where(fast_n[t] > 0, here[t], above)
                    turned = turn(flux_n, 1, 0)
                    below = jnp.where(sublane == 0, carry[len(result)], turned)
                    value = here[t] - ((flux_e[t] - before[t]) + (flux_n - below))
                    writes.append((out, (f, t, at, whole), value))
                    result.append(turned)
            return writes, tuple(result)

        in_groups(body, tuple(entering))
    spread_fields(rows, row_total, field_ref, base_u, base_v, third, force, push_x, push_y,
                  turn_a, turn_b)


def spread(ref, i, count, *lead):
    return ref[(*lead, pl.ds(i, SUBLANES, stride=count), slice(None))]


def wrap(ref, count, lanes=slice(None)):
    ref[0, :, lanes] = turn(ref[count, :, lanes], 1, 0)
    ref[count + 1, :, lanes] = turn(ref[1, :, lanes], -1, 0)


def spread_fields(rows, row_total, field_ref, base_u, base_v, third, force, push_x, push_y,
                  turn_a, turn_b):
    tiles = field_ref.shape[1]
    count = sublane_rows(rows)
    lane, sublane = lane_ids(), sublane_ids()
    lat = lax.axis_index("lat")

    def body(i):
        per_tile = [[spread(field_ref, i, count, f, t) for f in range(ICE)] for t in range(tiles)]
        extra = []
        for f in range(ICE):
            low, high = per_tile[0][f], per_tile[-1][f]
            middle = turn(jnp.where(lane < LANES // 2, high, low), 48)
            x = jnp.where(lane < 32, low, middle)
            extra.append(jnp.where(lane >= 64, turn(high, -24), x))
        writes = []
        for t, fields in enumerate(per_tile + [extra]):
            u0, v0, strength, covered, drive_x, drive_y = fields
            writes.append((base_u, (i + 1, slice(None), cut(t)), u0))
            writes.append((base_v, (i + 1, slice(None), cut(t)), v0))
            writes.append((third, (i, slice(None), cut(t)), covered * (1.0 / 3.0)))
            writes.append((force, (i, slice(None), cut(t)), strength * covered * (1.0 / 12.0)))
            writes.append((push_x, (i, slice(None), cut(t)), 0.5 * drive_x))
            writes.append((push_y, (i, slice(None), cut(t)), 0.5 * drive_y))
        y = lat * rows - HALO + sublane * count + i
        y = jnp.where(y >= row_total, 2 * row_total - 1 - y, y)
        coriolis = 0.5 * (2 * y + 1 - row_total).astype(F32) / row_total
        turning = 0.5 * coriolis
        scale = 3.0 / (DIAGONAL * DIAGONAL + turning * turning)
        writes.append((turn_a, (i,), DIAGONAL * scale))
        writes.append((turn_b, (i,), turning * scale))
        return writes

    in_groups_of(3, count, body, 17)
    wrap(base_u, count)
    wrap(base_v, count)


def advect(tracers, speeds, sea, halo, fields, levels, row_total):
    tiles, rows = sea.shape[:2]
    count = sublane_rows(rows)
    wide = LANES * (tiles + 1)
    looped = resident(count + 2, SUBLANES, wide)
    plain = resident(count, SUBLANES, wide)
    narrow = resident(count, SUBLANES, LANES)
    return pl.pallas_call(
        lambda *refs: advect_kernel(levels, row_total, *refs),
        in_specs=[VMEM_SPEC] * 5,
        out_specs=[VMEM_SPEC] * 9,
        out_shape=[
            resident(*tracers.shape), looped, looped, plain, plain, plain, plain, narrow, narrow,
        ],
        scratch_shapes=[pltpu.VMEM((tiles, rows, LANES), F32)] * 2,
        name="advect",
        compiler_params=pltpu.CompilerParams(vmem_limit_bytes=8 << 20),
        cost_estimate=pl.CostEstimate(flops=30000000, bytes_accessed=16 << 20, transcendentals=0),
    )(*[in_vmem(a) for a in (tracers, speeds, sea, halo, fields)])


def ice_kernel(levels, rows, *refs):
    (covered_in, tracers_in, speeds_in, inter_own, intra_own, inter_in, intra_in,
     base_u, base_v, third, force, push_x, push_y, turn_a, turn_b,
     temp_out, salt_out, u_out, v_out,
     moved, done, vel_u, vel_v, str_a, str_b, str_c,
     third_x, force_x, push_x_x, push_y_x, edges, diff_u, diff_v,
     out_sem, vel_sem) = refs
    tiles = tracers_in.shape[1]
    count = sublane_rows(rows)
    tracers = 2 * levels
    lane = lane_ids()
    own = pl.ds(HALO, rows)
    wide = tiles + 1
    whole = slice(None)

    even = on_even_lon()

    def sides(inter, intra):
        return jnp.where(even, inter, intra), jnp.where(even, intra, inter)

    def edge_fluxes(k):
        at, put = tile_rows(k + 1), tile_rows(k)
        west, east_side = sides(inter_in[at, :], intra_in[at, :])
        mine_w, mine_e = sides(inter_own[at, :], intra_own[at, :])
        speed = turn(west, -2 * tracers)
        inflow = speed * jnp.where(speed > 0, west, mine_w) * turn(mine_w, -2 * tracers)
        speed = turn(mine_e, -2 * tracers)
        outflow = speed * jnp.where(speed > 0, mine_e, east_side) * turn(east_side, -2 * tracers)
        flux = jnp.where(lane % 2 == TRACER_LANE % 2, inflow, turn(outflow, -1))
        return [(edges, (put, whole), flux)]

    straight(rows // SUBLANES, edge_fluxes, 8, 24)

    def fixed(f, put):
        flux = turn(edges[put, :], -(TRACER_LANE + 2 * f))
        low = tracers_in[f, 0, put, :] + jnp.where(lane == 0, flux, 0.0)
        return low, tracers_in[f, tiles - 1, put, :] - jnp.where(lane == LANES - 1, flux, 0.0)

    unused = ((lane >= 16) & (lane < 32)) | ((lane >= 64) & (lane < 88))
    unused = unused | ((lane >= 112) & (lane < 120))

    def insert(i):
        west, east_side = sides(spread(inter_in, i, count), spread(intra_in, i, count))
        writes = []
        targets = (
            (base_u, vel_u, 1, tiles, 1.0), (base_v, vel_v, 1, tiles, 1.0),
            (force, force_x, 0, 0, 1.0), (third, third_x, 0, 0, 1.0 / 3.0),
            (push_x, push_x_x, 0, 0, 0.5), (push_y, push_y_x, 0, 0, 0.5),
        )
        beyond = []
        for f in range(ICE):
            start = HALO * f + 2 * HALO
            x = jnp.where((lane >= start) & (lane < start + HALO), west, east_side)
            beyond.append(turn(x, 104 - HALO * f))
        beyond[2] = beyond[2] * beyond[3] * (1.0 / 12.0)
        for f_index, (x, (source, target, shift, t, factor)) in enumerate(zip(beyond, targets)):
            x = x if factor == 1.0 else x * factor
            x = jnp.where(lane >= 104, x, source[i + shift, :, cut(tiles)])
            if f_index in (2, 3):
                x = jnp.where(unused, 0.0, x)
            writes.append((target, (i + shift, whole, cut(t)), x))
        own_lanes = slice(0, LANES * tiles)
        for source, target in ((base_u, vel_u), (base_v, vel_v)):
            writes.append((target, (i + 1, whole, own_lanes), source[i + 1, :, own_lanes]))
        for ref in (str_a, str_b, str_c):
            writes.append((ref, (i + 1,), jnp.zeros(ref.shape[1:], F32)))
        return writes

    straight(count, insert, 3, 17)
    wrap(vel_u, count)
    wrap(vel_v, count)

    def constant(ref, extra, i, t):
        return ref[i, :, cut(t)] if t < tiles else extra[i]

    def load_once(ref, name, seen, j, t):
        if (name, j, t) not in seen:
            seen[name, j, t] = ref[(j, whole) if t is None else (j, whole, cut(t))]
        return seen[name, j, t]

    share = rows // SUBLANES // SUBCYCLES
    items = [(k, f) for k in range(share) for f in range(tracers)]

    def fix(step, i):
        for k, f in items[len(items) * i // count : len(items) * (i + 1) // count]:
            put = pl.ds(pl.multiple_of((step * share + k) * SUBLANES, SUBLANES), SUBLANES)
            low, high = fixed(f, put)
            moved[f, 0, put, :] = low
            moved[f, tiles - 1, put, :] = high

    def fixed_rows(step):
        part = pl.ds(pl.multiple_of(step * share * SUBLANES, SUBLANES), share * SUBLANES)
        return [
            pltpu.make_async_copy(
                moved.at[pl.ds(levels * n + 1, levels - 1), t, part, :],
                out.at[pl.ds(1, levels - 1), part, pl.ds(LANES * t, LANES)],
                out_sem.at[step, n, t],
            )
            for n, out in enumerate((temp_out, salt_out))
            for t in range(tiles)
        ]

    def lane_difference(source, target):
        k = lax.broadcasted_iota(jnp.int32, (2 * LANES, LANES), 0) % LANES
        x = lax.broadcasted_iota(jnp.int32, (2 * LANES, LANES), 1)
        after = jnp.where(k == (x + 1) % LANES, 1.0, 0.0)
        matrix = (after - jnp.where(k == (x + LANES - 1) % LANES, 1.0, 0.0)).astype(jnp.bfloat16)
        for t in range(wide):
            f = source[1 : count + 2, :, cut(t)].reshape((count + 1) * SUBLANES, LANES)
            high = f.astype(jnp.bfloat16)
            rest = (f - high.astype(F32)).astype(jnp.bfloat16)
            parts = jnp.concatenate([high, rest], axis=1)
            result = jnp.dot(parts, matrix, preferred_element_type=F32)
            target[:, :, cut(t)] = result.reshape(count + 1, SUBLANES, LANES)

    def strain_stress(step):
        seen = {}
        lane_difference(vel_u, diff_u)
        lane_difference(vel_v, diff_v)
        for i in range(count):
            for t in range(wide):
                dudx, dvdx = diff_u[i, :, cut(t)], diff_v[i, :, cut(t)]
                dudy, dvdy = (
                    load_once(r, n, seen, i + 2, t) - load_once(r, n, seen, i, t)
                    for n, r in enumerate((vel_u, vel_v))
                )
                div, ten, shr = dudx + dvdy, dudx - dvdy, dudy + dvdx
                square = div * div + 0.25 * (ten * ten + shr * shr) + 1.0
                base = constant(force, force_x, i, t)
                zeta = base * lax.rsqrt(square)
                quarter = 0.25 * zeta
                even = zeta * div - base
                odd = quarter * ten
                for ref, new in (
                    (str_a, even + odd), (str_b, even - odd), (str_c, quarter * shr)
                ):
                    ref[i + 1, :, cut(t)] = new + (1.0 / 3.0) * ref[i + 1, :, cut(t)]
            fix(step, i)
        wrap(str_b, count)
        wrap(str_c, count)

    def momentum():
        seen = {}
        for i in range(count):
            ar, br = turn_a[i], turn_b[i]
            for t in range(wide):
                a = str_a[i + 1, :, cut(t)]
                s = load_once(str_c, 2, seen, i + 1, t)
                fx = (turn(a, -1) - turn(a, 1)) + (
                    load_once(str_c, 2, seen, i + 2, t) - load_once(str_c, 2, seen, i, t)
                )
                fy = (turn(s, -1) - turn(s, 1)) + (
                    load_once(str_b, 1, seen, i + 2, t) - load_once(str_b, 1, seen, i, t)
                )
                ru = (vel_u[i + 1, :, cut(t)] + constant(push_x, push_x_x, i, t)) + fx
                rv = (vel_v[i + 1, :, cut(t)] + constant(push_y, push_y_x, i, t)) + fy
                keep = constant(third, third_x, i, t)
                vel_u[i + 1, :, cut(t)] = (ar * ru + br * rv) * keep
                vel_v[i + 1, :, cut(t)] = (ar * rv - br * ru) * keep
        wrap(vel_u, count)
        wrap(vel_v, count)

    def subcycle(step, carry):
        strain_stress(step)
        for copy in fixed_rows(step):
            copy.start()
        momentum()
        return carry

    lax.fori_loop(0, SUBCYCLES, subcycle, 0)

    def gather(i):
        writes = []
        for n, ref in enumerate((vel_u, vel_v)):
            borders = ref[i + 1, :, cut(tiles)]
            middle, outer = turn(borders, -48), turn(borders, 24)
            low, high = ref[i + 1, :, cut(0)], ref[i + 1, :, cut(tiles - 1)]
            low = jnp.where(lane < HALO, borders, jnp.where(lane >= LANES - HALO, middle, low))
            high = jnp.where(lane < HALO, middle, jnp.where(lane >= LANES - HALO, outer, high))
            put = pl.ds(i, SUBLANES, stride=count)
            writes.append((done, (n, 0, put, whole), low))
            writes.append((done, (n, tiles - 1, put, whole), high))
        return writes

    straight(count, gather, 6, 51)
    finals = []
    for n, out in enumerate((u_out, v_out)):
        for t in range(tiles):
            finals.append(
                pltpu.make_async_copy(
                    done.at[n, t, own, :], out.at[:, pl.ds(LANES * t, LANES)], vel_sem.at[n, t]
                )
            )
            finals[-1].start()

    def warm(k):
        put, at = tile_rows(k), tile_rows(k + 1)
        writes = []
        for t in range(tiles):
            sst, sss = moved[0, t, put, :], moved[levels, t, put, :]
            slip_u = done[0, t, at, :] - speeds_in[0, t, put, :]
            slip_v = done[1, t, at, :] - speeds_in[levels, t, put, :]
            heat = HEAT_RATE * covered_in[3, t, at, :] * (1.0 + (slip_u * slip_u + slip_v * slip_v))
            heat = heat * (sst + FREEZE_SLOPE * sss)
            writes.append((moved, (0, t, put, whole), sst - heat))
            writes.append((moved, (levels, t, put, whole), sss - SALT_RATE * heat))
        return writes

    straight(rows // SUBLANES, warm, 6, 24)
    for n, out in enumerate((temp_out, salt_out)):
        for t in range(tiles):
            finals.append(
                pltpu.make_async_copy(
                    moved.at[levels * n, t],
                    out.at[0, :, pl.ds(LANES * t, LANES)],
                    out_sem.at[SUBCYCLES, n, t],
                )
            )
            finals[-1].start()
    for step in range(SUBCYCLES):
        finals += fixed_rows(step)
    for copy in finals:
        copy.wait()


def ice_and_edges(operands, levels, rows, cols):
    tiles = cols // LANES
    count = sublane_rows(rows)
    deep = jax.ShapeDtypeStruct((levels, rows, cols), F32)
    flat = jax.ShapeDtypeStruct((rows, cols), F32)
    looped = pltpu.VMEM((count + 2, SUBLANES, LANES * (tiles + 1)), F32)
    narrow = pltpu.VMEM((count, SUBLANES, LANES), F32)
    difference = pltpu.VMEM((count + 1, SUBLANES, LANES * (tiles + 1)), F32)
    return pl.pallas_call(
        lambda *refs: ice_kernel(levels, rows, *refs),
        in_specs=[VMEM_SPEC] * len(operands),
        out_specs=[ANY_SPEC] * 4,
        out_shape=[deep, deep, flat, flat],
        scratch_shapes=[
            pltpu.VMEM((2 * levels, tiles, rows, LANES), F32),
            pltpu.VMEM((2, tiles, count * SUBLANES, LANES), F32),
            looped, looped, looped, looped, looped,
            narrow, narrow, narrow, narrow, pltpu.VMEM((rows, LANES), F32),
            difference, difference,
            pltpu.SemaphoreType.DMA((SUBCYCLES + 1, 2, tiles)),
            pltpu.SemaphoreType.DMA((2, tiles)),
        ],
        name="ice",
        compiler_params=pltpu.CompilerParams(vmem_limit_bytes=20 << 20),
        cost_estimate=pl.CostEstimate(flops=60000000, bytes_accessed=16 << 20, transcendentals=0),
    )(*[in_vmem(a) for a in operands])


def per_device(*arrays):
    levels, rows, cols = arrays[0].shape
    lon_count, lat_count = lax.axis_size("lon"), lax.axis_size("lat")
    assert cols == 2 * LANES and rows % (SUBLANES * SUBCYCLES) == 0
    assert lat_count % 2 == 0 and lon_count % 2 == 0
    height = -(-(HALO * ICE + 3 * levels) // SUBLANES) * SUBLANES

    def place(lat, lon):
        return lon * lat_count + lat

    first_pairs, second_pairs = [], []
    for lon in range(lon_count):
        for lat in range(lat_count):
            first_pairs.append((place(lat, lon), place(lat ^ 1, lon)))
            if lat == lat_count - 1:
                second_pairs.append((place(lat, lon), place(lat, lon_count - 1 - lon)))
            elif lat:
                second_pairs.append((place(lat, lon), place(((lat + 1) ^ 1) - 1, lon)))
    inter_pairs = [(i, (i - 1 if i % 2 == 0 else i + 1) % lon_count) for i in range(lon_count)]
    intra_pairs = [(i, i ^ 1) for i in range(lon_count)]
    first, second = pack_rows(arrays, levels, rows, cols, height)
    first = lax.ppermute(first, ("lon", "lat"), first_pairs)
    second = lax.ppermute(second, ("lon", "lat"), second_pairs)
    tracers, speeds, sea, fields, inter, intra = load_and_pack_columns(arrays, levels, rows, cols)
    halo, fields, inter, intra = merge_halo(first, second, fields, inter, intra, levels, rows)
    intra_in = lax.ppermute(intra, "lon", intra_pairs)
    inter_in = lax.ppermute(inter, "lon", inter_pairs)
    moved, *state = advect(tracers, speeds, sea, halo, fields, levels, rows * lat_count)
    return ice_and_edges(
        [fields, moved, speeds, inter, intra, inter_in, intra_in, *state], levels, rows, cols
    )


def solution(mesh):
    deep, flat = P(None, "lat", "lon"), P("lat", "lon")
    return jax.shard_map(
        per_device,
        mesh=mesh,
        in_specs=(deep,) * 4 + (flat,) * 7,
        out_specs=(deep, deep, flat, flat),
        check_vma=False,
    )
```

```python
import jax
import jax.numpy as jnp
from jax import lax
from jax.experimental import pallas as pl
from jax.experimental.pallas import tpu as pltpu
from jax.sharding import PartitionSpec as P

SUBCYCLES = 4
HEAT_RATE = 0.1
SALT_RATE = 0.5
FREEZE_SLOPE = 0.054
DIAGONAL = 1.5
HALO = 2 * SUBCYCLES
LANES = 128
SUBLANES = 8
ICE = 6
FOLD_SIGN = (-1.0, -1.0, 1.0, 1.0, -1.0, -1.0)
TRACER_LANE = 64
F32 = jnp.float32


def lane_ids():
    return lax.broadcasted_iota(jnp.int32, (SUBLANES, LANES), 1)


def sublane_ids():
    return lax.broadcasted_iota(jnp.int32, (SUBLANES, LANES), 0)


def turn(x, shift, axis=1):
    shift = shift % x.shape[axis]
    return pltpu.roll(x, shift, axis) if shift else x


def cut(t):
    return slice(LANES * t, LANES * (t + 1))


def ice_fields(land, ice, u, v, pressure, wind_x, wind_y, ocean_u, ocean_v):
    covered = land.astype(F32) * ice.astype(F32)
    return (u * covered, v * covered, pressure, covered, wind_x + ocean_u, wind_y + ocean_v)


def east_columns(fields, lane):
    packed = jnp.zeros((SUBLANES, LANES), F32)
    for f, tile in enumerate(fields):
        start = HALO * f + 2 * HALO
        moved = turn(tile, start - (LANES - HALO))
        packed = jnp.where((lane >= start) & (lane < start + HALO), moved, packed)
    return packed


def west_columns(fields, lane):
    packed = jnp.zeros((SUBLANES, LANES), F32)
    for f, tile in enumerate(fields):
        start = HALO * f
        packed = jnp.where((lane >= start) & (lane < start + HALO), turn(tile, start), packed)
    return packed


def sublane_rows(rows):
    return (rows + 2 * HALO) // SUBLANES | 1


class Trailing:
    def __init__(self, window):
        self.window, self.waiting = window, []

    def add(self, writes):
        self.waiting.append(writes)
        while len(self.waiting) > self.window:
            self.flush(self.waiting.pop(0))

    def finish(self):
        for writes in self.waiting:
            self.flush(writes)

    @staticmethod
    def flush(writes):
        for ref, where, value in writes:
            ref[where] = value


def straight(steps, body, window, size):
    size = max(c for c in range(1, size + 1) if steps % c == 0)

    def run(n, carry):
        pending = Trailing(window)
        for j in range(size):
            pending.add(body(n * size + j))
        pending.finish()
        return carry

    if size == steps:
        run(0, 0)
    else:
        lax.fori_loop(0, steps // size, run, 0)


def in_groups_of(group, steps, body, size=0):
    size = max(c for c in range(1, (size or group) + 1) if steps % c == 0)

    def run(n, carry):
        for start in range(0, size, group):
            writes = []
            for j in range(start, min(start + group, size)):
                writes += body(n * size + j)
            Trailing.flush(writes)
        return carry

    lax.fori_loop(0, steps // size, run, 0)


def tile_rows(k, offset=0):
    start = k * SUBLANES
    if not isinstance(k, int):
        start = pl.multiple_of(start, SUBLANES)
    return pl.ds(start + offset if offset else start, SUBLANES)


def rows_kernel(levels, *refs):
    tops, bottoms = refs[0:12], refs[12:24]
    first_ref, second_ref = refs[24:26]
    even = lax.rem(lax.axis_index("lat"), 2) == 0

    def message(group, row, northward):
        land, ice, u, v, pressure, wind_x, wind_y, east, north, temp, salt = (
            r for r in group[:11]
        )
        fields = ice_fields(
            land[...], ice[...], u[...], v[...], pressure[...], wind_x[...], wind_y[...],
            east[0], north[0],
        )
        sea = land[row : row + 1, :].astype(F32)
        parts = list(fields) + [temp[:, row, :], salt[:, row, :]]
        if northward:
            parts.append(north[:, row, :] * sea)
        else:
            parts.append(jnp.broadcast_to(sea, (levels, sea.shape[1])))
        return parts

    top = message(tops, SUBLANES - 1, True)
    bottom = message(bottoms, 0, False)
    at = 0
    for t, b in zip(top, bottom):
        size = t.shape[0]
        first_ref[at : at + size, :] = jnp.where(even, t, b)
        second_ref[at : at + size, :] = jnp.where(even, b, t)
        at += size
    pad = first_ref.shape[0] - at
    if pad:
        first_ref[at:, :] = jnp.zeros((pad, first_ref.shape[1]), F32)
        second_ref[at:, :] = jnp.zeros((pad, second_ref.shape[1]), F32)


def pack_rows(arrays, levels, rows, cols, height):
    temp, salt, east, north, land, ice, u, v, pressure, wind_x, wind_y = arrays
    operands = [land, ice, u, v, pressure, wind_x, wind_y, east, north, temp, salt, land]
    last = rows // SUBLANES - 1

    def spec(array, block, count):
        if array.ndim == 2:
            return pl.BlockSpec((SUBLANES, cols), lambda _: (block, 0))
        return pl.BlockSpec((count, SUBLANES, cols), lambda _: (0, block, 0))

    counts = [1] * 7 + [1, levels, levels, levels, 1]
    specs = [spec(a, last, c) for a, c in zip(operands, counts)]
    specs += [spec(a, 0, c) for a, c in zip(operands, counts)]
    out = jax.ShapeDtypeStruct((height, cols), F32)
    return pl.pallas_call(
        lambda *refs: rows_kernel(levels, *refs),
        grid=(1,),
        in_specs=specs,
        out_specs=[pl.BlockSpec((height, cols), lambda _: (0, 0))] * 2,
        out_shape=[out, out],
        name="edge_rows",
        compiler_params=pltpu.CompilerParams(vmem_limit_bytes=8 << 20),
        cost_estimate=pl.CostEstimate(flops=100000, bytes_accessed=1 << 20, transcendentals=0),
    )(*[in_hbm(a) for a in operands + operands])


def on_even_lon():
    return lax.rem(lax.axis_index("lon"), 2) == 0


def columns_kernel(levels, land, ice, u, v, pressure, wind_x, wind_y, east, north, temp, salt,
                   tracer_out, speed_out, sea_out, field_out, inter_out, intra_out, sem):
    lane = lane_ids()
    even = on_even_lon()
    rows = sea_out.shape[1]
    tiles = sea_out.shape[0]
    tracers = 2 * levels
    first_lane = TRACER_LANE
    mask_lane = TRACER_LANE + 2 * tracers

    copies = []
    for n, ref in enumerate((temp, salt, east, north)):
        out = tracer_out if n < 2 else speed_out
        for t in range(tiles):
            copies.append(
                pltpu.make_async_copy(
                    ref.at[..., pl.ds(LANES * t, LANES)],
                    out.at[pl.ds(levels * (n % 2), levels), t],
                    sem.at[n, t],
                )
            )
    for copy in copies:
        copy.start()

    whole = slice(None)

    def messages(put, eastward, westward):
        return [
            (inter_out, (put, whole), jnp.where(even, westward, eastward)),
            (intra_out, (put, whole), jnp.where(even, eastward, westward)),
        ]

    def packed(put):
        inter, intra = inter_out[put, :], intra_out[put, :]
        return jnp.where(even, intra, inter), jnp.where(even, inter, intra)

    def ice_part(k):
        at, put = tile_rows(k), tile_rows(k + 1)
        writes, fields = [], []
        for t in range(tiles):
            c = cut(t)
            fields.append(
                ice_fields(
                    *[r[at, c] for r in (land, ice, u, v, pressure, wind_x, wind_y)],
                    east[0, at, c], north[0, at, c],
                )
            )
            writes.append((sea_out, (t, at, whole), land[at, c].astype(F32)))
            for f in range(ICE):
                writes.append((field_out, (f, t, put, whole), fields[t][f]))
        return writes + messages(
            put, east_columns(fields[-1], lane), west_columns(fields[0], lane)
        )

    in_groups_of(4, rows // SUBLANES, ice_part)

    def tracer_part(k):
        at, put = tile_rows(k), tile_rows(k + 1)
        eastward, westward = packed(put)
        for f in range(tracers):
            ref, l, to = (temp, salt)[f // levels], f % levels, first_lane + 2 * f
            eastward = jnp.where(
                lane == to, turn(ref[l, at, cut(tiles - 1)], to - (LANES - 1)), eastward
            )
            westward = jnp.where(lane == to, turn(ref[l, at, cut(0)], to), westward)
        return messages(put, eastward, westward)

    in_groups_of(12, rows // SUBLANES, tracer_part)

    def speed_part(k):
        at, put = tile_rows(k), tile_rows(k + 1)
        masked = (lane >= mask_lane) & (lane < mask_lane + 2 * tracers)
        speeds = jnp.zeros((SUBLANES, LANES), F32)
        for f in range(levels):
            to = mask_lane + 2 * f
            speeds = jnp.where(
                lane == to, turn(east[f, at, cut(tiles - 1)], to - (LANES - 1)), speeds
            )
        speeds = speeds + turn(speeds, 2 * levels)
        last = land[at, LANES * tiles - 1 : LANES * tiles].astype(F32)
        first = jnp.broadcast_to(land[at, 0:1].astype(F32), (SUBLANES, LANES))
        eastward, westward = packed(put)
        eastward = jnp.where(masked, speeds * last, eastward)
        westward = jnp.where(masked, first, westward)
        return messages(put, eastward, westward)

    in_groups_of(12, rows // SUBLANES, speed_part)
    end = HALO + rows
    blank = jnp.zeros((field_out.shape[2] - end, LANES), F32)
    for t in range(tiles):
        for f in range(ICE):
            field_out[f, t, end:, :] = blank
    for ref in (inter_out, intra_out):
        ref[end:, :] = blank
    for copy in copies:
        copy.wait()


def in_vmem(x):
    return pltpu.with_memory_space_constraint(x, pltpu.VMEM)


def in_hbm(x):
    return pltpu.with_memory_space_constraint(x, pltpu.HBM)


def resident(*shape):
    return pltpu.VMEM(shape, F32)


VMEM_SPEC = pl.BlockSpec(memory_space=pltpu.VMEM)
ANY_SPEC = pl.BlockSpec(memory_space=pl.ANY)


def load_and_pack_columns(arrays, levels, rows, cols):
    temp, salt, east, north, land, ice, u, v, pressure, wind_x, wind_y = arrays
    tiles = cols // LANES
    message = resident(sublane_rows(rows) * SUBLANES, LANES)
    deep = resident(2 * levels, tiles, rows, LANES)
    return pl.pallas_call(
        lambda *refs: columns_kernel(levels, *refs),
        in_specs=[VMEM_SPEC] * 11,
        out_specs=[VMEM_SPEC] * 6,
        out_shape=[
            deep, deep, resident(tiles, rows, LANES),
            resident(ICE, tiles, sublane_rows(rows) * SUBLANES, LANES), message, message,
        ],
        scratch_shapes=[pltpu.SemaphoreType.DMA((4, tiles))],
        name="edge_columns",
        compiler_params=pltpu.CompilerParams(vmem_limit_bytes=4 << 20),
        cost_estimate=pl.CostEstimate(flops=5000000, bytes_accessed=12 << 20, transcendentals=0),
    )(*[in_vmem(a) for a in (land, ice, u, v, pressure, wind_x, wind_y, east, north, temp, salt)])


def halo_kernel(levels, rows, first, second, field_in, inter_in, intra_in,
                halo_ref, field_out, inter_out, intra_out):
    lat = lax.axis_index("lat")
    even = lax.rem(lat, 2) == 0
    top = lat == lax.axis_size("lat") - 1
    lane, sublane = lane_ids(), sublane_ids()
    tiles = field_out.shape[1]
    south_fields, north_fields = [], []
    for f in range(ICE):
        at = slice(HALO * f, HALO * (f + 1))
        north_row, south_row = [], []
        for t in range(tiles):
            cols = slice(LANES * t, LANES * (t + 1))
            mirror = slice(LANES * (tiles - 1 - t), LANES * (tiles - t))
            south = jnp.where(even, second[at, cols], first[at, cols])
            plain = jnp.where(even, first[at, cols], second[at, cols])
            turned = jnp.take_along_axis(second[at, mirror], LANES - 1 - lane, axis=1)
            turned = jnp.take_along_axis(turned, SUBLANES - 1 - sublane, axis=0)
            north = jnp.where(top, turned * FOLD_SIGN[f], plain)
            field_out[f, t, 0:HALO, :] = south
            field_out[f, t, rows + HALO : rows + 2 * HALO, :] = north
            south_row.append(south)
            north_row.append(north)
        south_fields.append(south_row)
        north_fields.append(north_row)
    rest = slice(HALO * ICE, first.shape[0])
    for t in range(tiles):
        c = cut(t)
        halo_ref[0, t] = jnp.where(even, second[rest, c], first[rest, c])
        halo_ref[1, t] = jnp.where(top, 0.0, jnp.where(even, first[rest, c], second[rest, c]))
    for at, fields in ((0, south_fields), (rows + HALO, north_fields)):
        eastward = east_columns([f[-1] for f in fields], lane)
        westward = west_columns([f[0] for f in fields], lane)
        inter_out[at : at + HALO, :] = jnp.where(on_even_lon(), westward, eastward)
        intra_out[at : at + HALO, :] = jnp.where(on_even_lon(), eastward, westward)


def merge_halo(first, second, fields, inter_msg, intra_msg, levels, rows):
    height, cols = first.shape
    return pl.pallas_call(
        lambda *refs: halo_kernel(levels, rows, *refs),
        in_specs=[VMEM_SPEC] * 5,
        out_specs=[VMEM_SPEC] * 4,
        out_shape=[
            resident(2, cols // LANES, height - HALO * ICE, LANES), resident(*fields.shape),
            resident(*inter_msg.shape), resident(*intra_msg.shape),
        ],
        input_output_aliases={2: 1, 3: 2, 4: 3},
        name="halo_rows",
        compiler_params=pltpu.CompilerParams(vmem_limit_bytes=8 << 20),
        cost_estimate=pl.CostEstimate(flops=100000, bytes_accessed=1 << 19, transcendentals=0),
    )(first, second, in_vmem(fields), in_vmem(inter_msg), in_vmem(intra_msg))


def advect_kernel(levels, row_total, tracer_ref, speed_ref, sea, halo, field_ref,
                  out, base_u, base_v, third, force, push_x, push_y, turn_a, turn_b,
                  mask_e, mask_n):
    tiles, rows = sea.shape[:2]
    count = rows // SUBLANES
    group = next(c for c in (12, 8, 4, 2) if count % c == 0)
    lane, sublane = lane_ids(), sublane_ids()
    extra_row = 2 * levels
    whole = slice(None)

    def rows_at(k, offset=0):
        start = pl.multiple_of(k * SUBLANES, SUBLANES)
        return pl.ds(start + offset if offset else start, SUBLANES)

    def row(side, index, t):
        return jnp.broadcast_to(halo[side, t, index : index + 1, :], (SUBLANES, LANES))

    def from_next(values):
        turned = [turn(v, -1) for v in values]
        return [
            jnp.where(lane == LANES - 1, turned[t + 1], turned[t]) if t + 1 < tiles else turned[t]
            for t in range(tiles)
        ]

    def from_last(values):
        turned = [turn(v, 1) for v in values]
        return [jnp.where(lane == 0, turned[t - 1], turned[t]) for t in range(tiles)]

    def in_groups(body, carry):
        def some(start, carry, last):
            writes = []
            for j in range(group):
                more, carry = body(start + j, last and j == group - 1, carry)
                writes += more
            for ref, where, value in writes:
                ref[where] = value
            return carry

        groups = count // group
        carry = lax.fori_loop(0, groups - 1, lambda n, c: some(n * group, c, False), carry)
        return some((groups - 1) * group, carry, True)

    def row_above(load, k, last, past):
        if not last:
            return load(rows_at(k, 1))
        return jnp.where(sublane == SUBLANES - 1, past, turn(load(rows_at(k)), -1, 0))

    def masks(k, last, carry):
        here = [sea[t, rows_at(k), :] for t in range(tiles)]
        beside = from_next(here)
        writes = []
        for t in range(tiles):
            above = row_above(lambda at, t=t: sea[t, at, :], k, last, row(1, extra_row, t))
            face = here[t] * beside[t]
            if t == tiles - 1:
                face = jnp.where(lane == LANES - 1, 0.0, face)
            writes.append((mask_e, (t, rows_at(k), whole), face))
            writes.append((mask_n, (t, rows_at(k), whole), here[t] * above))
        return writes, carry

    in_groups(masks, 0)
    for level in range(levels):
        entering = []
        for f in (level, levels + level):
            for t in range(tiles):
                speed = row(0, extra_row + level, t) * sea[t, 0:SUBLANES, :]
                start = tracer_ref[f, t, 0:SUBLANES, :]
                entering.append(speed * jnp.where(speed > 0, row(0, f, t), start))

        def body(k, last, carry, level=level):
            at = rows_at(k)
            fast_e = [speed_ref[level, t, at, :] * mask_e[t, at, :] for t in range(tiles)]
            fast_n = [speed_ref[levels + level, t, at, :] * mask_n[t, at, :] for t in range(tiles)]
            writes, result = [], []
            for f in (level, levels + level):
                here = [tracer_ref[f, t, at, :] for t in range(tiles)]
                beside = from_next(here)
                flux_e = [
                    fast_e[t] * jnp.where(fast_e[t] > 0, here[t], beside[t]) for t in range(tiles)
                ]
                before = from_last(flux_e)
                for t in range(tiles):
                    above = row_above(
                        lambda at, f=f, t=t: tracer_ref[f, t, at, :], k, last, row(1, f, t)
                    )
                    flux_n = fast_n[t] * jnp.where(fast_n[t] > 0, here[t], above)
                    turned = turn(flux_n, 1, 0)
                    below = jnp.where(sublane == 0, carry[len(result)], turned)
                    value = here[t] - ((flux_e[t] - before[t]) + (flux_n - below))
                    writes.append((out, (f, t, at, whole), value))
                    result.append(turned)
            return writes, tuple(result)

        in_groups(body, tuple(entering))
    spread_fields(rows, row_total, field_ref, base_u, base_v, third, force, push_x, push_y,
                  turn_a, turn_b)


def spread(ref, i, count, *lead):
    return ref[(*lead, pl.ds(i, SUBLANES, stride=count), slice(None))]


def wrap(ref, count, lanes=slice(None)):
    ref[0, :, lanes] = turn(ref[count, :, lanes], 1, 0)
    ref[count + 1, :, lanes] = turn(ref[1, :, lanes], -1, 0)


def spread_fields(rows, row_total, field_ref, base_u, base_v, third, force, push_x, push_y,
                  turn_a, turn_b):
    tiles = field_ref.shape[1]
    count = sublane_rows(rows)
    lane, sublane = lane_ids(), sublane_ids()
    lat = lax.axis_index("lat")

    def body(i):
        per_tile = [[spread(field_ref, i, count, f, t) for f in range(ICE)] for t in range(tiles)]
        extra = []
        for f in range(ICE):
            low, high = per_tile[0][f], per_tile[-1][f]
            middle = turn(jnp.where(lane < LANES // 2, high, low), 48)
            x = jnp.where(lane < 32, low, middle)
            extra.append(jnp.where(lane >= 64, turn(high, -24), x))
        writes = []
        for t, fields in enumerate(per_tile + [extra]):
            u0, v0, strength, covered, drive_x, drive_y = fields
            writes.append((base_u, (i + 1, slice(None), cut(t)), u0))
            writes.append((base_v, (i + 1, slice(None), cut(t)), v0))
            writes.append((third, (i, slice(None), cut(t)), covered * (1.0 / 3.0)))
            writes.append((force, (i, slice(None), cut(t)), strength * covered * (1.0 / 12.0)))
            writes.append((push_x, (i, slice(None), cut(t)), 0.5 * drive_x))
            writes.append((push_y, (i, slice(None), cut(t)), 0.5 * drive_y))
        y = lat * rows - HALO + sublane * count + i
        y = jnp.where(y >= row_total, 2 * row_total - 1 - y, y)
        coriolis = 0.5 * (2 * y + 1 - row_total).astype(F32) / row_total
        turning = 0.5 * coriolis
        scale = 3.0 / (DIAGONAL * DIAGONAL + turning * turning)
        writes.append((turn_a, (i,), DIAGONAL * scale))
        writes.append((turn_b, (i,), turning * scale))
        return writes

    in_groups_of(3, count, body, 17)
    wrap(base_u, count)
    wrap(base_v, count)


def advect(tracers, speeds, sea, halo, fields, levels, row_total):
    tiles, rows = sea.shape[:2]
    count = sublane_rows(rows)
    wide = LANES * (tiles + 1)
    looped = resident(count + 2, SUBLANES, wide)
    plain = resident(count, SUBLANES, wide)
    narrow = resident(count, SUBLANES, LANES)
    return pl.pallas_call(
        lambda *refs: advect_kernel(levels, row_total, *refs),
        in_specs=[VMEM_SPEC] * 5,
        out_specs=[VMEM_SPEC] * 9,
        out_shape=[
            resident(*tracers.shape), looped, looped, plain, plain, plain, plain, narrow, narrow,
        ],
        scratch_shapes=[pltpu.VMEM((tiles, rows, LANES), F32)] * 2,
        name="advect",
        compiler_params=pltpu.CompilerParams(vmem_limit_bytes=8 << 20),
        cost_estimate=pl.CostEstimate(flops=30000000, bytes_accessed=16 << 20, transcendentals=0),
    )(*[in_vmem(a) for a in (tracers, speeds, sea, halo, fields)])


def ice_kernel(levels, rows, *refs):
    (covered_in, tracers_in, speeds_in, inter_own, intra_own, inter_in, intra_in,
     base_u, base_v, third, force, push_x, push_y, turn_a, turn_b,
     temp_out, salt_out, u_out, v_out,
     moved, done, vel_u, vel_v, str_a, str_b, str_c,
     third_x, force_x, push_x_x, push_y_x, edges,
     out_sem, vel_sem) = refs
    tiles = tracers_in.shape[1]
    count = sublane_rows(rows)
    tracers = 2 * levels
    lane = lane_ids()
    own = pl.ds(HALO, rows)
    wide = tiles + 1
    whole = slice(None)

    even = on_even_lon()

    def sides(inter, intra):
        return jnp.where(even, inter, intra), jnp.where(even, intra, inter)

    def edge_fluxes(k):
        at, put = tile_rows(k + 1), tile_rows(k)
        west, east_side = sides(inter_in[at, :], intra_in[at, :])
        mine_w, mine_e = sides(inter_own[at, :], intra_own[at, :])
        speed = turn(west, -2 * tracers)
        inflow = speed * jnp.where(speed > 0, west, mine_w) * turn(mine_w, -2 * tracers)
        speed = turn(mine_e, -2 * tracers)
        outflow = speed * jnp.where(speed > 0, mine_e, east_side) * turn(east_side, -2 * tracers)
        flux = jnp.where(lane % 2 == TRACER_LANE % 2, inflow, turn(outflow, -1))
        return [(edges, (put, whole), flux)]

    straight(rows // SUBLANES, edge_fluxes, 8, 24)

    def fixed(f, put):
        flux = turn(edges[put, :], -(TRACER_LANE + 2 * f))
        low = tracers_in[f, 0, put, :] + jnp.where(lane == 0, flux, 0.0)
        return low, tracers_in[f, tiles - 1, put, :] - jnp.where(lane == LANES - 1, flux, 0.0)

    def insert(i):
        west, east_side = sides(spread(inter_in, i, count), spread(intra_in, i, count))
        writes = []
        targets = (
            (base_u, vel_u, 1, tiles, 1.0), (base_v, vel_v, 1, tiles, 1.0),
            (force, force_x, 0, 0, 1.0), (third, third_x, 0, 0, 1.0 / 3.0),
            (push_x, push_x_x, 0, 0, 0.5), (push_y, push_y_x, 0, 0, 0.5),
        )
        beyond = []
        for f in range(ICE):
            start = HALO * f + 2 * HALO
            x = jnp.where((lane >= start) & (lane < start + HALO), west, east_side)
            beyond.append(turn(x, 104 - HALO * f))
        beyond[2] = beyond[2] * beyond[3] * (1.0 / 12.0)
        for x, (source, target, shift, t, factor) in zip(beyond, targets):
            x = x if factor == 1.0 else x * factor
            x = jnp.where(lane >= 104, x, source[i + shift, :, cut(tiles)])
            writes.append((target, (i + shift, whole, cut(t)), x))
        own_lanes = slice(0, LANES * tiles)
        for source, target in ((base_u, vel_u), (base_v, vel_v)):
            writes.append((target, (i + 1, whole, own_lanes), source[i + 1, :, own_lanes]))
        for ref in (str_a, str_b, str_c):
            writes.append((ref, (i + 1,), jnp.zeros(ref.shape[1:], F32)))
        return writes

    straight(count, insert, 3, 17)
    wrap(vel_u, count)
    wrap(vel_v, count)

    def constant(ref, extra, i, t):
        return ref[i, :, cut(t)] if t < tiles else extra[i]

    def load_once(ref, name, seen, j, t):
        if (name, j, t) not in seen:
            seen[name, j, t] = ref[(j, whole) if t is None else (j, whole, cut(t))]
        return seen[name, j, t]

    share = rows // SUBLANES // SUBCYCLES
    items = [(k, f) for k in range(share) for f in range(tracers)]

    def fix(step, i):
        for k, f in items[len(items) * i // count : len(items) * (i + 1) // count]:
            put = pl.ds(pl.multiple_of((step * share + k) * SUBLANES, SUBLANES), SUBLANES)
            low, high = fixed(f, put)
            moved[f, 0, put, :] = low
            moved[f, tiles - 1, put, :] = high

    def fixed_rows(step):
        part = pl.ds(pl.multiple_of(step * share * SUBLANES, SUBLANES), share * SUBLANES)
        return [
            pltpu.make_async_copy(
                moved.at[pl.ds(levels * n + 1, levels - 1), t, part, :],
                out.at[pl.ds(1, levels - 1), part, pl.ds(LANES * t, LANES)],
                out_sem.at[step, n, t],
            )
            for n, out in enumerate((temp_out, salt_out))
            for t in range(tiles)
        ]

    def strain_stress(step):
        seen = {}
        for i in range(count):
            for t in range(wide):
                u, v = (load_once(r, n, seen, i + 1, t) for n, r in enumerate((vel_u, vel_v)))
                dudx, dvdx = turn(u, -1) - turn(u, 1), turn(v, -1) - turn(v, 1)
                dudy, dvdy = (
                    load_once(r, n, seen, i + 2, t) - load_once(r, n, seen, i, t)
                    for n, r in enumerate((vel_u, vel_v))
                )
                div, ten, shr = dudx + dvdy, dudx - dvdy, dudy + dvdx
                square = div * div + 0.25 * (ten * ten + shr * shr) + 1.0
                base = constant(force, force_x, i, t)
                zeta = base * lax.rsqrt(square)
                quarter = 0.25 * zeta
                even = zeta * div - base
                odd = quarter * ten
                for ref, new in (
                    (str_a, even + odd), (str_b, even - odd), (str_c, quarter * shr)
                ):
                    ref[i + 1, :, cut(t)] = new + (1.0 / 3.0) * ref[i + 1, :, cut(t)]
            fix(step, i)
        wrap(str_b, count)
        wrap(str_c, count)

    def momentum():
        seen = {}
        for i in range(count):
            ar, br = turn_a[i], turn_b[i]
            for t in range(wide):
                a = str_a[i + 1, :, cut(t)]
                s = load_once(str_c, 2, seen, i + 1, t)
                fx = (turn(a, -1) - turn(a, 1)) + (
                    load_once(str_c, 2, seen, i + 2, t) - load_once(str_c, 2, seen, i, t)
                )
                fy = (turn(s, -1) - turn(s, 1)) + (
                    load_once(str_b, 1, seen, i + 2, t) - load_once(str_b, 1, seen, i, t)
                )
                ru = (vel_u[i + 1, :, cut(t)] + constant(push_x, push_x_x, i, t)) + fx
                rv = (vel_v[i + 1, :, cut(t)] + constant(push_y, push_y_x, i, t)) + fy
                keep = constant(third, third_x, i, t)
                vel_u[i + 1, :, cut(t)] = (ar * ru + br * rv) * keep
                vel_v[i + 1, :, cut(t)] = (ar * rv - br * ru) * keep
        wrap(vel_u, count)
        wrap(vel_v, count)

    def subcycle(step, carry):
        strain_stress(step)
        for copy in fixed_rows(step):
            copy.start()
        momentum()
        return carry

    lax.fori_loop(0, SUBCYCLES, subcycle, 0)

    def gather(i):
        writes = []
        for n, ref in enumerate((vel_u, vel_v)):
            borders = ref[i + 1, :, cut(tiles)]
            middle, outer = turn(borders, -48), turn(borders, 24)
            low, high = ref[i + 1, :, cut(0)], ref[i + 1, :, cut(tiles - 1)]
            low = jnp.where(lane < HALO, borders, jnp.where(lane >= LANES - HALO, middle, low))
            high = jnp.where(lane < HALO, middle, jnp.where(lane >= LANES - HALO, outer, high))
            put = pl.ds(i, SUBLANES, stride=count)
            writes.append((done, (n, 0, put, whole), low))
            writes.append((done, (n, tiles - 1, put, whole), high))
        return writes

    straight(count, gather, 6, 51)
    finals = []
    for n, out in enumerate((u_out, v_out)):
        for t in range(tiles):
            finals.append(
                pltpu.make_async_copy(
                    done.at[n, t, own, :], out.at[:, pl.ds(LANES * t, LANES)], vel_sem.at[n, t]
                )
            )
            finals[-1].start()

    def warm(k):
        put, at = tile_rows(k), tile_rows(k + 1)
        writes = []
        for t in range(tiles):
            sst, sss = moved[0, t, put, :], moved[levels, t, put, :]
            slip_u = done[0, t, at, :] - speeds_in[0, t, put, :]
            slip_v = done[1, t, at, :] - speeds_in[levels, t, put, :]
            heat = HEAT_RATE * covered_in[3, t, at, :] * (1.0 + (slip_u * slip_u + slip_v * slip_v))
            heat = heat * (sst + FREEZE_SLOPE * sss)
            writes.append((moved, (0, t, put, whole), sst - heat))
            writes.append((moved, (levels, t, put, whole), sss - SALT_RATE * heat))
        return writes

    half = rows // SUBLANES // 2
    for h in range(2):
        straight(half, lambda k: warm(half * h + k), 6, half)
        part = pl.ds(half * h * SUBLANES, half * SUBLANES)
        for n, out in enumerate((temp_out, salt_out)):
            for t in range(tiles):
                finals.append(
                    pltpu.make_async_copy(
                        moved.at[levels * n, t, part, :],
                        out.at[0, part, pl.ds(LANES * t, LANES)],
                        out_sem.at[SUBCYCLES + h, n, t],
                    )
                )
                finals[-1].start()
    for step in range(SUBCYCLES):
        finals += fixed_rows(step)
    for copy in finals:
        copy.wait()


def ice_and_edges(operands, levels, rows, cols):
    tiles = cols // LANES
    count = sublane_rows(rows)
    deep = jax.ShapeDtypeStruct((levels, rows, cols), F32)
    flat = jax.ShapeDtypeStruct((rows, cols), F32)
    looped = pltpu.VMEM((count + 2, SUBLANES, LANES * (tiles + 1)), F32)
    narrow = pltpu.VMEM((count, SUBLANES, LANES), F32)
    return pl.pallas_call(
        lambda *refs: ice_kernel(levels, rows, *refs),
        in_specs=[VMEM_SPEC] * len(operands),
        out_specs=[ANY_SPEC] * 4,
        out_shape=[deep, deep, flat, flat],
        scratch_shapes=[
            pltpu.VMEM((2 * levels, tiles, rows, LANES), F32),
            pltpu.VMEM((2, tiles, count * SUBLANES, LANES), F32),
            looped, looped, looped, looped, looped,
            narrow, narrow, narrow, narrow, pltpu.VMEM((rows, LANES), F32),
            pltpu.SemaphoreType.DMA((SUBCYCLES + 2, 2, tiles)),
            pltpu.SemaphoreType.DMA((2, tiles)),
        ],
        name="ice",
        compiler_params=pltpu.CompilerParams(vmem_limit_bytes=20 << 20),
        cost_estimate=pl.CostEstimate(flops=60000000, bytes_accessed=16 << 20, transcendentals=0),
    )(*[in_vmem(a) for a in operands])


def per_device(*arrays):
    levels, rows, cols = arrays[0].shape
    lon_count, lat_count = lax.axis_size("lon"), lax.axis_size("lat")
    assert cols == 2 * LANES and rows % (SUBLANES * SUBCYCLES) == 0
    assert lat_count % 2 == 0 and lon_count % 2 == 0
    height = -(-(HALO * ICE + 3 * levels) // SUBLANES) * SUBLANES

    def place(lat, lon):
        return lon * lat_count + lat

    first_pairs, second_pairs = [], []
    for lon in range(lon_count):
        for lat in range(lat_count):
            first_pairs.append((place(lat, lon), place(lat ^ 1, lon)))
            if lat == lat_count - 1:
                second_pairs.append((place(lat, lon), place(lat, lon_count - 1 - lon)))
            elif lat:
                second_pairs.append((place(lat, lon), place(((lat + 1) ^ 1) - 1, lon)))
    inter_pairs = [(i, (i - 1 if i % 2 == 0 else i + 1) % lon_count) for i in range(lon_count)]
    intra_pairs = [(i, i ^ 1) for i in range(lon_count)]
    first, second = pack_rows(arrays, levels, rows, cols, height)
    first = lax.ppermute(first, ("lon", "lat"), first_pairs)
    second = lax.ppermute(second, ("lon", "lat"), second_pairs)
    tracers, speeds, sea, fields, inter, intra = load_and_pack_columns(arrays, levels, rows, cols)
    halo, fields, inter, intra = merge_halo(first, second, fields, inter, intra, levels, rows)
    intra_in = lax.ppermute(intra, "lon", intra_pairs)
    inter_in = lax.ppermute(inter, "lon", inter_pairs)
    moved, *state = advect(tracers, speeds, sea, halo, fields, levels, rows * lat_count)
    return ice_and_edges(
        [fields, moved, speeds, inter, intra, inter_in, intra_in, *state], levels, rows, cols
    )


def solution(mesh):
    deep, flat = P(None, "lat", "lon"), P("lat", "lon")
    return jax.shard_map(
        per_device,
        mesh=mesh,
        in_specs=(deep,) * 4 + (flat,) * 7,
        out_specs=(deep, deep, flat, flat),
        check_vma=False,
    )
```
